32 devices in a mesh: dp: 2 (over x), blk: 4 (over y, core), head: 4 (over z).
Axes of the slice: x: 2, y: 2, z: 4, core: 2. Of those that a mesh axis runs over, the one named last changes fastest.
Arguments:
- hidden: bfloat16 [2, 4096, 2048], P('dp', ('blk', 'head')), may hold values from -6 to 6
- teacher: bfloat16 [2, 4096, 2048], P('dp', ('blk', 'head')), may hold values from -6 to 6
- lengths: int32 [2], P('dp'), may hold values from 3073 to 4096, as said below
- attn_gain: bfloat16 [2048], P(('dp', 'blk', 'head')), may hold values from 0.5 to 1.5
- w_query: bfloat16 [2048, 2048], P(('dp', 'blk', 'head')), may hold values from -0.4375 to 0.4375
- key_projection: bfloat16 [2048, 512], P(('dp', 'blk', 'head')), may hold values from -0.4375 to 0.4375
- value_projection: bfloat16 [2048, 512], P(('dp', 'blk', 'head')), may hold values from -0.125 to 0.125
- w_out: bfloat16 [2048, 2048], P(('dp', 'blk', 'head')), may hold values from -4 to 4
- mlp_gain: bfloat16 [2048], P(('dp', 'blk', 'head')), may hold values from 0.5 to 1.5
- w_gate: bfloat16 [2048, 8192], P(('dp', 'blk', 'head')), may hold values from -0.125 to 0.125
- w_up: bfloat16 [2048, 8192], P(('dp', 'blk', 'head')), may hold values from -0.125 to 0.125
- w_down: bfloat16 [8192, 2048], P(('dp', 'blk', 'head')), may hold values from -0.25 to 0.25
Outputs:
- output: bfloat16 [2, 4096, 2048], P('dp', ('blk', 'head'))
- mse_loss: float32 [], replicated
- grad_hidden: float32 [2, 4096, 2048], P('dp', ('blk', 'head'))
- grad_attn_gain: float32 [2048], P(('dp', 'blk', 'head'))
- grad_query: float32 [2048, 2048], P(('dp', 'blk', 'head'))
- grad_key: float32 [2048, 512], P(('dp', 'blk', 'head'))
- grad_value: float32 [2048, 512], P(('dp', 'blk', 'head'))
- grad_out: float32 [2048, 2048], P(('dp', 'blk', 'head'))
- grad_mlp_gain: float32 [2048], P(('dp', 'blk', 'head'))
- grad_gate: float32 [2048, 8192], P(('dp', 'blk', 'head'))
- grad_up: float32 [2048, 8192], P(('dp', 'blk', 'head'))
- grad_down: float32 [8192, 2048], P(('dp', 'blk', 'head'))
The draws below stay inside these ranges and needn't reach their ends.
Inputs may be any that keep to these rules, and one draw needn't show every extreme that they name: `lengths`: in every draw some sequence has all 4096 slots valid; unused slots of a sequence lie within its last 1024 slots.
All inputs are finite; a program needn't handle non-finite values.
Results may differ from the reference program's by a relative error of at most 0.014.
Values may be sent and summed in bfloat16 or wider, within the bound.
A program may use at most 448 MiB of HBM per device.

```python
import jax
import jax.numpy as jnp
from jax import lax

MODEL_WIDTH = 2048
FF = 8192
QUERY_HEADS = 32
KEY_VALUE_HEADS = 8
HEAD_SIZE = 64
SEQ_LEN = 4096
SEQS = 2


def draw_lengths(key, part):
    key = jax.random.fold_in(key, 7)
    order_key, length_key = jax.random.split(key)
    shortest = SEQ_LEN - SEQ_LEN // 4 + 1
    full_one = jax.random.randint(order_key, (), 0, SEQS)
    drawn_lengths = jax.random.randint(length_key, (SEQS,), shortest, SEQ_LEN + 1)
    places = jnp.arange(SEQS)
    lengths = jnp.where(places == full_one, SEQ_LEN, drawn_lengths)
    return lengths.astype(jnp.int32)


def level_of(own_key, dims, cuts, low, top_value):
    def one(position, shards_of):
        draws = jax.random.uniform(jax.random.fold_in(jax.random.fold_in(own_key, 6), position), (shards_of,), jnp.float32, low / len(cuts), top_value / len(cuts))
        return jnp.repeat(jnp.exp(draws), dims[position] // shards_of).reshape((-1,) + (1,) * (len(dims) - position - 1))

    factor_of = one(*cuts[0])
    for cut in cuts[1:]:
        factor_of = factor_of * one(*cut)
    return factor_of


def scatter_about(stream_key, extent, scale, most, shards=(), held_as=jnp.bfloat16):
    entries = scale * jax.random.normal(stream_key, extent, jnp.float32)
    if shards:
        entries = entries * level_of(stream_key, extent, shards, -0.22, 0.18)
    return jnp.clip(entries, -most, most).astype(held_as)


def setup_inputs(seed: int = 0) -> dict:
    key_list = jax.random.split(jax.random.key(seed), 13)
    return {
        "hidden": scatter_about(key_list[0], (SEQS, SEQ_LEN, MODEL_WIDTH), 1.0, 6.0, ((0, 2), (1, 16))),
        "teacher": scatter_about(key_list[1], (SEQS, SEQ_LEN, MODEL_WIDTH), 1.0, 6.0, ((0, 2), (1, 16))),
        "lengths": draw_lengths(jax.random.fold_in(key_list[12], 71), 0),
        "attn_gain": jnp.clip(1.0 + 0.1 * jax.random.normal(key_list[3], (MODEL_WIDTH,), jnp.float32), 0.5, 1.5).astype(jnp.bfloat16),
        "w_query": scatter_about(key_list[4], (MODEL_WIDTH, QUERY_HEADS * HEAD_SIZE), (MODEL_WIDTH // 12) ** -0.5, 0.4375, ((0, 32),)),
        "key_projection": scatter_about(key_list[5], (MODEL_WIDTH, KEY_VALUE_HEADS * HEAD_SIZE), (MODEL_WIDTH // 12) ** -0.5, 0.4375, ((0, 32),)),
        "value_projection": scatter_about(key_list[6], (MODEL_WIDTH, KEY_VALUE_HEADS * HEAD_SIZE), MODEL_WIDTH ** -0.5, 0.125, ((0, 32),)),
        "w_out": scatter_about(key_list[7], (QUERY_HEADS * HEAD_SIZE, MODEL_WIDTH), (max(1, MODEL_WIDTH // 1024)) ** -0.5, 4.0, ((0, 32),)),
        "mlp_gain": jnp.clip(1.0 + 0.1 * jax.random.normal(key_list[8], (MODEL_WIDTH,), jnp.float32), 0.5, 1.5).astype(jnp.bfloat16),
        "w_gate": scatter_about(key_list[9], (MODEL_WIDTH, FF), MODEL_WIDTH ** -0.5, 0.125, ((0, 32),)),
        "w_up": scatter_about(key_list[10], (MODEL_WIDTH, FF), MODEL_WIDTH ** -0.5, 0.125, ((0, 32),)),
        "w_down": scatter_about(key_list[11], (FF, MODEL_WIDTH), (FF // 16) ** -0.5, 0.25, ((0, 32),)),
    }


@jax.custom_vjp
def reduced_cast(v):
    return lax.optimization_barrier(v.astype(jnp.bfloat16)).astype(jnp.float32)

@jax.custom_vjp
def reduced_cast_back(v):
    return v

def low_keep(v):
    return (reduced_cast(v), None)

def low_pass(kept, grad):
    return (grad,)

def back_keep(v):
    return (v, None)

def back_low(kept, grad):
    return (reduced_cast(grad),)
reduced_cast.defvjp(low_keep, low_pass)
reduced_cast_back.defvjp(back_keep, back_low)
ROPE_BASE = 10000000.0
NORM_EPS = 1e-05
ATTN_SCALE = 0.015625
RESIDUAL_SCALE = 0.22
TOP_PRECISION = lax.Precision.HIGHEST

def rms_norm(values, gain_vec):
    inverse_rms = lax.rsqrt(lax.optimization_barrier(jnp.mean(values * values, axis=-1, keepdims=True)) + NORM_EPS)
    return values * inverse_rms * gain_vec

def apply_rotary(values, head_count):
    length = values.shape[0]
    half_size = HEAD_SIZE // 2
    frequency = ROPE_BASE ** (-(jnp.arange(half_size).astype(jnp.float32) * 2.0) / HEAD_SIZE)
    angles = jnp.arange(length).astype(jnp.float32)[:, None] * frequency[None, :]
    cosine = jnp.concatenate([jnp.cos(angles), jnp.cos(angles)], axis=1)[:, None, :]
    sine_table = jnp.concatenate([jnp.sin(angles), jnp.sin(angles)], axis=1)[:, None, :]
    pieces = values.reshape(length, head_count, HEAD_SIZE)
    turned = jnp.concatenate([-pieces[..., half_size:], pieces[..., :half_size]], axis=-1)
    return (pieces * cosine + turned * sine_table).reshape(length, head_count * HEAD_SIZE)

def attend_head(query_one, key_one, value_one, allowed):
    scores = reduced_cast_back(jnp.dot(query_one, key_one.T, precision=TOP_PRECISION) * ATTN_SCALE)
    scores = jnp.where(allowed, scores, -1e+30)
    weights = jax.nn.softmax(scores, axis=-1)
    return jnp.dot(reduced_cast(weights), value_one, precision=TOP_PRECISION)

def layer(inputs, length, attn_gain, w_query, key_projection, value_projection, w_out, mlp_gain, w_gate, w_up, w_down):
    sequence_length = inputs.shape[0]
    places = jnp.arange(sequence_length)
    allowed = (places[None, :] <= places[:, None]) & (places[None, :] < length)
    normalized_rows = reduced_cast(rms_norm(inputs, attn_gain))
    queries = reduced_cast_back(reduced_cast(apply_rotary(reduced_cast_back(jnp.dot(normalized_rows, w_query, precision=TOP_PRECISION)), QUERY_HEADS)))
    key_row_block = reduced_cast_back(reduced_cast(apply_rotary(reduced_cast_back(jnp.dot(normalized_rows, key_projection, precision=TOP_PRECISION)), KEY_VALUE_HEADS)))
    value_row_block = reduced_cast_back(reduced_cast(jnp.dot(normalized_rows, value_projection, precision=TOP_PRECISION)))
    heads_per_group = QUERY_HEADS // KEY_VALUE_HEADS
    query_heads = queries.reshape(sequence_length, QUERY_HEADS, HEAD_SIZE).transpose(1, 0, 2)
    key_head_split = jnp.repeat(key_row_block.reshape(sequence_length, KEY_VALUE_HEADS, HEAD_SIZE).transpose(1, 0, 2), heads_per_group, axis=0)
    value_head_split = jnp.repeat(value_row_block.reshape(sequence_length, KEY_VALUE_HEADS, HEAD_SIZE).transpose(1, 0, 2), heads_per_group, axis=0)

    def one_head(triple):
        return attend_head(triple[0], triple[1], triple[2], allowed)
    mixed_heads = lax.map(jax.checkpoint(one_head), (query_heads, key_head_split, value_head_split))
    mixed_rows = reduced_cast_back(reduced_cast(mixed_heads.transpose(1, 0, 2).reshape(sequence_length, QUERY_HEADS * HEAD_SIZE)))
    attended = reduced_cast_back(jnp.dot(mixed_rows, w_out, precision=TOP_PRECISION))
    middle = inputs + RESIDUAL_SCALE * attended
    normed_two = reduced_cast(rms_norm(middle, mlp_gain))
    gate_proj = reduced_cast_back(jnp.dot(normed_two, w_gate, precision=TOP_PRECISION))
    upward = reduced_cast_back(jnp.dot(normed_two, w_up, precision=TOP_PRECISION))
    hidden_units = reduced_cast(jax.nn.silu(gate_proj) * upward)
    return middle + RESIDUAL_SCALE * reduced_cast_back(jnp.dot(hidden_units, w_down, precision=TOP_PRECISION))

def reference(hidden, teacher, lengths, attn_gain, w_query, key_projection, value_projection, w_out, mlp_gain, w_gate, w_up, w_down):
    params = tuple((weight.astype(jnp.float32) for weight in (attn_gain, w_query, key_projection, value_projection, w_out, mlp_gain, w_gate, w_up, w_down)))
    valid_count = jnp.sum(lengths).astype(jnp.float32)
    factor = SEQS * SEQ_LEN / valid_count
    places = jnp.arange(SEQ_LEN)

    def one_sequence(state_in, seq_item):
        sq_total, grad_sums = state_in
        seq_in, seq_teacher, length = seq_item

        def objective(inputs, weights):
            result = layer(inputs, length, *weights)
            misfit = jnp.where((places < length)[:, None], result - seq_teacher, 0.0)
            return (jnp.sum(misfit * misfit), result)
        squares, pull_back, result = jax.vjp(objective, seq_in, params, has_aux=True)
        grad_in, grad_weights = pull_back(0.5 * factor)
        grad_sums = jax.tree.map(lambda total, extra: total + extra, grad_sums, grad_weights)
        return ((sq_total + squares, grad_sums), (result.astype(jnp.bfloat16), grad_in))
    start_state = (jnp.zeros((), jnp.float32), jax.tree.map(jnp.zeros_like, params))
    (sq_total, grad_sums), (outputs, grad_inputs) = lax.scan(one_sequence, start_state, (hidden.astype(jnp.float32), teacher.astype(jnp.float32), lengths))
    total_loss = sq_total / (MODEL_WIDTH * valid_count)
    return (outputs, total_loss, grad_inputs, grad_sums[0], grad_sums[1], grad_sums[2], grad_sums[3], grad_sums[4], grad_sums[5], grad_sums[6], grad_sums[7], grad_sums[8])
```

```python
import functools

import jax
import jax.numpy as jnp
from jax import lax
from jax.experimental import pallas as pl
from jax.experimental.pallas import tpu as pltpu
from jax.sharding import Mesh, PartitionSpec as P

MODEL_WIDTH = 2048
HEAD_SIZE = 64
ROPE_BASE = 10000000.0
NORM_EPS = 1e-05
ATTN_SCALE = 0.015625
RESIDUAL_SCALE = 0.22
MASKED = -1e30

ALL = ("dp", "blk", "hi", "lo")
SQUARE = ("blk", "lo")
COPIES = ("dp", "hi")
SEQ = ("blk", "hi", "lo")
F32 = jnp.float32
BF16 = jnp.bfloat16
VMEM_LIMIT = 56 * 1024 * 1024


def dot32(a, b, dims=((1,), (0,))):
    return lax.dot_general(a, b, (dims, ((), ())), preferred_element_type=F32)


def proj_kernel(rows_ref, weight_ref, cos_ref, sina_ref, sinb_ref, out_ref):
    made = dot32(rows_ref[...], weight_ref[...])
    cosine, sina, sinb = cos_ref[...], sina_ref[...], sinb_ref[...]
    low = lanes_low(cosine.shape)
    half = HEAD_SIZE // 2
    for part in range(3):
        u = made[:, 128 * part : 128 * part + 128]
        up, down = pltpu.roll(u, 128 - half, 1), pltpu.roll(u, half, 1)
        turned = u * cosine + up * sina + down * sinb
        if part < 2:
            out_ref[:, 128 * part : 128 * part + 128] = (
                turned.astype(BF16).astype(F32) * ATTN_SCALE
            ).astype(BF16)
        else:
            out_ref[:, 256:384] = jnp.where(low, turned, u).astype(BF16)


def project(rows, weight, tables, tile):
    count, depth = rows.shape
    wide = weight.shape[1]
    table_spec = pl.BlockSpec((tile, 128), lambda i: (i, 0))
    return pl.pallas_call(
        proj_kernel,
        grid=(count // tile,),
        in_specs=[
            pl.BlockSpec((tile, depth), lambda i: (i, 0)),
            pl.BlockSpec((depth, wide), lambda i: (0, 0)),
            table_spec,
            table_spec,
            table_spec,
        ],
        out_specs=pl.BlockSpec((tile, wide), lambda i: (i, 0)),
        out_shape=jax.ShapeDtypeStruct((count, wide), BF16),
        compiler_params=pltpu.CompilerParams(vmem_limit_bytes=VMEM_LIMIT),
        cost_estimate=pl.CostEstimate(
            flops=2 * count * depth * wide, bytes_accessed=4 * count * depth, transcendentals=0
        ),
        name="project",
    )(rows, weight, *tables)


def back_rope_kernel(dq_ref, own_ref, other_ref, cos_ref, sina_ref, sinb_ref, out_ref):
    cosine, sina, sinb = cos_ref[...], sina_ref[...], sinb_ref[...]
    low = lanes_low(cosine.shape)
    half = HEAD_SIZE // 2
    shared = (own_ref[...].astype(F32) + other_ref[...].astype(F32)).astype(BF16)
    for part in range(3):
        w = (dq_ref[:, 128 * part : 128 * part + 128] if part < 2 else shared).astype(F32)
        turned = w * cosine + pltpu.roll(w * sinb, 128 - half, 1) + pltpu.roll(w * sina, half, 1)
        if part == 2:
            turned = jnp.where(low, turned, w)
        out_ref[:, 128 * part : 128 * part + 128] = turned.astype(BF16)


def back_rope(dq, own, other, tables, tile):
    count = dq.shape[0]
    rows = lambda wide: pl.BlockSpec((tile, wide), lambda i: (i, 0))
    return pl.pallas_call(
        back_rope_kernel,
        grid=(count // tile,),
        in_specs=[rows(256)] + [rows(128)] * 5,
        out_specs=rows(384),
        out_shape=jax.ShapeDtypeStruct((count, 384), BF16),
        compiler_params=pltpu.CompilerParams(vmem_limit_bytes=VMEM_LIMIT),
        name="back_rope",
    )(dq, own, other, *tables)


def lanes_low(shape):
    return lax.broadcasted_iota(jnp.int32, shape, 1) < HEAD_SIZE


def both_keys(kv):
    low = lanes_low(kv.shape)
    keys = kv.astype(F32)
    return (
        jnp.where(low, keys, 0.0).astype(BF16),
        jnp.where(low, 0.0, pltpu.roll(keys, HEAD_SIZE, 1)).astype(BF16),
    )


def both_values(kv):
    low = lanes_low(kv.shape)
    values = kv.astype(F32)
    return (
        jnp.where(low, pltpu.roll(values, HEAD_SIZE, 1), 0.0).astype(BF16),
        jnp.where(low, 0.0, values).astype(BF16),
    )


def attend_kernel(scalar_ref, qkv_ref, other_ref, out_ref, log_ref, keys, values, peak, sums):
    b = pl.program_id(0)
    blocks, unit, _ = qkv_ref.shape
    units = 2 * blocks
    length, hi = scalar_ref[0], scalar_ref[1]
    n = 2 * b + hi

    @pl.when(b == 0)
    def _():
        def spread(c, carry):
            for j, kv in (
                (2 * c + hi, qkv_ref[c, :, 256:384]),
                (2 * c + 1 - hi, other_ref[c]),
            ):
                keys[0, j], keys[1, j] = both_keys(kv)
                across = jnp.transpose(kv.astype(F32))[HEAD_SIZE:, :]
                values[j] = jnp.concatenate(
                    [across, jnp.ones((16, unit), F32)], axis=0
                ).astype(BF16)
            return carry

        lax.fori_loop(0, blocks, spread, 0)

    peak[...] = jnp.full_like(peak, MASKED)
    sums[...] = jnp.zeros_like(sums)

    def step(j, masked):
        for h in range(4):
            query = qkv_ref[b, :, 128 * (h // 2) : 128 * (h // 2) + 128]
            scores = dot32(keys[h % 2, j], query, ((1,), (1,)))
            if masked:
                row = j * unit + lax.broadcasted_iota(jnp.int32, scores.shape, 0)
                col = n * unit + lax.broadcasted_iota(jnp.int32, scores.shape, 1)
                scores = jnp.where((row <= col) & (row < length), scores, MASKED)
            old = peak[h, 0:1, :]
            new = jnp.maximum(old, jnp.max(scores, axis=0, keepdims=True))
            weights = jnp.exp(scores - new).astype(BF16)
            sums[h] = sums[h] * jnp.exp(old - new) + dot32(values[j], weights)
            peak[h, 0:1, :] = new

    first_ragged = units - units // 4

    def plain(j, carry):
        step(j, False)
        return carry

    def checked(j, carry):
        step(j, True)
        return carry

    lax.fori_loop(0, jnp.minimum(n, first_ragged), plain, 0)
    lax.fori_loop(jnp.minimum(n, first_ragged), n + 1, checked, 0)

    for pair in range(2):
        parts = []
        for h in (2 * pair, 2 * pair + 1):
            total = sums[h, HEAD_SIZE : HEAD_SIZE + 1, :]
            parts.append(sums[h, 0:HEAD_SIZE, :] / total)
            log_ref[0, h : h + 1, :] = peak[h, 0:1, :] + jnp.log(total)
        out_ref[0, :, 128 * pair : 128 * pair + 128] = jnp.transpose(
            jnp.concatenate(parts, axis=0)
        ).astype(BF16)


def attend(scalars, qkv, other):
    blocks, unit, _ = qkv.shape
    units = 2 * blocks
    whole = lambda a: pl.BlockSpec(a.shape, lambda i: (0,) * a.ndim)
    return pl.pallas_call(
        attend_kernel,
        grid=(blocks,),
        in_specs=[pl.BlockSpec(memory_space=pltpu.SMEM), whole(qkv), whole(other)],
        out_specs=[
            pl.BlockSpec((1, unit, 256), lambda i: (i, 0, 0)),
            pl.BlockSpec((1, 8, unit), lambda i: (i, 0, 0)),
        ],
        out_shape=[
            jax.ShapeDtypeStruct((blocks, unit, 256), BF16),
            jax.ShapeDtypeStruct((blocks, 8, unit), F32),
        ],
        scratch_shapes=[
            pltpu.VMEM((2, units, unit, 128), BF16),
            pltpu.VMEM((units, HEAD_SIZE + 16, unit), BF16),
            pltpu.VMEM((4, 8, unit), F32),
            pltpu.VMEM((4, HEAD_SIZE + 16, unit), F32),
        ],
        compiler_params=pltpu.CompilerParams(vmem_limit_bytes=VMEM_LIMIT),
        cost_estimate=pl.CostEstimate(
            flops=40_000_000_000, bytes_accessed=8_000_000, transcendentals=20_000_000
        ),
        name="attend",
    )(scalars, qkv, other)


def attend_back_kernel(
    scalar_ref, qkv_ref, other_ref, dout_ref, out_ref, log_ref, dq_ref, dkv_ref, delta, dq, dk, dv
):
    j = pl.program_id(0)
    blocks, unit, _ = qkv_ref.shape
    units = 2 * blocks
    length, hi = scalar_ref[0], scalar_ref[1]

    @pl.when(j == 0)
    def _():
        dq[...] = jnp.zeros_like(dq)
        pick = jnp.where(
            lax.broadcasted_iota(jnp.int32, (8, 256), 0)
            == lax.broadcasted_iota(jnp.int32, (8, 256), 1) // HEAD_SIZE,
            1.0,
            0.0,
        )

        def dots(b, carry):
            product = dout_ref[b].astype(F32) * out_ref[b].astype(F32)
            delta[b] = lax.dot_general(
                pick,
                product,
                (((1,), (1,)), ((), ())),
                precision=lax.Precision.HIGHEST,
                preferred_element_type=F32,
            )
            return carry

        lax.fori_loop(0, blocks, dots, 0)

    foreign = jnp.where(j % 2 == hi, 0, 1)
    kv = jnp.where(foreign == 0, qkv_ref[j // 2, :, 256:384], other_ref[j // 2])
    keys, values = both_keys(kv), both_values(kv)
    dk[...] = jnp.zeros_like(dk)
    dv[...] = jnp.zeros_like(dv)

    def step(b, masked):
        n = 2 * b + hi
        for pair in range(2):
            lanes = slice(128 * pair, 128 * pair + 128)
            query = qkv_ref[b, :, lanes]
            dout = dout_ref[b, :, lanes]
            dq_part = None
            for side in range(2):
                h = 2 * pair + side
                scores = dot32(keys[side], query, ((1,), (1,)))
                weights = jnp.exp(scores - log_ref[b, h : h + 1, :])
                if masked:
                    row = j * unit + lax.broadcasted_iota(jnp.int32, scores.shape, 0)
                    col = n * unit + lax.broadcasted_iota(jnp.int32, scores.shape, 1)
                    weights = jnp.where((row <= col) & (row < length), weights, 0.0)
                dweights = dot32(values[side], dout, ((1,), (1,)))
                dscores = (weights * (dweights - delta[b, h : h + 1, :])).astype(BF16)
                dv[side] += dot32(weights.astype(BF16), dout)
                dk[side] += dot32(dscores, query)
                part = dot32(dscores, keys[side], ((0,), (0,)))
                dq_part = part if dq_part is None else dq_part + part
            dq[b, :, lanes] += dq_part

    first_ragged = units - units // 4

    def plain(b, carry):
        step(b, False)
        return carry

    def checked(b, carry):
        step(b, True)
        return carry

    first = (j + 1 - hi) // 2
    masked_until = jnp.where(j >= first_ragged, blocks, jnp.where(foreign == 0, first + 1, first))
    lax.fori_loop(first, masked_until, checked, 0)
    lax.fori_loop(masked_until, blocks, plain, 0)

    low = lanes_low((unit, 128))
    dkey = dk[0] + pltpu.roll(dk[1], HEAD_SIZE, 1)
    dvalue = pltpu.roll(dv[0], HEAD_SIZE, 1) + dv[1]
    dkv_ref[foreign, j // 2] = jnp.where(low, dkey, dvalue).astype(BF16)

    @pl.when(j == units - 1)
    def _():
        def store(b, carry):
            dq_ref[b] = (dq[b] * ATTN_SCALE).astype(BF16)
            return carry

        lax.fori_loop(0, blocks, store, 0)


def attend_back(scalars, qkv, other, dout, out, log):
    blocks, unit, _ = qkv.shape
    units = 2 * blocks
    whole = lambda a: pl.BlockSpec(a.shape, lambda i: (0,) * a.ndim)
    dq_shape = jax.ShapeDtypeStruct((blocks, unit, 256), BF16)
    dkv_shape = jax.ShapeDtypeStruct((2, blocks, unit, 128), BF16)
    return pl.pallas_call(
        attend_back_kernel,
        grid=(units,),
        in_specs=[
            pl.BlockSpec(memory_space=pltpu.SMEM),
            whole(qkv),
            whole(other),
            whole(dout),
            whole(out),
            whole(log),
        ],
        out_specs=[whole(dq_shape), whole(dkv_shape)],
        out_shape=[dq_shape, dkv_shape],
        scratch_shapes=[
            pltpu.VMEM((blocks, 8, unit), F32),
            pltpu.VMEM((blocks, unit, 256), F32),
            pltpu.VMEM((2, unit, 128), F32),
            pltpu.VMEM((2, unit, 128), F32),
        ],
        compiler_params=pltpu.CompilerParams(vmem_limit_bytes=VMEM_LIMIT),
        cost_estimate=pl.CostEstimate(
            flops=60_000_000_000, bytes_accessed=10_000_000, transcendentals=20_000_000
        ),
        name="attend_back",
    )(scalars, qkv, other, dout, out, log)


PIECES = 4
MESH_ID = pl.DeviceIdType.MESH


def square_places():
    blk, lo = lax.axis_index("blk"), lax.axis_index("lo")
    mate, side = blk + 1 - 2 * (blk % 2), (blk + 2) % 4
    return blk, lo, mate, side


def greet(ids):
    barrier = pltpu.get_barrier_semaphore()
    for one in ids:
        pl.semaphore_signal(barrier, inc=1, device_id=one, device_id_type=MESH_ID)
    pl.semaphore_wait(barrier, len(ids))


def gather_kernel(rows_ref, out_ref, send, recv, local):
    blk, lo, mate, side = square_places()
    slot = lambda b, l: b * 2 + l
    mine = slot(blk, lo)
    to_mate, to_side, to_next = {"blk": mate}, {"blk": side}, {"lo": 1 - lo}
    greet([to_mate, to_side, to_next])
    step = rows_ref.shape[0] // PIECES

    def push(source, place, piece, kind, to):
        rows = pl.ds(piece * step, step)
        copy = pltpu.make_async_remote_copy(
            src_ref=source,
            dst_ref=out_ref.at[place, rows],
            send_sem=send.at[kind, piece],
            recv_sem=recv.at[kind, piece],
            device_id=to,
            device_id_type=MESH_ID,
        )
        copy.start()
        return copy

    own = pltpu.make_async_copy(rows_ref, out_ref.at[mine], local)
    own.start()
    piece_of = lambda p: rows_ref.at[pl.ds(p * step, step)]
    held = lambda place, p: out_ref.at[place, pl.ds(p * step, step)]
    side_order, next_order = (2, 3, 0, 1), (0, 1, 2, 3)
    by_side, by_next, by_mate, across = {}, {}, [], {}
    for k in range(PIECES):
        p, q = side_order[k], next_order[k]
        by_side[p] = push(piece_of(p), mine, p, 0, to_side)
        by_next[q] = push(piece_of(q), mine, q, 1, to_next)
    for p in range(PIECES):
        by_mate.append(push(piece_of(p), mine, p, 3, to_mate))
    from_side, from_next, from_across = slot(side, lo), slot(blk, 1 - lo), slot(side, 1 - lo)
    for k in range(PIECES):
        p, q = side_order[k], next_order[k]
        by_side[p].wait_recv()
        if p >= 2:
            across[p] = push(held(from_side, p), from_side, p, 2, to_next)
        by_mate.append(push(held(from_side, p), from_side, p, 4, to_mate))
        by_next[q].wait_recv()
        if q < 2:
            across[q] = push(held(from_next, q), from_next, q, 2, to_side)
        by_mate.append(push(held(from_next, q), from_next, q, 5, to_mate))
    for p in (0, 2, 1, 3):
        across[p].wait_recv()
        by_mate.append(push(held(from_across, p), from_across, p, 6, to_mate))
    for copy in by_mate:
        copy.wait()
    for copies in (by_side, by_next, across):
        for copy in copies.values():
            copy.wait_send()
    own.wait()


def gather_square(rows, number):
    tok, width = rows.shape
    return pl.pallas_call(
        gather_kernel,
        in_specs=[pl.BlockSpec(memory_space=pl.ANY)],
        out_specs=pl.BlockSpec(memory_space=pl.ANY),
        out_shape=jax.ShapeDtypeStruct((8, tok, width), rows.dtype),
        scratch_shapes=[
            pltpu.SemaphoreType.DMA((7, PIECES)),
            pltpu.SemaphoreType.DMA((7, PIECES)),
            pltpu.SemaphoreType.DMA,
        ],
        compiler_params=pltpu.CompilerParams(collective_id=number, has_side_effects=True),
        cost_estimate=pl.CostEstimate(flops=0, bytes_accessed=120_000_000, transcendentals=0),
        name="gather_square",
    )(rows).reshape(8 * tok, width)


def scatter_kernel(
    parts_ref, out_ref, mine, mates, made, got_across, got_side, got_next, send, recv, local
):
    blk, lo, mate, side = square_places()
    slot = lambda b, l: b * 2 + l
    to_mate, to_side, to_next = {"blk": mate}, {"blk": side}, {"lo": 1 - lo}
    mate_side = (mate + 2) % 4
    own_slots = (slot(side, 1 - lo), slot(side, lo), slot(blk, 1 - lo), slot(blk, lo))
    mate_slots = (slot(mate_side, 1 - lo), slot(mate_side, lo), slot(mate, 1 - lo), slot(mate, lo))
    step = parts_ref.shape[1] // PIECES
    loads = []
    for k in range(4):
        copy = pltpu.make_async_copy(parts_ref.at[own_slots[k]], mine.at[k], local.at[k])
        copy.start()
        loads.append(copy)
    greet([to_mate, to_side, to_next])

    def push(source, target, kind, piece, to):
        copy = pltpu.make_async_remote_copy(
            src_ref=source,
            dst_ref=target,
            send_sem=send.at[kind, piece],
            recv_sem=recv.at[kind, piece],
            device_id=to,
            device_id_type=MESH_ID,
        )
        copy.start()
        return copy

    rows = lambda p: pl.ds(p * step, step)
    orders = ((0, 2, 1, 3), (0, 1, 2, 3), (2, 3, 0, 1), (0, 1, 2, 3))
    from_mate = {}
    for k in range(4):
        for p in orders[k]:
            from_mate[k, p] = push(
                parts_ref.at[mate_slots[k], rows(p)], mates.at[k, rows(p)], k, p, to_mate
            )

    def summed(k, p):
        from_mate[k, p].wait_recv()
        return mine[k, rows(p), :].astype(F32) + mates[k, rows(p), :].astype(F32)

    sent = {}
    loads[0].wait()
    for p in orders[0]:
        made[0, rows(p), :] = summed(0, p).astype(BF16)
        sent[0, p] = push(
            made.at[0, rows(p)],
            got_across.at[rows(p)],
            4,
            p,
            to_side if p < 2 else to_next,
        )
    loads[1].wait()
    loads[2].wait()
    for k, p in ((1, 0), (2, 2), (1, 1), (2, 3), (1, 2), (2, 0), (1, 3), (2, 1)):
        total = summed(k, p)
        if (k == 1) == (p >= 2):
            sent[0, p].wait_recv()
            total = total + got_across[rows(p), :].astype(F32)
        made[k, rows(p), :] = total.astype(BF16)
        sent[k, p] = push(
            made.at[k, rows(p)],
            (got_side if k == 1 else got_next).at[rows(p)],
            4 + k,
            p,
            to_side if k == 1 else to_next,
        )
    loads[3].wait()
    for p in range(PIECES):
        total = summed(3, p)
        sent[1, p].wait_recv()
        sent[2, p].wait_recv()
        out_ref[rows(p), :] = (
            total + got_side[rows(p), :].astype(F32) + got_next[rows(p), :].astype(F32)
        )
    for copy in from_mate.values():
        copy.wait_send()
    for copy in sent.values():
        copy.wait_send()


def scatter_square(parts, number):
    count, width = parts.shape
    tok = count // 8
    return pl.pallas_call(
        scatter_kernel,
        in_specs=[pl.BlockSpec(memory_space=pl.ANY)],
        out_specs=pl.BlockSpec(memory_space=pltpu.VMEM),
        out_shape=jax.ShapeDtypeStruct((tok, width), F32),
        scratch_shapes=[
            pltpu.VMEM((4, tok, width), BF16),
            pltpu.VMEM((4, tok, width), BF16),
            pltpu.VMEM((3, tok, width), BF16),
            pltpu.VMEM((tok, width), BF16),
            pltpu.VMEM((tok, width), BF16),
            pltpu.VMEM((tok, width), BF16),
            pltpu.SemaphoreType.DMA((7, PIECES)),
            pltpu.SemaphoreType.DMA((7, PIECES)),
            pltpu.SemaphoreType.DMA((4,)),
        ],
        compiler_params=pltpu.CompilerParams(
            collective_id=number, has_side_effects=True, vmem_limit_bytes=VMEM_LIMIT
        ),
        cost_estimate=pl.CostEstimate(flops=0, bytes_accessed=120_000_000, transcendentals=0),
        name="scatter_square",
    )(parts.astype(BF16).reshape(8, tok, width))


def swap_square(blocks):
    return lax.all_to_all(blocks, SQUARE, split_axis=0, concat_axis=0, tiled=True)


def swap_pair(block, axis):
    return lax.ppermute(block, axis, [(0, 1), (1, 0)])


def gather_axis(rows, axis):
    if lax.axis_size(axis) != 2:
        return lax.all_gather(rows, axis, axis=0, tiled=False)
    other = swap_pair(rows, axis)
    first = lax.axis_index(axis) == 0
    return jnp.stack([jnp.where(first, rows, other), jnp.where(first, other, rows)])


def gather_copies(rows):
    both = gather_axis(gather_axis(rows, "hi"), "dp")
    return both.reshape((-1,) + rows.shape[1:])


def scatter_axis(parts, axis):
    if lax.axis_size(axis) != 2:
        return lax.psum_scatter(parts.astype(BF16), axis, scatter_dimension=0, tiled=False).astype(F32)
    place = lax.axis_index(axis)
    away = lax.dynamic_index_in_dim(parts, 1 - place, 0, False).astype(BF16)
    own = lax.dynamic_index_in_dim(parts, place, 0, False)
    return own + swap_pair(away, axis).astype(F32)


def scatter_copies(rows):
    dp_n, hi_n = lax.axis_size("dp"), lax.axis_size("hi")
    parts = rows.reshape((dp_n, hi_n, rows.shape[0] // (dp_n * hi_n)) + rows.shape[1:])
    return scatter_axis(scatter_axis(parts, "dp"), "hi")


def total_of(value, axes, count):
    spread = jnp.broadcast_to(value.reshape(1, 1), (count, 1))
    return jnp.sum(lax.all_to_all(spread, axes, split_axis=0, concat_axis=0, tiled=True))


def norm_parts(rows):
    inverse = lax.rsqrt(jnp.mean(rows * rows, axis=-1, keepdims=True) + NORM_EPS)
    return rows * inverse, inverse


def reorder(pairs, block, source, target, cast):
    for at, to in pairs:
        target[:, to * block : to * block + block] = cast(source[:, at * block : at * block + block])


def out_kernel(order, pairs, block, mixed_ref, weight_ref, rows_ref, gain_ref, middle_ref, normed_ref, total):
    f = pl.program_id(0)

    @pl.when(f == 0)
    def _():
        total[...] = jnp.zeros_like(total)

    total[...] += dot32(mixed_ref[0], weight_ref[...])

    @pl.when(f == pl.num_programs(0) - 1)
    def _():
        middle = rows_ref[...].astype(F32) + RESIDUAL_SCALE * total[...]
        middle_ref[...] = middle
        total[...] = norm_parts(middle)[0] * gain_ref[...]
        reorder(pairs, block, total, normed_ref, lambda v: v.astype(BF16))


def out_project(mixed, weight, rows, gain, order, pairs, block):
    group, tok, cols = mixed.shape
    width = weight.shape[1]
    whole = pl.BlockSpec((tok, width), lambda f: (0, 0))
    return pl.pallas_call(
        functools.partial(out_kernel, order, pairs, block),
        grid=(group,),
        in_specs=[
            pl.BlockSpec((1, tok, cols), lambda f: (f, 0, 0)),
            pl.BlockSpec((cols, width), lambda f: (order(f), 0)),
            whole,
            pl.BlockSpec((1, width), lambda f: (0, 0)),
        ],
        out_specs=[whole, whole],
        out_shape=[
            jax.ShapeDtypeStruct((tok, width), F32),
            jax.ShapeDtypeStruct((tok, width), BF16),
        ],
        scratch_shapes=[pltpu.VMEM((tok, width), F32)],
        compiler_params=pltpu.CompilerParams(vmem_limit_bytes=VMEM_LIMIT),
        cost_estimate=pl.CostEstimate(
            flops=2 * tok * width * width, bytes_accessed=16_000_000, transcendentals=0
        ),
        name="out_project",
    )(mixed, weight, rows, gain)


def out_back_kernel(
    pairs, block, grad_ref, middle_ref, result_ref, gain_ref, weight_ref, sum_ref, rows_ref, mixed_ref, work
):
    f = pl.program_id(0)

    @pl.when(f == 0)
    def _():
        reorder(pairs, block, grad_ref, work, lambda v: v)
        normal, inverse = norm_parts(middle_ref[...])
        grad = work[...] * gain_ref[...]
        total = result_ref[...] + inverse * (
            grad - normal * jnp.mean(grad * normal, axis=-1, keepdims=True)
        )
        sum_ref[...] = total
        rows_ref[...] = (RESIDUAL_SCALE * total).astype(BF16)

    mixed_ref[0] = dot32(rows_ref[...], weight_ref[...], ((1,), (1,))).astype(BF16)


def out_back(grad, middle, result, gain, weight, cols, order, pairs, block):
    tok, width = middle.shape
    group = width // cols
    whole = pl.BlockSpec((tok, width), lambda f: (0, 0))
    return pl.pallas_call(
        functools.partial(out_back_kernel, pairs, block),
        grid=(group,),
        in_specs=[
            whole,
            whole,
            whole,
            pl.BlockSpec((1, width), lambda f: (0, 0)),
            pl.BlockSpec((cols, width), lambda f: (order(f), 0)),
        ],
        out_specs=[whole, whole, pl.BlockSpec((1, tok, cols), lambda f: (f, 0, 0))],
        out_shape=[
            jax.ShapeDtypeStruct((tok, width), F32),
            jax.ShapeDtypeStruct((tok, width), BF16),
            jax.ShapeDtypeStruct((group, tok, cols), BF16),
        ],
        scratch_shapes=[pltpu.VMEM((tok, width), F32)],
        compiler_params=pltpu.CompilerParams(vmem_limit_bytes=VMEM_LIMIT),
        cost_estimate=pl.CostEstimate(
            flops=2 * tok * width * width, bytes_accessed=20_000_000, transcendentals=0
        ),
        name="out_back",
    )(grad, middle, result, gain, weight)


def deal_kernel(places, wide, gate_ref, up_ref, gates_ref, ups_ref):
    for at, (f, to) in enumerate(places):
        here, there = slice(at * wide, at * wide + wide), slice(to * wide, to * wide + wide)
        gates_ref[f, :, there] = gate_ref[:, here]
        ups_ref[f, :, there] = up_ref[:, here]


def collect_kernel(
    places, wide, gates_ref, ups_ref, gate_ref, up_ref, gain_ref, dgate_ref, dup_ref, dgain_ref
):
    total = jnp.zeros((gate_ref.shape[0], wide), F32)
    for at, (f, to) in enumerate(places):
        here, there = slice(at * wide, at * wide + wide), slice(to * wide, to * wide + wide)
        dgate, dup = gates_ref[f, :, there].astype(F32), ups_ref[f, :, there].astype(F32)
        dgate_ref[:, here] = dgate
        dup_ref[:, here] = dup
        total += gate_ref[:, here].astype(F32) * dgate + up_ref[:, here].astype(F32) * dup
    dgain_ref[...] = jnp.sum(total, axis=1, keepdims=True) / gain_ref[...]


def shards(
    hidden,
    teacher,
    lengths,
    attn_gain,
    w_query,
    key_projection,
    value_projection,
    w_out,
    mlp_gain,
    w_gate,
    w_up,
    w_down,
):
    dp_n, blk_n, hi_n, lo_n = (lax.axis_size(a) for a in ALL)
    group = blk_n * lo_n
    every = dp_n * blk_n * hi_n * lo_n
    hi, lo = lax.axis_index("hi"), lax.axis_index("lo")
    blk = lax.axis_index("blk")
    tok = hidden.shape[1]
    seq_len = tok * blk_n * hi_n * lo_n
    width = hidden.shape[2]
    rows_w = w_query.shape[0]
    units_w = w_down.shape[0]
    ff_part = w_gate.shape[1] // group

    block = lo_n * rows_w
    if block % 128 == 0:
        to_inner = [
            ((d * blk_n + b) * hi_n + h, (d * hi_n + h) * blk_n + b)
            for d in range(dp_n)
            for b in range(blk_n)
            for h in range(hi_n)
        ]
        reblock = block
    else:
        to_inner, reblock = [(0, 0)], width
    to_outer = [(to, at) for at, to in to_inner]

    def inner(a):
        if reblock == block:
            return a
        return a.reshape(-1, dp_n, blk_n, hi_n, block).transpose(0, 1, 3, 2, 4).reshape(-1, width)

    def outer(a):
        if reblock == block:
            return a
        return a.reshape(-1, dp_n, hi_n, blk_n, block).transpose(0, 1, 3, 2, 4).reshape(-1, width)

    key_head = lambda f: (f % lo_n) * blk_n + f // lo_n

    def head_columns(w):
        cols = w.shape[1] // group
        return w.reshape(rows_w, lo_n, blk_n, cols).transpose(2, 1, 0, 3).reshape(group, rows_w, cols)

    def head_columns_back(g):
        cols = g.shape[2]
        return (
            g.reshape(blk_n, lo_n, rows_w, cols).transpose(2, 1, 0, 3).reshape(rows_w, group * cols)
        )

    def unit_columns(w):
        return (
            w.reshape(rows_w, dp_n, blk_n, hi_n, lo_n, units_w)
            .transpose(2, 4, 0, 1, 3, 5)
            .reshape(group, rows_w, ff_part)
        )

    def unit_columns_back(g):
        return (
            g.reshape(blk_n, lo_n, rows_w, dp_n, hi_n, units_w)
            .transpose(2, 3, 0, 4, 1, 5)
            .reshape(rows_w, group * ff_part)
        )

    gains = jnp.stack([attn_gain, mlp_gain]).reshape(1, 2 * rows_w)
    gains = lax.all_to_all(
        jnp.broadcast_to(gains, (every, 2 * rows_w)), ALL, split_axis=0, concat_axis=0, tiled=True
    )
    gains = gains.astype(F32).reshape(every, 2, rows_w)
    gain_one, gain_two = gains[:, 0].reshape(1, width), gains[:, 1].reshape(1, width)

    q_cols = w_query.shape[1] // group
    k_cols = key_projection.shape[1] // group
    head_parts = jnp.concatenate(
        [head_columns(w) for w in (w_query, key_projection, value_projection)], axis=2
    )
    head_wide = head_parts.shape[2]
    head_parts = jnp.broadcast_to(
        head_parts.reshape(1, blk_n, 1, lo_n, rows_w, head_wide),
        (dp_n, blk_n, hi_n, lo_n, rows_w, head_wide),
    ).reshape(every, rows_w, head_wide)
    qkv_weight = lax.all_to_all(head_parts, ALL, split_axis=0, concat_axis=0, tiled=True).reshape(
        width, head_wide
    )

    ff_places = [
        (b * lo_n + l, d * hi_n + h)
        for d in range(dp_n)
        for b in range(blk_n)
        for h in range(hi_n)
        for l in range(lo_n)
    ]
    part_shape = jax.ShapeDtypeStruct((group, rows_w, ff_part), BF16)
    params = pltpu.CompilerParams(vmem_limit_bytes=VMEM_LIMIT)
    if units_w % 128 == 0:
        gate_parts, up_parts = pl.pallas_call(
            functools.partial(deal_kernel, ff_places, units_w),
            out_shape=[part_shape, part_shape],
            compiler_params=params,
            name="deal",
        )(w_gate, w_up)
    else:
        gate_parts, up_parts = unit_columns(w_gate), unit_columns(w_up)

    places = (
        (jnp.arange(blk_n)[:, None, None] * hi_n + hi) * lo_n + jnp.arange(lo_n)[None, :, None]
    ) * tok + jnp.arange(tok)[None, None, :]
    places = places.reshape(-1)
    half = HEAD_SIZE // 2
    frequency = ROPE_BASE ** (-(jnp.arange(half).astype(F32) * 2.0) / HEAD_SIZE)
    angles = places.astype(F32)[:, None] * frequency[None, :]
    cosine, sine, none = jnp.cos(angles), jnp.sin(angles), jnp.zeros_like(angles)
    tables = (
        jnp.concatenate([cosine] * 4, axis=1),
        jnp.concatenate([-sine, none] * 2, axis=1),
        jnp.concatenate([none, sine] * 2, axis=1),
    )

    inputs = hidden[0].astype(F32)
    normal_one, inverse_one = norm_parts(inputs)
    normed_one = gather_square((normal_one * gain_one).astype(BF16), 0)
    qkv = project(normed_one, qkv_weight, tables, tok)
    normed_one, w_out, w_down, gate_parts, up_parts = lax.optimization_barrier(
        (normed_one, w_out, w_down, gate_parts, up_parts)
    )
    down_weight = gather_copies(w_down)
    gate_weight = gather_copies(swap_square(gate_parts).reshape(group * rows_w, -1))
    up_weight = gather_copies(swap_square(up_parts).reshape(group * rows_w, -1))
    out_weight = gather_axis(gather_axis(w_out, "lo"), "hi").reshape(-1, width)
    out_weight = lax.all_gather(out_weight, ("dp", "blk"), axis=0, tiled=True)
    unit = lo_n * tok
    other_kv = swap_pair(qkv[:, q_cols:], "hi").reshape(blk_n, unit, 2 * k_cols)
    qkv = qkv.reshape(blk_n, unit, -1)
    scalars = jnp.stack([lengths[0], hi.astype(jnp.int32)])
    out_heads, log_heads = attend(scalars, qkv, other_kv)
    mixed = swap_square(out_heads.reshape(group, tok, q_cols))
    middle, normed_two = out_project(
        mixed, out_weight, hidden[0], gain_two, key_head, to_inner, reblock
    )

    normed_two = gather_square(inner(normed_two), 0)
    gate = dot32(normed_two, gate_weight)
    upward = dot32(normed_two, up_weight)
    sigma = jax.nn.sigmoid(gate)
    silu = gate * sigma
    units = (silu * upward).astype(BF16)
    gate_slope = (upward * sigma * (1.0 + gate * (1.0 - sigma))).astype(BF16)
    up_slope = silu.astype(BF16)
    result = middle + RESIDUAL_SCALE * scatter_square(dot32(units, down_weight), 1)

    own_places = ((blk * hi_n + hi) * lo_n + lo) * tok + jnp.arange(tok)
    valid = own_places < lengths[0]
    misfit = jnp.where(valid[:, None], result - teacher[0].astype(F32), 0.0)
    valid_count = total_of(lengths, ("dp",), dp_n).astype(F32)
    squares = total_of(jnp.sum(misfit * misfit), ALL, every)
    mse_loss = squares / (width * valid_count)
    grad_result = misfit * (dp_n * seq_len / valid_count)

    branch = gather_square((RESIDUAL_SCALE * grad_result).astype(BF16), 0)
    grad_units = dot32(branch, down_weight, ((1,), (1,)))
    grad_gate_rows = (grad_units * gate_slope.astype(F32)).astype(BF16)
    grad_up_rows = (grad_units * up_slope.astype(F32)).astype(BF16)
    grad_normal = outer(
        scatter_square(
            dot32(grad_gate_rows, gate_weight, ((1,), (1,)))
            + dot32(grad_up_rows, up_weight, ((1,), (1,))),
            1,
        )
    )
    down_sum = scatter_copies(dot32(units, branch, ((0,), (0,))))
    gate_sum = scatter_copies(dot32(normed_two, grad_gate_rows, ((0,), (0,))))
    up_sum = scatter_copies(dot32(normed_two, grad_up_rows, ((0,), (0,))))

    grad_middle, attn_rows, grad_mixed = out_back(
        grad_normal, middle, grad_result, gain_two, out_weight, q_cols, key_head, to_outer, reblock
    )
    dout = swap_square(grad_mixed).reshape(blk_n, unit, q_cols)
    dq, dkv = attend_back(scalars, qkv, other_kv, dout, out_heads, log_heads)
    dkv = dkv.reshape(2, group * tok, 2 * k_cols)
    dqkv = back_rope(
        dq.reshape(group * tok, q_cols), dkv[0], swap_pair(dkv[1], "hi"), tables, tok
    )
    grad_first = scatter_square(dot32(dqkv, qkv_weight, ((1,), (1,))), 1) * gain_one
    grad_hidden = grad_middle + inverse_one * (
        grad_first - normal_one * jnp.mean(grad_first * normal_one, axis=-1, keepdims=True)
    )
    head_grads = dot32(normed_one, dqkv, ((0,), (0,))).astype(BF16).reshape(every, rows_w, head_wide)
    head_grads = lax.all_to_all(head_grads, ALL, split_axis=0, concat_axis=0, tiled=True)
    head_grads = jnp.sum(
        head_grads.reshape(dp_n, blk_n, hi_n, lo_n, rows_w, head_wide).astype(F32), axis=(0, 2)
    ).reshape(group, rows_w, head_wide)

    square_attn = lax.all_gather(attn_rows, SQUARE, axis=0, tiled=True)
    own_out = dot32(out_heads.reshape(group * tok, q_cols), square_attn, ((0,), (0,))).astype(BF16)
    own_head = lo * blk_n + blk
    if rows_w * hi_n * lo_n == q_cols:
        spread = jnp.where((jnp.arange(dp_n) == lo)[:, None, None], own_out[None], 0)
        grad_out = lax.psum_scatter(
            spread.reshape(dp_n * q_cols, width), ("dp", "hi", "lo"), scatter_dimension=0, tiled=True
        ).astype(F32)
    else:
        spread = jnp.where((jnp.arange(group) == own_head)[:, None, None], own_out[None], 0)
        grad_out = lax.psum_scatter(
            spread.reshape(width, width), ALL, scatter_dimension=0, tiled=True
        ).astype(F32)

    own_one, own_two = attn_gain.astype(F32)[:, None], mlp_gain.astype(F32)[:, None]
    grad_query = head_columns_back(head_grads[:, :, :q_cols])
    grad_key = head_columns_back(head_grads[:, :, q_cols : q_cols + k_cols])
    grad_value = head_columns_back(head_grads[:, :, q_cols + k_cols :])

    def row_sums(*pairs):
        return sum(jnp.sum(w.astype(F32) * g, axis=1, keepdims=True) for w, g in pairs)

    grad_gain_one = (
        row_sums((w_query, grad_query), (key_projection, grad_key), (value_projection, grad_value))
        / own_one
    )
    gate_parts, up_parts = (
        swap_square(g.astype(BF16).reshape(group, rows_w, -1)) for g in (gate_sum, up_sum)
    )
    if units_w % 128 == 0:
        ff_shape = jax.ShapeDtypeStruct(w_gate.shape, F32)
        grad_gate, grad_up, grad_gain_two = pl.pallas_call(
            functools.partial(collect_kernel, ff_places, units_w),
            out_shape=[ff_shape, ff_shape, jax.ShapeDtypeStruct((rows_w, 1), F32)],
            compiler_params=params,
            name="collect",
        )(gate_parts, up_parts, w_gate, w_up, own_two)
    else:
        grad_gate = unit_columns_back(gate_parts.astype(F32))
        grad_up = unit_columns_back(up_parts.astype(F32))
        grad_gain_two = row_sums((w_gate, grad_gate), (w_up, grad_up)) / own_two
    return (
        result.astype(BF16)[None],
        mse_loss,
        grad_hidden[None],
        grad_gain_one[:, 0],
        grad_query,
        grad_key,
        grad_value,
        grad_out,
        grad_gain_two[:, 0],
        grad_gate,
        grad_up,
        down_sum,
    )


def solution(mesh):
    dp_n, blk_n, head_n = (mesh.shape[a] for a in ("dp", "blk", "head"))
    fine = Mesh(mesh.devices.reshape(dp_n, blk_n, 2, head_n // 2), ALL)
    tokens = P("dp", SEQ, None)
    rows, row = P(ALL, None), P(ALL)
    return jax.shard_map(
        shards,
        mesh=fine,
        in_specs=(tokens, tokens, P("dp"), row, rows, rows, rows, rows, row, rows, rows, rows),
        out_specs=(tokens, P(), tokens, row, rows, rows, rows, rows, row, rows, rows, rows),
        check_vma=False,
    )
```

```python
import functools
import math

import jax
import jax.numpy as jnp
import numpy as np
from jax import lax
from jax.experimental import pallas as pl
from jax.experimental.pallas import tpu as pltpu
from jax.sharding import Mesh, PartitionSpec as P

MODEL_WIDTH = 2048
HEAD_SIZE = 64
ROPE_BASE = 10000000.0
NORM_EPS = 1e-05
ATTN_SCALE = 0.015625
RESIDUAL_SCALE = 0.22
MASKED = -1e30

ALL = ("dp", "blk", "hi", "lo")
SQUARE = ("blk", "lo")
COPIES = ("dp", "hi")
SEQ = ("blk", "hi", "lo")
F32 = jnp.float32
BF16 = jnp.bfloat16
VMEM_LIMIT = 56 * 1024 * 1024


def dot32(a, b, dims=((1,), (0,))):
    return lax.dot_general(a, b, (dims, ((), ())), preferred_element_type=F32)


def rope_tables(seq_len):
    half = HEAD_SIZE // 2
    frequency = ROPE_BASE ** (-(np.arange(half) * 2.0) / HEAD_SIZE)
    angles = np.arange(seq_len).astype(np.float32)[:, None] * frequency.astype(np.float32)[None, :]
    cosine, sine = np.cos(angles.astype(np.float64)), np.sin(angles.astype(np.float64))
    none = np.zeros_like(cosine)
    rows = ([cosine] * 4, [-sine, none] * 2, [none, sine] * 2)
    return tuple(np.concatenate(row, axis=1).astype(np.float32) for row in rows)


def table_spec(tok):
    return pl.BlockSpec((tok, 128), lambda i, hi: ((i // 2 * 2 + hi[0]) * 2 + i % 2, 0))


def proj_kernel(hi_ref, rows_ref, gain_ref, weight_ref, cos_ref, sina_ref, sinb_ref, normed_ref, q_ref, kv_ref):
    normed_ref[...] = (norm_parts(rows_ref[...].astype(F32))[0] * gain_ref[...]).astype(BF16)
    made = dot32(normed_ref[...], weight_ref[...])
    cosine, sina, sinb = cos_ref[...], sina_ref[...], sinb_ref[...]
    low = lanes_low(cosine.shape)
    half = HEAD_SIZE // 2
    for part in range(3):
        u = made[:, 128 * part : 128 * part + 128]
        up, down = pltpu.roll(u, 128 - half, 1), pltpu.roll(u, half, 1)
        turned = u * cosine + up * sina + down * sinb
        if part < 2:
            q_ref[:, 128 * part : 128 * part + 128] = (
                turned.astype(BF16).astype(F32) * ATTN_SCALE
            ).astype(BF16)
        else:
            kv_ref[...] = jnp.where(low, turned, u).astype(BF16)


def project(hi, rows, gain, weight, tables, tile):
    count, depth = rows.shape
    wide = weight.shape[1]
    by_rows = lambda cols: pl.BlockSpec((tile, cols), lambda i, hi: (i, 0))
    whole = lambda *shape: pl.BlockSpec(shape, lambda i, hi: (0, 0))
    return pl.pallas_call(
        proj_kernel,
        grid_spec=pltpu.PrefetchScalarGridSpec(
            num_scalar_prefetch=1,
            grid=(count // tile,),
            in_specs=[by_rows(depth), whole(1, depth), whole(depth, wide)] + [table_spec(tile)] * 3,
            out_specs=[by_rows(depth), by_rows(256), by_rows(128)],
        ),
        out_shape=[
            jax.ShapeDtypeStruct((count, depth), BF16),
            jax.ShapeDtypeStruct((count, 256), BF16),
            jax.ShapeDtypeStruct((count, 128), BF16),
        ],
        compiler_params=pltpu.CompilerParams(vmem_limit_bytes=VMEM_LIMIT),
        cost_estimate=pl.CostEstimate(
            flops=2 * count * depth * wide, bytes_accessed=4 * count * depth, transcendentals=0
        ),
        name="project",
    )(hi, rows, gain, weight, *tables)


def back_rope_kernel(
    hi_ref, dq_ref, own_ref, other_ref, cos_ref, sina_ref, sinb_ref, first_ref, out_ref
):
    cosine, sina, sinb = cos_ref[...], sina_ref[...], sinb_ref[...]
    low = lanes_low(cosine.shape)
    half = HEAD_SIZE // 2
    shared = (own_ref[...].astype(F32) + other_ref[...].astype(F32)).astype(BF16)
    for part in range(3):
        w = (dq_ref[:, 128 * part : 128 * part + 128] if part < 2 else shared).astype(F32)
        turned = w * cosine + pltpu.roll(w * sinb, 128 - half, 1) + pltpu.roll(w * sina, half, 1)
        if part == 2:
            turned = jnp.where(low, turned, w)
        out_ref[:, 128 * part : 128 * part + 128] = turned.astype(BF16)


def back_rope(hi, dq, own, other, tables, first, tile):
    count = dq.shape[0]
    by_rows = lambda wide: pl.BlockSpec((tile, wide), lambda i, hi: (i, 0))
    return pl.pallas_call(
        back_rope_kernel,
        grid_spec=pltpu.PrefetchScalarGridSpec(
            num_scalar_prefetch=1,
            grid=(count // tile,),
            in_specs=[by_rows(256), by_rows(128), by_rows(128)]
            + [table_spec(tile)] * 3
            + [pl.BlockSpec(memory_space=pl.ANY)],
            out_specs=by_rows(384),
        ),
        out_shape=jax.ShapeDtypeStruct((count, 384), BF16),
        compiler_params=pltpu.CompilerParams(vmem_limit_bytes=VMEM_LIMIT),
        cost_estimate=pl.CostEstimate(flops=0, bytes_accessed=20_000_000, transcendentals=0),
        name="back_rope",
    )(hi, dq, own, other, *tables, first)


def lanes_low(shape):
    return lax.broadcasted_iota(jnp.int32, shape, 1) < HEAD_SIZE


def both_keys(kv):
    low = lanes_low(kv.shape)
    keys = kv.astype(F32)
    return (
        jnp.where(low, keys, 0.0).astype(BF16),
        jnp.where(low, 0.0, pltpu.roll(keys, HEAD_SIZE, 1)).astype(BF16),
    )


def both_values(kv):
    low = lanes_low(kv.shape)
    values = kv.astype(F32)
    return (
        jnp.where(low, pltpu.roll(values, HEAD_SIZE, 1), 0.0).astype(BF16),
        jnp.where(low, 0.0, values).astype(BF16),
    )


def attend_kernel(scalar_ref, q_ref, kv_ref, other_ref, out_ref, log_ref, keys, values, peak, sums):
    b = pl.program_id(0)
    blocks, unit, _ = q_ref.shape
    units = 2 * blocks
    length, hi = scalar_ref[0], scalar_ref[1]
    n = 2 * b + hi

    @pl.when(b == 0)
    def _():
        def spread(c, carry):
            for j, kv in (
                (2 * c + hi, kv_ref[c]),
                (2 * c + 1 - hi, other_ref[c]),
            ):
                keys[0, j], keys[1, j] = both_keys(kv)
                across = jnp.transpose(kv.astype(F32))[HEAD_SIZE:, :]
                values[j] = jnp.concatenate(
                    [across, jnp.ones((16, unit), F32)], axis=0
                ).astype(BF16)
            return carry

        lax.fori_loop(0, blocks, spread, 0)

    peak[...] = jnp.full_like(peak, MASKED)
    sums[...] = jnp.zeros_like(sums)

    def step(j, masked):
        for h in range(4):
            query = q_ref[b, :, 128 * (h // 2) : 128 * (h // 2) + 128]
            scores = dot32(keys[h % 2, j], query, ((1,), (1,)))
            if masked:
                row = j * unit + lax.broadcasted_iota(jnp.int32, scores.shape, 0)
                col = n * unit + lax.broadcasted_iota(jnp.int32, scores.shape, 1)
                scores = jnp.where((row <= col) & (row < length), scores, MASKED)
            old = peak[h, 0:1, :]
            new = jnp.maximum(old, jnp.max(scores, axis=0, keepdims=True))
            weights = jnp.exp(scores - new).astype(BF16)
            sums[h] = sums[h] * jnp.exp(old - new) + dot32(values[j], weights)
            peak[h, 0:1, :] = new

    first_ragged = units - units // 4

    def plain(j, carry):
        step(j, False)
        return carry

    def checked(j, carry):
        step(j, True)
        return carry

    lax.fori_loop(0, jnp.minimum(n, first_ragged), plain, 0)
    lax.fori_loop(jnp.minimum(n, first_ragged), n + 1, checked, 0)

    for pair in range(2):
        parts = []
        for h in (2 * pair, 2 * pair + 1):
            total = sums[h, HEAD_SIZE : HEAD_SIZE + 1, :]
            parts.append(sums[h, 0:HEAD_SIZE, :] / total)
            log_ref[0, h : h + 1, :] = peak[h, 0:1, :] + jnp.log(total)
        out_ref[0, :, 128 * pair : 128 * pair + 128] = jnp.transpose(
            jnp.concatenate(parts, axis=0)
        ).astype(BF16)


def attend(scalars, q, kv, other):
    blocks, unit, _ = q.shape
    units = 2 * blocks
    whole = lambda a: pl.BlockSpec(a.shape, lambda i: (0,) * a.ndim)
    return pl.pallas_call(
        attend_kernel,
        grid=(blocks,),
        in_specs=[pl.BlockSpec(memory_space=pltpu.SMEM), whole(q), whole(kv), whole(other)],
        out_specs=[
            pl.BlockSpec((1, unit, 256), lambda i: (i, 0, 0)),
            pl.BlockSpec((1, 8, unit), lambda i: (i, 0, 0)),
        ],
        out_shape=[
            jax.ShapeDtypeStruct((blocks, unit, 256), BF16),
            jax.ShapeDtypeStruct((blocks, 8, unit), F32),
        ],
        scratch_shapes=[
            pltpu.VMEM((2, units, unit, 128), BF16),
            pltpu.VMEM((units, HEAD_SIZE + 16, unit), BF16),
            pltpu.VMEM((4, 8, unit), F32),
            pltpu.VMEM((4, HEAD_SIZE + 16, unit), F32),
        ],
        compiler_params=pltpu.CompilerParams(vmem_limit_bytes=VMEM_LIMIT),
        cost_estimate=pl.CostEstimate(
            flops=40_000_000_000, bytes_accessed=8_000_000, transcendentals=20_000_000
        ),
        name="attend",
    )(scalars, q, kv, other)


def attend_back_kernel(
    scalar_ref,
    q_ref,
    kv_ref,
    other_ref,
    dout_ref,
    out_ref,
    log_ref,
    first_ref,
    dq_ref,
    dkv_ref,
    delta,
    dq,
    dk,
    dv,
):
    j = pl.program_id(0)
    blocks, unit, _ = q_ref.shape
    units = 2 * blocks
    length, hi = scalar_ref[0], scalar_ref[1]

    @pl.when(j == 0)
    def _():
        dq[...] = jnp.zeros_like(dq)
        pick = jnp.where(
            lax.broadcasted_iota(jnp.int32, (8, 256), 0)
            == lax.broadcasted_iota(jnp.int32, (8, 256), 1) // HEAD_SIZE,
            1.0,
            0.0,
        )

        def dots(b, carry):
            product = dout_ref[b].astype(F32) * out_ref[b].astype(F32)
            delta[b] = lax.dot_general(
                pick,
                product,
                (((1,), (1,)), ((), ())),
                precision=lax.Precision.HIGHEST,
                preferred_element_type=F32,
            )
            return carry

        lax.fori_loop(0, blocks, dots, 0)

    foreign = jnp.where(j % 2 == hi, 0, 1)
    kv = jnp.where(foreign == 0, kv_ref[j // 2], other_ref[j // 2])
    keys, values = both_keys(kv), both_values(kv)
    dk[...] = jnp.zeros_like(dk)
    dv[...] = jnp.zeros_like(dv)

    def step(b, masked):
        n = 2 * b + hi
        for pair in range(2):
            lanes = slice(128 * pair, 128 * pair + 128)
            query = q_ref[b, :, lanes]
            dout = dout_ref[b, :, lanes]
            dq_part = None
            for side in range(2):
                h = 2 * pair + side
                scores = dot32(keys[side], query, ((1,), (1,)))
                weights = jnp.exp(scores - log_ref[b, h : h + 1, :])
                if masked:
                    row = j * unit + lax.broadcasted_iota(jnp.int32, scores.shape, 0)
                    col = n * unit + lax.broadcasted_iota(jnp.int32, scores.shape, 1)
                    weights = jnp.where((row <= col) & (row < length), weights, 0.0)
                dweights = dot32(values[side], dout, ((1,), (1,)))
                dscores = (weights * (dweights - delta[b, h : h + 1, :])).astype(BF16)
                dv[side] += dot32(weights.astype(BF16), dout)
                dk[side] += dot32(dscores, query)
                part = dot32(dscores, keys[side], ((0,), (0,)))
                dq_part = part if dq_part is None else dq_part + part
            dq[b, :, lanes] += dq_part

    first_ragged = units - units // 4

    def plain(b, carry):
        step(b, False)
        return carry

    def checked(b, carry):
        step(b, True)
        return carry

    first = (j + 1 - hi) // 2
    masked_until = jnp.where(j >= first_ragged, blocks, jnp.where(foreign == 0, first + 1, first))
    lax.fori_loop(first, masked_until, checked, 0)
    lax.fori_loop(masked_until, blocks, plain, 0)

    low = lanes_low((unit, 128))
    dkey = dk[0] + pltpu.roll(dk[1], HEAD_SIZE, 1)
    dvalue = pltpu.roll(dv[0], HEAD_SIZE, 1) + dv[1]
    dkv_ref[foreign, j // 2] = jnp.where(low, dkey, dvalue).astype(BF16)

    @pl.when(j == units - 1)
    def _():
        def store(b, carry):
            dq_ref[b] = (dq[b] * ATTN_SCALE).astype(BF16)
            return carry

        lax.fori_loop(0, blocks, store, 0)


def attend_back(scalars, q, kv, other, dout, out, log, first):
    blocks, unit, _ = q.shape
    units = 2 * blocks
    whole = lambda a: pl.BlockSpec(a.shape, lambda i: (0,) * a.ndim)
    dq_shape = jax.ShapeDtypeStruct((blocks, unit, 256), BF16)
    dkv_shape = jax.ShapeDtypeStruct((2, blocks, unit, 128), BF16)
    return pl.pallas_call(
        attend_back_kernel,
        grid=(units,),
        in_specs=[
            pl.BlockSpec(memory_space=pltpu.SMEM),
            whole(q),
            whole(kv),
            whole(other),
            whole(dout),
            whole(out),
            whole(log),
            pl.BlockSpec(memory_space=pl.ANY),
        ],
        out_specs=[whole(dq_shape), whole(dkv_shape)],
        out_shape=[dq_shape, dkv_shape],
        scratch_shapes=[
            pltpu.VMEM((blocks, 8, unit), F32),
            pltpu.VMEM((blocks, unit, 256), F32),
            pltpu.VMEM((2, unit, 128), F32),
            pltpu.VMEM((2, unit, 128), F32),
        ],
        compiler_params=pltpu.CompilerParams(vmem_limit_bytes=VMEM_LIMIT),
        cost_estimate=pl.CostEstimate(
            flops=60_000_000_000, bytes_accessed=10_000_000, transcendentals=20_000_000
        ),
        name="attend_back",
    )(scalars, q, kv, other, dout, out, log, first)


PIECES = 4
MESH_ID = pl.DeviceIdType.MESH


def square_places():
    blk, lo = lax.axis_index("blk"), lax.axis_index("lo")
    mate, side = blk + 1 - 2 * (blk % 2), (blk + 2) % 4
    return blk, lo, mate, side


def greet(ids):
    barrier = pltpu.get_barrier_semaphore()
    for one in ids:
        pl.semaphore_signal(barrier, inc=1, device_id=one, device_id_type=MESH_ID)
    pl.semaphore_wait(barrier, len(ids))


def remote(source, target, send, recv, to):
    copy = pltpu.make_async_remote_copy(
        src_ref=source,
        dst_ref=target,
        send_sem=send,
        recv_sem=recv,
        device_id=to,
        device_id_type=MESH_ID,
    )
    copy.start()
    return copy


def local_copy(source, target, sem):
    copy = pltpu.make_async_copy(source, target, sem)
    copy.start()
    return copy


class Carried:
    def __init__(self, source, target, held, sem):
        self.held, self.target, self.sem = held, target, sem
        self.copy = local_copy(source, held, sem)

    def turn(self):
        self.copy.wait()
        self.copy = local_copy(self.held, self.target, self.sem)

    def wait(self):
        self.copy.wait()


def finish(copies):
    for copy in copies:
        if isinstance(copy, Carried):
            copy.turn()
    for copy in copies:
        copy.wait()


def square_peers():
    blk, lo = lax.axis_index("blk"), lax.axis_index("lo")
    mine = blk * 2 + lo
    others = [lax.rem(mine + d, 8) for d in range(1, 8)]
    return mine, others, [{"blk": o // 2, "lo": lax.rem(o, 2)} for o in others]


def other_hi():
    return {"hi": 1 - lax.axis_index("hi")}


def dp_peers():
    dp, dp_n = lax.axis_index("dp"), lax.axis_size("dp")
    return [{"dp": lax.rem(dp + d, dp_n)} for d in range(1, dp_n)]


def every_peer():
    sizes = [lax.axis_size(a) for a in ALL]
    places = [lax.axis_index(a) for a in ALL]
    found = []
    for k in range(1, math.prod(sizes)):
        to, rest = {}, k
        for a, size, place in reversed(list(zip(ALL, sizes, places))):
            to[a] = lax.rem(place + rest % size, size)
            rest //= size
        found.append(to)
    return found


def gather_begin(rows_ref, out_ref, send, recv, local, held):
    blk, lo, mate, side = square_places()
    slot = lambda b, l: b * 2 + l
    mine = slot(blk, lo)
    to_mate, to_side, to_next = {"blk": mate}, {"blk": side}, {"lo": 1 - lo}
    step = rows_ref.shape[0] // PIECES

    def push(source, place, piece, kind, to):
        target = out_ref.at[place, pl.ds(piece * step, step)]
        return remote(source, target, send.at[kind, piece], recv.at[kind, piece], to)

    own = Carried(rows_ref, out_ref.at[mine], held, local)
    piece_of = lambda p: rows_ref.at[pl.ds(p * step, step)]
    came = lambda place, p: out_ref.at[place, pl.ds(p * step, step)]
    side_order, next_order = (2, 3, 0, 1), (0, 1, 2, 3)
    by_side, by_next, by_mate, across = {}, {}, [], {}
    for k in range(PIECES):
        p, q = side_order[k], next_order[k]
        by_side[p] = push(piece_of(p), mine, p, 0, to_side)
        by_next[q] = push(piece_of(q), mine, q, 1, to_next)
    for p in range(PIECES):
        by_mate.append(push(piece_of(p), mine, p, 3, to_mate))

    def end(between=lambda k: None):
        own.turn()
        from_side, from_next, from_across = slot(side, lo), slot(blk, 1 - lo), slot(side, 1 - lo)
        for k in range(PIECES):
            p, q = side_order[k], next_order[k]
            by_side[p].wait_recv()
            if p >= 2:
                across[p] = push(came(from_side, p), from_side, p, 2, to_next)
            by_mate.append(push(came(from_side, p), from_side, p, 4, to_mate))
            by_next[q].wait_recv()
            if q < 2:
                across[q] = push(came(from_next, q), from_next, q, 2, to_side)
            by_mate.append(push(came(from_next, q), from_next, q, 5, to_mate))
            between(k)
        for p in (0, 2, 1, 3):
            across[p].wait_recv()
            by_mate.append(push(came(from_across, p), from_across, p, 6, to_mate))
            between(PIECES + p)
        for copy in by_mate:
            copy.wait()
        for copies in (by_side, by_next, across):
            for copy in copies.values():
                copy.wait_send()
        own.wait()

    return end


def gather_scratch(tok, width):
    return [
        pltpu.SemaphoreType.DMA((7, PIECES)),
        pltpu.SemaphoreType.DMA((7, PIECES)),
        pltpu.SemaphoreType.DMA,
        pltpu.VMEM((tok, width), BF16),
    ]


def sems(count):
    return [pltpu.SemaphoreType.DMA((count,))] * 2


def swap_scratch(part):
    return sems(7) + [pltpu.SemaphoreType.DMA, pltpu.VMEM(part, BF16)]


def square_greeting():
    blk, lo, mate, side = square_places()
    return [{"blk": mate}, {"blk": side}, {"lo": 1 - lo}]


def gather_kernel(rows_ref, out_ref, send, recv, local, held):
    greet(square_greeting())
    gather_begin(rows_ref, out_ref, send, recv, local, held)()


def comm_call(kernel, number, arrays, shapes, scratch, name):
    anywhere = pl.BlockSpec(memory_space=pl.ANY)
    return pl.pallas_call(
        kernel,
        in_specs=[anywhere] * len(arrays),
        out_specs=[anywhere] * len(shapes),
        out_shape=[jax.ShapeDtypeStruct(shape, dtype) for shape, dtype in shapes],
        scratch_shapes=scratch,
        compiler_params=pltpu.CompilerParams(
            collective_id=number, has_side_effects=True, vmem_limit_bytes=VMEM_LIMIT
        ),
        cost_estimate=pl.CostEstimate(flops=0, bytes_accessed=120_000_000, transcendentals=0),
        name=name,
    )(*arrays)


def gather_square(rows, number):
    tok, width = rows.shape
    (out,) = comm_call(
        gather_kernel,
        number,
        [rows],
        [((8, tok, width), rows.dtype)],
        gather_scratch(tok, width),
        "gather_square",
    )
    return out.reshape(8 * tok, width)


def swap_begin(parts_ref, out_ref, send, recv, local, held):
    mine, others, ids = square_peers()
    own = Carried(parts_ref.at[mine], out_ref.at[mine], held, local)
    copies = [
        remote(parts_ref.at[o], out_ref.at[mine], send.at[d], recv.at[d], to)
        for d, (o, to) in enumerate(zip(others, ids))
    ]
    return copies + [own]


def dp_begin(pieces, out_ref, send, recv, local, held):
    dp = lax.axis_index("dp")
    copies = []
    for k, (place, ref) in enumerate(pieces):
        copies.append(Carried(ref, out_ref.at[dp, place], held.at[k], local.at[k]))
        for d, to in enumerate(dp_peers()):
            n = 2 * d + k
            copies.append(remote(ref, out_ref.at[dp, place], send.at[n], recv.at[n], to))
    return copies


def device_place():
    mine = 0
    for a in ALL:
        mine = mine * lax.axis_size(a) + lax.axis_index(a)
    return mine


def seq_peers():
    sizes = [lax.axis_size(a) for a in SEQ]
    places = [lax.axis_index(a) for a in SEQ]
    found = []
    for k in range(1, math.prod(sizes)):
        to, source, digits, rest = {}, 0, [], k
        for size in reversed(sizes):
            digits.append(rest % size)
            rest //= size
        for a, size, place, digit in zip(SEQ, sizes, places, reversed(digits)):
            to[a] = lax.rem(place + digit, size)
            source = source * size + lax.rem(place + size - digit, size)
        found.append((to, source))
    return found


def seq_place(to):
    place = 0
    for a in SEQ:
        place = place * lax.axis_size(a) + to[a]
    return place


def open_kernel(
    rows_ref, heads_ref, small_ref, wout_ref, out_ref, weight_ref, smalls_ref, wouts_ref, g_send, g_recv,
    g_local, g_held, w_send, w_recv, d_send, d_recv, s_send, s_recv, o_send, o_recv, local, w_held, o_held,
):
    blk, hi, lo = (lax.axis_index(a) for a in SEQ)
    mine = device_place()
    peers = every_peer()
    greet(peers)
    copies = [
        Carried(heads_ref.at[blk * 2 + lo], weight_ref.at[mine], w_held, local.at[0]),
        local_copy(small_ref, smalls_ref.at[mine], local.at[1]),
        Carried(wout_ref, wouts_ref.at[hi, lo], o_held, local.at[2]),
    ]
    for k, to in enumerate(peers):
        copies.append(remote(small_ref, smalls_ref.at[mine], s_send.at[k], s_recv.at[k], to))
    end = gather_begin(rows_ref, out_ref, g_send, g_recv, g_local, g_held)
    wout = remote(wout_ref, wouts_ref.at[hi, lo], o_send.at[0], o_recv.at[0], other_hi())
    next_lo = {"lo": 1 - lo}
    copies.append(remote(wout_ref, wouts_ref.at[hi, lo], o_send.at[1], o_recv.at[1], next_lo))
    dp, seq = lax.axis_index("dp"), seq_peers()
    seq_n = len(seq) + 1
    straight = []
    for k, (to, source) in enumerate(seq):
        part = heads_ref.at[to["blk"] * 2 + to["lo"]]
        straight.append(remote(part, weight_ref.at[mine], w_send.at[k], w_recv.at[k], to))

    def hand_on(part, place, k):
        for d, to in enumerate(dp_peers()):
            n = d * seq_n + k
            copies.append(remote(part, weight_ref.at[place], d_send.at[n], d_recv.at[n], to))

    hand_on(heads_ref.at[blk * 2 + lo], mine, seq_n - 1)

    def pass_on(turn):
        for k, (to, source) in enumerate(seq):
            if k * 2 * PIECES // len(seq) == turn:
                straight[k].wait()
                place = dp * seq_n + source
                hand_on(weight_ref.at[place], place, k)

    end(pass_on)
    wout.wait()
    there = wouts_ref.at[1 - hi, lo]
    copies.append(remote(there, there, o_send.at[2], o_recv.at[2], next_lo))
    finish(copies)


def keys_kernel(
    kv_ref, gate_ref, up_ref, down_ref, other_ref, gates_ref, ups_ref, downs_ref, k_send, k_recv, g_send,
    g_recv, g_local, g_held, u_send, u_recv, u_local, u_held, d_send, d_recv,
):
    greet(square_peers()[2] + [other_hi()] + dp_peers())
    copies = [remote(kv_ref, other_ref, k_send.at[0], k_recv.at[0], other_hi())]
    for d, to in enumerate(dp_peers()):
        copies.append(remote(down_ref, downs_ref.at[d], d_send.at[d], d_recv.at[d], to))
    copies += swap_begin(gate_ref, gates_ref, g_send, g_recv, g_local, g_held)
    copies += swap_begin(up_ref, ups_ref, u_send, u_recv, u_local, u_held)
    finish(copies)


def heads_kernel(
    heads_ref, gate_ref, gate_other_ref, up_ref, mixed_ref, gates_ref, up_other_ref, m_send, m_recv,
    m_local, m_held, g_send, g_recv, u_send, u_recv, g_local, g_held,
):
    hi = lax.axis_index("hi")
    greet(square_peers()[2] + [other_hi()] + dp_peers())
    copies = swap_begin(heads_ref, mixed_ref, m_send, m_recv, m_local, m_held)
    copies.append(remote(up_ref, up_other_ref, u_send.at[0], u_recv.at[0], other_hi()))
    copies += dp_begin(
        [(hi, gate_ref), (1 - hi, gate_other_ref)], gates_ref, g_send, g_recv, g_local, g_held
    )
    finish(copies)


def rows_kernel(
    rows_ref, up_ref, up_other_ref, down_ref, out_ref, ups_ref, down_other_ref, r_send, r_recv, r_local,
    r_held, u_send, u_recv, d_send, d_recv, u_local, u_held,
):
    hi = lax.axis_index("hi")
    greet(square_greeting() + [other_hi()] + dp_peers())
    end = gather_begin(rows_ref, out_ref, r_send, r_recv, r_local, r_held)
    copies = [remote(down_ref, down_other_ref, d_send.at[0], d_recv.at[0], other_hi())]
    copies += dp_begin(
        [(hi, up_ref), (1 - hi, up_other_ref)], ups_ref, u_send, u_recv, u_local, u_held
    )
    end()
    finish(copies)


def sum_begin(own_ref, got_ref, place, own, got, sem):
    return [
        local_copy(own_ref.at[place], own, sem.at[0]),
        local_copy(got_ref.at[place], got, sem.at[1]),
    ]


def wait_all(copies):
    for copy in copies:
        copy.wait()


def douts_kernel(
    over_dp, parts_ref, gate_ref, gate_got_ref, up_ref, up_got_ref, gate_made_ref, out_ref, gate_away_ref,
    up_away_ref, gate_kept_ref, send, recv, local, held, own, got, sem, d_send, d_recv,
):
    hi = lax.axis_index("hi")
    loads = [
        [local_copy(ref.at[1 - hi], own.at[k], sem.at[k, 0]), local_copy(got_ref, got.at[k], sem.at[k, 1])]
        for k, (ref, got_ref) in enumerate(((gate_ref, gate_got_ref), (up_ref, up_got_ref)))
    ]
    loads.append([local_copy(gate_ref.at[hi], own.at[2], sem.at[2, 0])])
    greet(square_peers()[2] + (dp_peers() if over_dp else []))
    loads[2] += pair_begin(gate_made_ref, hi, got.at[2], d_send.at[0], d_recv.at[0], over_dp)
    copies = swap_begin(parts_ref, out_ref, send, recv, local, held)
    for k, target in enumerate((gate_away_ref, up_away_ref, gate_kept_ref)):
        wait_all(loads[k])
        target[...] = (own[k] + got[k].astype(F32)).astype(target.dtype)
    finish(copies)


def dkeys_kernel(
    over_dp, dkv_ref, gate_ref, gate_got_ref, up_ref, up_made_ref, first_ref, other_ref, gates_ref, up_kept_ref,
    k_send, k_recv, g_send, g_recv, g_local, g_held, own, got, made, sem, up_own, up_got, d_send, d_recv,
):
    hi = lax.axis_index("hi")
    loads = [local_copy(gate_ref, own, sem.at[0]), local_copy(gate_got_ref, got, sem.at[1])]
    up_loads = [local_copy(up_ref.at[hi], up_own, sem.at[2])]
    greet(square_peers()[2] + [other_hi()] + (dp_peers() if over_dp else []))
    copies = [remote(dkv_ref.at[1], other_ref, k_send.at[0], k_recv.at[0], other_hi())]
    up_loads += pair_begin(up_made_ref, hi, up_got, d_send.at[0], d_recv.at[0], over_dp)
    wait_all(loads)
    made[...] = (own[...] + got[...].astype(F32)).astype(BF16)
    copies += swap_begin(made, gates_ref, g_send, g_recv, g_local, g_held)
    wait_all(up_loads)
    up_kept_ref[...] = up_own[...] + up_got[...].astype(F32)
    finish(copies)


def own_out_begin(out_ref, outs_ref, send, recv, local, held):
    dp, hi, lo = (lax.axis_index(a) for a in ("dp", "hi", "lo"))
    away = dp != lo
    mine = dp * 2 + hi

    def push(a, b, start):
        hi_to, lo_to = lax.rem(hi + a, 2), lax.rem(lo + b, 2)
        copy = pltpu.make_async_remote_copy(
            src_ref=out_ref.at[hi_to, lo_to],
            dst_ref=outs_ref.at[mine],
            send_sem=send.at[2 * a + b],
            recv_sem=recv.at[mine],
            device_id={"dp": lo, "hi": hi_to, "lo": lo_to},
            device_id_type=MESH_ID,
        )
        if start:
            copy.start()
        else:
            copy.wait_send()

    def own_copy():
        copy = local_copy(out_ref.at[hi, lo], held, local)
        copy.wait()
        copy = local_copy(held, outs_ref.at[mine], local)
        copy.wait()

    for a, b in ((0, 1), (1, 0), (1, 1)):
        push(a, b, True)
    pl.when(away)(lambda: push(0, 0, True))

    def arrive(slot):
        pltpu.make_async_remote_copy(
            src_ref=out_ref.at[0, 0],
            dst_ref=outs_ref.at[slot],
            send_sem=send.at[0],
            recv_sem=recv.at[slot],
            device_id={"dp": lo},
            device_id_type=MESH_ID,
        ).wait_recv()

    def end():
        pl.when(jnp.logical_not(away))(own_copy)
        for a, b in ((0, 1), (1, 0), (1, 1)):
            push(a, b, False)
        pl.when(away)(lambda: push(0, 0, False))
        for d in range(2):
            for h in range(2):
                itself = (d == dp) & (h == hi) & (dp == lo)
                pl.when(jnp.logical_not(itself))(functools.partial(arrive, 2 * d + h))

    return end


def close_kernel(with_out, *refs):
    refs = iter(refs)
    take = lambda n: [next(refs) for _ in range(n)]
    parts_ref, heads_ref, up_ref, up_got_ref, square_ref = take(5)
    out_rows_ref = next(refs) if with_out else None
    total_ref, head_ref, ups_ref, squares_ref = take(4)
    outs_ref = next(refs) if with_out else None
    scatter = take(9)
    h_send, h_recv, s_send, s_recv, local, h_held = take(6)
    swap = take(4)
    own, got, made, sem = take(4)
    out_scratch = take(4) if with_out else None
    mine = device_place()
    peers, seq = every_peer(), seq_peers()
    place = seq_place({a: lax.axis_index(a) for a in SEQ})
    loads = scatter_load(parts_ref, scatter)
    up_loads = [local_copy(up_ref, own, sem.at[0]), local_copy(up_got_ref, got, sem.at[1])]
    greet(peers)
    copies = [
        Carried(heads_ref.at[place], head_ref.at[place], h_held, local.at[0]),
        local_copy(square_ref, squares_ref.at[mine], local.at[1]),
    ]
    mates = scatter_mates(parts_ref, scatter)
    for k, to in enumerate(peers):
        copies.append(remote(square_ref, squares_ref.at[mine], s_send.at[k], s_recv.at[k], to))
    for k, (to, source) in enumerate(seq):
        part = heads_ref.at[seq_place(to)]
        copies.append(remote(part, head_ref.at[place], h_send.at[k], h_recv.at[k], to))
    end = own_out_begin(out_rows_ref, outs_ref, *out_scratch) if with_out else None
    wait_all(up_loads)
    made[...] = (own[...] + got[...].astype(F32)).astype(BF16)
    copies += swap_begin(made, ups_ref, *swap)
    scatter_end_square(loads, mates, total_ref, scatter)
    if with_out:
        end()
    finish(copies)


def remote_to(source, target, sems_of, kind, piece, to):
    send, recv = sems_of
    return remote(source, target, send.at[kind, piece], recv.at[kind, piece], to)


def scatter_load(parts_ref, scratch):
    mine, local = scratch[0], scratch[8]
    blk, lo, mate, side = square_places()
    places = (side * 2 + 1 - lo, side * 2 + lo, blk * 2 + 1 - lo, blk * 2 + lo)
    return [local_copy(parts_ref.at[p], mine.at[k], local.at[k]) for k, p in enumerate(places)]


def scatter_mates(parts_ref, scratch):
    mates, sems_of = scratch[1], scratch[6:8]
    blk, lo, mate, side = square_places()
    mate_side = (mate + 2) % 4
    places = (mate_side * 2 + 1 - lo, mate_side * 2 + lo, mate * 2 + 1 - lo, mate * 2 + lo)
    step = parts_ref.shape[1] // PIECES
    rows = lambda p: pl.ds(p * step, step)
    orders = ((0, 2, 1, 3), (0, 1, 2, 3), (2, 3, 0, 1), (0, 1, 2, 3))
    return {
        (k, p): remote_to(
            parts_ref.at[places[k], rows(p)], mates.at[k, rows(p)], sems_of, k, p, {"blk": mate}
        )
        for k in range(4)
        for p in orders[k]
    }


def scatter_end_square(loads, from_mate, out_ref, scratch):
    mine, mates, made, got_across, got_side, got_next = scratch[:6]
    sems_of = scratch[6:8]
    blk, lo, mate, side = square_places()
    to_side, to_next = {"blk": side}, {"lo": 1 - lo}
    step = mine.shape[1] // PIECES
    rows = lambda p: pl.ds(p * step, step)

    def summed(k, p):
        from_mate[k, p].wait_recv()
        return mine[k, rows(p), :].astype(F32) + mates[k, rows(p), :].astype(F32)

    sent = {}
    loads[0].wait()
    for p in (0, 2, 1, 3):
        made[0, rows(p), :] = summed(0, p).astype(BF16)
        sent[0, p] = remote_to(
            made.at[0, rows(p)],
            got_across.at[rows(p)],
            sems_of,
            4,
            p,
            to_side if p < 2 else to_next,
        )
    loads[1].wait()
    loads[2].wait()
    for k, p in ((1, 0), (2, 2), (1, 1), (2, 3), (1, 2), (2, 0), (1, 3), (2, 1)):
        total = summed(k, p)
        if (k == 1) == (p >= 2):
            sent[0, p].wait_recv()
            total = total + got_across[rows(p), :].astype(F32)
        made[k, rows(p), :] = total.astype(BF16)
        sent[k, p] = remote_to(
            made.at[k, rows(p)],
            (got_side if k == 1 else got_next).at[rows(p)],
            sems_of,
            4 + k,
            p,
            to_side if k == 1 else to_next,
        )
    loads[3].wait()
    for p in range(PIECES):
        total = summed(3, p)
        sent[1, p].wait_recv()
        sent[2, p].wait_recv()
        out_ref[rows(p), :] = (
            total + got_side[rows(p), :].astype(F32) + got_next[rows(p), :].astype(F32)
        )
    for copy in from_mate.values():
        copy.wait_send()
    for copy in sent.values():
        copy.wait_send()


def scatter_scratch(tok, width):
    return [
        pltpu.VMEM((4, tok, width), BF16),
        pltpu.VMEM((4, tok, width), BF16),
        pltpu.VMEM((3, tok, width), BF16),
        pltpu.VMEM((tok, width), BF16),
        pltpu.VMEM((tok, width), BF16),
        pltpu.VMEM((tok, width), BF16),
        pltpu.SemaphoreType.DMA((7, PIECES)),
        pltpu.SemaphoreType.DMA((7, PIECES)),
        pltpu.SemaphoreType.DMA((4,)),
    ]


def scatter_kernel(firsts, parts_ref, *refs):
    out_ref, scratch = refs[firsts], refs[firsts + 1 :]
    loads = scatter_load(parts_ref, scratch)
    greet(square_greeting())
    scatter_end_square(loads, scatter_mates(parts_ref, scratch), out_ref, scratch)


def scatter_square(parts, number, *first):
    count, width = parts.shape
    tok = count // 8
    return pl.pallas_call(
        functools.partial(scatter_kernel, len(first)),
        in_specs=[pl.BlockSpec(memory_space=pl.ANY)] * (1 + len(first)),
        out_specs=pl.BlockSpec(memory_space=pltpu.VMEM),
        out_shape=jax.ShapeDtypeStruct((tok, width), F32),
        scratch_shapes=scatter_scratch(tok, width),
        compiler_params=pltpu.CompilerParams(
            collective_id=number, has_side_effects=True, vmem_limit_bytes=VMEM_LIMIT
        ),
        cost_estimate=pl.CostEstimate(flops=0, bytes_accessed=120_000_000, transcendentals=0),
        name="scatter_square",
    )(parts.astype(BF16).reshape(8, tok, width), *first)


def pair_begin(parts_ref, place, out_ref, send, recv, over_dp):
    if not over_dp:
        return [local_copy(parts_ref.at[place], out_ref, recv)]
    return [remote(parts_ref.at[place], out_ref, send, recv, dp_peers()[0])]


def scatter_down_kernel(
    over_dp, parts_ref, down_ref, got_ref, gate_ref, up_ref, out_ref, sum_ref, gate_got_ref, up_got_ref, *scratch
):
    scratch, (own, got, away, came, sem, send, recv) = scratch[:9], scratch[9:]
    hi = lax.axis_index("hi")
    down = sum_begin(down_ref, got_ref, 1 - hi, own, got, sem)
    loads = scatter_load(parts_ref, scratch)
    greet(square_greeting() + [other_hi()] + (dp_peers() if over_dp else []))
    mates = scatter_mates(parts_ref, scratch)
    pairs = pair_begin(gate_ref, 1 - hi, gate_got_ref, send.at[1], recv.at[1], over_dp)
    pairs += pair_begin(up_ref, 1 - hi, up_got_ref, send.at[2], recv.at[2], over_dp)
    wait_all(down)
    away[...] = (own[...] + got[...].astype(F32)).astype(BF16)
    over = remote(away, came, send.at[0], recv.at[0], other_hi())
    down = sum_begin(down_ref, got_ref, hi, own, got, sem)
    scatter_end_square(loads, mates, out_ref, scratch)
    wait_all(down)
    over.wait()
    sum_ref[...] = own[...] + got[...].astype(F32) + came[...].astype(F32)
    wait_all(pairs)


def scatter_down(parts, number, down, gate_away, up_away):
    count, width = parts.shape
    tok = count // 8
    part = down[0].shape[1:]
    anywhere = pl.BlockSpec(memory_space=pl.ANY)
    return pl.pallas_call(
        functools.partial(scatter_down_kernel, lax.axis_size("dp") == 2),
        in_specs=[anywhere] * 5,
        out_specs=[pl.BlockSpec(memory_space=pltpu.VMEM)] * 2 + [anywhere] * 2,
        out_shape=[
            jax.ShapeDtypeStruct((tok, width), F32),
            jax.ShapeDtypeStruct(part, F32),
            jax.ShapeDtypeStruct(gate_away.shape[1:], BF16),
            jax.ShapeDtypeStruct(up_away.shape[1:], BF16),
        ],
        scratch_shapes=scatter_scratch(tok, width)
        + [
            pltpu.VMEM(part, F32),
            pltpu.VMEM(part, BF16),
            pltpu.VMEM(part, BF16),
            pltpu.VMEM(part, BF16),
            pltpu.SemaphoreType.DMA((2,)),
        ]
        + sems(3),
        compiler_params=pltpu.CompilerParams(
            collective_id=number, has_side_effects=True, vmem_limit_bytes=VMEM_LIMIT
        ),
        cost_estimate=pl.CostEstimate(flops=0, bytes_accessed=160_000_000, transcendentals=0),
        name="scatter_down",
    )(parts.reshape(8, tok, width), *down, gate_away, up_away)


def swap_square(blocks):
    return lax.all_to_all(blocks, SQUARE, split_axis=0, concat_axis=0, tiled=True)


def swap_pair(block, axis):
    return lax.ppermute(block, axis, [(0, 1), (1, 0)])


def gather_start(rows, axis):
    if lax.axis_size(axis) != 2:
        return lax.all_gather(rows, axis, axis=0, tiled=False)
    return rows, swap_pair(rows, axis)


def gather_end(parts, axis):
    if lax.axis_size(axis) != 2:
        return parts
    rows, other = parts
    first = lax.axis_index(axis) == 0
    return jnp.stack([jnp.where(first, rows, other), jnp.where(first, other, rows)])


def scatter_start(parts, axis):
    if lax.axis_size(axis) != 2:
        return lax.psum_scatter(parts.astype(BF16), axis, scatter_dimension=0, tiled=False)
    place = lax.axis_index(axis)
    away = lax.dynamic_index_in_dim(parts, 1 - place, 0, False).astype(BF16)
    own = lax.dynamic_index_in_dim(parts, place, 0, False)
    return own, swap_pair(away, axis)


def scatter_end(parts, axis):
    if lax.axis_size(axis) != 2:
        return parts.astype(F32)
    return parts[0] + parts[1].astype(F32)


def by_copy(rows):
    dp_n, hi_n = lax.axis_size("dp"), lax.axis_size("hi")
    return rows.reshape((dp_n, hi_n, rows.shape[0] // (dp_n * hi_n)) + rows.shape[1:])


def total_of(value, axes, count):
    spread = jnp.broadcast_to(value.reshape(1, 1), (count, 1))
    return jnp.sum(lax.all_to_all(spread, axes, split_axis=0, concat_axis=0, tiled=True))


def norm_parts(rows):
    inverse = lax.rsqrt(jnp.mean(rows * rows, axis=-1, keepdims=True) + NORM_EPS)
    return rows * inverse, inverse


def reorder(pairs, block, source, target, cast):
    for at, to in pairs:
        target[:, to * block : to * block + block] = cast(source[:, at * block : at * block + block])


def out_kernel(order, pairs, block, mixed_ref, weight_ref, rows_ref, gain_ref, middle_ref, normed_ref, total):
    f = pl.program_id(0)

    @pl.when(f == 0)
    def _():
        total[...] = jnp.zeros_like(total)

    total[...] += dot32(mixed_ref[0], weight_ref[...])

    @pl.when(f == pl.num_programs(0) - 1)
    def _():
        middle = rows_ref[...].astype(F32) + RESIDUAL_SCALE * total[...]
        middle_ref[...] = middle
        total[...] = norm_parts(middle)[0] * gain_ref[...]
        reorder(pairs, block, total, normed_ref, lambda v: v.astype(BF16))


def out_project(mixed, weight, rows, gain, order, pairs, block):
    group, tok, cols = mixed.shape
    width = weight.shape[1]
    whole = pl.BlockSpec((tok, width), lambda f: (0, 0))
    return pl.pallas_call(
        functools.partial(out_kernel, order, pairs, block),
        grid=(group,),
        in_specs=[
            pl.BlockSpec((1, tok, cols), lambda f: (f, 0, 0)),
            pl.BlockSpec((cols, width), lambda f: (order(f), 0)),
            whole,
            pl.BlockSpec((1, width), lambda f: (0, 0)),
        ],
        out_specs=[whole, whole],
        out_shape=[
            jax.ShapeDtypeStruct((tok, width), F32),
            jax.ShapeDtypeStruct((tok, width), BF16),
        ],
        scratch_shapes=[pltpu.VMEM((tok, width), F32)],
        compiler_params=pltpu.CompilerParams(vmem_limit_bytes=VMEM_LIMIT),
        cost_estimate=pl.CostEstimate(
            flops=2 * tok * width * width, bytes_accessed=16_000_000, transcendentals=0
        ),
        name="out_project",
    )(mixed, weight, rows, gain)


def out_back_kernel(
    pairs, block, grad_ref, middle_ref, result_ref, gain_ref, weight_ref, first_ref, sum_ref, rows_ref, mixed_ref, work
):
    f = pl.program_id(0)

    @pl.when(f == 0)
    def _():
        reorder(pairs, block, grad_ref, work, lambda v: v)
        normal, inverse = norm_parts(middle_ref[...])
        grad = work[...] * gain_ref[...]
        total = result_ref[...] + inverse * (
            grad - normal * jnp.mean(grad * normal, axis=-1, keepdims=True)
        )
        sum_ref[...] = total
        rows_ref[...] = (RESIDUAL_SCALE * total).astype(BF16)

    mixed_ref[0] = dot32(rows_ref[...], weight_ref[...], ((1,), (1,))).astype(BF16)


def out_back(grad, middle, result, gain, weight, first, cols, order, pairs, block):
    tok, width = middle.shape
    group = width // cols
    whole = pl.BlockSpec((tok, width), lambda f: (0, 0))
    return pl.pallas_call(
        functools.partial(out_back_kernel, pairs, block),
        grid=(group,),
        in_specs=[
            whole,
            whole,
            whole,
            pl.BlockSpec((1, width), lambda f: (0, 0)),
            pl.BlockSpec((cols, width), lambda f: (order(f), 0)),
            pl.BlockSpec(memory_space=pl.ANY),
        ],
        out_specs=[whole, whole, pl.BlockSpec((1, tok, cols), lambda f: (f, 0, 0))],
        out_shape=[
            jax.ShapeDtypeStruct((tok, width), F32),
            jax.ShapeDtypeStruct((tok, width), BF16),
            jax.ShapeDtypeStruct((group, tok, cols), BF16),
        ],
        scratch_shapes=[pltpu.VMEM((tok, width), F32)],
        compiler_params=pltpu.CompilerParams(vmem_limit_bytes=VMEM_LIMIT),
        cost_estimate=pl.CostEstimate(
            flops=2 * tok * width * width, bytes_accessed=20_000_000, transcendentals=0
        ),
        name="out_back",
    )(grad, middle, result, gain, weight, first)


def weight_grad_kernel(dp_ref, left_ref, right_ref, first_ref, away_ref, own_ref):
    i = pl.program_id(0)
    total = dot32(left_ref[...], right_ref[...], ((0,), (0,)))

    @pl.when(i < 2)
    def _():
        away_ref[0] = total.astype(BF16)

    @pl.when(i >= 2)
    def _():
        own_ref[0] = total


def weight_grad_start(left, right, first):
    dp_n, hi_n = lax.axis_size("dp"), lax.axis_size("hi")
    depth, rows = left.shape
    cols = right.shape[1]
    if dp_n != 2:
        sums = scatter_start(by_copy(dot32(left, right, ((0,), (0,)))), "dp")
        return sums.astype(F32), jnp.zeros(sums.shape, BF16)
    part = rows // (dp_n * hi_n)
    place = lax.axis_index("dp").astype(jnp.int32).reshape(1)
    away, own = pl.pallas_call(
        weight_grad_kernel,
        grid_spec=pltpu.PrefetchScalarGridSpec(
            num_scalar_prefetch=1,
            grid=(4,),
            in_specs=[
                pl.BlockSpec(
                    (depth, part),
                    lambda i, dp: (0, jnp.where(i < 2, 2 * (1 - dp[0]) + i, 2 * dp[0] + i - 2)),
                ),
                pl.BlockSpec((depth, cols), lambda i, dp: (0, 0)),
                pl.BlockSpec(memory_space=pl.ANY),
            ],
            out_specs=[
                pl.BlockSpec((1, part, cols), lambda i, dp: (jnp.minimum(i, 1), 0, 0)),
                pl.BlockSpec((1, part, cols), lambda i, dp: (jnp.maximum(i - 2, 0), 0, 0)),
            ],
        ),
        out_shape=[
            jax.ShapeDtypeStruct((2, part, cols), BF16),
            jax.ShapeDtypeStruct((2, part, cols), F32),
        ],
        compiler_params=pltpu.CompilerParams(vmem_limit_bytes=VMEM_LIMIT),
        cost_estimate=pl.CostEstimate(
            flops=2 * depth * rows * cols, bytes_accessed=24_000_000, transcendentals=0
        ),
        name="weight_grad",
    )(place, left, right, first)
    return own, away


def ff_back_kernel(
    tile, grad_ref, gate_slope_ref, up_slope_ref, gate_ref, up_ref, down_ref, first_ref, dgate_ref, dup_ref,
    out_ref, total,
):
    total[...] = jnp.zeros_like(total)

    def step(t, carry):
        cols = pl.ds(pl.multiple_of(t * tile, tile), tile)
        dunits = dot32(grad_ref[...], down_ref[cols, :], ((1,), (1,)))
        dgate = (dunits * gate_slope_ref[:, cols].astype(F32)).astype(BF16)
        dup = (dunits * up_slope_ref[:, cols].astype(F32)).astype(BF16)
        dgate_ref[:, cols] = dgate
        dup_ref[:, cols] = dup
        total[...] += dot32(dgate, gate_ref[:, cols], ((1,), (1,))) + dot32(
            dup, up_ref[:, cols], ((1,), (1,))
        )
        return carry

    lax.fori_loop(0, down_ref.shape[0] // tile, step, 0)
    out_ref[...] = total[...].astype(BF16)


def ff_back(grad, gate_slope, up_slope, gate_weight, up_weight, down_weight, first, tok):
    count, width = grad.shape
    ff = down_weight.shape[0]
    rows = lambda cols: pl.BlockSpec((tok, cols), lambda i: (i, 0))
    whole = lambda a: pl.BlockSpec(a.shape, lambda i: (0, 0), pipeline_mode=pl.Buffered(1))
    return pl.pallas_call(
        functools.partial(ff_back_kernel, ff),
        grid=(count // tok,),
        in_specs=[
            rows(width),
            rows(ff),
            rows(ff),
            whole(gate_weight),
            whole(up_weight),
            whole(down_weight),
            pl.BlockSpec(memory_space=pl.ANY),
        ],
        out_specs=[rows(ff), rows(ff), rows(width)],
        out_shape=[
            jax.ShapeDtypeStruct((count, ff), BF16),
            jax.ShapeDtypeStruct((count, ff), BF16),
            jax.ShapeDtypeStruct((count, width), BF16),
        ],
        scratch_shapes=[pltpu.VMEM((tok, width), F32)],
        compiler_params=pltpu.CompilerParams(vmem_limit_bytes=VMEM_LIMIT),
        cost_estimate=pl.CostEstimate(
            flops=6 * count * width * ff, bytes_accessed=40_000_000, transcendentals=0
        ),
        name="ff_back",
    )(grad, gate_slope, up_slope, gate_weight, up_weight, down_weight, first)


def deal_kernel(places, wide, gate_ref, up_ref, gates_ref, ups_ref):
    for at, (f, to) in enumerate(places):
        here, there = slice(at * wide, at * wide + wide), slice(to * wide, to * wide + wide)
        gates_ref[f, :, there] = gate_ref[:, here]
        ups_ref[f, :, there] = up_ref[:, here]


def collect_kernel(
    places, wide, gates_ref, ups_ref, gate_ref, up_ref, gain_ref, dgate_ref, dup_ref, dgain_ref
):
    total = jnp.zeros((gate_ref.shape[0], wide), F32)
    for at, (f, to) in enumerate(places):
        here, there = slice(at * wide, at * wide + wide), slice(to * wide, to * wide + wide)
        dgate, dup = gates_ref[f, :, there].astype(F32), ups_ref[f, :, there].astype(F32)
        dgate_ref[:, here] = dgate
        dup_ref[:, here] = dup
        total += gate_ref[:, here].astype(F32) * dgate + up_ref[:, here].astype(F32) * dup
    dgain_ref[...] = jnp.sum(total, axis=1, keepdims=True) / gain_ref[...]


def shards(
    hidden,
    teacher,
    lengths,
    attn_gain,
    w_query,
    key_projection,
    value_projection,
    w_out,
    mlp_gain,
    w_gate,
    w_up,
    w_down,
):
    dp_n, blk_n, hi_n, lo_n = (lax.axis_size(a) for a in ALL)
    group = blk_n * lo_n
    every = dp_n * blk_n * hi_n * lo_n
    hi, lo = lax.axis_index("hi"), lax.axis_index("lo")
    blk = lax.axis_index("blk")
    tok = hidden.shape[1]
    seq_len = tok * blk_n * hi_n * lo_n
    width = hidden.shape[2]
    rows_w = w_query.shape[0]
    units_w = w_down.shape[0]
    ff_part = w_gate.shape[1] // group

    block = lo_n * rows_w
    if block % 128 == 0:
        to_inner = [
            ((d * blk_n + b) * hi_n + h, (d * hi_n + h) * blk_n + b)
            for d in range(dp_n)
            for b in range(blk_n)
            for h in range(hi_n)
        ]
        reblock = block
    else:
        to_inner, reblock = [(0, 0)], width
    to_outer = [(to, at) for at, to in to_inner]

    def inner(a):
        if reblock == block:
            return a
        return a.reshape(-1, dp_n, blk_n, hi_n, block).transpose(0, 1, 3, 2, 4).reshape(-1, width)

    def outer(a):
        if reblock == block:
            return a
        return a.reshape(-1, dp_n, hi_n, blk_n, block).transpose(0, 1, 3, 2, 4).reshape(-1, width)

    key_head = lambda f: (f % lo_n) * blk_n + f // lo_n

    def head_columns(w):
        cols = w.shape[1] // group
        return w.reshape(rows_w, lo_n, blk_n, cols).transpose(2, 1, 0, 3).reshape(group, rows_w, cols)

    def head_columns_back(g):
        cols = g.shape[2]
        return (
            g.reshape(blk_n, lo_n, rows_w, cols).transpose(2, 1, 0, 3).reshape(rows_w, group * cols)
        )

    def unit_columns(w):
        return (
            w.reshape(rows_w, dp_n, blk_n, hi_n, lo_n, units_w)
            .transpose(2, 4, 0, 1, 3, 5)
            .reshape(group, rows_w, ff_part)
        )

    def unit_columns_back(g):
        return (
            g.reshape(blk_n, lo_n, rows_w, dp_n, hi_n, units_w)
            .transpose(2, 3, 0, 4, 1, 5)
            .reshape(rows_w, group * ff_part)
        )

    q_cols = w_query.shape[1] // group
    k_cols = key_projection.shape[1] // group
    head_parts = jnp.concatenate(
        [head_columns(w) for w in (w_query, key_projection, value_projection)], axis=2
    )
    head_wide = head_parts.shape[2]
    ff_places = [
        (b * lo_n + l, d * hi_n + h)
        for d in range(dp_n)
        for b in range(blk_n)
        for h in range(hi_n)
        for l in range(lo_n)
    ]
    part_shape = jax.ShapeDtypeStruct((group, rows_w, ff_part), BF16)
    params = pltpu.CompilerParams(vmem_limit_bytes=VMEM_LIMIT)
    if units_w % 128 == 0:
        gate_parts, up_parts = pl.pallas_call(
            functools.partial(deal_kernel, ff_places, units_w),
            out_shape=[part_shape, part_shape],
            compiler_params=params,
            name="deal",
        )(w_gate, w_up)
    else:
        gate_parts, up_parts = unit_columns(w_gate), unit_columns(w_up)

    pad = jnp.zeros((7 * 128 + 128 - 2 * rows_w - 1,), F32)
    small = jnp.concatenate(
        [attn_gain.astype(F32), mlp_gain.astype(F32), lengths.astype(F32), pad]
    ).reshape(8, 128)
    rows_all, qkv_weight, smalls, out_rows = comm_call(
        open_kernel,
        0,
        [hidden[0], head_parts, small, w_out],
        [
            ((group, tok, width), BF16),
            ((every, rows_w, head_wide), BF16),
            ((every, 8, 128), F32),
            ((hi_n, lo_n, rows_w, width), BF16),
        ],
        gather_scratch(tok, width)
        + sems(every // dp_n - 1)
        + sems((dp_n - 1) * every // dp_n)
        + sems(every - 1)
        + sems(3)
        + [
            pltpu.SemaphoreType.DMA((3,)),
            pltpu.VMEM((rows_w, head_wide), BF16),
            pltpu.VMEM((rows_w, width), BF16),
        ],
        "open",
    )
    qkv_weight = qkv_weight.reshape(width, head_wide)
    gain_one = smalls[:, 0, :rows_w].reshape(1, width)
    gain_two = smalls[:, 0, rows_w : 2 * rows_w].reshape(1, width)
    valid_count = jnp.sum(smalls.reshape(every, -1)[:: every // dp_n, 2 * rows_w])
    hi_index = hi.astype(jnp.int32).reshape(1)
    tables = rope_tables(seq_len)
    normed_one, q, kv = project(
        hi_index, rows_all.reshape(group * tok, width), gain_one, qkv_weight, tables, tok
    )
    unit = lo_n * tok
    part_rows = group * rows_w
    other_kv, gate_parts, up_parts, downs = comm_call(
        keys_kernel,
        2,
        [kv, gate_parts, up_parts, w_down],
        [
            (kv.shape, BF16),
            (gate_parts.shape, BF16),
            (up_parts.shape, BF16),
            ((dp_n - 1,) + w_down.shape, BF16),
        ],
        sems(1) + swap_scratch((rows_w, ff_part)) * 2 + sems(dp_n - 1),
        "keys",
    )
    gate_parts = gate_parts.reshape(part_rows, -1)
    up_parts = up_parts.reshape(part_rows, -1)
    gate_other = swap_pair(gate_parts, "hi")
    out_weight = lax.all_gather(out_rows.reshape(-1, width), ("dp", "blk"), axis=0, tiled=True)
    q = q.reshape(blk_n, unit, q_cols)
    kv, other_kv = kv.reshape(blk_n, unit, -1), other_kv.reshape(blk_n, unit, -1)
    scalars = jnp.stack([lengths[0], hi.astype(jnp.int32)])
    out_heads, log_heads = attend(scalars, q, kv, other_kv)
    dp_sems = sems(2 * (dp_n - 1))
    dp_scratch = [pltpu.SemaphoreType.DMA((2,)), pltpu.VMEM((2, part_rows, ff_part), BF16)]
    weight_shape = ((dp_n, hi_n, part_rows, ff_part), BF16)
    mixed, gate_weight, up_other = comm_call(
        heads_kernel,
        3,
        [out_heads.reshape(group, tok, q_cols), gate_parts, gate_other, up_parts],
        [((group, tok, q_cols), BF16), weight_shape, (up_parts.shape, BF16)],
        swap_scratch((tok, q_cols)) + dp_sems + sems(1) + dp_scratch,
        "heads",
    )
    gate_weight = gate_weight.reshape(width, ff_part)
    middle, normed_two = out_project(
        mixed, out_weight, hidden[0], gain_two, key_head, to_inner, reblock
    )

    normed_two, up_weight, down_other = comm_call(
        rows_kernel,
        4,
        [inner(normed_two), up_parts, up_other, w_down],
        [((group, tok, width), BF16), weight_shape, (w_down.shape, BF16)],
        gather_scratch(tok, width) + dp_sems + sems(1) + dp_scratch,
        "rows",
    )
    normed_two = normed_two.reshape(group * tok, width)
    up_weight = up_weight.reshape(width, ff_part)
    dp_index = lax.axis_index("dp")
    own_first = hi == 0

    def by_hi(own, other):
        return jnp.stack([jnp.where(own_first, own, other), jnp.where(own_first, other, own)])

    down_parts = by_hi(w_down, down_other)
    if dp_n == 2:
        far = by_hi(downs[0], swap_pair(down_other, "dp"))
        dp_first = dp_index == 0
        down_parts = jnp.stack(
            [jnp.where(dp_first, down_parts, far), jnp.where(dp_first, far, down_parts)]
        )
    else:
        down_parts = lax.all_gather(down_parts, "dp", axis=0, tiled=False)
    down_weight = down_parts.reshape(-1, width)
    gate = dot32(normed_two, gate_weight)
    upward = dot32(normed_two, up_weight)
    sigma = jax.nn.sigmoid(gate)
    silu = gate * sigma
    units = (silu * upward).astype(BF16)
    gate_slope = (upward * sigma * (1.0 + gate * (1.0 - sigma))).astype(BF16)
    up_slope = silu.astype(BF16)
    result = middle + RESIDUAL_SCALE * scatter_square(dot32(units, down_weight), 1)

    own_places = ((blk * hi_n + hi) * lo_n + lo) * tok + jnp.arange(tok)
    valid = own_places < lengths[0]
    misfit = jnp.where(valid[:, None], result - teacher[0].astype(F32), 0.0)
    squares = jnp.broadcast_to(jnp.sum(misfit * misfit), (8, 128))
    grad_result = misfit * (dp_n * seq_len / valid_count)

    branch = gather_square((RESIDUAL_SCALE * grad_result).astype(BF16), 5)
    down_sum = weight_grad_start(units, branch, branch)
    grad_gate_rows, grad_up_rows, grad_normal = ff_back(
        branch, gate_slope, up_slope, gate_weight, up_weight, down_weight, down_sum[0], 2 * tok
    )
    gate_sum = weight_grad_start(normed_two, grad_gate_rows, down_sum[0])
    up_sum = weight_grad_start(normed_two, grad_up_rows, gate_sum[0])
    down_got = swap_pair(down_sum[1], "dp") if dp_n == 2 else down_sum[1]
    grad_normal, down_sum, gate_got, up_got = scatter_down(
        grad_normal, 9, (down_sum[0], down_got), gate_sum[1], up_sum[1]
    )
    grad_normal = outer(grad_normal)

    grad_middle, attn_rows, grad_mixed = out_back(
        grad_normal, middle, grad_result, gain_two, out_weight, up_sum[0], q_cols, key_head, to_outer, reblock
    )
    square_attn = lax.all_gather(attn_rows, SQUARE, axis=0, tiled=True)
    part_shape = (part_rows, ff_part)
    anywhere, inside = pl.BlockSpec(memory_space=pl.ANY), pl.BlockSpec(memory_space=pltpu.VMEM)
    over_dp = dp_n == 2
    dout, gate_away, up_away, gate_kept = pl.pallas_call(
        functools.partial(douts_kernel, over_dp),
        in_specs=[anywhere] * 6,
        out_specs=[anywhere] + [inside] * 3,
        out_shape=[jax.ShapeDtypeStruct(grad_mixed.shape, BF16)]
        + [jax.ShapeDtypeStruct(part_shape, dtype) for dtype in (BF16, BF16, F32)],
        scratch_shapes=swap_scratch((tok, q_cols))
        + [
            pltpu.VMEM((3,) + part_shape, F32),
            pltpu.VMEM((3,) + part_shape, BF16),
            pltpu.SemaphoreType.DMA((3, 2)),
        ]
        + sems(1),
        compiler_params=pltpu.CompilerParams(
            collective_id=6, has_side_effects=True, vmem_limit_bytes=VMEM_LIMIT
        ),
        cost_estimate=pl.CostEstimate(flops=0, bytes_accessed=40_000_000, transcendentals=0),
        name="douts",
    )(grad_mixed, gate_sum[0], gate_got, up_sum[0], up_got, gate_sum[1])
    gate_got, up_got = swap_pair(gate_away, "hi"), swap_pair(up_away, "hi")
    dout = dout.reshape(blk_n, unit, q_cols)
    dq, dkv = attend_back(scalars, q, kv, other_kv, dout, out_heads, log_heads, gate_away)
    dkv = dkv.reshape(2, group * tok, 2 * k_cols)
    columns = (group, rows_w, ff_part)
    sum_scratch = [
        pltpu.VMEM(columns, F32),
        pltpu.VMEM(columns, BF16),
        pltpu.VMEM(columns, BF16),
        pltpu.SemaphoreType.DMA((3,)),
    ]
    own_out = dot32(out_heads.reshape(group * tok, q_cols), square_attn, ((0,), (0,))).astype(BF16)
    other_dkv, gate_parts, up_kept = pl.pallas_call(
        functools.partial(dkeys_kernel, over_dp),
        in_specs=[anywhere] * 6,
        out_specs=[anywhere, anywhere, inside],
        out_shape=[
            jax.ShapeDtypeStruct(dkv.shape[1:], BF16),
            jax.ShapeDtypeStruct(columns, BF16),
            jax.ShapeDtypeStruct(part_shape, F32),
        ],
        scratch_shapes=sems(1)
        + swap_scratch((rows_w, ff_part))
        + sum_scratch
        + [pltpu.VMEM(part_shape, F32), pltpu.VMEM(part_shape, BF16)]
        + sems(1),
        compiler_params=pltpu.CompilerParams(
            collective_id=7, has_side_effects=True, vmem_limit_bytes=VMEM_LIMIT
        ),
        cost_estimate=pl.CostEstimate(flops=0, bytes_accessed=40_000_000, transcendentals=0),
        name="dkeys",
    )(dkv, gate_kept.reshape(columns), gate_got.reshape(columns), up_sum[0], up_sum[1], own_out)
    dqkv = back_rope(
        hi_index, dq.reshape(group * tok, q_cols), dkv[0], other_dkv, tables, up_got, tok
    )
    head_grads = dot32(normed_one, dqkv, ((0,), (0,))).reshape(dp_n, -1, rows_w, head_wide)
    head_grads = scatter_end(scatter_start(head_grads, "dp"), "dp").astype(BF16)
    grad_first = dot32(dqkv, qkv_weight, ((1,), (1,))).astype(BF16)
    with_out = dp_n == 2 and rows_w * hi_n * lo_n == q_cols
    arrays = [grad_first.reshape(group, tok, width), head_grads]
    arrays += [up_kept.reshape(columns), up_got.reshape(columns), squares]
    shapes = [
        ((tok, width), F32),
        (head_grads.shape, BF16),
        (columns, BF16),
        ((every, 8, 128), F32),
    ]
    scratch = scatter_scratch(tok, width) + sems(every // dp_n - 1) + sems(every - 1)
    scratch += [pltpu.SemaphoreType.DMA((2,)), pltpu.VMEM((rows_w, head_wide), BF16)]
    scratch += swap_scratch((rows_w, ff_part)) + sum_scratch
    if with_out:
        arrays.append(own_out.reshape(hi_n, lo_n, rows_w, width))
        shapes.append(((dp_n * hi_n, rows_w, width), BF16))
        scratch += sems(4) + [pltpu.SemaphoreType.DMA, pltpu.VMEM((rows_w, width), BF16)]
    grad_first, head_grads, up_parts, squares, *outs = pl.pallas_call(
        functools.partial(close_kernel, with_out),
        in_specs=[anywhere] * len(arrays),
        out_specs=[pl.BlockSpec(memory_space=pltpu.VMEM)] + [anywhere] * (len(shapes) - 1),
        out_shape=[jax.ShapeDtypeStruct(shape, dtype) for shape, dtype in shapes],
        scratch_shapes=scratch,
        compiler_params=pltpu.CompilerParams(
            collective_id=8, has_side_effects=True, vmem_limit_bytes=VMEM_LIMIT
        ),
        cost_estimate=pl.CostEstimate(flops=0, bytes_accessed=120_000_000, transcendentals=0),
        name="close",
    )(*arrays)
    mse_loss = jnp.sum(squares[:, 0, 0]) / (width * valid_count)
    if with_out:
        grad_out = jnp.sum(outs[0].astype(F32), axis=0)
    else:
        own_head = lo * blk_n + blk
        spread = jnp.where((jnp.arange(group) == own_head)[:, None, None], own_out[None], 0)
        grad_out = lax.psum_scatter(
            spread.reshape(width, width), ALL, scatter_dimension=0, tiled=True
        ).astype(F32)
    grad_first = grad_first * gain_one
    normal_one, inverse_one = norm_parts(hidden[0].astype(F32))
    grad_hidden = grad_middle + inverse_one * (
        grad_first - normal_one * jnp.mean(grad_first * normal_one, axis=-1, keepdims=True)
    )
    head_grads = jnp.sum(
        head_grads.reshape(blk_n, hi_n, lo_n, rows_w, head_wide).astype(F32), axis=1
    ).reshape(group, rows_w, head_wide)

    own_one, own_two = attn_gain.astype(F32)[:, None], mlp_gain.astype(F32)[:, None]
    grad_query = head_columns_back(head_grads[:, :, :q_cols])
    grad_key = head_columns_back(head_grads[:, :, q_cols : q_cols + k_cols])
    grad_value = head_columns_back(head_grads[:, :, q_cols + k_cols :])

    def row_sums(*pairs):
        return sum(jnp.sum(w.astype(F32) * g, axis=1, keepdims=True) for w, g in pairs)

    grad_gain_one = (
        row_sums((w_query, grad_query), (key_projection, grad_key), (value_projection, grad_value))
        / own_one
    )
    if units_w % 128 == 0:
        ff_shape = jax.ShapeDtypeStruct(w_gate.shape, F32)
        grad_gate, grad_up, grad_gain_two = pl.pallas_call(
            functools.partial(collect_kernel, ff_places, units_w),
            out_shape=[ff_shape, ff_shape, jax.ShapeDtypeStruct((rows_w, 1), F32)],
            compiler_params=params,
            name="collect",
        )(gate_parts, up_parts, w_gate, w_up, own_two)
    else:
        grad_gate = unit_columns_back(gate_parts.astype(F32))
        grad_up = unit_columns_back(up_parts.astype(F32))
        grad_gain_two = row_sums((w_gate, grad_gate), (w_up, grad_up)) / own_two
    return (
        result.astype(BF16)[None],
        mse_loss,
        grad_hidden[None],
        grad_gain_one[:, 0],
        grad_query,
        grad_key,
        grad_value,
        grad_out,
        grad_gain_two[:, 0],
        grad_gate,
        grad_up,
        down_sum,
    )


def solution(mesh):
    dp_n, blk_n, head_n = (mesh.shape[a] for a in ("dp", "blk", "head"))
    fine = Mesh(mesh.devices.reshape(dp_n, blk_n, 2, head_n // 2), ALL)
    tokens = P("dp", SEQ, None)
    rows, row = P(ALL, None), P(ALL)
    return jax.shard_map(
        shards,
        mesh=fine,
        in_specs=(tokens, tokens, P("dp"), row, rows, rows, rows, rows, row, rows, rows, rows),
        out_specs=(tokens, P(), tokens, row, rows, rows, rows, rows, row, rows, rows, rows),
        check_vma=False,
    )
```

```python
import functools
import math

import jax
import jax.numpy as jnp
import numpy as np
from jax import lax
from jax.experimental import pallas as pl
from jax.experimental.pallas import tpu as pltpu
from jax.sharding import Mesh, PartitionSpec as P

MODEL_WIDTH = 2048
HEAD_SIZE = 64
ROPE_BASE = 10000000.0
NORM_EPS = 1e-05
ATTN_SCALE = 0.015625
RESIDUAL_SCALE = 0.22
MASKED = -1e30

ALL = ("dp", "blk", "hi", "lo")
SQUARE = ("blk", "lo")
COPIES = ("dp", "hi")
SEQ = ("blk", "hi", "lo")
F32 = jnp.float32
BF16 = jnp.bfloat16
VMEM_LIMIT = 56 * 1024 * 1024


def dot32(a, b, dims=((1,), (0,))):
    return lax.dot_general(a, b, (dims, ((), ())), preferred_element_type=F32)


def rope_tables(seq_len):
    half = HEAD_SIZE // 2
    frequency = ROPE_BASE ** (-(np.arange(half) * 2.0) / HEAD_SIZE)
    angles = np.arange(seq_len).astype(np.float32)[:, None] * frequency.astype(np.float32)[None, :]
    cosine, sine = np.cos(angles.astype(np.float64)), np.sin(angles.astype(np.float64))
    none = np.zeros_like(cosine)
    rows = ([cosine] * 4, [-sine, none] * 2, [none, sine] * 2)
    return tuple(np.concatenate(row, axis=1).astype(np.float32) for row in rows)


def table_spec(tok):
    return pl.BlockSpec((tok, 128), lambda i, hi: ((i // 2 * 2 + hi[0]) * 2 + i % 2, 0))


def proj_kernel(hi_ref, rows_ref, gain_ref, weight_ref, cos_ref, sina_ref, sinb_ref, normed_ref, q_ref, kv_ref):
    normed_ref[...] = (norm_parts(rows_ref[...].astype(F32))[0] * gain_ref[...]).astype(BF16)
    made = dot32(normed_ref[...], weight_ref[...])
    cosine, sina, sinb = cos_ref[...], sina_ref[...], sinb_ref[...]
    low = lanes_low(cosine.shape)
    half = HEAD_SIZE // 2
    for part in range(3):
        u = made[:, 128 * part : 128 * part + 128]
        up, down = pltpu.roll(u, 128 - half, 1), pltpu.roll(u, half, 1)
        turned = u * cosine + up * sina + down * sinb
        if part < 2:
            q_ref[:, 128 * part : 128 * part + 128] = (
                turned.astype(BF16).astype(F32) * ATTN_SCALE
            ).astype(BF16)
        else:
            kv_ref[...] = jnp.where(low, turned, u).astype(BF16)


def project(hi, rows, gain, weight, tables, tile):
    count, depth = rows.shape
    wide = weight.shape[1]
    by_rows = lambda cols: pl.BlockSpec((tile, cols), lambda i, hi: (i, 0))
    whole = lambda *shape: pl.BlockSpec(shape, lambda i, hi: (0, 0))
    return pl.pallas_call(
        proj_kernel,
        grid_spec=pltpu.PrefetchScalarGridSpec(
            num_scalar_prefetch=1,
            grid=(count // tile,),
            in_specs=[by_rows(depth), whole(1, depth), whole(depth, wide)] + [table_spec(tile)] * 3,
            out_specs=[by_rows(depth), by_rows(256), by_rows(128)],
        ),
        out_shape=[
            jax.ShapeDtypeStruct((count, depth), BF16),
            jax.ShapeDtypeStruct((count, 256), BF16),
            jax.ShapeDtypeStruct((count, 128), BF16),
        ],
        compiler_params=pltpu.CompilerParams(vmem_limit_bytes=VMEM_LIMIT),
        cost_estimate=pl.CostEstimate(
            flops=2 * count * depth * wide, bytes_accessed=4 * count * depth, transcendentals=0
        ),
        name="project",
    )(hi, rows, gain, weight, *tables)


def back_rope_kernel(
    hi_ref, dq_ref, own_ref, other_ref, cos_ref, sina_ref, sinb_ref, first_ref, out_ref
):
    cosine, sina, sinb = cos_ref[...], sina_ref[...], sinb_ref[...]
    low = lanes_low(cosine.shape)
    half = HEAD_SIZE // 2
    shared = (own_ref[...].astype(F32) + other_ref[...].astype(F32)).astype(BF16)
    for part in range(3):
        w = (dq_ref[:, 128 * part : 128 * part + 128] if part < 2 else shared).astype(F32)
        turned = w * cosine + pltpu.roll(w * sinb, 128 - half, 1) + pltpu.roll(w * sina, half, 1)
        if part == 2:
            turned = jnp.where(low, turned, w)
        out_ref[:, 128 * part : 128 * part + 128] = turned.astype(BF16)


def back_rope(hi, dq, own, other, tables, first, tile):
    count = dq.shape[0]
    by_rows = lambda wide: pl.BlockSpec((tile, wide), lambda i, hi: (i, 0))
    return pl.pallas_call(
        back_rope_kernel,
        grid_spec=pltpu.PrefetchScalarGridSpec(
            num_scalar_prefetch=1,
            grid=(count // tile,),
            in_specs=[by_rows(256), by_rows(128), by_rows(128)]
            + [table_spec(tile)] * 3
            + [pl.BlockSpec(memory_space=pl.ANY)],
            out_specs=by_rows(384),
        ),
        out_shape=jax.ShapeDtypeStruct((count, 384), BF16),
        compiler_params=pltpu.CompilerParams(vmem_limit_bytes=VMEM_LIMIT),
        cost_estimate=pl.CostEstimate(flops=0, bytes_accessed=20_000_000, transcendentals=0),
        name="back_rope",
    )(hi, dq, own, other, *tables, first)


def lanes_low(shape):
    return lax.broadcasted_iota(jnp.int32, shape, 1) < HEAD_SIZE


def both_keys(kv):
    low = lanes_low(kv.shape)
    keys = kv.astype(F32)
    return (
        jnp.where(low, keys, 0.0).astype(BF16),
        jnp.where(low, 0.0, pltpu.roll(keys, HEAD_SIZE, 1)).astype(BF16),
    )


def both_values(kv):
    low = lanes_low(kv.shape)
    values = kv.astype(F32)
    return (
        jnp.where(low, pltpu.roll(values, HEAD_SIZE, 1), 0.0).astype(BF16),
        jnp.where(low, 0.0, values).astype(BF16),
    )


def attend_kernel(scalar_ref, q_ref, kv_ref, other_ref, out_ref, log_ref, keys, values, peak, sums):
    b = pl.program_id(0)
    blocks, unit, _ = q_ref.shape
    units = 2 * blocks
    length, hi = scalar_ref[0], scalar_ref[1]
    n = 2 * b + hi

    @pl.when(b == 0)
    def _():
        def spread(c, carry):
            for j, kv in (
                (2 * c + hi, kv_ref[c]),
                (2 * c + 1 - hi, other_ref[c]),
            ):
                keys[0, j], keys[1, j] = both_keys(kv)
                across = jnp.transpose(kv.astype(F32))[HEAD_SIZE:, :]
                values[j] = jnp.concatenate(
                    [across, jnp.ones((16, unit), F32)], axis=0
                ).astype(BF16)
            return carry

        lax.fori_loop(0, blocks, spread, 0)

    peak[...] = jnp.full_like(peak, MASKED)
    sums[...] = jnp.zeros_like(sums)

    def step(j, masked):
        for h in range(4):
            query = q_ref[b, :, 128 * (h // 2) : 128 * (h // 2) + 128]
            scores = dot32(keys[h % 2, j], query, ((1,), (1,)))
            if masked:
                row = j * unit + lax.broadcasted_iota(jnp.int32, scores.shape, 0)
                col = n * unit + lax.broadcasted_iota(jnp.int32, scores.shape, 1)
                scores = jnp.where((row <= col) & (row < length), scores, MASKED)
            old = peak[h, 0:1, :]
            new = jnp.maximum(old, jnp.max(scores, axis=0, keepdims=True))
            weights = jnp.exp(scores - new).astype(BF16)
            sums[h] = sums[h] * jnp.exp(old - new) + dot32(values[j], weights)
            peak[h, 0:1, :] = new

    first_ragged = units - units // 4

    def plain(j, carry):
        step(j, False)
        return carry

    def checked(j, carry):
        step(j, True)
        return carry

    lax.fori_loop(0, jnp.minimum(n, first_ragged), plain, 0)
    lax.fori_loop(jnp.minimum(n, first_ragged), n + 1, checked, 0)

    for pair in range(2):
        parts = []
        for h in (2 * pair, 2 * pair + 1):
            total = sums[h, HEAD_SIZE : HEAD_SIZE + 1, :]
            parts.append(sums[h, 0:HEAD_SIZE, :] / total)
            log_ref[0, h : h + 1, :] = peak[h, 0:1, :] + jnp.log(total)
        out_ref[0, :, 128 * pair : 128 * pair + 128] = jnp.transpose(
            jnp.concatenate(parts, axis=0)
        ).astype(BF16)


def attend(scalars, q, kv, other):
    blocks, unit, _ = q.shape
    units = 2 * blocks
    whole = lambda a: pl.BlockSpec(a.shape, lambda i: (0,) * a.ndim)
    return pl.pallas_call(
        attend_kernel,
        grid=(blocks,),
        in_specs=[pl.BlockSpec(memory_space=pltpu.SMEM), whole(q), whole(kv), whole(other)],
        out_specs=[
            pl.BlockSpec((1, unit, 256), lambda i: (i, 0, 0)),
            pl.BlockSpec((1, 8, unit), lambda i: (i, 0, 0)),
        ],
        out_shape=[
            jax.ShapeDtypeStruct((blocks, unit, 256), BF16),
            jax.ShapeDtypeStruct((blocks, 8, unit), F32),
        ],
        scratch_shapes=[
            pltpu.VMEM((2, units, unit, 128), BF16),
            pltpu.VMEM((units, HEAD_SIZE + 16, unit), BF16),
            pltpu.VMEM((4, 8, unit), F32),
            pltpu.VMEM((4, HEAD_SIZE + 16, unit), F32),
        ],
        compiler_params=pltpu.CompilerParams(vmem_limit_bytes=VMEM_LIMIT),
        cost_estimate=pl.CostEstimate(
            flops=40_000_000_000, bytes_accessed=8_000_000, transcendentals=20_000_000
        ),
        name="attend",
    )(scalars, q, kv, other)


def attend_back_kernel(
    scalar_ref,
    q_ref,
    kv_ref,
    other_ref,
    dout_ref,
    out_ref,
    log_ref,
    first_ref,
    dq_ref,
    dkv_ref,
    delta,
    dq,
    dk,
    dv,
):
    j = pl.program_id(0)
    blocks, unit, _ = q_ref.shape
    units = 2 * blocks
    length, hi = scalar_ref[0], scalar_ref[1]

    @pl.when(j == 0)
    def _():
        dq[...] = jnp.zeros_like(dq)
        pick = jnp.where(
            lax.broadcasted_iota(jnp.int32, (8, 256), 0)
            == lax.broadcasted_iota(jnp.int32, (8, 256), 1) // HEAD_SIZE,
            1.0,
            0.0,
        )

        def dots(b, carry):
            product = dout_ref[b].astype(F32) * out_ref[b].astype(F32)
            delta[b] = lax.dot_general(
                pick,
                product,
                (((1,), (1,)), ((), ())),
                precision=lax.Precision.HIGHEST,
                preferred_element_type=F32,
            )
            return carry

        lax.fori_loop(0, blocks, dots, 0)

    foreign = jnp.where(j % 2 == hi, 0, 1)
    kv = jnp.where(foreign == 0, kv_ref[j // 2], other_ref[j // 2])
    keys, values = both_keys(kv), both_values(kv)
    dk[...] = jnp.zeros_like(dk)
    dv[...] = jnp.zeros_like(dv)

    def step(b, masked):
        n = 2 * b + hi
        for pair in range(2):
            lanes = slice(128 * pair, 128 * pair + 128)
            query = q_ref[b, :, lanes]
            dout = dout_ref[b, :, lanes]
            dq_part = None
            for side in range(2):
                h = 2 * pair + side
                scores = dot32(keys[side], query, ((1,), (1,)))
                weights = jnp.exp(scores - log_ref[b, h : h + 1, :])
                if masked:
                    row = j * unit + lax.broadcasted_iota(jnp.int32, scores.shape, 0)
                    col = n * unit + lax.broadcasted_iota(jnp.int32, scores.shape, 1)
                    weights = jnp.where((row <= col) & (row < length), weights, 0.0)
                dweights = dot32(values[side], dout, ((1,), (1,)))
                dscores = (weights * (dweights - delta[b, h : h + 1, :])).astype(BF16)
                dv[side] += dot32(weights.astype(BF16), dout)
                dk[side] += dot32(dscores, query)
                part = dot32(dscores, keys[side], ((0,), (0,)))
                dq_part = part if dq_part is None else dq_part + part
            dq[b, :, lanes] += dq_part

    first_ragged = units - units // 4

    def plain(b, carry):
        step(b, False)
        return carry

    def checked(b, carry):
        step(b, True)
        return carry

    first = (j + 1 - hi) // 2
    masked_until = jnp.where(j >= first_ragged, blocks, jnp.where(foreign == 0, first + 1, first))
    lax.fori_loop(first, masked_until, checked, 0)
    lax.fori_loop(masked_until, blocks, plain, 0)

    low = lanes_low((unit, 128))
    dkey = dk[0] + pltpu.roll(dk[1], HEAD_SIZE, 1)
    dvalue = pltpu.roll(dv[0], HEAD_SIZE, 1) + dv[1]
    dkv_ref[foreign, j // 2] = jnp.where(low, dkey, dvalue).astype(BF16)

    @pl.when(j == units - 1)
    def _():
        def store(b, carry):
            dq_ref[b] = (dq[b] * ATTN_SCALE).astype(BF16)
            return carry

        lax.fori_loop(0, blocks, store, 0)


def attend_back(scalars, q, kv, other, dout, out, log, first):
    blocks, unit, _ = q.shape
    units = 2 * blocks
    whole = lambda a: pl.BlockSpec(a.shape, lambda i: (0,) * a.ndim)
    dq_shape = jax.ShapeDtypeStruct((blocks, unit, 256), BF16)
    dkv_shape = jax.ShapeDtypeStruct((2, blocks, unit, 128), BF16)
    return pl.pallas_call(
        attend_back_kernel,
        grid=(units,),
        in_specs=[
            pl.BlockSpec(memory_space=pltpu.SMEM),
            whole(q),
            whole(kv),
            whole(other),
            whole(dout),
            whole(out),
            whole(log),
            pl.BlockSpec(memory_space=pl.ANY),
        ],
        out_specs=[whole(dq_shape), whole(dkv_shape)],
        out_shape=[dq_shape, dkv_shape],
        scratch_shapes=[
            pltpu.VMEM((blocks, 8, unit), F32),
            pltpu.VMEM((blocks, unit, 256), F32),
            pltpu.VMEM((2, unit, 128), F32),
            pltpu.VMEM((2, unit, 128), F32),
        ],
        compiler_params=pltpu.CompilerParams(vmem_limit_bytes=VMEM_LIMIT),
        cost_estimate=pl.CostEstimate(
            flops=60_000_000_000, bytes_accessed=10_000_000, transcendentals=20_000_000
        ),
        name="attend_back",
    )(scalars, q, kv, other, dout, out, log, first)


PIECES = 4
MESH_ID = pl.DeviceIdType.MESH


def square_places():
    blk, lo = lax.axis_index("blk"), lax.axis_index("lo")
    mate, side = blk + 1 - 2 * (blk % 2), (blk + 2) % 4
    return blk, lo, mate, side


def greet(ids):
    barrier = pltpu.get_barrier_semaphore()
    for one in ids:
        pl.semaphore_signal(barrier, inc=1, device_id=one, device_id_type=MESH_ID)
    pl.semaphore_wait(barrier, len(ids))


def remote(source, target, send, recv, to):
    copy = pltpu.make_async_remote_copy(
        src_ref=source,
        dst_ref=target,
        send_sem=send,
        recv_sem=recv,
        device_id=to,
        device_id_type=MESH_ID,
    )
    copy.start()
    return copy


def local_copy(source, target, sem):
    copy = pltpu.make_async_copy(source, target, sem)
    copy.start()
    return copy


class Carried:
    def __init__(self, source, target, held, sem):
        self.held, self.target, self.sem = held, target, sem
        self.copy = local_copy(source, held, sem)

    def turn(self):
        self.copy.wait()
        self.copy = local_copy(self.held, self.target, self.sem)

    def wait(self):
        self.copy.wait()


def finish(copies):
    for copy in copies:
        if isinstance(copy, Carried):
            copy.turn()
    for copy in copies:
        copy.wait()


def square_peers():
    blk, lo = lax.axis_index("blk"), lax.axis_index("lo")
    mine = blk * 2 + lo
    others = [lax.rem(mine + d, 8) for d in range(1, 8)]
    return mine, others, [{"blk": o // 2, "lo": lax.rem(o, 2)} for o in others]


def other_hi():
    return {"hi": 1 - lax.axis_index("hi")}


def dp_peers():
    dp, dp_n = lax.axis_index("dp"), lax.axis_size("dp")
    return [{"dp": lax.rem(dp + d, dp_n)} for d in range(1, dp_n)]


def every_peer():
    sizes = [lax.axis_size(a) for a in ALL]
    places = [lax.axis_index(a) for a in ALL]
    found = []
    for k in range(1, math.prod(sizes)):
        to, rest = {}, k
        for a, size, place in reversed(list(zip(ALL, sizes, places))):
            to[a] = lax.rem(place + rest % size, size)
            rest //= size
        found.append(to)
    return found


def gather_begin(rows_ref, out_ref, send, recv, local, held):
    blk, lo, mate, side = square_places()
    slot = lambda b, l: b * 2 + l
    mine = slot(blk, lo)
    to_mate, to_side, to_next = {"blk": mate}, {"blk": side}, {"lo": 1 - lo}
    step = rows_ref.shape[0] // PIECES

    def push(source, place, piece, kind, to):
        target = out_ref.at[place, pl.ds(piece * step, step)]
        return remote(source, target, send.at[kind, piece], recv.at[kind, piece], to)

    own = Carried(rows_ref, out_ref.at[mine], held, local)
    piece_of = lambda p: rows_ref.at[pl.ds(p * step, step)]
    came = lambda place, p: out_ref.at[place, pl.ds(p * step, step)]
    side_order, next_order = (2, 3, 0, 1), (0, 1, 2, 3)
    by_side, by_next, by_mate, across = {}, {}, [], {}
    for k in range(PIECES):
        p, q = side_order[k], next_order[k]
        by_side[p] = push(piece_of(p), mine, p, 0, to_side)
        by_next[q] = push(piece_of(q), mine, q, 1, to_next)
    for p in range(PIECES):
        by_mate.append(push(piece_of(p), mine, p, 3, to_mate))

    def end(between=lambda k: None):
        own.turn()
        from_side, from_next, from_across = slot(side, lo), slot(blk, 1 - lo), slot(side, 1 - lo)
        for k in range(PIECES):
            p, q = side_order[k], next_order[k]
            by_side[p].wait_recv()
            if p >= 2:
                across[p] = push(came(from_side, p), from_side, p, 2, to_next)
            by_mate.append(push(came(from_side, p), from_side, p, 4, to_mate))
            by_next[q].wait_recv()
            if q < 2:
                across[q] = push(came(from_next, q), from_next, q, 2, to_side)
            by_mate.append(push(came(from_next, q), from_next, q, 5, to_mate))
            between(k)
        for p in (0, 2, 1, 3):
            across[p].wait_recv()
            by_mate.append(push(came(from_across, p), from_across, p, 6, to_mate))
            between(PIECES + p)
        for copy in by_mate:
            copy.wait()
        for copies in (by_side, by_next, across):
            for copy in copies.values():
                copy.wait_send()
        own.wait()

    return end


def gather_scratch(tok, width):
    return [
        pltpu.SemaphoreType.DMA((7, PIECES)),
        pltpu.SemaphoreType.DMA((7, PIECES)),
        pltpu.SemaphoreType.DMA,
        pltpu.VMEM((tok, width), BF16),
    ]


def sems(count):
    return [pltpu.SemaphoreType.DMA((count,))] * 2


def swap_scratch(part):
    return sems(7) + [pltpu.SemaphoreType.DMA, pltpu.VMEM(part, BF16)]


def square_greeting():
    blk, lo, mate, side = square_places()
    return [{"blk": mate}, {"blk": side}, {"lo": 1 - lo}]


def gather_kernel(rows_ref, out_ref, send, recv, local, held):
    greet(square_greeting())
    gather_begin(rows_ref, out_ref, send, recv, local, held)()


def comm_call(kernel, number, arrays, shapes, scratch, name):
    anywhere = pl.BlockSpec(memory_space=pl.ANY)
    return pl.pallas_call(
        kernel,
        in_specs=[anywhere] * len(arrays),
        out_specs=[anywhere] * len(shapes),
        out_shape=[jax.ShapeDtypeStruct(shape, dtype) for shape, dtype in shapes],
        scratch_shapes=scratch,
        compiler_params=pltpu.CompilerParams(
            collective_id=number, has_side_effects=True, vmem_limit_bytes=VMEM_LIMIT
        ),
        cost_estimate=pl.CostEstimate(flops=0, bytes_accessed=120_000_000, transcendentals=0),
        name=name,
    )(*arrays)


def gather_square(rows, number):
    tok, width = rows.shape
    (out,) = comm_call(
        gather_kernel,
        number,
        [rows],
        [((8, tok, width), rows.dtype)],
        gather_scratch(tok, width),
        "gather_square",
    )
    return out.reshape(8 * tok, width)


def swap_begin(parts_ref, out_ref, send, recv, local, held):
    mine, others, ids = square_peers()
    own = Carried(parts_ref.at[mine], out_ref.at[mine], held, local)
    copies = [
        remote(parts_ref.at[o], out_ref.at[mine], send.at[d], recv.at[d], to)
        for d, (o, to) in enumerate(zip(others, ids))
    ]
    return copies + [own]


def dp_begin(pieces, out_ref, send, recv, local, held):
    dp = lax.axis_index("dp")
    copies = []
    for k, (place, ref) in enumerate(pieces):
        copies.append(Carried(ref, out_ref.at[dp, place], held.at[k], local.at[k]))
        for d, to in enumerate(dp_peers()):
            n = 2 * d + k
            copies.append(remote(ref, out_ref.at[dp, place], send.at[n], recv.at[n], to))
    return copies


def device_place():
    mine = 0
    for a in ALL:
        mine = mine * lax.axis_size(a) + lax.axis_index(a)
    return mine


def seq_peers():
    sizes = [lax.axis_size(a) for a in SEQ]
    places = [lax.axis_index(a) for a in SEQ]
    found = []
    for k in range(1, math.prod(sizes)):
        to, source, digits, rest = {}, 0, [], k
        for size in reversed(sizes):
            digits.append(rest % size)
            rest //= size
        for a, size, place, digit in zip(SEQ, sizes, places, reversed(digits)):
            to[a] = lax.rem(place + digit, size)
            source = source * size + lax.rem(place + size - digit, size)
        found.append((to, source))
    return found


def seq_place(to):
    place = 0
    for a in SEQ:
        place = place * lax.axis_size(a) + to[a]
    return place


def open_kernel(
    rows_ref, heads_ref, small_ref, wout_ref, out_ref, weight_ref, smalls_ref, wouts_ref, g_send, g_recv,
    g_local, g_held, w_send, w_recv, d_send, d_recv, s_send, s_recv, o_send, o_recv, local, w_held, o_held,
):
    blk, hi, lo = (lax.axis_index(a) for a in SEQ)
    mine = device_place()
    peers = every_peer()
    greet(peers)
    copies = [
        Carried(heads_ref.at[blk * 2 + lo], weight_ref.at[mine], w_held, local.at[0]),
        local_copy(small_ref, smalls_ref.at[mine], local.at[1]),
        Carried(wout_ref, wouts_ref.at[hi, lo], o_held, local.at[2]),
    ]
    for k, to in enumerate(peers):
        copies.append(remote(small_ref, smalls_ref.at[mine], s_send.at[k], s_recv.at[k], to))
    end = gather_begin(rows_ref, out_ref, g_send, g_recv, g_local, g_held)
    wout = remote(wout_ref, wouts_ref.at[hi, lo], o_send.at[0], o_recv.at[0], other_hi())
    next_lo = {"lo": 1 - lo}
    copies.append(remote(wout_ref, wouts_ref.at[hi, lo], o_send.at[1], o_recv.at[1], next_lo))
    dp, seq = lax.axis_index("dp"), seq_peers()
    seq_n = len(seq) + 1
    straight = []
    for k, (to, source) in enumerate(seq):
        part = heads_ref.at[to["blk"] * 2 + to["lo"]]
        straight.append(remote(part, weight_ref.at[mine], w_send.at[k], w_recv.at[k], to))

    def hand_on(part, place, k):
        for d, to in enumerate(dp_peers()):
            n = d * seq_n + k
            copies.append(remote(part, weight_ref.at[place], d_send.at[n], d_recv.at[n], to))

    hand_on(heads_ref.at[blk * 2 + lo], mine, seq_n - 1)

    def pass_on(turn):
        for k, (to, source) in enumerate(seq):
            if k * 2 * PIECES // len(seq) == turn:
                straight[k].wait()
                place = dp * seq_n + source
                hand_on(weight_ref.at[place], place, k)

    end(pass_on)
    wout.wait()
    there = wouts_ref.at[1 - hi, lo]
    copies.append(remote(there, there, o_send.at[2], o_recv.at[2], next_lo))
    finish(copies)


def keys_kernel(
    kv_ref, gate_ref, up_ref, down_ref, other_ref, gates_ref, ups_ref, downs_ref, k_send, k_recv, g_send,
    g_recv, g_local, g_held, u_send, u_recv, u_local, u_held, d_send, d_recv,
):
    greet(square_peers()[2] + [other_hi()] + dp_peers())
    copies = [remote(kv_ref, other_ref, k_send.at[0], k_recv.at[0], other_hi())]
    for d, to in enumerate(dp_peers()):
        copies.append(remote(down_ref, downs_ref.at[d], d_send.at[d], d_recv.at[d], to))
    copies += swap_begin(gate_ref, gates_ref, g_send, g_recv, g_local, g_held)
    copies += swap_begin(up_ref, ups_ref, u_send, u_recv, u_local, u_held)
    finish(copies)


def heads_kernel(
    heads_ref, gate_ref, gate_other_ref, up_ref, mixed_ref, gates_ref, up_other_ref, m_send, m_recv,
    m_local, m_held, g_send, g_recv, u_send, u_recv, g_local, g_held,
):
    hi = lax.axis_index("hi")
    greet(square_peers()[2] + [other_hi()] + dp_peers())
    copies = swap_begin(heads_ref, mixed_ref, m_send, m_recv, m_local, m_held)
    copies.append(remote(up_ref, up_other_ref, u_send.at[0], u_recv.at[0], other_hi()))
    copies += dp_begin(
        [(hi, gate_ref), (1 - hi, gate_other_ref)], gates_ref, g_send, g_recv, g_local, g_held
    )
    finish(copies)


def rows_kernel(
    rows_ref, up_ref, up_other_ref, down_ref, out_ref, ups_ref, down_other_ref, r_send, r_recv, r_local,
    r_held, u_send, u_recv, d_send, d_recv, u_local, u_held,
):
    hi = lax.axis_index("hi")
    greet(square_greeting() + [other_hi()] + dp_peers())
    end = gather_begin(rows_ref, out_ref, r_send, r_recv, r_local, r_held)
    copies = [remote(down_ref, down_other_ref, d_send.at[0], d_recv.at[0], other_hi())]
    copies += dp_begin(
        [(hi, up_ref), (1 - hi, up_other_ref)], ups_ref, u_send, u_recv, u_local, u_held
    )
    end()
    finish(copies)


def sum_begin(own_ref, got_ref, place, own, got, sem):
    return [
        local_copy(own_ref.at[place], own, sem.at[0]),
        local_copy(got_ref.at[place], got, sem.at[1]),
    ]


def wait_all(copies):
    for copy in copies:
        copy.wait()


def douts_kernel(
    parts_ref, gate_ref, gate_got_ref, up_ref, up_got_ref, out_ref, gate_away_ref, up_away_ref, send, recv, local,
    held, own, got, sem,
):
    hi = lax.axis_index("hi")
    loads = [
        [local_copy(ref.at[1 - hi], own.at[k], sem.at[k, 0]), local_copy(got_ref, got.at[k], sem.at[k, 1])]
        for k, (ref, got_ref) in enumerate(((gate_ref, gate_got_ref), (up_ref, up_got_ref)))
    ]
    greet(square_peers()[2])
    copies = swap_begin(parts_ref, out_ref, send, recv, local, held)
    for k, target in enumerate((gate_away_ref, up_away_ref)):
        wait_all(loads[k])
        target[...] = (own[k] + got[k].astype(F32)).astype(BF16)
    finish(copies)


def sum_three(place, own_ref, over_dp_ref, over_hi_ref, own, over_dp, over_hi, sem):
    return [
        local_copy(own_ref.at[place], own, sem.at[0]),
        local_copy(over_dp_ref, over_dp, sem.at[1]),
        local_copy(over_hi_ref, over_hi, sem.at[2]),
    ]


def dkeys_kernel(
    dkv_ref, gate_ref, gate_dp_ref, gate_hi_ref, other_ref, gates_ref, k_send, k_recv, g_send, g_recv, g_local,
    g_held, own, over_dp, over_hi, made, sem,
):
    hi = lax.axis_index("hi")
    loads = sum_three(hi, gate_ref, gate_dp_ref, gate_hi_ref, own, over_dp, over_hi, sem)
    greet(square_peers()[2] + [other_hi()])
    copies = [remote(dkv_ref.at[1], other_ref, k_send.at[0], k_recv.at[0], other_hi())]
    wait_all(loads)
    made[...] = (own[...] + over_dp[...].astype(F32) + over_hi[...].astype(F32)).astype(BF16)
    copies += swap_begin(made, gates_ref, g_send, g_recv, g_local, g_held)
    finish(copies)


class OwnOut:
    def __init__(self, out_ref, outs_ref, send, recv, local, own, got, made):
        self.outs_ref, self.made, self.send, self.recv, self.local = outs_ref, made, send, recv, local
        self.own, self.got = own, got
        self.dp, self.hi, self.lo = (lax.axis_index(a) for a in ("dp", "hi", "lo"))
        self.load = local_copy(out_ref, own, local.at[0])
        self.over = remote(out_ref, got, send.at[0], recv.at[0], dp_peers()[0])

    def push(self, a, b):
        hi, lo = lax.rem(self.hi + a, 2), lax.rem(self.lo + b, 2)
        return pltpu.make_async_remote_copy(
            src_ref=self.made.at[hi, lo],
            dst_ref=self.outs_ref.at[self.hi],
            send_sem=self.send.at[1 + 2 * a + b],
            recv_sem=self.recv.at[1 + self.hi],
            device_id={"hi": hi, "lo": lo},
            device_id_type=MESH_ID,
        )

    def own_copy(self):
        return pltpu.make_async_copy(
            self.made.at[self.hi, self.lo], self.outs_ref.at[self.hi], self.local.at[1]
        )

    def turn(self):
        self.load.wait()
        self.over.wait()
        self.made[...] = (self.own[...].astype(F32) + self.got[...].astype(F32)).astype(BF16)

        @pl.when(self.dp == self.lo)
        def _():
            for a, b in ((0, 1), (1, 0), (1, 1)):
                self.push(a, b).start()
            self.own_copy().start()

    def wait(self):
        @pl.when(self.dp == self.lo)
        def _():
            for a, b in ((0, 1), (1, 0), (1, 1)):
                self.push(a, b).wait_send()
            self.own_copy().wait()

        for h in range(2):

            @pl.when(jnp.logical_not((h == self.hi) & (self.dp == self.lo)))
            def _(h=h):
                pltpu.make_async_remote_copy(
                    src_ref=self.made.at[0, 0],
                    dst_ref=self.outs_ref.at[h],
                    send_sem=self.send.at[1],
                    recv_sem=self.recv.at[1 + h],
                    device_id={"lo": 1 - self.lo},
                    device_id_type=MESH_ID,
                ).wait_recv()


def close_kernel(with_out, *refs):
    refs = iter(refs)
    take = lambda n: [next(refs) for _ in range(n)]
    parts_ref, heads_ref, up_ref, up_dp_ref, up_hi_ref, square_ref = take(6)
    out_rows_ref = next(refs) if with_out else None
    total_ref, head_ref, ups_ref, squares_ref = take(4)
    outs_ref = next(refs) if with_out else None
    scatter = take(9)
    h_send, h_recv, s_send, s_recv, local, h_held = take(6)
    swap = take(4)
    own, over_dp, over_hi, made, sem = take(5)
    out_scratch = take(6) if with_out else None
    mine = device_place()
    peers, seq = every_peer(), seq_peers()
    place = seq_place({a: lax.axis_index(a) for a in SEQ})
    loads = scatter_load(parts_ref, scatter)
    hi = lax.axis_index("hi")
    up_loads = sum_three(hi, up_ref, up_dp_ref, up_hi_ref, own, over_dp, over_hi, sem)
    greet(peers)
    copies = [
        Carried(heads_ref.at[place], head_ref.at[place], h_held, local.at[0]),
        local_copy(square_ref, squares_ref.at[mine], local.at[1]),
    ]
    mates = scatter_mates(parts_ref, scatter)
    for k, to in enumerate(peers):
        copies.append(remote(square_ref, squares_ref.at[mine], s_send.at[k], s_recv.at[k], to))
    for k, (to, source) in enumerate(seq):
        part = heads_ref.at[seq_place(to)]
        copies.append(remote(part, head_ref.at[place], h_send.at[k], h_recv.at[k], to))
    own_out = OwnOut(out_rows_ref, outs_ref, *out_scratch) if with_out else None
    wait_all(up_loads)
    made[...] = (own[...] + over_dp[...].astype(F32) + over_hi[...].astype(F32)).astype(BF16)
    copies += swap_begin(made, ups_ref, *swap)
    scatter_end_square(loads, mates, total_ref, scatter, own_out.turn if with_out else None)
    finish(copies)
    if with_out:
        own_out.wait()


def remote_to(source, target, sems_of, kind, piece, to):
    send, recv = sems_of
    return remote(source, target, send.at[kind, piece], recv.at[kind, piece], to)


def scatter_load(parts_ref, scratch):
    mine, local = scratch[0], scratch[8]
    blk, lo, mate, side = square_places()
    places = (side * 2 + 1 - lo, side * 2 + lo, blk * 2 + 1 - lo, blk * 2 + lo)
    return [local_copy(parts_ref.at[p], mine.at[k], local.at[k]) for k, p in enumerate(places)]


def scatter_mates(parts_ref, scratch):
    mates, sems_of = scratch[1], scratch[6:8]
    blk, lo, mate, side = square_places()
    mate_side = (mate + 2) % 4
    places = (mate_side * 2 + 1 - lo, mate_side * 2 + lo, mate * 2 + 1 - lo, mate * 2 + lo)
    step = parts_ref.shape[1] // PIECES
    rows = lambda p: pl.ds(p * step, step)
    orders = ((0, 2, 1, 3), (0, 1, 2, 3), (2, 3, 0, 1), (0, 1, 2, 3))
    return {
        (k, p): remote_to(
            parts_ref.at[places[k], rows(p)], mates.at[k, rows(p)], sems_of, k, p, {"blk": mate}
        )
        for k in range(4)
        for p in orders[k]
    }


def scatter_end_square(loads, from_mate, out_ref, scratch, between=None, work=()):
    work = list(work)
    mine, mates, made, got_across, got_side, got_next = scratch[:6]
    sems_of = scratch[6:8]
    blk, lo, mate, side = square_places()
    to_side, to_next = {"blk": side}, {"lo": 1 - lo}
    step = mine.shape[1] // PIECES
    rows = lambda p: pl.ds(p * step, step)

    def summed(k, p):
        from_mate[k, p].wait_recv()
        return mine[k, rows(p), :].astype(F32) + mates[k, rows(p), :].astype(F32)

    sent = {}
    loads[0].wait()
    for p in (0, 2, 1, 3):
        made[0, rows(p), :] = summed(0, p).astype(BF16)
        sent[0, p] = remote_to(
            made.at[0, rows(p)],
            got_across.at[rows(p)],
            sems_of,
            4,
            p,
            to_side if p < 2 else to_next,
        )
    loads[1].wait()
    loads[2].wait()
    for n, (k, p) in enumerate(((1, 0), (2, 2), (1, 1), (2, 3), (1, 2), (2, 0), (1, 3), (2, 1))):
        if work and n % 2 == 0:
            work.pop(0)()
        total = summed(k, p)
        if (k == 1) == (p >= 2):
            sent[0, p].wait_recv()
            total = total + got_across[rows(p), :].astype(F32)
        made[k, rows(p), :] = total.astype(BF16)
        sent[k, p] = remote_to(
            made.at[k, rows(p)],
            (got_side if k == 1 else got_next).at[rows(p)],
            sems_of,
            4 + k,
            p,
            to_side if k == 1 else to_next,
        )
    for one in work:
        one()
    if between is not None:
        between()
    loads[3].wait()
    for p in range(PIECES):
        total = summed(3, p)
        sent[1, p].wait_recv()
        sent[2, p].wait_recv()
        out_ref[rows(p), :] = (
            total + got_side[rows(p), :].astype(F32) + got_next[rows(p), :].astype(F32)
        )
    for copy in from_mate.values():
        copy.wait_send()
    for copy in sent.values():
        copy.wait_send()


def scatter_scratch(tok, width):
    return [
        pltpu.VMEM((4, tok, width), BF16),
        pltpu.VMEM((4, tok, width), BF16),
        pltpu.VMEM((3, tok, width), BF16),
        pltpu.VMEM((tok, width), BF16),
        pltpu.VMEM((tok, width), BF16),
        pltpu.VMEM((tok, width), BF16),
        pltpu.SemaphoreType.DMA((7, PIECES)),
        pltpu.SemaphoreType.DMA((7, PIECES)),
        pltpu.SemaphoreType.DMA((4,)),
    ]


def scatter_kernel(firsts, parts_ref, *refs):
    out_ref, scratch = refs[firsts], refs[firsts + 1 :]
    loads = scatter_load(parts_ref, scratch)
    greet(square_greeting())
    scatter_end_square(loads, scatter_mates(parts_ref, scratch), out_ref, scratch)


def scatter_square(parts, number, *first):
    count, width = parts.shape
    tok = count // 8
    return pl.pallas_call(
        functools.partial(scatter_kernel, len(first)),
        in_specs=[pl.BlockSpec(memory_space=pl.ANY)] * (1 + len(first)),
        out_specs=pl.BlockSpec(memory_space=pltpu.VMEM),
        out_shape=jax.ShapeDtypeStruct((tok, width), F32),
        scratch_shapes=scatter_scratch(tok, width),
        compiler_params=pltpu.CompilerParams(
            collective_id=number, has_side_effects=True, vmem_limit_bytes=VMEM_LIMIT
        ),
        cost_estimate=pl.CostEstimate(flops=0, bytes_accessed=120_000_000, transcendentals=0),
        name="scatter_square",
    )(parts.astype(BF16).reshape(8, tok, width), *first)


def scatter_down_kernel(
    parts_ref, down_ref, got_ref, rows_ref, dgate_ref, dup_ref, out_ref, sum_ref, gate_own_ref, up_own_ref,
    gate_stay_ref, up_stay_ref, gate_got_ref, up_got_ref, *scratch,
):
    scratch, rest = scratch[:9], scratch[9:]
    own, got, away, came, sem, send, recv, left, gate_right, up_right, gate_away, up_away, w_sem = rest
    dp, hi = lax.axis_index("dp"), lax.axis_index("hi")
    part = left.shape[2]
    blocks = ((1 - dp, 1 - hi), (dp, 1 - hi), (1 - dp, hi), (dp, hi))

    def load_left(n):
        d, h = blocks[n]
        cols = pl.ds(pl.multiple_of((d * 2 + h) * part, part), part)
        return local_copy(rows_ref.at[:, cols], left.at[n % 2], w_sem.at[n % 2])

    rights = [local_copy(dgate_ref, gate_right, w_sem.at[2]), local_copy(dup_ref, up_right, w_sem.at[3])]
    lefts = {0: load_left(0), 1: load_left(1)}
    down = sum_begin(down_ref, got_ref, 1 - hi, own, got, sem)
    loads = scatter_load(parts_ref, scratch)
    greet(square_greeting() + [other_hi()] + dp_peers())
    mates = scatter_mates(parts_ref, scratch)
    wait_all(down)
    away[...] = (own[...] + got[...].astype(F32)).astype(BF16)
    over = remote(away, came, send.at[0], recv.at[0], other_hi())
    down = sum_begin(down_ref, got_ref, hi, own, got, sem)
    pairs = []

    def gradient(n, up):
        if not up:
            lefts[n].wait()
        if n == 0:
            rights[up].wait()
        total = dot32(left[n % 2], (up_right if up else gate_right)[...], ((0,), (0,)))
        if n == 0:
            target, got_there = (up_away, up_got_ref) if up else (gate_away, gate_got_ref)
            target[...] = total.astype(BF16)
            pairs.append(remote(target, got_there, send.at[1 + up], recv.at[1 + up], dp_peers()[0]))
        elif n == 2:
            (up_stay_ref if up else gate_stay_ref)[...] = total.astype(BF16)
        else:
            (up_own_ref if up else gate_own_ref)[blocks[n][1]] = total
        if up and n < 2:
            lefts[n + 2] = load_left(n + 2)

    work = [functools.partial(gradient, n, up) for n in range(4) for up in range(2)]
    scatter_end_square(loads, mates, out_ref, scratch, work=work)
    wait_all(down)
    over.wait()
    sum_ref[...] = own[...] + got[...].astype(F32) + came[...].astype(F32)
    wait_all(pairs)


def scatter_down(parts, number, down, rows, dgate, dup):
    count, width = parts.shape
    tok = count // 8
    part = down[0].shape[1:]
    depth, cols = dgate.shape
    grad = (rows.shape[1] // 4, cols)
    anywhere, inside = pl.BlockSpec(memory_space=pl.ANY), pl.BlockSpec(memory_space=pltpu.VMEM)
    return pl.pallas_call(
        scatter_down_kernel,
        in_specs=[anywhere] * 6,
        out_specs=[inside] * 6 + [anywhere] * 2,
        out_shape=[
            jax.ShapeDtypeStruct((tok, width), F32),
            jax.ShapeDtypeStruct(part, F32),
            jax.ShapeDtypeStruct((2,) + grad, F32),
            jax.ShapeDtypeStruct((2,) + grad, F32),
        ]
        + [jax.ShapeDtypeStruct(grad, BF16)] * 4,
        scratch_shapes=scatter_scratch(tok, width)
        + [pltpu.VMEM(part, F32)]
        + [pltpu.VMEM(part, BF16)] * 3
        + [pltpu.SemaphoreType.DMA((2,))]
        + sems(3)
        + [
            pltpu.VMEM((2, depth, grad[0]), BF16),
            pltpu.VMEM((depth, cols), BF16),
            pltpu.VMEM((depth, cols), BF16),
            pltpu.VMEM(grad, BF16),
            pltpu.VMEM(grad, BF16),
            pltpu.SemaphoreType.DMA((4,)),
        ],
        compiler_params=pltpu.CompilerParams(
            collective_id=number, has_side_effects=True, vmem_limit_bytes=VMEM_LIMIT
        ),
        cost_estimate=pl.CostEstimate(
            flops=4 * depth * cols * rows.shape[1], bytes_accessed=160_000_000, transcendentals=0
        ),
        name="scatter_down",
    )(parts.reshape(8, tok, width), *down, rows, dgate, dup)


def swap_square(blocks):
    return lax.all_to_all(blocks, SQUARE, split_axis=0, concat_axis=0, tiled=True)


def swap_pair(block, axis):
    return lax.ppermute(block, axis, [(0, 1), (1, 0)])


def gather_start(rows, axis):
    if lax.axis_size(axis) != 2:
        return lax.all_gather(rows, axis, axis=0, tiled=False)
    return rows, swap_pair(rows, axis)


def gather_end(parts, axis):
    if lax.axis_size(axis) != 2:
        return parts
    rows, other = parts
    first = lax.axis_index(axis) == 0
    return jnp.stack([jnp.where(first, rows, other), jnp.where(first, other, rows)])


def scatter_start(parts, axis):
    if lax.axis_size(axis) != 2:
        return lax.psum_scatter(parts.astype(BF16), axis, scatter_dimension=0, tiled=False)
    place = lax.axis_index(axis)
    away = lax.dynamic_index_in_dim(parts, 1 - place, 0, False).astype(BF16)
    own = lax.dynamic_index_in_dim(parts, place, 0, False)
    return own, swap_pair(away, axis)


def scatter_end(parts, axis):
    if lax.axis_size(axis) != 2:
        return parts.astype(F32)
    return parts[0] + parts[1].astype(F32)


def by_copy(rows):
    dp_n, hi_n = lax.axis_size("dp"), lax.axis_size("hi")
    return rows.reshape((dp_n, hi_n, rows.shape[0] // (dp_n * hi_n)) + rows.shape[1:])


def total_of(value, axes, count):
    spread = jnp.broadcast_to(value.reshape(1, 1), (count, 1))
    return jnp.sum(lax.all_to_all(spread, axes, split_axis=0, concat_axis=0, tiled=True))


def norm_parts(rows):
    inverse = lax.rsqrt(jnp.mean(rows * rows, axis=-1, keepdims=True) + NORM_EPS)
    return rows * inverse, inverse


def reorder(pairs, block, source, target, cast):
    for at, to in pairs:
        target[:, to * block : to * block + block] = cast(source[:, at * block : at * block + block])


def out_kernel(order, pairs, block, mixed_ref, weight_ref, rows_ref, gain_ref, middle_ref, normed_ref, total):
    f = pl.program_id(0)

    @pl.when(f == 0)
    def _():
        total[...] = jnp.zeros_like(total)

    total[...] += dot32(mixed_ref[0], weight_ref[...])

    @pl.when(f == pl.num_programs(0) - 1)
    def _():
        middle = rows_ref[...].astype(F32) + RESIDUAL_SCALE * total[...]
        middle_ref[...] = middle
        total[...] = norm_parts(middle)[0] * gain_ref[...]
        reorder(pairs, block, total, normed_ref, lambda v: v.astype(BF16))


def out_project(mixed, weight, rows, gain, order, pairs, block):
    group, tok, cols = mixed.shape
    width = weight.shape[1]
    whole = pl.BlockSpec((tok, width), lambda f: (0, 0))
    return pl.pallas_call(
        functools.partial(out_kernel, order, pairs, block),
        grid=(group,),
        in_specs=[
            pl.BlockSpec((1, tok, cols), lambda f: (f, 0, 0)),
            pl.BlockSpec((cols, width), lambda f: (order(f), 0)),
            whole,
            pl.BlockSpec((1, width), lambda f: (0, 0)),
        ],
        out_specs=[whole, whole],
        out_shape=[
            jax.ShapeDtypeStruct((tok, width), F32),
            jax.ShapeDtypeStruct((tok, width), BF16),
        ],
        scratch_shapes=[pltpu.VMEM((tok, width), F32)],
        compiler_params=pltpu.CompilerParams(vmem_limit_bytes=VMEM_LIMIT),
        cost_estimate=pl.CostEstimate(
            flops=2 * tok * width * width, bytes_accessed=16_000_000, transcendentals=0
        ),
        name="out_project",
    )(mixed, weight, rows, gain)


def out_back_kernel(
    pairs, block, grad_ref, middle_ref, result_ref, gain_ref, weight_ref, first_ref, sum_ref, rows_ref, mixed_ref, work
):
    f = pl.program_id(0)

    @pl.when(f == 0)
    def _():
        reorder(pairs, block, grad_ref, work, lambda v: v)
        normal, inverse = norm_parts(middle_ref[...])
        grad = work[...] * gain_ref[...]
        total = result_ref[...] + inverse * (
            grad - normal * jnp.mean(grad * normal, axis=-1, keepdims=True)
        )
        sum_ref[...] = total
        rows_ref[...] = (RESIDUAL_SCALE * total).astype(BF16)

    mixed_ref[0] = dot32(rows_ref[...], weight_ref[...], ((1,), (1,))).astype(BF16)


def out_back(grad, middle, result, gain, weight, first, cols, order, pairs, block):
    tok, width = middle.shape
    group = width // cols
    whole = pl.BlockSpec((tok, width), lambda f: (0, 0))
    return pl.pallas_call(
        functools.partial(out_back_kernel, pairs, block),
        grid=(group,),
        in_specs=[
            whole,
            whole,
            whole,
            pl.BlockSpec((1, width), lambda f: (0, 0)),
            pl.BlockSpec((cols, width), lambda f: (order(f), 0)),
            pl.BlockSpec(memory_space=pl.ANY),
        ],
        out_specs=[whole, whole, pl.BlockSpec((1, tok, cols), lambda f: (f, 0, 0))],
        out_shape=[
            jax.ShapeDtypeStruct((tok, width), F32),
            jax.ShapeDtypeStruct((tok, width), BF16),
            jax.ShapeDtypeStruct((group, tok, cols), BF16),
        ],
        scratch_shapes=[pltpu.VMEM((tok, width), F32)],
        compiler_params=pltpu.CompilerParams(vmem_limit_bytes=VMEM_LIMIT),
        cost_estimate=pl.CostEstimate(
            flops=2 * tok * width * width, bytes_accessed=20_000_000, transcendentals=0
        ),
        name="out_back",
    )(grad, middle, result, gain, weight, first)


def weight_grad_kernel(dp_ref, left_ref, right_ref, first_ref, away_ref, own_ref):
    i = pl.program_id(0)
    total = dot32(left_ref[...], right_ref[...], ((0,), (0,)))

    @pl.when(i < 2)
    def _():
        away_ref[0] = total.astype(BF16)

    @pl.when(i >= 2)
    def _():
        own_ref[0] = total


def weight_grad_start(left, right, first):
    dp_n, hi_n = lax.axis_size("dp"), lax.axis_size("hi")
    depth, rows = left.shape
    cols = right.shape[1]
    if dp_n != 2:
        sums = scatter_start(by_copy(dot32(left, right, ((0,), (0,)))), "dp")
        return sums.astype(F32), jnp.zeros(sums.shape, BF16)
    part = rows // (dp_n * hi_n)
    place = lax.axis_index("dp").astype(jnp.int32).reshape(1)
    away, own = pl.pallas_call(
        weight_grad_kernel,
        grid_spec=pltpu.PrefetchScalarGridSpec(
            num_scalar_prefetch=1,
            grid=(4,),
            in_specs=[
                pl.BlockSpec(
                    (depth, part),
                    lambda i, dp: (0, jnp.where(i < 2, 2 * (1 - dp[0]) + i, 2 * dp[0] + i - 2)),
                ),
                pl.BlockSpec((depth, cols), lambda i, dp: (0, 0)),
                pl.BlockSpec(memory_space=pl.ANY),
            ],
            out_specs=[
                pl.BlockSpec((1, part, cols), lambda i, dp: (jnp.minimum(i, 1), 0, 0)),
                pl.BlockSpec((1, part, cols), lambda i, dp: (jnp.maximum(i - 2, 0), 0, 0)),
            ],
        ),
        out_shape=[
            jax.ShapeDtypeStruct((2, part, cols), BF16),
            jax.ShapeDtypeStruct((2, part, cols), F32),
        ],
        compiler_params=pltpu.CompilerParams(vmem_limit_bytes=VMEM_LIMIT),
        cost_estimate=pl.CostEstimate(
            flops=2 * depth * rows * cols, bytes_accessed=24_000_000, transcendentals=0
        ),
        name="weight_grad",
    )(place, left, right, first)
    return own, away


def ff_back_kernel(
    tile, grad_ref, gate_slope_ref, up_slope_ref, gate_ref, up_ref, down_ref, first_ref, dgate_ref, dup_ref,
    out_ref, total,
):
    total[...] = jnp.zeros_like(total)

    def step(t, carry):
        cols = pl.ds(pl.multiple_of(t * tile, tile), tile)
        dunits = dot32(grad_ref[...], down_ref[cols, :], ((1,), (1,)))
        dgate = (dunits * gate_slope_ref[:, cols].astype(F32)).astype(BF16)
        dup = (dunits * up_slope_ref[:, cols].astype(F32)).astype(BF16)
        dgate_ref[:, cols] = dgate
        dup_ref[:, cols] = dup
        total[...] += dot32(dgate, gate_ref[:, cols], ((1,), (1,))) + dot32(
            dup, up_ref[:, cols], ((1,), (1,))
        )
        return carry

    lax.fori_loop(0, down_ref.shape[0] // tile, step, 0)
    out_ref[...] = total[...].astype(BF16)


def ff_back(grad, gate_slope, up_slope, gate_weight, up_weight, down_weight, first, tok):
    count, width = grad.shape
    ff = down_weight.shape[0]
    rows = lambda cols: pl.BlockSpec((tok, cols), lambda i: (i, 0))
    whole = lambda a: pl.BlockSpec(a.shape, lambda i: (0, 0), pipeline_mode=pl.Buffered(1))
    return pl.pallas_call(
        functools.partial(ff_back_kernel, ff),
        grid=(count // tok,),
        in_specs=[
            rows(width),
            rows(ff),
            rows(ff),
            whole(gate_weight),
            whole(up_weight),
            whole(down_weight),
            pl.BlockSpec(memory_space=pl.ANY),
        ],
        out_specs=[rows(ff), rows(ff), rows(width)],
        out_shape=[
            jax.ShapeDtypeStruct((count, ff), BF16),
            jax.ShapeDtypeStruct((count, ff), BF16),
            jax.ShapeDtypeStruct((count, width), BF16),
        ],
        scratch_shapes=[pltpu.VMEM((tok, width), F32)],
        compiler_params=pltpu.CompilerParams(vmem_limit_bytes=VMEM_LIMIT),
        cost_estimate=pl.CostEstimate(
            flops=6 * count * width * ff, bytes_accessed=40_000_000, transcendentals=0
        ),
        name="ff_back",
    )(grad, gate_slope, up_slope, gate_weight, up_weight, down_weight, first)


def deal_kernel(
    key_head, places, wide, query_ref, key_ref, value_ref, gate_ref, up_ref, heads_ref, gates_ref, ups_ref
):
    columns, k_columns = query_ref.shape[1] // 8, key_ref.shape[1] // 8
    for f in range(8):
        g = key_head(f)
        cols, k_cols = slice(g * columns, g * columns + columns), slice(g * k_columns, g * k_columns + k_columns)
        heads_ref[f, :, :columns] = query_ref[:, cols]
        heads_ref[f, :, columns:] = jnp.concatenate([key_ref[:, k_cols], value_ref[:, k_cols]], axis=1)
    for at, (f, to) in enumerate(places):
        here, there = slice(at * wide, at * wide + wide), slice(to * wide, to * wide + wide)
        gates_ref[f, :, there] = gate_ref[:, here]
        ups_ref[f, :, there] = up_ref[:, here]


def collect_kernel(
    places, wide, gates_ref, ups_ref, gate_ref, up_ref, gain_ref, dgate_ref, dup_ref, dgain_ref
):
    total = jnp.zeros((gate_ref.shape[0], wide), F32)
    for at, (f, to) in enumerate(places):
        here, there = slice(at * wide, at * wide + wide), slice(to * wide, to * wide + wide)
        dgate, dup = gates_ref[f, :, there].astype(F32), ups_ref[f, :, there].astype(F32)
        dgate_ref[:, here] = dgate
        dup_ref[:, here] = dup
        total += gate_ref[:, here].astype(F32) * dgate + up_ref[:, here].astype(F32) * dup
    dgain_ref[...] = jnp.sum(total, axis=1, keepdims=True) / gain_ref[...]


def final_kernel(
    key_head, places, wide, first_ref, middle_ref, rows_ref, gain_ref, heads_ref, query_ref, key_ref, value_ref,
    gates_ref, ups_ref, gate_ref, up_ref, small_ref, outs_ref, down_ref, dhidden_ref, dquery_ref, dkey_ref,
    dvalue_ref, dgain_one_ref, dgate_ref, dup_ref, dgain_two_ref, dout_ref, ddown_ref,
):
    rows_w = gate_ref.shape[0]
    normal, inverse = norm_parts(rows_ref[...].astype(F32))
    grad = first_ref[...] * gain_ref[...]
    dhidden_ref[...] = middle_ref[...] + inverse * (
        grad - normal * jnp.mean(grad * normal, axis=-1, keepdims=True)
    )
    gains = jnp.transpose(jnp.broadcast_to(small_ref[0:1, :], (128, 128)))[:, 0:1]
    columns = query_ref.shape[1] // 8
    k_columns = key_ref.shape[1] // 8
    total = jnp.zeros((rows_w, columns), F32)
    k_total = jnp.zeros((rows_w, k_columns), F32)
    for f in range(8):
        b, l, g = f // 2, f % 2, key_head(f)
        both = heads_ref[b * 4 + l].astype(F32) + heads_ref[b * 4 + 2 + l].astype(F32)
        cols, k_cols = slice(g * columns, g * columns + columns), slice(g * k_columns, g * k_columns + k_columns)
        dquery = both[:, :columns]
        dkey, dvalue = both[:, columns : columns + k_columns], both[:, columns + k_columns :]
        dquery_ref[:, cols], dkey_ref[:, k_cols], dvalue_ref[:, k_cols] = dquery, dkey, dvalue
        total += query_ref[:, cols].astype(F32) * dquery
        k_total += key_ref[:, k_cols].astype(F32) * dkey + value_ref[:, k_cols].astype(F32) * dvalue
    dgain_one_ref[...] = (
        jnp.sum(total, axis=1, keepdims=True) + jnp.sum(k_total, axis=1, keepdims=True)
    ) / gains[:rows_w]
    total = jnp.zeros((rows_w, wide), F32)
    for at, (f, to) in enumerate(places):
        here, there = slice(at * wide, at * wide + wide), slice(to * wide, to * wide + wide)
        dgate, dup = gates_ref[f, :, there].astype(F32), ups_ref[f, :, there].astype(F32)
        dgate_ref[:, here] = dgate
        dup_ref[:, here] = dup
        total += gate_ref[:, here].astype(F32) * dgate + up_ref[:, here].astype(F32) * dup
    dgain_two_ref[...] = jnp.sum(total, axis=1, keepdims=True) / gains[rows_w : 2 * rows_w]
    dout_ref[...] = outs_ref[0].astype(F32) + outs_ref[1].astype(F32)
    ddown_ref[...] = down_ref[...]


def shards(
    hidden,
    teacher,
    lengths,
    attn_gain,
    w_query,
    key_projection,
    value_projection,
    w_out,
    mlp_gain,
    w_gate,
    w_up,
    w_down,
):
    dp_n, blk_n, hi_n, lo_n = (lax.axis_size(a) for a in ALL)
    group = blk_n * lo_n
    every = dp_n * blk_n * hi_n * lo_n
    hi, lo = lax.axis_index("hi"), lax.axis_index("lo")
    blk = lax.axis_index("blk")
    tok = hidden.shape[1]
    seq_len = tok * blk_n * hi_n * lo_n
    width = hidden.shape[2]
    rows_w = w_query.shape[0]
    units_w = w_down.shape[0]
    ff_part = w_gate.shape[1] // group

    block = lo_n * rows_w
    if block % 128 == 0:
        to_inner = [
            ((d * blk_n + b) * hi_n + h, (d * hi_n + h) * blk_n + b)
            for d in range(dp_n)
            for b in range(blk_n)
            for h in range(hi_n)
        ]
        reblock = block
    else:
        to_inner, reblock = [(0, 0)], width
    to_outer = [(to, at) for at, to in to_inner]

    def inner(a):
        if reblock == block:
            return a
        return a.reshape(-1, dp_n, blk_n, hi_n, block).transpose(0, 1, 3, 2, 4).reshape(-1, width)

    def outer(a):
        if reblock == block:
            return a
        return a.reshape(-1, dp_n, hi_n, blk_n, block).transpose(0, 1, 3, 2, 4).reshape(-1, width)

    key_head = lambda f: (f % lo_n) * blk_n + f // lo_n

    def head_columns(w):
        cols = w.shape[1] // group
        return w.reshape(rows_w, lo_n, blk_n, cols).transpose(2, 1, 0, 3).reshape(group, rows_w, cols)

    def head_columns_back(g):
        cols = g.shape[2]
        return (
            g.reshape(blk_n, lo_n, rows_w, cols).transpose(2, 1, 0, 3).reshape(rows_w, group * cols)
        )

    def unit_columns(w):
        return (
            w.reshape(rows_w, dp_n, blk_n, hi_n, lo_n, units_w)
            .transpose(2, 4, 0, 1, 3, 5)
            .reshape(group, rows_w, ff_part)
        )

    def unit_columns_back(g):
        return (
            g.reshape(blk_n, lo_n, rows_w, dp_n, hi_n, units_w)
            .transpose(2, 3, 0, 4, 1, 5)
            .reshape(rows_w, group * ff_part)
        )

    q_cols = w_query.shape[1] // group
    k_cols = key_projection.shape[1] // group
    ff_places = [
        (b * lo_n + l, d * hi_n + h)
        for d in range(dp_n)
        for b in range(blk_n)
        for h in range(hi_n)
        for l in range(lo_n)
    ]
    part_shape = jax.ShapeDtypeStruct((group, rows_w, ff_part), BF16)
    params = pltpu.CompilerParams(vmem_limit_bytes=VMEM_LIMIT)
    if units_w % 128 == 0:
        head_shape = jax.ShapeDtypeStruct((group, rows_w, q_cols + 2 * k_cols), BF16)
        head_parts, gate_parts, up_parts = pl.pallas_call(
            functools.partial(deal_kernel, key_head, ff_places, units_w),
            out_shape=[head_shape, part_shape, part_shape],
            compiler_params=params,
            name="deal",
        )(w_query, key_projection, value_projection, w_gate, w_up)
    else:
        head_parts = jnp.concatenate(
            [head_columns(w) for w in (w_query, key_projection, value_projection)], axis=2
        )
        gate_parts, up_parts = unit_columns(w_gate), unit_columns(w_up)
    head_wide = head_parts.shape[2]

    pad = jnp.zeros((7 * 128 + 128 - 2 * rows_w - 1,), F32)
    small = jnp.concatenate(
        [attn_gain.astype(F32), mlp_gain.astype(F32), lengths.astype(F32), pad]
    ).reshape(8, 128)
    rows_all, qkv_weight, smalls, out_rows = comm_call(
        open_kernel,
        0,
        [hidden[0], head_parts, small, w_out],
        [
            ((group, tok, width), BF16),
            ((every, rows_w, head_wide), BF16),
            ((every, 8, 128), F32),
            ((hi_n, lo_n, rows_w, width), BF16),
        ],
        gather_scratch(tok, width)
        + sems(every // dp_n - 1)
        + sems((dp_n - 1) * every // dp_n)
        + sems(every - 1)
        + sems(3)
        + [
            pltpu.SemaphoreType.DMA((3,)),
            pltpu.VMEM((rows_w, head_wide), BF16),
            pltpu.VMEM((rows_w, width), BF16),
        ],
        "open",
    )
    qkv_weight = qkv_weight.reshape(width, head_wide)
    gain_one = smalls[:, 0, :rows_w].reshape(1, width)
    gain_two = smalls[:, 0, rows_w : 2 * rows_w].reshape(1, width)
    valid_count = jnp.sum(smalls.reshape(every, -1)[:: every // dp_n, 2 * rows_w])
    hi_index = hi.astype(jnp.int32).reshape(1)
    tables = rope_tables(seq_len)
    normed_one, q, kv = project(
        hi_index, rows_all.reshape(group * tok, width), gain_one, qkv_weight, tables, tok
    )
    unit = lo_n * tok
    part_rows = group * rows_w
    other_kv, gate_parts, up_parts, downs = comm_call(
        keys_kernel,
        2,
        [kv, gate_parts, up_parts, w_down],
        [
            (kv.shape, BF16),
            (gate_parts.shape, BF16),
            (up_parts.shape, BF16),
            ((dp_n - 1,) + w_down.shape, BF16),
        ],
        sems(1) + swap_scratch((rows_w, ff_part)) * 2 + sems(dp_n - 1),
        "keys",
    )
    gate_parts = gate_parts.reshape(part_rows, -1)
    up_parts = up_parts.reshape(part_rows, -1)
    gate_other = swap_pair(gate_parts, "hi")
    out_weight = lax.all_gather(out_rows.reshape(-1, width), ("dp", "blk"), axis=0, tiled=True)
    q = q.reshape(blk_n, unit, q_cols)
    kv, other_kv = kv.reshape(blk_n, unit, -1), other_kv.reshape(blk_n, unit, -1)
    scalars = jnp.stack([lengths[0], hi.astype(jnp.int32)])
    out_heads, log_heads = attend(scalars, q, kv, other_kv)
    dp_sems = sems(2 * (dp_n - 1))
    dp_scratch = [pltpu.SemaphoreType.DMA((2,)), pltpu.VMEM((2, part_rows, ff_part), BF16)]
    weight_shape = ((dp_n, hi_n, part_rows, ff_part), BF16)
    mixed, gate_weight, up_other = comm_call(
        heads_kernel,
        3,
        [out_heads.reshape(group, tok, q_cols), gate_parts, gate_other, up_parts],
        [((group, tok, q_cols), BF16), weight_shape, (up_parts.shape, BF16)],
        swap_scratch((tok, q_cols)) + dp_sems + sems(1) + dp_scratch,
        "heads",
    )
    gate_weight = gate_weight.reshape(width, ff_part)
    middle, normed_two = out_project(
        mixed, out_weight, hidden[0], gain_two, key_head, to_inner, reblock
    )

    normed_two, up_weight, down_other = comm_call(
        rows_kernel,
        4,
        [inner(normed_two), up_parts, up_other, w_down],
        [((group, tok, width), BF16), weight_shape, (w_down.shape, BF16)],
        gather_scratch(tok, width) + dp_sems + sems(1) + dp_scratch,
        "rows",
    )
    normed_two = normed_two.reshape(group * tok, width)
    up_weight = up_weight.reshape(width, ff_part)
    dp_index = lax.axis_index("dp")
    own_first = hi == 0

    def by_hi(own, other):
        return jnp.stack([jnp.where(own_first, own, other), jnp.where(own_first, other, own)])

    down_parts = by_hi(w_down, down_other)
    if dp_n == 2:
        far = by_hi(downs[0], swap_pair(down_other, "dp"))
        dp_first = dp_index == 0
        down_parts = jnp.stack(
            [jnp.where(dp_first, down_parts, far), jnp.where(dp_first, far, down_parts)]
        )
    else:
        down_parts = lax.all_gather(down_parts, "dp", axis=0, tiled=False)
    down_weight = down_parts.reshape(-1, width)
    gate = dot32(normed_two, gate_weight)
    upward = dot32(normed_two, up_weight)
    sigma = jax.nn.sigmoid(gate)
    silu = gate * sigma
    units = (silu * upward).astype(BF16)
    gate_slope = (upward * sigma * (1.0 + gate * (1.0 - sigma))).astype(BF16)
    up_slope = silu.astype(BF16)
    result = middle + RESIDUAL_SCALE * scatter_square(dot32(units, down_weight), 1)

    own_places = ((blk * hi_n + hi) * lo_n + lo) * tok + jnp.arange(tok)
    valid = own_places < lengths[0]
    misfit = jnp.where(valid[:, None], result - teacher[0].astype(F32), 0.0)
    squares = jnp.broadcast_to(jnp.sum(misfit * misfit), (8, 128))
    grad_result = misfit * (dp_n * seq_len / valid_count)

    branch = gather_square((RESIDUAL_SCALE * grad_result).astype(BF16), 5)
    down_sum = weight_grad_start(units, branch, branch)
    grad_gate_rows, grad_up_rows, grad_normal = ff_back(
        branch, gate_slope, up_slope, gate_weight, up_weight, down_weight, down_sum[0], 2 * tok
    )
    if dp_n == 2:
        down_got = swap_pair(down_sum[1], "dp")
        grad_normal, down_sum, gate_own, up_own, gate_stay, up_stay, gate_got, up_got = scatter_down(
            grad_normal, 9, (down_sum[0], down_got), normed_two, grad_gate_rows, grad_up_rows
        )
        gate_stay, up_stay = swap_pair(gate_stay, "dp"), swap_pair(up_stay, "dp")
    else:
        grad_normal = scatter_square(grad_normal, 9)
        down_sum = scatter_end(scatter_start(down_sum[0], "hi"), "hi")
        gate_own = weight_grad_start(normed_two, grad_gate_rows, grad_normal)[0]
        up_own = weight_grad_start(normed_two, grad_up_rows, grad_normal)[0]
        gate_stay = up_stay = gate_got = up_got = jnp.zeros(gate_own.shape[1:], BF16)
    grad_normal = outer(grad_normal)

    grad_middle, attn_rows, grad_mixed = out_back(
        grad_normal, middle, grad_result, gain_two, out_weight, grad_normal, q_cols, key_head, to_outer, reblock
    )
    part_shape = (part_rows, ff_part)
    anywhere, inside = pl.BlockSpec(memory_space=pl.ANY), pl.BlockSpec(memory_space=pltpu.VMEM)
    dout, gate_away, up_away = pl.pallas_call(
        douts_kernel,
        in_specs=[anywhere] * 5,
        out_specs=[anywhere] + [inside] * 2,
        out_shape=[jax.ShapeDtypeStruct(grad_mixed.shape, BF16)]
        + [jax.ShapeDtypeStruct(part_shape, BF16)] * 2,
        scratch_shapes=swap_scratch((tok, q_cols))
        + [
            pltpu.VMEM((2,) + part_shape, F32),
            pltpu.VMEM((2,) + part_shape, BF16),
            pltpu.SemaphoreType.DMA((2, 2)),
        ],
        compiler_params=pltpu.CompilerParams(
            collective_id=6, has_side_effects=True, vmem_limit_bytes=VMEM_LIMIT
        ),
        cost_estimate=pl.CostEstimate(flops=0, bytes_accessed=40_000_000, transcendentals=0),
        name="douts",
    )(grad_mixed, gate_own, gate_got, up_own, up_got)
    columns = (group, rows_w, ff_part)

    gate_dp, up_dp = gate_stay.reshape(columns), up_stay.reshape(columns)
    gate_hi, up_hi = (swap_pair(a, "hi").reshape(columns) for a in (gate_away, up_away))
    square_attn = lax.all_gather(attn_rows, SQUARE, axis=0, tiled=True)
    dout = dout.reshape(blk_n, unit, q_cols)
    dq, dkv = attend_back(scalars, q, kv, other_kv, dout, out_heads, log_heads, gate_away)
    dkv = dkv.reshape(2, group * tok, 2 * k_cols)
    sum_scratch = [pltpu.VMEM(columns, F32)] + [pltpu.VMEM(columns, BF16)] * 3
    sum_scratch.append(pltpu.SemaphoreType.DMA((3,)))
    own_out = dot32(out_heads.reshape(group * tok, q_cols), square_attn, ((0,), (0,))).astype(BF16)
    other_dkv, gate_parts = comm_call(
        dkeys_kernel,
        7,
        [dkv, gate_own.reshape((hi_n,) + columns), gate_dp, gate_hi],
        [(dkv.shape[1:], BF16), (columns, BF16)],
        sems(1) + swap_scratch((rows_w, ff_part)) + sum_scratch,
        "dkeys",
    )
    dqkv = back_rope(
        hi_index, dq.reshape(group * tok, q_cols), dkv[0], other_dkv, tables, up_hi, tok
    )
    head_grads = dot32(normed_one, dqkv, ((0,), (0,))).reshape(dp_n, -1, rows_w, head_wide)
    head_grads = scatter_end(scatter_start(head_grads, "dp"), "dp").astype(BF16)
    grad_first = dot32(dqkv, qkv_weight, ((1,), (1,))).astype(BF16)
    with_out = dp_n == 2 and rows_w * hi_n * lo_n == q_cols
    arrays = [grad_first.reshape(group, tok, width), head_grads]
    arrays += [up_own.reshape((hi_n,) + columns), up_dp, up_hi, squares]
    shapes = [
        ((tok, width), F32),
        (head_grads.shape, BF16),
        (columns, BF16),
        ((every, 8, 128), F32),
    ]
    scratch = scatter_scratch(tok, width) + sems(every // dp_n - 1) + sems(every - 1)
    scratch += [pltpu.SemaphoreType.DMA((2,)), pltpu.VMEM((rows_w, head_wide), BF16)]
    scratch += swap_scratch((rows_w, ff_part)) + sum_scratch
    if with_out:
        arrays.append(own_out.reshape(hi_n, lo_n, rows_w, width))
        shapes.append(((hi_n, rows_w, width), BF16))
        scratch += sems(5) + [pltpu.SemaphoreType.DMA((2,))]
        scratch += [pltpu.VMEM((hi_n, lo_n, rows_w, width), BF16)] * 3
    grad_first, head_grads, up_parts, squares, *outs = pl.pallas_call(
        functools.partial(close_kernel, with_out),
        in_specs=[anywhere] * len(arrays),
        out_specs=[pl.BlockSpec(memory_space=pltpu.VMEM)] + [anywhere] * (len(shapes) - 1),
        out_shape=[jax.ShapeDtypeStruct(shape, dtype) for shape, dtype in shapes],
        scratch_shapes=scratch,
        compiler_params=pltpu.CompilerParams(
            collective_id=8, has_side_effects=True, vmem_limit_bytes=VMEM_LIMIT
        ),
        cost_estimate=pl.CostEstimate(flops=0, bytes_accessed=120_000_000, transcendentals=0),
        name="close",
    )(*arrays)
    mse_loss = jnp.sum(squares[:, 0, 0]) / (width * valid_count)
    if with_out and units_w % 128 == 0 and 2 * rows_w == 128:
        shape = lambda *dims: jax.ShapeDtypeStruct(dims, F32)
        grads = pl.pallas_call(
            functools.partial(final_kernel, key_head, ff_places, units_w),
            out_shape=[
                shape(tok, width),
                shape(*w_query.shape),
                shape(*key_projection.shape),
                shape(*value_projection.shape),
                shape(rows_w, 1),
                shape(*w_gate.shape),
                shape(*w_up.shape),
                shape(rows_w, 1),
                shape(*w_out.shape),
                shape(*w_down.shape),
            ],
            compiler_params=params,
            name="final",
        )(
            grad_first,
            grad_middle,
            hidden[0],
            gain_one,
            head_grads,
            w_query,
            key_projection,
            value_projection,
            gate_parts,
            up_parts,
            w_gate,
            w_up,
            small,
            outs[0],
            down_sum,
        )
        return (
            result.astype(BF16)[None],
            mse_loss,
            grads[0][None],
            grads[4][:, 0],
            *grads[1:4],
            grads[8],
            grads[7][:, 0],
            grads[5],
            grads[6],
            grads[9],
        )
    if with_out:
        grad_out = jnp.sum(outs[0].astype(F32), axis=0)
    else:
        own_head = lo * blk_n + blk
        spread = jnp.where((jnp.arange(group) == own_head)[:, None, None], own_out[None], 0)
        grad_out = lax.psum_scatter(
            spread.reshape(width, width), ALL, scatter_dimension=0, tiled=True
        ).astype(F32)
    grad_first = grad_first * gain_one
    normal_one, inverse_one = norm_parts(hidden[0].astype(F32))
    grad_hidden = grad_middle + inverse_one * (
        grad_first - normal_one * jnp.mean(grad_first * normal_one, axis=-1, keepdims=True)
    )
    head_grads = jnp.sum(
        head_grads.reshape(blk_n, hi_n, lo_n, rows_w, head_wide).astype(F32), axis=1
    ).reshape(group, rows_w, head_wide)

    own_one, own_two = attn_gain.astype(F32)[:, None], mlp_gain.astype(F32)[:, None]
    grad_query = head_columns_back(head_grads[:, :, :q_cols])
    grad_key = head_columns_back(head_grads[:, :, q_cols : q_cols + k_cols])
    grad_value = head_columns_back(head_grads[:, :, q_cols + k_cols :])

    def row_sums(*pairs):
        return sum(jnp.sum(w.astype(F32) * g, axis=1, keepdims=True) for w, g in pairs)

    grad_gain_one = (
        row_sums((w_query, grad_query), (key_projection, grad_key), (value_projection, grad_value))
        / own_one
    )
    if units_w % 128 == 0:
        ff_shape = jax.ShapeDtypeStruct(w_gate.shape, F32)
        grad_gate, grad_up, grad_gain_two = pl.pallas_call(
            functools.partial(collect_kernel, ff_places, units_w),
            out_shape=[ff_shape, ff_shape, jax.ShapeDtypeStruct((rows_w, 1), F32)],
            compiler_params=params,
            name="collect",
        )(gate_parts, up_parts, w_gate, w_up, own_two)
    else:
        grad_gate = unit_columns_back(gate_parts.astype(F32))
        grad_up = unit_columns_back(up_parts.astype(F32))
        grad_gain_two = row_sums((w_gate, grad_gate), (w_up, grad_up)) / own_two
    return (
        result.astype(BF16)[None],
        mse_loss,
        grad_hidden[None],
        grad_gain_one[:, 0],
        grad_query,
        grad_key,
        grad_value,
        grad_out,
        grad_gain_two[:, 0],
        grad_gate,
        grad_up,
        down_sum,
    )


def solution(mesh):
    dp_n, blk_n, head_n = (mesh.shape[a] for a in ("dp", "blk", "head"))
    fine = Mesh(mesh.devices.reshape(dp_n, blk_n, 2, head_n // 2), ALL)
    tokens = P("dp", SEQ, None)
    rows, row = P(ALL, None), P(ALL)
    return jax.shard_map(
        shards,
        mesh=fine,
        in_specs=(tokens, tokens, P("dp"), row, rows, rows, rows, rows, row, rows, rows, rows),
        out_specs=(tokens, P(), tokens, row, rows, rows, rows, rows, row, rows, rows, rows),
        check_vma=False,
    )
```

```python
import functools
import math

import jax
import jax.numpy as jnp
import numpy as np
from jax import lax
from jax.experimental import pallas as pl
from jax.experimental.pallas import tpu as pltpu
from jax.sharding import Mesh, PartitionSpec as P

MODEL_WIDTH = 2048
HEAD_SIZE = 64
ROPE_BASE = 10000000.0
NORM_EPS = 1e-05
ATTN_SCALE = 0.015625
RESIDUAL_SCALE = 0.22
MASKED = -1e30

ALL = ("dp", "blk", "hi", "lo")
SQUARE = ("blk", "lo")
COPIES = ("dp", "hi")
SEQ = ("blk", "hi", "lo")
F32 = jnp.float32
BF16 = jnp.bfloat16
VMEM_LIMIT = 56 * 1024 * 1024


def dot32(a, b, dims=((1,), (0,))):
    return lax.dot_general(a, b, (dims, ((), ())), preferred_element_type=F32)


def rope_tables(seq_len):
    half = HEAD_SIZE // 2
    frequency = ROPE_BASE ** (-(np.arange(half) * 2.0) / HEAD_SIZE)
    angles = np.arange(seq_len).astype(np.float32)[:, None] * frequency.astype(np.float32)[None, :]
    cosine, sine = np.cos(angles.astype(np.float64)), np.sin(angles.astype(np.float64))
    none = np.zeros_like(cosine)
    rows = ([cosine] * 4, [-sine, none] * 2, [none, sine] * 2)
    return tuple(np.concatenate(row, axis=1).astype(np.float32) for row in rows)


def table_spec(tok):
    return pl.BlockSpec((tok, 128), lambda i, hi: ((i // 2 * 2 + hi[0]) * 2 + i % 2, 0))


def proj_kernel(hi_ref, rows_ref, gain_ref, weight_ref, cos_ref, sina_ref, sinb_ref, normed_ref, q_ref, kv_ref):
    normed_ref[...] = (norm_parts(rows_ref[...].astype(F32))[0] * gain_ref[...]).astype(BF16)
    made = dot32(normed_ref[...], weight_ref[...])
    cosine, sina, sinb = cos_ref[...], sina_ref[...], sinb_ref[...]
    low = lanes_low(cosine.shape)
    half = HEAD_SIZE // 2
    for part in range(3):
        u = made[:, 128 * part : 128 * part + 128]
        up, down = pltpu.roll(u, 128 - half, 1), pltpu.roll(u, half, 1)
        turned = u * cosine + up * sina + down * sinb
        if part < 2:
            q_ref[:, 128 * part : 128 * part + 128] = (
                turned.astype(BF16).astype(F32) * ATTN_SCALE
            ).astype(BF16)
        else:
            kv_ref[...] = jnp.where(low, turned, u).astype(BF16)


def project(hi, rows, gain, weight, tables, tile):
    count, depth = rows.shape
    wide = weight.shape[1]
    by_rows = lambda cols: pl.BlockSpec((tile, cols), lambda i, hi: (i, 0))
    whole = lambda *shape: pl.BlockSpec(shape, lambda i, hi: (0, 0))
    return pl.pallas_call(
        proj_kernel,
        grid_spec=pltpu.PrefetchScalarGridSpec(
            num_scalar_prefetch=1,
            grid=(count // tile,),
            in_specs=[by_rows(depth), whole(1, depth), whole(depth, wide)] + [table_spec(tile)] * 3,
            out_specs=[by_rows(depth), by_rows(256), by_rows(128)],
        ),
        out_shape=[
            jax.ShapeDtypeStruct((count, depth), BF16),
            jax.ShapeDtypeStruct((count, 256), BF16),
            jax.ShapeDtypeStruct((count, 128), BF16),
        ],
        compiler_params=pltpu.CompilerParams(vmem_limit_bytes=VMEM_LIMIT),
        cost_estimate=pl.CostEstimate(
            flops=2 * count * depth * wide, bytes_accessed=4 * count * depth, transcendentals=0
        ),
        name="project",
    )(hi, rows, gain, weight, *tables)


def proj_back_kernel(
    hi_ref, dq_ref, own_ref, other_ref, rows_ref, weight_ref, cos_ref, sina_ref, sinb_ref, first_ref, drows_ref,
    dweight_ref, made, total,
):
    i = pl.program_id(0)
    cosine, sina, sinb = cos_ref[...], sina_ref[...], sinb_ref[...]
    low = lanes_low(cosine.shape)
    half = HEAD_SIZE // 2
    shared = (own_ref[...].astype(F32) + other_ref[...].astype(F32)).astype(BF16)
    for part in range(3):
        w = (dq_ref[:, 128 * part : 128 * part + 128] if part < 2 else shared).astype(F32)
        turned = w * cosine + pltpu.roll(w * sinb, 128 - half, 1) + pltpu.roll(w * sina, half, 1)
        if part == 2:
            turned = jnp.where(low, turned, w)
        made[:, 128 * part : 128 * part + 128] = turned.astype(BF16)
    drows_ref[...] = dot32(made[...], weight_ref[...], ((1,), (1,))).astype(BF16)
    dweight = dot32(rows_ref[...], made[...], ((0,), (0,)))

    @pl.when(i == 0)
    def _():
        total[...] = dweight

    @pl.when(i > 0)
    def _():
        total[...] += dweight

    @pl.when(i == pl.num_programs(0) - 1)
    def _():
        dweight_ref[...] = total[...].astype(BF16)


def project_back(hi, dq, own, other, rows, weight, tables, first, unit):
    count, width = rows.shape
    wide = weight.shape[1]
    by_rows = lambda cols: pl.BlockSpec((unit, cols), lambda i, hi: (i, 0))
    whole = pl.BlockSpec((width, wide), lambda i, hi: (0, 0))
    table = pl.BlockSpec((unit, 128), lambda i, hi: (2 * i + hi[0], 0))
    return pl.pallas_call(
        proj_back_kernel,
        grid_spec=pltpu.PrefetchScalarGridSpec(
            num_scalar_prefetch=1,
            grid=(count // unit,),
            in_specs=[by_rows(256), by_rows(128), by_rows(128), by_rows(width), whole]
            + [table] * 3
            + [pl.BlockSpec(memory_space=pl.ANY)],
            out_specs=[by_rows(width), whole],
            scratch_shapes=[pltpu.VMEM((unit, wide), BF16), pltpu.VMEM((width, wide), F32)],
        ),
        out_shape=[
            jax.ShapeDtypeStruct((count, width), BF16),
            jax.ShapeDtypeStruct((width, wide), BF16),
        ],
        compiler_params=pltpu.CompilerParams(vmem_limit_bytes=VMEM_LIMIT),
        cost_estimate=pl.CostEstimate(
            flops=4 * count * width * wide, bytes_accessed=24_000_000, transcendentals=0
        ),
        name="project_back",
    )(hi, dq, own, other, rows, weight, *tables, first)


def lanes_low(shape):
    return lax.broadcasted_iota(jnp.int32, shape, 1) < HEAD_SIZE


def both_keys(kv):
    low = lanes_low(kv.shape)
    keys = kv.astype(F32)
    return (
        jnp.where(low, keys, 0.0).astype(BF16),
        jnp.where(low, 0.0, pltpu.roll(keys, HEAD_SIZE, 1)).astype(BF16),
    )


def both_values(kv):
    low = lanes_low(kv.shape)
    values = kv.astype(F32)
    return (
        jnp.where(low, pltpu.roll(values, HEAD_SIZE, 1), 0.0).astype(BF16),
        jnp.where(low, 0.0, values).astype(BF16),
    )


def attend_kernel(scalar_ref, q_ref, kv_ref, other_ref, out_ref, log_ref, keys, values, peak, sums):
    b = pl.program_id(0)
    blocks, unit, _ = q_ref.shape
    units = 2 * blocks
    length, hi = scalar_ref[0], scalar_ref[1]
    n = 2 * b + hi

    @pl.when(b == 0)
    def _():
        def spread(c, carry):
            for j, kv in (
                (2 * c + hi, kv_ref[c]),
                (2 * c + 1 - hi, other_ref[c]),
            ):
                keys[0, j], keys[1, j] = both_keys(kv)
                across = jnp.transpose(kv.astype(F32))[HEAD_SIZE:, :]
                values[j] = jnp.concatenate(
                    [across, jnp.ones((16, unit), F32)], axis=0
                ).astype(BF16)
            return carry

        lax.fori_loop(0, blocks, spread, 0)

    peak[...] = jnp.full_like(peak, MASKED)
    sums[...] = jnp.zeros_like(sums)

    def step(j, masked):
        for h in range(4):
            query = q_ref[b, :, 128 * (h // 2) : 128 * (h // 2) + 128]
            scores = dot32(keys[h % 2, j], query, ((1,), (1,)))
            if masked:
                row = j * unit + lax.broadcasted_iota(jnp.int32, scores.shape, 0)
                col = n * unit + lax.broadcasted_iota(jnp.int32, scores.shape, 1)
                scores = jnp.where((row <= col) & (row < length), scores, MASKED)
            old = peak[h, 0:1, :]
            new = jnp.maximum(old, jnp.max(scores, axis=0, keepdims=True))
            weights = jnp.exp(scores - new).astype(BF16)
            sums[h] = sums[h] * jnp.exp(old - new) + dot32(values[j], weights)
            peak[h, 0:1, :] = new

    first_ragged = units - units // 4

    def plain(j, carry):
        step(j, False)
        return carry

    def checked(j, carry):
        step(j, True)
        return carry

    lax.fori_loop(0, jnp.minimum(n, first_ragged), plain, 0)
    lax.fori_loop(jnp.minimum(n, first_ragged), n + 1, checked, 0)

    for pair in range(2):
        parts = []
        for h in (2 * pair, 2 * pair + 1):
            total = sums[h, HEAD_SIZE : HEAD_SIZE + 1, :]
            parts.append(sums[h, 0:HEAD_SIZE, :] / total)
            log_ref[0, h : h + 1, :] = peak[h, 0:1, :] + jnp.log(total)
        out_ref[0, :, 128 * pair : 128 * pair + 128] = jnp.transpose(
            jnp.concatenate(parts, axis=0)
        ).astype(BF16)


def attend(scalars, q, kv, other):
    blocks, unit, _ = q.shape
    units = 2 * blocks
    whole = lambda a: pl.BlockSpec(a.shape, lambda i: (0,) * a.ndim)
    return pl.pallas_call(
        attend_kernel,
        grid=(blocks,),
        in_specs=[pl.BlockSpec(memory_space=pltpu.SMEM), whole(q), whole(kv), whole(other)],
        out_specs=[
            pl.BlockSpec((1, unit, 256), lambda i: (i, 0, 0)),
            pl.BlockSpec((1, 8, unit), lambda i: (i, 0, 0)),
        ],
        out_shape=[
            jax.ShapeDtypeStruct((blocks, unit, 256), BF16),
            jax.ShapeDtypeStruct((blocks, 8, unit), F32),
        ],
        scratch_shapes=[
            pltpu.VMEM((2, units, unit, 128), BF16),
            pltpu.VMEM((units, HEAD_SIZE + 16, unit), BF16),
            pltpu.VMEM((4, 8, unit), F32),
            pltpu.VMEM((4, HEAD_SIZE + 16, unit), F32),
        ],
        compiler_params=pltpu.CompilerParams(vmem_limit_bytes=VMEM_LIMIT),
        cost_estimate=pl.CostEstimate(
            flops=40_000_000_000, bytes_accessed=8_000_000, transcendentals=20_000_000
        ),
        name="attend",
    )(scalars, q, kv, other)


def attend_back_kernel(
    scalar_ref,
    q_ref,
    kv_ref,
    other_ref,
    dout_ref,
    out_ref,
    log_ref,
    first_ref,
    dq_ref,
    dkv_ref,
    delta,
    dq,
    dk,
    dv,
):
    j = pl.program_id(0)
    blocks, unit, _ = q_ref.shape
    units = 2 * blocks
    length, hi = scalar_ref[0], scalar_ref[1]

    @pl.when(j == 0)
    def _():
        dq[...] = jnp.zeros_like(dq)
        pick = jnp.where(
            lax.broadcasted_iota(jnp.int32, (8, 256), 0)
            == lax.broadcasted_iota(jnp.int32, (8, 256), 1) // HEAD_SIZE,
            1.0,
            0.0,
        )

        def dots(b, carry):
            product = dout_ref[b].astype(F32) * out_ref[b].astype(F32)
            delta[b] = lax.dot_general(
                pick,
                product,
                (((1,), (1,)), ((), ())),
                precision=lax.Precision.HIGHEST,
                preferred_element_type=F32,
            )
            return carry

        lax.fori_loop(0, blocks, dots, 0)

    foreign = jnp.where(j % 2 == hi, 0, 1)
    kv = jnp.where(foreign == 0, kv_ref[j // 2], other_ref[j // 2])
    keys, values = both_keys(kv), both_values(kv)
    dk[...] = jnp.zeros_like(dk)
    dv[...] = jnp.zeros_like(dv)

    def step(b, masked):
        n = 2 * b + hi
        for pair in range(2):
            lanes = slice(128 * pair, 128 * pair + 128)
            query = q_ref[b, :, lanes]
            dout = dout_ref[b, :, lanes]
            dq_part = None
            for side in range(2):
                h = 2 * pair + side
                scores = dot32(keys[side], query, ((1,), (1,)))
                weights = jnp.exp(scores - log_ref[b, h : h + 1, :])
                if masked:
                    row = j * unit + lax.broadcasted_iota(jnp.int32, scores.shape, 0)
                    col = n * unit + lax.broadcasted_iota(jnp.int32, scores.shape, 1)
                    weights = jnp.where((row <= col) & (row < length), weights, 0.0)
                dweights = dot32(values[side], dout, ((1,), (1,)))
                dscores = (weights * (dweights - delta[b, h : h + 1, :])).astype(BF16)
                dv[side] += dot32(weights.astype(BF16), dout)
                dk[side] += dot32(dscores, query)
                part = dot32(dscores, keys[side], ((0,), (0,)))
                dq_part = part if dq_part is None else dq_part + part
            dq[b, :, lanes] += dq_part

    first_ragged = units - units // 4

    def plain(b, carry):
        step(b, False)
        return carry

    def checked(b, carry):
        step(b, True)
        return carry

    first = (j + 1 - hi) // 2
    masked_until = jnp.where(j >= first_ragged, blocks, jnp.where(foreign == 0, first + 1, first))
    lax.fori_loop(first, masked_until, checked, 0)
    lax.fori_loop(masked_until, blocks, plain, 0)

    low = lanes_low((unit, 128))
    dkey = dk[0] + pltpu.roll(dk[1], HEAD_SIZE, 1)
    dvalue = pltpu.roll(dv[0], HEAD_SIZE, 1) + dv[1]
    dkv_ref[foreign, j // 2] = jnp.where(low, dkey, dvalue).astype(BF16)

    @pl.when(j == units - 1)
    def _():
        def store(b, carry):
            dq_ref[b] = (dq[b] * ATTN_SCALE).astype(BF16)
            return carry

        lax.fori_loop(0, blocks, store, 0)


def attend_back(scalars, q, kv, other, dout, out, log, first):
    blocks, unit, _ = q.shape
    units = 2 * blocks
    whole = lambda a: pl.BlockSpec(a.shape, lambda i: (0,) * a.ndim)
    dq_shape = jax.ShapeDtypeStruct((blocks, unit, 256), BF16)
    dkv_shape = jax.ShapeDtypeStruct((2, blocks, unit, 128), BF16)
    return pl.pallas_call(
        attend_back_kernel,
        grid=(units,),
        in_specs=[
            pl.BlockSpec(memory_space=pltpu.SMEM),
            whole(q),
            whole(kv),
            whole(other),
            whole(dout),
            whole(out),
            whole(log),
            pl.BlockSpec(memory_space=pl.ANY),
        ],
        out_specs=[whole(dq_shape), whole(dkv_shape)],
        out_shape=[dq_shape, dkv_shape],
        scratch_shapes=[
            pltpu.VMEM((blocks, 8, unit), F32),
            pltpu.VMEM((blocks, unit, 256), F32),
            pltpu.VMEM((2, unit, 128), F32),
            pltpu.VMEM((2, unit, 128), F32),
        ],
        compiler_params=pltpu.CompilerParams(vmem_limit_bytes=VMEM_LIMIT),
        cost_estimate=pl.CostEstimate(
            flops=60_000_000_000, bytes_accessed=10_000_000, transcendentals=20_000_000
        ),
        name="attend_back",
    )(scalars, q, kv, other, dout, out, log, first)


PIECES = 4
MESH_ID = pl.DeviceIdType.MESH


def square_places():
    blk, lo = lax.axis_index("blk"), lax.axis_index("lo")
    mate, side = blk + 1 - 2 * (blk % 2), (blk + 2) % 4
    return blk, lo, mate, side


def greet(ids):
    barrier = pltpu.get_barrier_semaphore()
    for one in ids:
        pl.semaphore_signal(barrier, inc=1, device_id=one, device_id_type=MESH_ID)
    pl.semaphore_wait(barrier, len(ids))


def remote(source, target, send, recv, to):
    copy = pltpu.make_async_remote_copy(
        src_ref=source,
        dst_ref=target,
        send_sem=send,
        recv_sem=recv,
        device_id=to,
        device_id_type=MESH_ID,
    )
    copy.start()
    return copy


def local_copy(source, target, sem):
    copy = pltpu.make_async_copy(source, target, sem)
    copy.start()
    return copy


class Carried:
    def __init__(self, source, target, held, sem):
        self.held, self.target, self.sem = held, target, sem
        self.copy = local_copy(source, held, sem)

    def turn(self):
        self.copy.wait()
        self.copy = local_copy(self.held, self.target, self.sem)

    def wait(self):
        self.copy.wait()


def finish(copies):
    for copy in copies:
        if isinstance(copy, Carried):
            copy.turn()
    for copy in copies:
        copy.wait()


def square_peers():
    blk, lo = lax.axis_index("blk"), lax.axis_index("lo")
    mine = blk * 2 + lo
    others = [lax.rem(mine + d, 8) for d in range(1, 8)]
    return mine, others, [{"blk": o // 2, "lo": lax.rem(o, 2)} for o in others]


def other_hi():
    return {"hi": 1 - lax.axis_index("hi")}


def dp_peers():
    dp, dp_n = lax.axis_index("dp"), lax.axis_size("dp")
    return [{"dp": lax.rem(dp + d, dp_n)} for d in range(1, dp_n)]


def every_peer():
    sizes = [lax.axis_size(a) for a in ALL]
    places = [lax.axis_index(a) for a in ALL]
    found = []
    for k in range(1, math.prod(sizes)):
        to, rest = {}, k
        for a, size, place in reversed(list(zip(ALL, sizes, places))):
            to[a] = lax.rem(place + rest % size, size)
            rest //= size
        found.append(to)
    return found


def gather_begin(rows_ref, out_ref, send, recv, local, held):
    blk, lo, mate, side = square_places()
    slot = lambda b, l: b * 2 + l
    mine = slot(blk, lo)
    to_mate, to_side, to_next = {"blk": mate}, {"blk": side}, {"lo": 1 - lo}
    step = rows_ref.shape[0] // PIECES

    def push(source, place, piece, kind, to):
        target = out_ref.at[place, pl.ds(piece * step, step)]
        return remote(source, target, send.at[kind, piece], recv.at[kind, piece], to)

    own = Carried(rows_ref, out_ref.at[mine], held, local)
    piece_of = lambda p: rows_ref.at[pl.ds(p * step, step)]
    came = lambda place, p: out_ref.at[place, pl.ds(p * step, step)]
    side_order, next_order = (2, 3, 0, 1), (0, 1, 2, 3)
    by_side, by_next, by_mate, across = {}, {}, [], {}
    for k in range(PIECES):
        p, q = side_order[k], next_order[k]
        by_side[p] = push(piece_of(p), mine, p, 0, to_side)
        by_next[q] = push(piece_of(q), mine, q, 1, to_next)
    for p in range(PIECES):
        by_mate.append(push(piece_of(p), mine, p, 3, to_mate))

    def end(between=lambda k: None):
        own.turn()
        from_side, from_next, from_across = slot(side, lo), slot(blk, 1 - lo), slot(side, 1 - lo)
        for k in range(PIECES):
            p, q = side_order[k], next_order[k]
            by_side[p].wait_recv()
            if p >= 2:
                across[p] = push(came(from_side, p), from_side, p, 2, to_next)
            by_mate.append(push(came(from_side, p), from_side, p, 4, to_mate))
            by_next[q].wait_recv()
            if q < 2:
                across[q] = push(came(from_next, q), from_next, q, 2, to_side)
            by_mate.append(push(came(from_next, q), from_next, q, 5, to_mate))
            between(k)
        for p in (0, 2, 1, 3):
            across[p].wait_recv()
            by_mate.append(push(came(from_across, p), from_across, p, 6, to_mate))
            between(PIECES + p)
        for copy in by_mate:
            copy.wait()
        for copies in (by_side, by_next, across):
            for copy in copies.values():
                copy.wait_send()
        own.wait()

    return end


def gather_scratch(tok, width):
    return [
        pltpu.SemaphoreType.DMA((7, PIECES)),
        pltpu.SemaphoreType.DMA((7, PIECES)),
        pltpu.SemaphoreType.DMA,
        pltpu.VMEM((tok, width), BF16),
    ]


def sems(count):
    return [pltpu.SemaphoreType.DMA((count,))] * 2


def swap_scratch(part):
    return sems(7) + [pltpu.SemaphoreType.DMA, pltpu.VMEM(part, BF16)]


def square_greeting():
    blk, lo, mate, side = square_places()
    return [{"blk": mate}, {"blk": side}, {"lo": 1 - lo}]


def gather_kernel(rows_ref, out_ref, send, recv, local, held):
    greet(square_greeting())
    gather_begin(rows_ref, out_ref, send, recv, local, held)()


def comm_call(kernel, number, arrays, shapes, scratch, name):
    anywhere = pl.BlockSpec(memory_space=pl.ANY)
    return pl.pallas_call(
        kernel,
        in_specs=[anywhere] * len(arrays),
        out_specs=[anywhere] * len(shapes),
        out_shape=[jax.ShapeDtypeStruct(shape, dtype) for shape, dtype in shapes],
        scratch_shapes=scratch,
        compiler_params=pltpu.CompilerParams(
            collective_id=number, has_side_effects=True, vmem_limit_bytes=VMEM_LIMIT
        ),
        cost_estimate=pl.CostEstimate(flops=0, bytes_accessed=120_000_000, transcendentals=0),
        name=name,
    )(*arrays)


def gather_square(rows, number):
    tok, width = rows.shape
    (out,) = comm_call(
        gather_kernel,
        number,
        [rows],
        [((8, tok, width), rows.dtype)],
        gather_scratch(tok, width),
        "gather_square",
    )
    return out.reshape(8 * tok, width)


def swap_begin(parts_ref, out_ref, send, recv, local, held):
    mine, others, ids = square_peers()
    own = Carried(parts_ref.at[mine], out_ref.at[mine], held, local)
    copies = [
        remote(parts_ref.at[o], out_ref.at[mine], send.at[d], recv.at[d], to)
        for d, (o, to) in enumerate(zip(others, ids))
    ]
    return copies + [own]


def dp_begin(pieces, out_ref, send, recv, local, held, first=0):
    dp = lax.axis_index("dp")
    copies = []
    for k, (place, ref) in enumerate(pieces, first):
        copies.append(Carried(ref, out_ref.at[dp, place], held.at[k], local.at[k]))
        for d, to in enumerate(dp_peers()):
            n = 2 * d + k
            copies.append(remote(ref, out_ref.at[dp, place], send.at[n], recv.at[n], to))
    return copies


def device_place():
    mine = 0
    for a in ALL:
        mine = mine * lax.axis_size(a) + lax.axis_index(a)
    return mine


def seq_peers():
    sizes = [lax.axis_size(a) for a in SEQ]
    places = [lax.axis_index(a) for a in SEQ]
    found = []
    for k in range(1, math.prod(sizes)):
        to, source, digits, rest = {}, 0, [], k
        for size in reversed(sizes):
            digits.append(rest % size)
            rest //= size
        for a, size, place, digit in zip(SEQ, sizes, places, reversed(digits)):
            to[a] = lax.rem(place + digit, size)
            source = source * size + lax.rem(place + size - digit, size)
        found.append((to, source))
    return found


def seq_place(to):
    place = 0
    for a in SEQ:
        place = place * lax.axis_size(a) + to[a]
    return place


def open_kernel(
    rows_ref, heads_ref, small_ref, wout_ref, out_ref, weight_ref, smalls_ref, wouts_ref, g_send, g_recv,
    g_local, g_held, w_send, w_recv, d_send, d_recv, s_send, s_recv, o_send, o_recv, local, w_held, o_held,
):
    blk, hi, lo = (lax.axis_index(a) for a in SEQ)
    mine = device_place()
    peers = every_peer()
    greet(peers)
    copies = [
        Carried(heads_ref.at[blk * 2 + lo], weight_ref.at[mine], w_held, local.at[0]),
        local_copy(small_ref, smalls_ref.at[mine], local.at[1]),
        Carried(wout_ref, wouts_ref.at[hi, lo], o_held, local.at[2]),
    ]
    for k, to in enumerate(peers):
        copies.append(remote(small_ref, smalls_ref.at[mine], s_send.at[k], s_recv.at[k], to))
    end = gather_begin(rows_ref, out_ref, g_send, g_recv, g_local, g_held)
    wout = remote(wout_ref, wouts_ref.at[hi, lo], o_send.at[0], o_recv.at[0], other_hi())
    next_lo = {"lo": 1 - lo}
    copies.append(remote(wout_ref, wouts_ref.at[hi, lo], o_send.at[1], o_recv.at[1], next_lo))
    dp, seq = lax.axis_index("dp"), seq_peers()
    seq_n = len(seq) + 1
    straight = []
    for k, (to, source) in enumerate(seq):
        part = heads_ref.at[to["blk"] * 2 + to["lo"]]
        straight.append(remote(part, weight_ref.at[mine], w_send.at[k], w_recv.at[k], to))

    def hand_on(part, place, k):
        for d, to in enumerate(dp_peers()):
            n = d * seq_n + k
            copies.append(remote(part, weight_ref.at[place], d_send.at[n], d_recv.at[n], to))

    hand_on(heads_ref.at[blk * 2 + lo], mine, seq_n - 1)

    def pass_on(turn):
        for k, (to, source) in enumerate(seq):
            if k * 2 * PIECES // len(seq) == turn:
                straight[k].wait()
                place = dp * seq_n + source
                hand_on(weight_ref.at[place], place, k)

    end(pass_on)
    wout.wait()
    there = wouts_ref.at[1 - hi, lo]
    copies.append(remote(there, there, o_send.at[2], o_recv.at[2], next_lo))
    finish(copies)


def keys_kernel(
    kv_ref, gate_ref, up_ref, down_ref, other_ref, gates_ref, ups_ref, downs_ref, k_send, k_recv, g_send,
    g_recv, g_local, g_held, u_send, u_recv, u_local, u_held, d_send, d_recv,
):
    greet(square_peers()[2] + [other_hi()] + dp_peers())
    copies = [remote(kv_ref, other_ref, k_send.at[0], k_recv.at[0], other_hi())]
    for d, to in enumerate(dp_peers()):
        copies.append(remote(down_ref, downs_ref.at[d], d_send.at[d], d_recv.at[d], to))
    copies += swap_begin(gate_ref, gates_ref, g_send, g_recv, g_local, g_held)
    copies += swap_begin(up_ref, ups_ref, u_send, u_recv, u_local, u_held)
    finish(copies)


def heads_kernel(
    heads_ref, gate_ref, gate_other_ref, up_ref, mixed_ref, gates_ref, up_other_ref, m_send, m_recv,
    m_local, m_held, g_send, g_recv, u_send, u_recv, g_local, g_held,
):
    hi = lax.axis_index("hi")
    greet(square_peers()[2] + [other_hi()] + dp_peers())
    copies = swap_begin(heads_ref, mixed_ref, m_send, m_recv, m_local, m_held)
    copies.append(remote(up_ref, up_other_ref, u_send.at[0], u_recv.at[0], other_hi()))
    copies += dp_begin(
        [(hi, gate_ref), (1 - hi, gate_other_ref)], gates_ref, g_send, g_recv, g_local, g_held
    )
    finish(copies)


def rows_kernel(
    rows_ref, up_ref, up_other_ref, down_ref, out_ref, ups_ref, down_other_ref, r_send, r_recv, r_local,
    r_held, u_send, u_recv, d_send, d_recv, u_local, u_held,
):
    hi = lax.axis_index("hi")
    greet(square_greeting() + [other_hi()] + dp_peers())
    end = gather_begin(rows_ref, out_ref, r_send, r_recv, r_local, r_held)
    copies = [remote(down_ref, down_other_ref, d_send.at[0], d_recv.at[0], other_hi())]
    copies += dp_begin(
        [(hi, up_ref), (1 - hi, up_other_ref)], ups_ref, u_send, u_recv, u_local, u_held
    )
    end()
    finish(copies)


def sum_begin(own_ref, got_ref, place, own, got, sem):
    return [
        local_copy(own_ref.at[place], own, sem.at[0]),
        local_copy(got_ref.at[place], got, sem.at[1]),
    ]


def wait_all(copies):
    for copy in copies:
        copy.wait()


def out_back_kernel(
    order, pairs, block, grad_ref, middle_ref, result_ref, gain_ref, weight_ref, gate_ref, gate_got_ref, up_ref,
    up_got_ref, sum_ref, rows_ref, out_ref, gate_away_ref, up_away_ref, weight, work, parts, send, recv, own, got, sem,
    w_sem,
):
    hi = lax.axis_index("hi")
    load = local_copy(weight_ref, weight, w_sem.at[0])
    loads = [
        [local_copy(ref.at[1 - hi], own.at[k], sem.at[k, 0]), local_copy(got_ref, got.at[k], sem.at[k, 1])]
        for k, (ref, got_ref) in enumerate(((gate_ref, gate_got_ref), (up_ref, up_got_ref)))
    ]
    mine, others, ids = square_peers()
    greet(ids)
    reorder(pairs, block, grad_ref, work, lambda v: v)
    normal, inverse = norm_parts(middle_ref[...])
    grad = work[...] * gain_ref[...]
    total = result_ref[...] + inverse * (
        grad - normal * jnp.mean(grad * normal, axis=-1, keepdims=True)
    )
    sum_ref[...] = total
    rows_ref[...] = (RESIDUAL_SCALE * total).astype(BF16)
    load.wait()
    cols = parts.shape[2]

    def make(n, f):
        part = weight[pl.ds(pl.multiple_of(order(f) * cols, cols), cols), :]
        parts[n] = dot32(rows_ref[...], part, ((1,), (1,))).astype(BF16)

    copies = []
    for d, (other, to) in enumerate(zip(others, ids)):
        make(d, other)
        copies.append(remote(parts.at[d], out_ref.at[mine], send.at[d], recv.at[d], to))
    make(7, mine)
    copies.append(local_copy(parts.at[7], out_ref.at[mine], w_sem.at[0]))
    for k, target in enumerate((gate_away_ref, up_away_ref)):
        wait_all(loads[k])
        target[...] = (own[k] + got[k].astype(F32)).astype(BF16)
    wait_all(copies)


def sum_three(place, own_ref, over_dp_ref, over_hi_ref, own, over_dp, over_hi, sem):
    return [
        local_copy(own_ref.at[place], own, sem.at[0]),
        local_copy(over_dp_ref, over_dp, sem.at[1]),
        local_copy(over_hi_ref, over_hi, sem.at[2]),
    ]


def dkeys_kernel(
    dkv_ref, gate_ref, gate_dp_ref, gate_hi_ref, first_ref, other_ref, gates_ref, k_send, k_recv, g_send, g_recv, g_local,
    g_held, own, over_dp, over_hi, made, sem,
):
    hi = lax.axis_index("hi")
    loads = sum_three(hi, gate_ref, gate_dp_ref, gate_hi_ref, own, over_dp, over_hi, sem)
    greet(square_peers()[2] + [other_hi()])
    copies = [remote(dkv_ref.at[1], other_ref, k_send.at[0], k_recv.at[0], other_hi())]
    wait_all(loads)
    made[...] = (own[...] + over_dp[...].astype(F32) + over_hi[...].astype(F32)).astype(BF16)
    copies += swap_begin(made, gates_ref, g_send, g_recv, g_local, g_held)
    finish(copies)


class OwnOut:
    def __init__(self, out_ref, outs_ref, send, recv, local, own, got, made):
        self.outs_ref, self.made, self.send, self.recv, self.local = outs_ref, made, send, recv, local
        self.own, self.got = own, got
        self.dp, self.hi, self.lo = (lax.axis_index(a) for a in ("dp", "hi", "lo"))
        self.load = local_copy(out_ref, own, local.at[0])
        self.over = remote(out_ref, got, send.at[0], recv.at[0], dp_peers()[0])

    def push(self, a, b):
        hi, lo = lax.rem(self.hi + a, 2), lax.rem(self.lo + b, 2)
        return pltpu.make_async_remote_copy(
            src_ref=self.made.at[hi, lo],
            dst_ref=self.outs_ref.at[self.hi],
            send_sem=self.send.at[1 + 2 * a + b],
            recv_sem=self.recv.at[1 + self.hi],
            device_id={"hi": hi, "lo": lo},
            device_id_type=MESH_ID,
        )

    def own_copy(self):
        return pltpu.make_async_copy(
            self.made.at[self.hi, self.lo], self.outs_ref.at[self.hi], self.local.at[1]
        )

    def turn(self):
        self.load.wait()
        self.over.wait()
        self.made[...] = (self.own[...].astype(F32) + self.got[...].astype(F32)).astype(BF16)

        @pl.when(self.dp == self.lo)
        def _():
            for a, b in ((0, 1), (1, 0), (1, 1)):
                self.push(a, b).start()
            self.own_copy().start()

    def wait(self):
        @pl.when(self.dp == self.lo)
        def _():
            for a, b in ((0, 1), (1, 0), (1, 1)):
                self.push(a, b).wait_send()
            self.own_copy().wait()

        for h in range(2):

            @pl.when(jnp.logical_not((h == self.hi) & (self.dp == self.lo)))
            def _(h=h):
                pltpu.make_async_remote_copy(
                    src_ref=self.made.at[0, 0],
                    dst_ref=self.outs_ref.at[h],
                    send_sem=self.send.at[1],
                    recv_sem=self.recv.at[1 + h],
                    device_id={"lo": 1 - self.lo},
                    device_id_type=MESH_ID,
                ).wait_recv()


def close_kernel(with_out, *refs):
    refs = iter(refs)
    take = lambda n: [next(refs) for _ in range(n)]
    parts_ref, heads_ref, up_ref, up_dp_ref, up_hi_ref, square_ref = take(6)
    out_rows_ref = next(refs) if with_out else None
    total_ref, head_ref, ups_ref, squares_ref = take(4)
    outs_ref = next(refs) if with_out else None
    scatter = take(9)
    h_send, h_recv, s_send, s_recv, local, h_own, h_got, h_made, h_sem = take(9)
    swap = take(4)
    own, over_dp, over_hi, made, sem = take(5)
    out_scratch = take(6) if with_out else None
    mine = device_place()
    peers, seq = every_peer(), seq_peers()
    place = seq_place({a: lax.axis_index(a) for a in SEQ})
    loads = scatter_load(parts_ref, scatter)
    hi = lax.axis_index("hi")
    up_loads = sum_three(hi, up_ref, up_dp_ref, up_hi_ref, own, over_dp, over_hi, sem)
    greet(peers)
    copies = [local_copy(square_ref, squares_ref.at[mine], local.at[1])]
    dp = lax.axis_index("dp")
    own_heads = local_copy(heads_ref.at[dp], h_own, local.at[0])
    over_heads = []
    for d, to in enumerate(dp_peers()):
        part = heads_ref.at[to["dp"]]
        over_heads.append(remote(part, h_got.at[d], h_sem.at[0, d], h_sem.at[1, d], to))
    mates = scatter_mates(parts_ref, scatter)
    for k, to in enumerate(peers):
        copies.append(remote(square_ref, squares_ref.at[mine], s_send.at[k], s_recv.at[k], to))

    def send_heads():
        own_heads.wait()
        wait_all(over_heads)
        total = h_own[...].astype(F32)
        for d in range(len(over_heads)):
            total = total + h_got[d].astype(F32)
        h_made[...] = total.astype(BF16)
        copies.append(local_copy(h_made.at[place], head_ref.at[place], local.at[0]))
        for k, (to, source) in enumerate(seq):
            part = h_made.at[seq_place(to)]
            copies.append(remote(part, head_ref.at[place], h_send.at[k], h_recv.at[k], to))

    own_out = OwnOut(out_rows_ref, outs_ref, *out_scratch) if with_out else None
    wait_all(up_loads)
    made[...] = (own[...] + over_dp[...].astype(F32) + over_hi[...].astype(F32)).astype(BF16)
    copies += swap_begin(made, ups_ref, *swap)
    nothing = lambda: None
    work = [nothing, send_heads, nothing, nothing, own_out.turn if with_out else nothing]
    scatter_end_square(loads, mates, total_ref, scatter, work)
    finish(copies)
    if with_out:
        own_out.wait()


def remote_to(source, target, sems_of, kind, piece, to):
    send, recv = sems_of
    return remote(source, target, send.at[kind, piece], recv.at[kind, piece], to)


def scatter_load(parts_ref, scratch):
    mine, local = scratch[0], scratch[8]
    blk, lo, mate, side = square_places()
    places = (side * 2 + 1 - lo, side * 2 + lo, blk * 2 + 1 - lo, blk * 2 + lo)
    return [local_copy(parts_ref.at[p], mine.at[k], local.at[k]) for k, p in enumerate(places)]


def scatter_mates(parts_ref, scratch):
    mates, sems_of = scratch[1], scratch[6:8]
    blk, lo, mate, side = square_places()
    mate_side = (mate + 2) % 4
    places = (mate_side * 2 + 1 - lo, mate_side * 2 + lo, mate * 2 + 1 - lo, mate * 2 + lo)
    step = parts_ref.shape[1] // PIECES
    rows = lambda p: pl.ds(p * step, step)
    orders = ((0, 2, 1, 3), (0, 1, 2, 3), (2, 3, 0, 1), (0, 1, 2, 3))
    return {
        (k, p): remote_to(
            parts_ref.at[places[k], rows(p)], mates.at[k, rows(p)], sems_of, k, p, {"blk": mate}
        )
        for k in range(4)
        for p in orders[k]
    }


def scatter_end_square(loads, from_mate, out_ref, scratch, work=()):
    work = list(work)
    mine, mates, made, got_across, got_side, got_next = scratch[:6]
    sems_of = scratch[6:8]
    blk, lo, mate, side = square_places()
    to_side, to_next = {"blk": side}, {"lo": 1 - lo}
    step = mine.shape[1] // PIECES
    rows = lambda p: pl.ds(p * step, step)

    def summed(k, p):
        from_mate[k, p].wait_recv()
        return mine[k, rows(p), :].astype(F32) + mates[k, rows(p), :].astype(F32)

    sent = {}
    loads[0].wait()
    for p in (0, 2, 1, 3):
        made[0, rows(p), :] = summed(0, p).astype(BF16)
        sent[0, p] = remote_to(
            made.at[0, rows(p)],
            got_across.at[rows(p)],
            sems_of,
            4,
            p,
            to_side if p < 2 else to_next,
        )
    loads[1].wait()
    loads[2].wait()
    for n, (k, p) in enumerate(((1, 0), (2, 2), (1, 1), (2, 3), (1, 2), (2, 0), (1, 3), (2, 1))):
        if work and n % 2 == 0:
            work.pop(0)()
        total = summed(k, p)
        if (k == 1) == (p >= 2):
            sent[0, p].wait_recv()
            total = total + got_across[rows(p), :].astype(F32)
        made[k, rows(p), :] = total.astype(BF16)
        sent[k, p] = remote_to(
            made.at[k, rows(p)],
            (got_side if k == 1 else got_next).at[rows(p)],
            sems_of,
            4 + k,
            p,
            to_side if k == 1 else to_next,
        )
    for one in work:
        one()
    loads[3].wait()
    for p in range(PIECES):
        total = summed(3, p)
        sent[1, p].wait_recv()
        sent[2, p].wait_recv()
        out_ref[rows(p), :] = (
            total + got_side[rows(p), :].astype(F32) + got_next[rows(p), :].astype(F32)
        )
    for copy in from_mate.values():
        copy.wait_send()
    for copy in sent.values():
        copy.wait_send()


def scatter_scratch(tok, width):
    return [
        pltpu.VMEM((4, tok, width), BF16),
        pltpu.VMEM((4, tok, width), BF16),
        pltpu.VMEM((3, tok, width), BF16),
        pltpu.VMEM((tok, width), BF16),
        pltpu.VMEM((tok, width), BF16),
        pltpu.VMEM((tok, width), BF16),
        pltpu.SemaphoreType.DMA((7, PIECES)),
        pltpu.SemaphoreType.DMA((7, PIECES)),
        pltpu.SemaphoreType.DMA((4,)),
    ]


def scatter_kernel(firsts, parts_ref, *refs):
    out_ref, scratch = refs[firsts], refs[firsts + 1 :]
    loads = scatter_load(parts_ref, scratch)
    greet(square_greeting())
    scatter_end_square(loads, scatter_mates(parts_ref, scratch), out_ref, scratch)


def scatter_square(parts, number, *first):
    count, width = parts.shape
    tok = count // 8
    return pl.pallas_call(
        functools.partial(scatter_kernel, len(first)),
        in_specs=[pl.BlockSpec(memory_space=pl.ANY)] * (1 + len(first)),
        out_specs=pl.BlockSpec(memory_space=pltpu.VMEM),
        out_shape=jax.ShapeDtypeStruct((tok, width), F32),
        scratch_shapes=scatter_scratch(tok, width),
        compiler_params=pltpu.CompilerParams(
            collective_id=number, has_side_effects=True, vmem_limit_bytes=VMEM_LIMIT
        ),
        cost_estimate=pl.CostEstimate(flops=0, bytes_accessed=120_000_000, transcendentals=0),
        name="scatter_square",
    )(parts.astype(BF16).reshape(8, tok, width), *first)


def scatter_down_kernel(
    parts_ref, down_ref, got_ref, rows_ref, dgate_ref, dup_ref, out_ref, sum_ref, gate_own_ref, up_own_ref,
    gate_stay_ref, up_stay_ref, gate_got_ref, up_got_ref, *scratch,
):
    scratch, rest = scratch[:9], scratch[9:]
    own, got, away, came, sem, send, recv, left, gate_right, up_right, gate_away, up_away, w_sem = rest
    dp, hi = lax.axis_index("dp"), lax.axis_index("hi")
    part = left.shape[2]
    blocks = ((1 - dp, 1 - hi), (dp, 1 - hi), (1 - dp, hi), (dp, hi))

    def load_left(n):
        d, h = blocks[n]
        cols = pl.ds(pl.multiple_of((d * 2 + h) * part, part), part)
        return local_copy(rows_ref.at[:, cols], left.at[n % 2], w_sem.at[n % 2])

    rights = [local_copy(dgate_ref, gate_right, w_sem.at[2]), local_copy(dup_ref, up_right, w_sem.at[3])]
    lefts = {0: load_left(0), 1: load_left(1)}
    down = sum_begin(down_ref, got_ref, 1 - hi, own, got, sem)
    loads = scatter_load(parts_ref, scratch)
    greet(square_greeting() + [other_hi()] + dp_peers())
    mates = scatter_mates(parts_ref, scratch)
    wait_all(down)
    away[...] = (own[...] + got[...].astype(F32)).astype(BF16)
    over = remote(away, came, send.at[0], recv.at[0], other_hi())
    down = sum_begin(down_ref, got_ref, hi, own, got, sem)
    pairs = []

    def gradient(n, up):
        if not up:
            lefts[n].wait()
        if n == 0:
            rights[up].wait()
        total = dot32(left[n % 2], (up_right if up else gate_right)[...], ((0,), (0,)))
        if n == 0:
            target, got_there = (up_away, up_got_ref) if up else (gate_away, gate_got_ref)
            target[...] = total.astype(BF16)
            pairs.append(remote(target, got_there, send.at[1 + up], recv.at[1 + up], dp_peers()[0]))
        elif n == 2:
            (up_stay_ref if up else gate_stay_ref)[...] = total.astype(BF16)
        else:
            (up_own_ref if up else gate_own_ref)[blocks[n][1]] = total
        if up and n < 2:
            lefts[n + 2] = load_left(n + 2)

    work = [functools.partial(gradient, n, up) for n in range(4) for up in range(2)]
    scatter_end_square(loads, mates, out_ref, scratch, work)
    wait_all(down)
    over.wait()
    sum_ref[...] = own[...] + got[...].astype(F32) + came[...].astype(F32)
    wait_all(pairs)


def scatter_down(parts, number, down, rows, dgate, dup):
    count, width = parts.shape
    tok = count // 8
    part = down[0].shape[1:]
    depth, cols = dgate.shape
    grad = (rows.shape[1] // 4, cols)
    anywhere, inside = pl.BlockSpec(memory_space=pl.ANY), pl.BlockSpec(memory_space=pltpu.VMEM)
    return pl.pallas_call(
        scatter_down_kernel,
        in_specs=[anywhere] * 6,
        out_specs=[inside] * 6 + [anywhere] * 2,
        out_shape=[
            jax.ShapeDtypeStruct((tok, width), F32),
            jax.ShapeDtypeStruct(part, F32),
            jax.ShapeDtypeStruct((2,) + grad, F32),
            jax.ShapeDtypeStruct((2,) + grad, F32),
        ]
        + [jax.ShapeDtypeStruct(grad, BF16)] * 4,
        scratch_shapes=scatter_scratch(tok, width)
        + [pltpu.VMEM(part, F32)]
        + [pltpu.VMEM(part, BF16)] * 3
        + [pltpu.SemaphoreType.DMA((2,))]
        + sems(3)
        + [
            pltpu.VMEM((2, depth, grad[0]), BF16),
            pltpu.VMEM((depth, cols), BF16),
            pltpu.VMEM((depth, cols), BF16),
            pltpu.VMEM(grad, BF16),
            pltpu.VMEM(grad, BF16),
            pltpu.SemaphoreType.DMA((4,)),
        ],
        compiler_params=pltpu.CompilerParams(
            collective_id=number, has_side_effects=True, vmem_limit_bytes=VMEM_LIMIT
        ),
        cost_estimate=pl.CostEstimate(
            flops=4 * depth * cols * rows.shape[1], bytes_accessed=160_000_000, transcendentals=0
        ),
        name="scatter_down",
    )(parts.reshape(8, tok, width), *down, rows, dgate, dup)


def swap_square(blocks):
    return lax.all_to_all(blocks, SQUARE, split_axis=0, concat_axis=0, tiled=True)


def swap_pair(block, axis):
    return lax.ppermute(block, axis, [(0, 1), (1, 0)])


def gather_start(rows, axis):
    if lax.axis_size(axis) != 2:
        return lax.all_gather(rows, axis, axis=0, tiled=False)
    return rows, swap_pair(rows, axis)


def gather_end(parts, axis):
    if lax.axis_size(axis) != 2:
        return parts
    rows, other = parts
    first = lax.axis_index(axis) == 0
    return jnp.stack([jnp.where(first, rows, other), jnp.where(first, other, rows)])


def scatter_start(parts, axis):
    if lax.axis_size(axis) != 2:
        return lax.psum_scatter(parts.astype(BF16), axis, scatter_dimension=0, tiled=False)
    place = lax.axis_index(axis)
    away = lax.dynamic_index_in_dim(parts, 1 - place, 0, False).astype(BF16)
    own = lax.dynamic_index_in_dim(parts, place, 0, False)
    return own, swap_pair(away, axis)


def scatter_end(parts, axis):
    if lax.axis_size(axis) != 2:
        return parts.astype(F32)
    return parts[0] + parts[1].astype(F32)


def by_copy(rows):
    dp_n, hi_n = lax.axis_size("dp"), lax.axis_size("hi")
    return rows.reshape((dp_n, hi_n, rows.shape[0] // (dp_n * hi_n)) + rows.shape[1:])


def total_of(value, axes, count):
    spread = jnp.broadcast_to(value.reshape(1, 1), (count, 1))
    return jnp.sum(lax.all_to_all(spread, axes, split_axis=0, concat_axis=0, tiled=True))


def norm_parts(rows):
    inverse = lax.rsqrt(jnp.mean(rows * rows, axis=-1, keepdims=True) + NORM_EPS)
    return rows * inverse, inverse


def reorder(pairs, block, source, target, cast):
    for at, to in pairs:
        target[:, to * block : to * block + block] = cast(source[:, at * block : at * block + block])


def out_kernel(order, pairs, block, mixed_ref, weight_ref, rows_ref, gain_ref, middle_ref, normed_ref, total):
    f = pl.program_id(0)

    @pl.when(f == 0)
    def _():
        total[...] = jnp.zeros_like(total)

    total[...] += dot32(mixed_ref[0], weight_ref[...])

    @pl.when(f == pl.num_programs(0) - 1)
    def _():
        middle = rows_ref[...].astype(F32) + RESIDUAL_SCALE * total[...]
        middle_ref[...] = middle
        total[...] = norm_parts(middle)[0] * gain_ref[...]
        reorder(pairs, block, total, normed_ref, lambda v: v.astype(BF16))


def out_project(mixed, weight, rows, gain, order, pairs, block):
    group, tok, cols = mixed.shape
    width = weight.shape[1]
    whole = pl.BlockSpec((tok, width), lambda f: (0, 0))
    return pl.pallas_call(
        functools.partial(out_kernel, order, pairs, block),
        grid=(group,),
        in_specs=[
            pl.BlockSpec((1, tok, cols), lambda f: (f, 0, 0)),
            pl.BlockSpec((cols, width), lambda f: (order(f), 0)),
            whole,
            pl.BlockSpec((1, width), lambda f: (0, 0)),
        ],
        out_specs=[whole, whole],
        out_shape=[
            jax.ShapeDtypeStruct((tok, width), F32),
            jax.ShapeDtypeStruct((tok, width), BF16),
        ],
        scratch_shapes=[pltpu.VMEM((tok, width), F32)],
        compiler_params=pltpu.CompilerParams(vmem_limit_bytes=VMEM_LIMIT),
        cost_estimate=pl.CostEstimate(
            flops=2 * tok * width * width, bytes_accessed=16_000_000, transcendentals=0
        ),
        name="out_project",
    )(mixed, weight, rows, gain)


def middle_kernel(
    order, pairs, block, heads_ref, gate_ref, gate_other_ref, up_ref, down_ref, weight_ref, rows_ref, gain_ref,
    out_ref, middle_ref, gates_ref, ups_ref, down_other_ref, up_other_ref, made_ref, m_send, m_recv, m_local,
    m_held, g_send, g_recv, g_local, g_held, u_send, u_recv, u_local, u_held, o_send, o_recv, r_send, r_recv,
    r_local, r_held, mixed, weight, rows, normed, total, gate_weight, chunks, sem,
):
    hi = lax.axis_index("hi")
    loads = [local_copy(weight_ref, weight, sem.at[0]), local_copy(rows_ref, rows, sem.at[1])]
    mine, others, ids = square_peers()
    greet(ids + [other_hi()] + dp_peers())
    heads = swap_begin(heads_ref, mixed, m_send, m_recv, m_local, m_held)
    up_over = remote(up_ref, up_other_ref, o_send.at[0], o_recv.at[0], other_hi())
    gates = dp_begin([(hi, gate_ref), (1 - hi, gate_other_ref)], gates_ref, g_send, g_recv, g_local, g_held)
    copies = dp_begin([(hi, up_ref)], ups_ref, u_send, u_recv, u_local, u_held)
    wait_all(loads)
    cols = mixed.shape[2]

    def add(f):
        g = order(f)
        part = weight[pl.ds(pl.multiple_of(g * cols, cols), cols), :]
        return dot32(mixed[f], part)

    heads[7].turn()
    heads[7].wait()
    total[...] = add(mine)
    for d in range(7):
        heads[d].wait_recv()
        total[...] += add(lax.rem(mine + 7 - d, 8))
    middle = rows[...].astype(F32) + RESIDUAL_SCALE * total[...]
    middle_ref[...] = middle
    total[...] = norm_parts(middle)[0] * gain_ref[...]
    reorder(pairs, block, total, normed, lambda v: v.astype(BF16))
    end = gather_begin(normed, out_ref, r_send, r_recv, r_local, r_held)

    def more(turn):
        if turn == PIECES - 1:
            up_over.wait()
            copies.append(remote(down_ref, down_other_ref, o_send.at[1], o_recv.at[1], other_hi()))
            copies.extend(
                dp_begin([(1 - hi, up_other_ref)], ups_ref, u_send, u_recv, u_local, u_held, 1)
            )

    end(more)
    finish(gates)
    step = 2
    load_gate = local_copy(gates_ref, gate_weight, sem.at[0])
    load_rows = lambda n: local_copy(out_ref.at[pl.ds(n * step, step)], chunks.at[n % 2], sem.at[1 + n % 2])
    loads = [load_rows(0), load_rows(1)]
    load_gate.wait()
    tok, width = rows.shape
    for n in range(8 // step):
        loads[n].wait()
        made_ref[n * step * tok : (n + 1) * step * tok, :] = dot32(
            chunks[n % 2].reshape(step * tok, width), gate_weight[...].reshape(width, -1)
        )
        if n + 2 < 8 // step:
            loads.append(load_rows(n + 2))
    for d in range(7):
        heads[d].wait_send()
    finish(copies)


def through_middle(heads, gate, gate_other, up, down, weight, rows, gain, order, pairs, block):
    group, tok, cols = heads.shape
    width = weight.shape[1]
    part_rows, ff_part = up.shape
    dp_n = lax.axis_size("dp")
    anywhere, inside = pl.BlockSpec(memory_space=pl.ANY), pl.BlockSpec(memory_space=pltpu.VMEM)
    dp_part = sems(2 * (dp_n - 1)) + [
        pltpu.SemaphoreType.DMA((2,)),
        pltpu.VMEM((2, part_rows, ff_part), BF16),
    ]
    spread = (dp_n, 2, part_rows, ff_part)
    return pl.pallas_call(
        functools.partial(middle_kernel, order, pairs, block),
        in_specs=[anywhere] * 7 + [inside],
        out_specs=[anywhere, inside, anywhere, anywhere, anywhere, anywhere, inside],
        out_shape=[
            jax.ShapeDtypeStruct((group, tok, width), BF16),
            jax.ShapeDtypeStruct((tok, width), F32),
            jax.ShapeDtypeStruct(spread, BF16),
            jax.ShapeDtypeStruct(spread, BF16),
            jax.ShapeDtypeStruct(down.shape, BF16),
            jax.ShapeDtypeStruct(up.shape, BF16),
            jax.ShapeDtypeStruct((group * tok, ff_part), F32),
        ],
        scratch_shapes=swap_scratch((tok, cols))
        + dp_part
        + dp_part
        + sems(2)
        + gather_scratch(tok, width)
        + [
            pltpu.VMEM((group, tok, cols), BF16),
            pltpu.VMEM(weight.shape, BF16),
            pltpu.VMEM((tok, width), BF16),
            pltpu.VMEM((tok, width), BF16),
            pltpu.VMEM((tok, width), F32),
            pltpu.VMEM(spread, BF16),
            pltpu.VMEM((2, 2, tok, width), BF16),
            pltpu.SemaphoreType.DMA((3,)),
        ],
        compiler_params=pltpu.CompilerParams(
            collective_id=10, has_side_effects=True, vmem_limit_bytes=VMEM_LIMIT
        ),
        cost_estimate=pl.CostEstimate(
            flops=2 * group * tok * width * ff_part, bytes_accessed=250_000_000, transcendentals=0
        ),
        name="middle",
    )(heads, gate, gate_other, up, down, weight, rows, gain)


def weight_grad_kernel(dp_ref, left_ref, right_ref, first_ref, away_ref, own_ref):
    i = pl.program_id(0)
    total = dot32(left_ref[...], right_ref[...], ((0,), (0,)))

    @pl.when(i < 2)
    def _():
        away_ref[0] = total.astype(BF16)

    @pl.when(i >= 2)
    def _():
        own_ref[0] = total


def weight_grad_start(left, right, first):
    dp_n, hi_n = lax.axis_size("dp"), lax.axis_size("hi")
    depth, rows = left.shape
    cols = right.shape[1]
    if dp_n != 2:
        sums = scatter_start(by_copy(dot32(left, right, ((0,), (0,)))), "dp")
        return sums.astype(F32), jnp.zeros(sums.shape, BF16)
    part = rows // (dp_n * hi_n)
    place = lax.axis_index("dp").astype(jnp.int32).reshape(1)
    away, own = pl.pallas_call(
        weight_grad_kernel,
        grid_spec=pltpu.PrefetchScalarGridSpec(
            num_scalar_prefetch=1,
            grid=(4,),
            in_specs=[
                pl.BlockSpec(
                    (depth, part),
                    lambda i, dp: (0, jnp.where(i < 2, 2 * (1 - dp[0]) + i, 2 * dp[0] + i - 2)),
                ),
                pl.BlockSpec((depth, cols), lambda i, dp: (0, 0)),
                pl.BlockSpec(memory_space=pl.ANY),
            ],
            out_specs=[
                pl.BlockSpec((1, part, cols), lambda i, dp: (jnp.minimum(i, 1), 0, 0)),
                pl.BlockSpec((1, part, cols), lambda i, dp: (jnp.maximum(i - 2, 0), 0, 0)),
            ],
        ),
        out_shape=[
            jax.ShapeDtypeStruct((2, part, cols), BF16),
            jax.ShapeDtypeStruct((2, part, cols), F32),
        ],
        compiler_params=pltpu.CompilerParams(vmem_limit_bytes=VMEM_LIMIT),
        cost_estimate=pl.CostEstimate(
            flops=2 * depth * rows * cols, bytes_accessed=24_000_000, transcendentals=0
        ),
        name="weight_grad",
    )(place, left, right, first)
    return own, away


def ff_back_kernel(
    tile, grad_ref, gate_slope_ref, up_slope_ref, gate_ref, up_ref, down_ref, first_ref, dgate_ref, dup_ref,
    out_ref, total,
):
    total[...] = jnp.zeros_like(total)

    def step(t, carry):
        cols = pl.ds(pl.multiple_of(t * tile, tile), tile)
        dunits = dot32(grad_ref[...], down_ref[cols, :], ((1,), (1,)))
        dgate = (dunits * gate_slope_ref[:, cols].astype(F32)).astype(BF16)
        dup = (dunits * up_slope_ref[:, cols].astype(F32)).astype(BF16)
        dgate_ref[:, cols] = dgate
        dup_ref[:, cols] = dup
        total[...] += dot32(dgate, gate_ref[:, cols], ((1,), (1,))) + dot32(
            dup, up_ref[:, cols], ((1,), (1,))
        )
        return carry

    lax.fori_loop(0, down_ref.shape[0] // tile, step, 0)
    out_ref[...] = total[...].astype(BF16)


def ff_back(grad, gate_slope, up_slope, gate_weight, up_weight, down_weight, first, tok):
    count, width = grad.shape
    ff = down_weight.shape[0]
    rows = lambda cols: pl.BlockSpec((tok, cols), lambda i: (i, 0))
    whole = lambda a: pl.BlockSpec(a.shape, lambda i: (0, 0), pipeline_mode=pl.Buffered(1))
    return pl.pallas_call(
        functools.partial(ff_back_kernel, ff),
        grid=(count // tok,),
        in_specs=[
            rows(width),
            rows(ff),
            rows(ff),
            whole(gate_weight),
            whole(up_weight),
            whole(down_weight),
            pl.BlockSpec(memory_space=pl.ANY),
        ],
        out_specs=[rows(ff), rows(ff), rows(width)],
        out_shape=[
            jax.ShapeDtypeStruct((count, ff), BF16),
            jax.ShapeDtypeStruct((count, ff), BF16),
            jax.ShapeDtypeStruct((count, width), BF16),
        ],
        scratch_shapes=[pltpu.VMEM((tok, width), F32)],
        compiler_params=pltpu.CompilerParams(vmem_limit_bytes=VMEM_LIMIT),
        cost_estimate=pl.CostEstimate(
            flops=6 * count * width * ff, bytes_accessed=40_000_000, transcendentals=0
        ),
        name="ff_back",
    )(grad, gate_slope, up_slope, gate_weight, up_weight, down_weight, first)


def deal_kernel(
    key_head, places, wide, query_ref, key_ref, value_ref, gate_ref, up_ref, heads_ref, gates_ref, ups_ref
):
    columns, k_columns = query_ref.shape[1] // 8, key_ref.shape[1] // 8
    for f in range(8):
        g = key_head(f)
        cols, k_cols = slice(g * columns, g * columns + columns), slice(g * k_columns, g * k_columns + k_columns)
        heads_ref[f, :, :columns] = query_ref[:, cols]
        heads_ref[f, :, columns:] = jnp.concatenate([key_ref[:, k_cols], value_ref[:, k_cols]], axis=1)
    for at, (f, to) in enumerate(places):
        here, there = slice(at * wide, at * wide + wide), slice(to * wide, to * wide + wide)
        gates_ref[f, :, there] = gate_ref[:, here]
        ups_ref[f, :, there] = up_ref[:, here]


def collect_kernel(
    places, wide, gates_ref, ups_ref, gate_ref, up_ref, gain_ref, dgate_ref, dup_ref, dgain_ref
):
    total = jnp.zeros((gate_ref.shape[0], wide), F32)
    for at, (f, to) in enumerate(places):
        here, there = slice(at * wide, at * wide + wide), slice(to * wide, to * wide + wide)
        dgate, dup = gates_ref[f, :, there].astype(F32), ups_ref[f, :, there].astype(F32)
        dgate_ref[:, here] = dgate
        dup_ref[:, here] = dup
        total += gate_ref[:, here].astype(F32) * dgate + up_ref[:, here].astype(F32) * dup
    dgain_ref[...] = jnp.sum(total, axis=1, keepdims=True) / gain_ref[...]


def final_kernel(
    key_head, places, wide, first_ref, middle_ref, rows_ref, gain_ref, heads_ref, query_ref, key_ref, value_ref,
    gates_ref, ups_ref, gate_ref, up_ref, small_ref, outs_ref, down_ref, dhidden_ref, dquery_ref, dkey_ref,
    dvalue_ref, dgain_one_ref, dgate_ref, dup_ref, dgain_two_ref, dout_ref, ddown_ref,
):
    rows_w = gate_ref.shape[0]
    normal, inverse = norm_parts(rows_ref[...].astype(F32))
    grad = first_ref[...] * gain_ref[...]
    dhidden_ref[...] = middle_ref[...] + inverse * (
        grad - normal * jnp.mean(grad * normal, axis=-1, keepdims=True)
    )
    gains = jnp.transpose(jnp.broadcast_to(small_ref[0:1, :], (128, 128)))[:, 0:1]
    columns = query_ref.shape[1] // 8
    k_columns = key_ref.shape[1] // 8
    total = jnp.zeros((rows_w, columns), F32)
    k_total = jnp.zeros((rows_w, k_columns), F32)
    for f in range(8):
        b, l, g = f // 2, f % 2, key_head(f)
        both = heads_ref[b * 4 + l].astype(F32) + heads_ref[b * 4 + 2 + l].astype(F32)
        cols, k_cols = slice(g * columns, g * columns + columns), slice(g * k_columns, g * k_columns + k_columns)
        dquery = both[:, :columns]
        dkey, dvalue = both[:, columns : columns + k_columns], both[:, columns + k_columns :]
        dquery_ref[:, cols], dkey_ref[:, k_cols], dvalue_ref[:, k_cols] = dquery, dkey, dvalue
        total += query_ref[:, cols].astype(F32) * dquery
        k_total += key_ref[:, k_cols].astype(F32) * dkey + value_ref[:, k_cols].astype(F32) * dvalue
    dgain_one_ref[...] = (
        jnp.sum(total, axis=1, keepdims=True) + jnp.sum(k_total, axis=1, keepdims=True)
    ) / gains[:rows_w]
    total = jnp.zeros((rows_w, wide), F32)
    for at, (f, to) in enumerate(places):
        here, there = slice(at * wide, at * wide + wide), slice(to * wide, to * wide + wide)
        dgate, dup = gates_ref[f, :, there].astype(F32), ups_ref[f, :, there].astype(F32)
        dgate_ref[:, here] = dgate
        dup_ref[:, here] = dup
        total += gate_ref[:, here].astype(F32) * dgate + up_ref[:, here].astype(F32) * dup
    dgain_two_ref[...] = jnp.sum(total, axis=1, keepdims=True) / gains[rows_w : 2 * rows_w]
    dout_ref[...] = outs_ref[0].astype(F32) + outs_ref[1].astype(F32)
    ddown_ref[...] = down_ref[...]


def shards(
    hidden,
    teacher,
    lengths,
    attn_gain,
    w_query,
    key_projection,
    value_projection,
    w_out,
    mlp_gain,
    w_gate,
    w_up,
    w_down,
):
    dp_n, blk_n, hi_n, lo_n = (lax.axis_size(a) for a in ALL)
    group = blk_n * lo_n
    every = dp_n * blk_n * hi_n * lo_n
    hi, lo = lax.axis_index("hi"), lax.axis_index("lo")
    blk = lax.axis_index("blk")
    tok = hidden.shape[1]
    seq_len = tok * blk_n * hi_n * lo_n
    width = hidden.shape[2]
    rows_w = w_query.shape[0]
    units_w = w_down.shape[0]
    ff_part = w_gate.shape[1] // group

    block = lo_n * rows_w
    if block % 128 == 0:
        to_inner = [
            ((d * blk_n + b) * hi_n + h, (d * hi_n + h) * blk_n + b)
            for d in range(dp_n)
            for b in range(blk_n)
            for h in range(hi_n)
        ]
        reblock = block
    else:
        to_inner, reblock = [(0, 0)], width
    to_outer = [(to, at) for at, to in to_inner]

    def inner(a):
        if reblock == block:
            return a
        return a.reshape(-1, dp_n, blk_n, hi_n, block).transpose(0, 1, 3, 2, 4).reshape(-1, width)

    def outer(a):
        if reblock == block:
            return a
        return a.reshape(-1, dp_n, hi_n, blk_n, block).transpose(0, 1, 3, 2, 4).reshape(-1, width)

    key_head = lambda f: (f % lo_n) * blk_n + f // lo_n

    def head_columns(w):
        cols = w.shape[1] // group
        return w.reshape(rows_w, lo_n, blk_n, cols).transpose(2, 1, 0, 3).reshape(group, rows_w, cols)

    def head_columns_back(g):
        cols = g.shape[2]
        return (
            g.reshape(blk_n, lo_n, rows_w, cols).transpose(2, 1, 0, 3).reshape(rows_w, group * cols)
        )

    def unit_columns(w):
        return (
            w.reshape(rows_w, dp_n, blk_n, hi_n, lo_n, units_w)
            .transpose(2, 4, 0, 1, 3, 5)
            .reshape(group, rows_w, ff_part)
        )

    def unit_columns_back(g):
        return (
            g.reshape(blk_n, lo_n, rows_w, dp_n, hi_n, units_w)
            .transpose(2, 3, 0, 4, 1, 5)
            .reshape(rows_w, group * ff_part)
        )

    q_cols = w_query.shape[1] // group
    k_cols = key_projection.shape[1] // group
    ff_places = [
        (b * lo_n + l, d * hi_n + h)
        for d in range(dp_n)
        for b in range(blk_n)
        for h in range(hi_n)
        for l in range(lo_n)
    ]
    part_shape = jax.ShapeDtypeStruct((group, rows_w, ff_part), BF16)
    params = pltpu.CompilerParams(vmem_limit_bytes=VMEM_LIMIT)
    if units_w % 128 == 0:
        head_shape = jax.ShapeDtypeStruct((group, rows_w, q_cols + 2 * k_cols), BF16)
        head_parts, gate_parts, up_parts = pl.pallas_call(
            functools.partial(deal_kernel, key_head, ff_places, units_w),
            out_shape=[head_shape, part_shape, part_shape],
            compiler_params=params,
            name="deal",
        )(w_query, key_projection, value_projection, w_gate, w_up)
    else:
        head_parts = jnp.concatenate(
            [head_columns(w) for w in (w_query, key_projection, value_projection)], axis=2
        )
        gate_parts, up_parts = unit_columns(w_gate), unit_columns(w_up)
    head_wide = head_parts.shape[2]

    pad = jnp.zeros((7 * 128 + 128 - 2 * rows_w - 1,), F32)
    small = jnp.concatenate(
        [attn_gain.astype(F32), mlp_gain.astype(F32), lengths.astype(F32), pad]
    ).reshape(8, 128)
    rows_all, qkv_weight, smalls, out_rows = comm_call(
        open_kernel,
        0,
        [hidden[0], head_parts, small, w_out],
        [
            ((group, tok, width), BF16),
            ((every, rows_w, head_wide), BF16),
            ((every, 8, 128), F32),
            ((hi_n, lo_n, rows_w, width), BF16),
        ],
        gather_scratch(tok, width)
        + sems(every // dp_n - 1)
        + sems((dp_n - 1) * every // dp_n)
        + sems(every - 1)
        + sems(3)
        + [
            pltpu.SemaphoreType.DMA((3,)),
            pltpu.VMEM((rows_w, head_wide), BF16),
            pltpu.VMEM((rows_w, width), BF16),
        ],
        "open",
    )
    qkv_weight = qkv_weight.reshape(width, head_wide)
    gain_one = smalls[:, 0, :rows_w].reshape(1, width)
    gain_two = smalls[:, 0, rows_w : 2 * rows_w].reshape(1, width)
    valid_count = jnp.sum(smalls.reshape(every, -1)[:: every // dp_n, 2 * rows_w])
    hi_index = hi.astype(jnp.int32).reshape(1)
    tables = rope_tables(seq_len)
    normed_one, q, kv = project(
        hi_index, rows_all.reshape(group * tok, width), gain_one, qkv_weight, tables, tok
    )
    unit = lo_n * tok
    part_rows = group * rows_w
    other_kv, gate_parts, up_parts, downs = comm_call(
        keys_kernel,
        2,
        [kv, gate_parts, up_parts, w_down],
        [
            (kv.shape, BF16),
            (gate_parts.shape, BF16),
            (up_parts.shape, BF16),
            ((dp_n - 1,) + w_down.shape, BF16),
        ],
        sems(1) + swap_scratch((rows_w, ff_part)) * 2 + sems(dp_n - 1),
        "keys",
    )
    gate_parts = gate_parts.reshape(part_rows, -1)
    up_parts = up_parts.reshape(part_rows, -1)
    gate_other = swap_pair(gate_parts, "hi")
    out_weight = lax.all_gather(out_rows.reshape(-1, width), ("dp", "blk"), axis=0, tiled=True)
    q = q.reshape(blk_n, unit, q_cols)
    kv, other_kv = kv.reshape(blk_n, unit, -1), other_kv.reshape(blk_n, unit, -1)
    scalars = jnp.stack([lengths[0], hi.astype(jnp.int32)])
    out_heads, log_heads = attend(scalars, q, kv, other_kv)
    if reblock == block:
        normed_two, middle, gate_weight, up_weight, down_other, _, gate = through_middle(
            out_heads.reshape(group, tok, q_cols),
            gate_parts,
            gate_other,
            up_parts,
            w_down,
            out_weight,
            hidden[0],
            gain_two,
            key_head,
            to_inner,
            reblock,
        )
        gate_weight = gate_weight.reshape(width, ff_part)
    else:
        dp_sems = sems(2 * (dp_n - 1))
        dp_scratch = [pltpu.SemaphoreType.DMA((2,)), pltpu.VMEM((2, part_rows, ff_part), BF16)]
        weight_shape = ((dp_n, hi_n, part_rows, ff_part), BF16)
        mixed, gate_weight, up_other = comm_call(
            heads_kernel,
            3,
            [out_heads.reshape(group, tok, q_cols), gate_parts, gate_other, up_parts],
            [((group, tok, q_cols), BF16), weight_shape, (up_parts.shape, BF16)],
            swap_scratch((tok, q_cols)) + dp_sems + sems(1) + dp_scratch,
            "heads",
        )
        gate_weight = gate_weight.reshape(width, ff_part)
        middle, normed_two = out_project(
            mixed, out_weight, hidden[0], gain_two, key_head, to_inner, reblock
        )

        normed_two, up_weight, down_other = comm_call(
            rows_kernel,
            4,
            [inner(normed_two), up_parts, up_other, w_down],
            [((group, tok, width), BF16), weight_shape, (w_down.shape, BF16)],
            gather_scratch(tok, width) + dp_sems + sems(1) + dp_scratch,
            "rows",
        )
        gate = dot32(normed_two.reshape(group * tok, width), gate_weight)
    normed_two = normed_two.reshape(group * tok, width)
    up_weight = up_weight.reshape(width, ff_part)
    dp_index = lax.axis_index("dp")
    own_first = hi == 0

    def by_hi(own, other):
        return jnp.stack([jnp.where(own_first, own, other), jnp.where(own_first, other, own)])

    down_parts = by_hi(w_down, down_other)
    if dp_n == 2:
        far = by_hi(downs[0], swap_pair(down_other, "dp"))
        dp_first = dp_index == 0
        down_parts = jnp.stack(
            [jnp.where(dp_first, down_parts, far), jnp.where(dp_first, far, down_parts)]
        )
    else:
        down_parts = lax.all_gather(down_parts, "dp", axis=0, tiled=False)
    down_weight = down_parts.reshape(-1, width)
    upward = dot32(normed_two, up_weight)
    sigma = jax.nn.sigmoid(gate)
    silu = gate * sigma
    units = (silu * upward).astype(BF16)
    gate_slope = (upward * sigma * (1.0 + gate * (1.0 - sigma))).astype(BF16)
    up_slope = silu.astype(BF16)
    result = middle + RESIDUAL_SCALE * scatter_square(dot32(units, down_weight), 1)

    own_places = ((blk * hi_n + hi) * lo_n + lo) * tok + jnp.arange(tok)
    valid = own_places < lengths[0]
    misfit = jnp.where(valid[:, None], result - teacher[0].astype(F32), 0.0)
    squares = jnp.broadcast_to(jnp.sum(misfit * misfit), (8, 128))
    grad_result = misfit * (dp_n * seq_len / valid_count)

    branch = gather_square((RESIDUAL_SCALE * grad_result).astype(BF16), 5)
    down_sum = weight_grad_start(units, branch, branch)
    grad_gate_rows, grad_up_rows, grad_normal = ff_back(
        branch, gate_slope, up_slope, gate_weight, up_weight, down_weight, down_sum[0], 2 * tok
    )
    if dp_n == 2:
        down_got = swap_pair(down_sum[1], "dp")
        grad_normal, down_sum, gate_own, up_own, gate_stay, up_stay, gate_got, up_got = scatter_down(
            grad_normal, 9, (down_sum[0], down_got), normed_two, grad_gate_rows, grad_up_rows
        )
        gate_stay, up_stay = swap_pair(gate_stay, "dp"), swap_pair(up_stay, "dp")
    else:
        grad_normal = scatter_square(grad_normal, 9)
        down_sum = scatter_end(scatter_start(down_sum[0], "hi"), "hi")
        gate_own = weight_grad_start(normed_two, grad_gate_rows, grad_normal)[0]
        up_own = weight_grad_start(normed_two, grad_up_rows, grad_normal)[0]
        gate_stay = up_stay = gate_got = up_got = jnp.zeros(gate_own.shape[1:], BF16)
    grad_normal = outer(grad_normal)

    part_shape = (part_rows, ff_part)
    anywhere, inside = pl.BlockSpec(memory_space=pl.ANY), pl.BlockSpec(memory_space=pltpu.VMEM)
    grad_middle, attn_rows, dout, gate_away, up_away = pl.pallas_call(
        functools.partial(out_back_kernel, key_head, to_outer, reblock),
        in_specs=[inside] * 4 + [anywhere] * 5,
        out_specs=[inside] * 2 + [anywhere] + [inside] * 2,
        out_shape=[
            jax.ShapeDtypeStruct((tok, width), F32),
            jax.ShapeDtypeStruct((tok, width), BF16),
            jax.ShapeDtypeStruct((group, tok, q_cols), BF16),
            jax.ShapeDtypeStruct(part_shape, BF16),
            jax.ShapeDtypeStruct(part_shape, BF16),
        ],
        scratch_shapes=[
            pltpu.VMEM(out_weight.shape, BF16),
            pltpu.VMEM((tok, width), F32),
            pltpu.VMEM((group, tok, q_cols), BF16),
        ]
        + sems(7)
        + [
            pltpu.VMEM((2,) + part_shape, F32),
            pltpu.VMEM((2,) + part_shape, BF16),
            pltpu.SemaphoreType.DMA((2, 2)),
            pltpu.SemaphoreType.DMA((1,)),
        ],
        compiler_params=pltpu.CompilerParams(
            collective_id=6, has_side_effects=True, vmem_limit_bytes=VMEM_LIMIT
        ),
        cost_estimate=pl.CostEstimate(
            flops=2 * tok * width * width, bytes_accessed=60_000_000, transcendentals=0
        ),
        name="out_back",
    )(grad_normal, middle, grad_result, gain_two, out_weight, gate_own, gate_got, up_own, up_got)
    columns = (group, rows_w, ff_part)

    gate_dp, up_dp = gate_stay.reshape(columns), up_stay.reshape(columns)
    gate_hi, up_hi = (swap_pair(a, "hi").reshape(columns) for a in (gate_away, up_away))
    square_attn = lax.all_gather(attn_rows, SQUARE, axis=0, tiled=True)
    dout = dout.reshape(blk_n, unit, q_cols)
    dq, dkv = attend_back(scalars, q, kv, other_kv, dout, out_heads, log_heads, gate_away)
    dkv = dkv.reshape(2, group * tok, 2 * k_cols)
    sum_scratch = [pltpu.VMEM(columns, F32)] + [pltpu.VMEM(columns, BF16)] * 3
    sum_scratch.append(pltpu.SemaphoreType.DMA((3,)))
    own_out = dot32(out_heads.reshape(group * tok, q_cols), square_attn, ((0,), (0,))).astype(BF16)
    other_dkv, gate_parts = comm_call(
        dkeys_kernel,
        7,
        [dkv, gate_own.reshape((hi_n,) + columns), gate_dp, gate_hi, up_dp],
        [(dkv.shape[1:], BF16), (columns, BF16)],
        sems(1) + swap_scratch((rows_w, ff_part)) + sum_scratch,
        "dkeys",
    )
    grad_first, head_grads = project_back(
        hi_index,
        dq.reshape(group * tok, q_cols),
        dkv[0],
        other_dkv,
        normed_one,
        qkv_weight,
        tables,
        up_hi,
        unit,
    )
    head_grads = head_grads.reshape(dp_n, every // dp_n, rows_w, head_wide)
    with_out = dp_n == 2 and rows_w * hi_n * lo_n == q_cols
    arrays = [grad_first.reshape(group, tok, width), head_grads]
    arrays += [up_own.reshape((hi_n,) + columns), up_dp, up_hi, squares]
    shapes = [
        ((tok, width), F32),
        (head_grads.shape[1:], BF16),
        (columns, BF16),
        ((every, 8, 128), F32),
    ]
    scratch = scatter_scratch(tok, width) + sems(every // dp_n - 1) + sems(every - 1)
    scratch += [pltpu.SemaphoreType.DMA((2,)), pltpu.VMEM(head_grads.shape[1:], BF16)]
    scratch += [pltpu.VMEM((dp_n - 1,) + head_grads.shape[1:], BF16)]
    scratch += [pltpu.VMEM(head_grads.shape[1:], BF16), pltpu.SemaphoreType.DMA((2, dp_n - 1))]
    scratch += swap_scratch((rows_w, ff_part)) + sum_scratch
    if with_out:
        arrays.append(own_out.reshape(hi_n, lo_n, rows_w, width))
        shapes.append(((hi_n, rows_w, width), BF16))
        scratch += sems(5) + [pltpu.SemaphoreType.DMA((2,))]
        scratch += [pltpu.VMEM((hi_n, lo_n, rows_w, width), BF16)] * 3
    grad_first, head_grads, up_parts, squares, *outs = pl.pallas_call(
        functools.partial(close_kernel, with_out),
        in_specs=[anywhere] * len(arrays),
        out_specs=[pl.BlockSpec(memory_space=pltpu.VMEM)] + [anywhere] * (len(shapes) - 1),
        out_shape=[jax.ShapeDtypeStruct(shape, dtype) for shape, dtype in shapes],
        scratch_shapes=scratch,
        compiler_params=pltpu.CompilerParams(
            collective_id=8, has_side_effects=True, vmem_limit_bytes=VMEM_LIMIT
        ),
        cost_estimate=pl.CostEstimate(flops=0, bytes_accessed=120_000_000, transcendentals=0),
        name="close",
    )(*arrays)
    mse_loss = jnp.sum(squares[:, 0, 0]) / (width * valid_count)
    if with_out and units_w % 128 == 0 and 2 * rows_w == 128:
        shape = lambda *dims: jax.ShapeDtypeStruct(dims, F32)
        grads = pl.pallas_call(
            functools.partial(final_kernel, key_head, ff_places, units_w),
            out_shape=[
                shape(tok, width),
                shape(*w_query.shape),
                shape(*key_projection.shape),
                shape(*value_projection.shape),
                shape(rows_w, 1),
                shape(*w_gate.shape),
                shape(*w_up.shape),
                shape(rows_w, 1),
                shape(*w_out.shape),
                shape(*w_down.shape),
            ],
            compiler_params=params,
            name="final",
        )(
            grad_first,
            grad_middle,
            hidden[0],
            gain_one,
            head_grads,
            w_query,
            key_projection,
            value_projection,
            gate_parts,
            up_parts,
            w_gate,
            w_up,
            small,
            outs[0],
            down_sum,
        )
        return (
            result.astype(BF16)[None],
            mse_loss,
            grads[0][None],
            grads[4][:, 0],
            *grads[1:4],
            grads[8],
            grads[7][:, 0],
            grads[5],
            grads[6],
            grads[9],
        )
    if with_out:
        grad_out = jnp.sum(outs[0].astype(F32), axis=0)
    else:
        own_head = lo * blk_n + blk
        spread = jnp.where((jnp.arange(group) == own_head)[:, None, None], own_out[None], 0)
        grad_out = lax.psum_scatter(
            spread.reshape(width, width), ALL, scatter_dimension=0, tiled=True
        ).astype(F32)
    grad_first = grad_first * gain_one
    normal_one, inverse_one = norm_parts(hidden[0].astype(F32))
    grad_hidden = grad_middle + inverse_one * (
        grad_first - normal_one * jnp.mean(grad_first * normal_one, axis=-1, keepdims=True)
    )
    head_grads = jnp.sum(
        head_grads.reshape(blk_n, hi_n, lo_n, rows_w, head_wide).astype(F32), axis=1
    ).reshape(group, rows_w, head_wide)

    own_one, own_two = attn_gain.astype(F32)[:, None], mlp_gain.astype(F32)[:, None]
    grad_query = head_columns_back(head_grads[:, :, :q_cols])
    grad_key = head_columns_back(head_grads[:, :, q_cols : q_cols + k_cols])
    grad_value = head_columns_back(head_grads[:, :, q_cols + k_cols :])

    def row_sums(*pairs):
        return sum(jnp.sum(w.astype(F32) * g, axis=1, keepdims=True) for w, g in pairs)

    grad_gain_one = (
        row_sums((w_query, grad_query), (key_projection, grad_key), (value_projection, grad_value))
        / own_one
    )
    if units_w % 128 == 0:
        ff_shape = jax.ShapeDtypeStruct(w_gate.shape, F32)
        grad_gate, grad_up, grad_gain_two = pl.pallas_call(
            functools.partial(collect_kernel, ff_places, units_w),
            out_shape=[ff_shape, ff_shape, jax.ShapeDtypeStruct((rows_w, 1), F32)],
            compiler_params=params,
            name="collect",
        )(gate_parts, up_parts, w_gate, w_up, own_two)
    else:
        grad_gate = unit_columns_back(gate_parts.astype(F32))
        grad_up = unit_columns_back(up_parts.astype(F32))
        grad_gain_two = row_sums((w_gate, grad_gate), (w_up, grad_up)) / own_two
    return (
        result.astype(BF16)[None],
        mse_loss,
        grad_hidden[None],
        grad_gain_one[:, 0],
        grad_query,
        grad_key,
        grad_value,
        grad_out,
        grad_gain_two[:, 0],
        grad_gate,
        grad_up,
        down_sum,
    )


def solution(mesh):
    dp_n, blk_n, head_n = (mesh.shape[a] for a in ("dp", "blk", "head"))
    fine = Mesh(mesh.devices.reshape(dp_n, blk_n, 2, head_n // 2), ALL)
    tokens = P("dp", SEQ, None)
    rows, row = P(ALL, None), P(ALL)
    return jax.shard_map(
        shards,
        mesh=fine,
        in_specs=(tokens, tokens, P("dp"), row, rows, rows, rows, rows, row, rows, rows, rows),
        out_specs=(tokens, P(), tokens, row, rows, rows, rows, rows, row, rows, rows, rows),
        check_vma=False,
    )
```

```python
import functools
import math

import jax
import jax.numpy as jnp
import numpy as np
from jax import lax
from jax.experimental import pallas as pl
from jax.experimental.pallas import tpu as pltpu
from jax.sharding import Mesh, PartitionSpec as P

MODEL_WIDTH = 2048
HEAD_SIZE = 64
ROPE_BASE = 10000000.0
NORM_EPS = 1e-05
ATTN_SCALE = 0.015625
RESIDUAL_SCALE = 0.22
MASKED = -1e30

ALL = ("dp", "blk", "hi", "lo")
SQUARE = ("blk", "lo")
COPIES = ("dp", "hi")
SEQ = ("blk", "hi", "lo")
F32 = jnp.float32
BF16 = jnp.bfloat16
VMEM_LIMIT = 56 * 1024 * 1024


def dot32(a, b, dims=((1,), (0,))):
    return lax.dot_general(a, b, (dims, ((), ())), preferred_element_type=F32)


def rope_tables(seq_len):
    half = HEAD_SIZE // 2
    frequency = ROPE_BASE ** (-(np.arange(half) * 2.0) / HEAD_SIZE)
    angles = np.arange(seq_len).astype(np.float32)[:, None] * frequency.astype(np.float32)[None, :]
    cosine, sine = np.cos(angles.astype(np.float64)), np.sin(angles.astype(np.float64))
    none = np.zeros_like(cosine)
    rows = ([cosine] * 4, [-sine, none] * 2, [none, sine] * 2)
    return tuple(np.concatenate(row, axis=1).astype(np.float32) for row in rows)


def table_spec(tok):
    return pl.BlockSpec((tok, 128), lambda i, hi: ((i // 2 * 2 + hi[0]) * 2 + i % 2, 0))


def proj_kernel(hi_ref, rows_ref, gain_ref, weight_ref, cos_ref, sina_ref, sinb_ref, normed_ref, q_ref, kv_ref):
    normed_ref[...] = (norm_parts(rows_ref[...].astype(F32))[0] * gain_ref[...]).astype(BF16)
    made = dot32(normed_ref[...], weight_ref[...])
    cosine, sina, sinb = cos_ref[...], sina_ref[...], sinb_ref[...]
    low = lanes_low(cosine.shape)
    half = HEAD_SIZE // 2
    for part in range(3):
        u = made[:, 128 * part : 128 * part + 128]
        up, down = pltpu.roll(u, 128 - half, 1), pltpu.roll(u, half, 1)
        turned = u * cosine + up * sina + down * sinb
        if part < 2:
            q_ref[:, 128 * part : 128 * part + 128] = (
                turned.astype(BF16).astype(F32) * ATTN_SCALE
            ).astype(BF16)
        else:
            kv_ref[...] = jnp.where(low, turned, u).astype(BF16)


def project(hi, rows, gain, weight, tables, tile):
    count, depth = rows.shape
    wide = weight.shape[1]
    by_rows = lambda cols: pl.BlockSpec((tile, cols), lambda i, hi: (i, 0))
    whole = lambda *shape: pl.BlockSpec(shape, lambda i, hi: (0, 0))
    return pl.pallas_call(
        proj_kernel,
        grid_spec=pltpu.PrefetchScalarGridSpec(
            num_scalar_prefetch=1,
            grid=(count // tile,),
            in_specs=[by_rows(depth), whole(1, depth), whole(depth, wide)] + [table_spec(tile)] * 3,
            out_specs=[by_rows(depth), by_rows(256), by_rows(128)],
        ),
        out_shape=[
            jax.ShapeDtypeStruct((count, depth), BF16),
            jax.ShapeDtypeStruct((count, 256), BF16),
            jax.ShapeDtypeStruct((count, 128), BF16),
        ],
        compiler_params=pltpu.CompilerParams(vmem_limit_bytes=VMEM_LIMIT),
        cost_estimate=pl.CostEstimate(
            flops=2 * count * depth * wide, bytes_accessed=4 * count * depth, transcendentals=0
        ),
        name="project",
    )(hi, rows, gain, weight, *tables)


def proj_back_kernel(
    hi_ref, dq_ref, own_ref, other_ref, rows_ref, weight_ref, cos_ref, sina_ref, sinb_ref, first_ref, drows_ref,
    dweight_ref, made, total,
):
    i = pl.program_id(0)
    cosine, sina, sinb = cos_ref[...], sina_ref[...], sinb_ref[...]
    low = lanes_low(cosine.shape)
    half = HEAD_SIZE // 2
    shared = (own_ref[...].astype(F32) + other_ref[...].astype(F32)).astype(BF16)
    for part in range(3):
        w = (dq_ref[:, 128 * part : 128 * part + 128] if part < 2 else shared).astype(F32)
        turned = w * cosine + pltpu.roll(w * sinb, 128 - half, 1) + pltpu.roll(w * sina, half, 1)
        if part == 2:
            turned = jnp.where(low, turned, w)
        made[:, 128 * part : 128 * part + 128] = turned.astype(BF16)
    drows_ref[...] = dot32(made[...], weight_ref[...], ((1,), (1,))).astype(BF16)
    dweight = dot32(rows_ref[...], made[...], ((0,), (0,)))

    @pl.when(i == 0)
    def _():
        total[...] = dweight

    @pl.when(i > 0)
    def _():
        total[...] += dweight

    @pl.when(i == pl.num_programs(0) - 1)
    def _():
        dweight_ref[...] = total[...].astype(BF16)


def project_back(hi, dq, own, other, rows, weight, tables, first, unit):
    count, width = rows.shape
    wide = weight.shape[1]
    by_rows = lambda cols: pl.BlockSpec((unit, cols), lambda i, hi: (i, 0))
    whole = pl.BlockSpec((width, wide), lambda i, hi: (0, 0))
    table = pl.BlockSpec((unit, 128), lambda i, hi: (2 * i + hi[0], 0))
    return pl.pallas_call(
        proj_back_kernel,
        grid_spec=pltpu.PrefetchScalarGridSpec(
            num_scalar_prefetch=1,
            grid=(count // unit,),
            in_specs=[by_rows(256), by_rows(128), by_rows(128), by_rows(width), whole]
            + [table] * 3
            + [pl.BlockSpec(memory_space=pl.ANY)],
            out_specs=[by_rows(width), whole],
            scratch_shapes=[pltpu.VMEM((unit, wide), BF16), pltpu.VMEM((width, wide), F32)],
        ),
        out_shape=[
            jax.ShapeDtypeStruct((count, width), BF16),
            jax.ShapeDtypeStruct((width, wide), BF16),
        ],
        compiler_params=pltpu.CompilerParams(vmem_limit_bytes=VMEM_LIMIT),
        cost_estimate=pl.CostEstimate(
            flops=4 * count * width * wide, bytes_accessed=24_000_000, transcendentals=0
        ),
        name="project_back",
    )(hi, dq, own, other, rows, weight, *tables, first)


def lanes_low(shape):
    return lax.broadcasted_iota(jnp.int32, shape, 1) < HEAD_SIZE


def both_keys(kv):
    low = lanes_low(kv.shape)
    keys = kv.astype(F32)
    return (
        jnp.where(low, keys, 0.0).astype(BF16),
        jnp.where(low, 0.0, pltpu.roll(keys, HEAD_SIZE, 1)).astype(BF16),
    )


def both_values(kv):
    low = lanes_low(kv.shape)
    values = kv.astype(F32)
    return (
        jnp.where(low, pltpu.roll(values, HEAD_SIZE, 1), 0.0).astype(BF16),
        jnp.where(low, 0.0, values).astype(BF16),
    )


def attend_kernel(scalar_ref, q_ref, kv_ref, other_ref, out_ref, log_ref, keys, values, peak, sums):
    b = pl.program_id(0)
    blocks, unit, _ = q_ref.shape
    units = 2 * blocks
    length, hi = scalar_ref[0], scalar_ref[1]
    n = 2 * b + hi

    @pl.when(b == 0)
    def _():
        def spread(c, carry):
            for j, kv in (
                (2 * c + hi, kv_ref[c]),
                (2 * c + 1 - hi, other_ref[c]),
            ):
                keys[0, j], keys[1, j] = both_keys(kv)
                across = jnp.transpose(kv.astype(F32))[HEAD_SIZE:, :]
                values[j] = jnp.concatenate(
                    [across, jnp.ones((16, unit), F32)], axis=0
                ).astype(BF16)
            return carry

        lax.fori_loop(0, blocks, spread, 0)

    peak[...] = jnp.full_like(peak, MASKED)
    sums[...] = jnp.zeros_like(sums)

    def step(j, masked):
        for h in range(4):
            query = q_ref[b, :, 128 * (h // 2) : 128 * (h // 2) + 128]
            scores = dot32(keys[h % 2, j], query, ((1,), (1,)))
            if masked:
                row = j * unit + lax.broadcasted_iota(jnp.int32, scores.shape, 0)
                col = n * unit + lax.broadcasted_iota(jnp.int32, scores.shape, 1)
                scores = jnp.where((row <= col) & (row < length), scores, MASKED)
            old = peak[h, 0:1, :]
            new = jnp.maximum(old, jnp.max(scores, axis=0, keepdims=True))
            weights = jnp.exp(scores - new).astype(BF16)
            sums[h] = sums[h] * jnp.exp(old - new) + dot32(values[j], weights)
            peak[h, 0:1, :] = new

    first_ragged = units - units // 4

    def plain(j, carry):
        step(j, False)
        return carry

    def checked(j, carry):
        step(j, True)
        return carry

    lax.fori_loop(0, jnp.minimum(n, first_ragged), plain, 0)
    lax.fori_loop(jnp.minimum(n, first_ragged), n + 1, checked, 0)

    for pair in range(2):
        parts = []
        for h in (2 * pair, 2 * pair + 1):
            total = sums[h, HEAD_SIZE : HEAD_SIZE + 1, :]
            parts.append(sums[h, 0:HEAD_SIZE, :] / total)
            log_ref[0, h : h + 1, :] = peak[h, 0:1, :] + jnp.log(total)
        out_ref[0, :, 128 * pair : 128 * pair + 128] = jnp.transpose(
            jnp.concatenate(parts, axis=0)
        ).astype(BF16)


def attend(scalars, q, kv, other):
    blocks, unit, _ = q.shape
    units = 2 * blocks
    whole = lambda a: pl.BlockSpec(a.shape, lambda i: (0,) * a.ndim)
    return pl.pallas_call(
        attend_kernel,
        grid=(blocks,),
        in_specs=[pl.BlockSpec(memory_space=pltpu.SMEM), whole(q), whole(kv), whole(other)],
        out_specs=[
            pl.BlockSpec((1, unit, 256), lambda i: (i, 0, 0)),
            pl.BlockSpec((1, 8, unit), lambda i: (i, 0, 0)),
        ],
        out_shape=[
            jax.ShapeDtypeStruct((blocks, unit, 256), BF16),
            jax.ShapeDtypeStruct((blocks, 8, unit), F32),
        ],
        scratch_shapes=[
            pltpu.VMEM((2, units, unit, 128), BF16),
            pltpu.VMEM((units, HEAD_SIZE + 16, unit), BF16),
            pltpu.VMEM((4, 8, unit), F32),
            pltpu.VMEM((4, HEAD_SIZE + 16, unit), F32),
        ],
        compiler_params=pltpu.CompilerParams(vmem_limit_bytes=VMEM_LIMIT),
        cost_estimate=pl.CostEstimate(
            flops=40_000_000_000, bytes_accessed=8_000_000, transcendentals=20_000_000
        ),
        name="attend",
    )(scalars, q, kv, other)


def attend_back_kernel(
    scalar_ref,
    q_ref,
    kv_ref,
    other_ref,
    dout_ref,
    out_ref,
    log_ref,
    first_ref,
    dq_ref,
    dkv_ref,
    delta,
    dq,
    dk,
    dv,
):
    j = pl.program_id(0)
    blocks, unit, _ = q_ref.shape
    units = 2 * blocks
    length, hi = scalar_ref[0], scalar_ref[1]

    @pl.when(j == 0)
    def _():
        dq[...] = jnp.zeros_like(dq)
        pick = jnp.where(
            lax.broadcasted_iota(jnp.int32, (8, 256), 0)
            == lax.broadcasted_iota(jnp.int32, (8, 256), 1) // HEAD_SIZE,
            1.0,
            0.0,
        )

        def dots(b, carry):
            product = dout_ref[b].astype(F32) * out_ref[b].astype(F32)
            delta[b] = lax.dot_general(
                pick,
                product,
                (((1,), (1,)), ((), ())),
                precision=lax.Precision.HIGHEST,
                preferred_element_type=F32,
            )
            return carry

        lax.fori_loop(0, blocks, dots, 0)

    foreign = jnp.where(j % 2 == hi, 0, 1)
    kv = jnp.where(foreign == 0, kv_ref[j // 2], other_ref[j // 2])
    keys, values = both_keys(kv), both_values(kv)
    dk[...] = jnp.zeros_like(dk)
    dv[...] = jnp.zeros_like(dv)

    def step(b, masked):
        n = 2 * b + hi
        for pair in range(2):
            lanes = slice(128 * pair, 128 * pair + 128)
            query = q_ref[b, :, lanes]
            dout = dout_ref[b, :, lanes]
            dq_part = None
            for side in range(2):
                h = 2 * pair + side
                scores = dot32(keys[side], query, ((1,), (1,)))
                weights = jnp.exp(scores - log_ref[b, h : h + 1, :])
                if masked:
                    row = j * unit + lax.broadcasted_iota(jnp.int32, scores.shape, 0)
                    col = n * unit + lax.broadcasted_iota(jnp.int32, scores.shape, 1)
                    weights = jnp.where((row <= col) & (row < length), weights, 0.0)
                dweights = dot32(values[side], dout, ((1,), (1,)))
                dscores = (weights * (dweights - delta[b, h : h + 1, :])).astype(BF16)
                dv[side] += dot32(weights.astype(BF16), dout)
                dk[side] += dot32(dscores, query)
                part = dot32(dscores, keys[side], ((0,), (0,)))
                dq_part = part if dq_part is None else dq_part + part
            dq[b, :, lanes] += dq_part

    first_ragged = units - units // 4

    def plain(b, carry):
        step(b, False)
        return carry

    def checked(b, carry):
        step(b, True)
        return carry

    first = (j + 1 - hi) // 2
    masked_until = jnp.where(j >= first_ragged, blocks, jnp.where(foreign == 0, first + 1, first))
    lax.fori_loop(first, masked_until, checked, 0)
    lax.fori_loop(masked_until, blocks, plain, 0)

    low = lanes_low((unit, 128))
    dkey = dk[0] + pltpu.roll(dk[1], HEAD_SIZE, 1)
    dvalue = pltpu.roll(dv[0], HEAD_SIZE, 1) + dv[1]
    dkv_ref[foreign, j // 2] = jnp.where(low, dkey, dvalue).astype(BF16)

    @pl.when(j == units - 1)
    def _():
        def store(b, carry):
            dq_ref[b] = (dq[b] * ATTN_SCALE).astype(BF16)
            return carry

        lax.fori_loop(0, blocks, store, 0)


def attend_back(scalars, q, kv, other, dout, out, log, first):
    blocks, unit, _ = q.shape
    units = 2 * blocks
    whole = lambda a: pl.BlockSpec(a.shape, lambda i: (0,) * a.ndim)
    dq_shape = jax.ShapeDtypeStruct((blocks, unit, 256), BF16)
    dkv_shape = jax.ShapeDtypeStruct((2, blocks, unit, 128), BF16)
    return pl.pallas_call(
        attend_back_kernel,
        grid=(units,),
        in_specs=[
            pl.BlockSpec(memory_space=pltpu.SMEM),
            whole(q),
            whole(kv),
            whole(other),
            whole(dout),
            whole(out),
            whole(log),
            pl.BlockSpec(memory_space=pl.ANY),
        ],
        out_specs=[whole(dq_shape), whole(dkv_shape)],
        out_shape=[dq_shape, dkv_shape],
        scratch_shapes=[
            pltpu.VMEM((blocks, 8, unit), F32),
            pltpu.VMEM((blocks, unit, 256), F32),
            pltpu.VMEM((2, unit, 128), F32),
            pltpu.VMEM((2, unit, 128), F32),
        ],
        compiler_params=pltpu.CompilerParams(vmem_limit_bytes=VMEM_LIMIT),
        cost_estimate=pl.CostEstimate(
            flops=60_000_000_000, bytes_accessed=10_000_000, transcendentals=20_000_000
        ),
        name="attend_back",
    )(scalars, q, kv, other, dout, out, log, first)


PIECES = 4
MESH_ID = pl.DeviceIdType.MESH


def square_places():
    blk, lo = lax.axis_index("blk"), lax.axis_index("lo")
    mate, side = blk + 1 - 2 * (blk % 2), (blk + 2) % 4
    return blk, lo, mate, side


def greet(ids):
    barrier = pltpu.get_barrier_semaphore()
    for one in ids:
        pl.semaphore_signal(barrier, inc=1, device_id=one, device_id_type=MESH_ID)
    pl.semaphore_wait(barrier, len(ids))


def remote(source, target, send, recv, to):
    copy = pltpu.make_async_remote_copy(
        src_ref=source,
        dst_ref=target,
        send_sem=send,
        recv_sem=recv,
        device_id=to,
        device_id_type=MESH_ID,
    )
    copy.start()
    return copy


def local_copy(source, target, sem):
    copy = pltpu.make_async_copy(source, target, sem)
    copy.start()
    return copy


class Carried:
    def __init__(self, source, target, held, sem):
        self.held, self.target, self.sem = held, target, sem
        self.copy = local_copy(source, held, sem)

    def turn(self):
        self.copy.wait()
        self.copy = local_copy(self.held, self.target, self.sem)

    def wait(self):
        self.copy.wait()


def finish(copies):
    for copy in copies:
        if isinstance(copy, Carried):
            copy.turn()
    for copy in copies:
        copy.wait()


def square_peers():
    blk, lo = lax.axis_index("blk"), lax.axis_index("lo")
    mine = blk * 2 + lo
    others = [lax.rem(mine + d, 8) for d in range(1, 8)]
    return mine, others, [{"blk": o // 2, "lo": lax.rem(o, 2)} for o in others]


def other_hi():
    return {"hi": 1 - lax.axis_index("hi")}


def dp_peers():
    dp, dp_n = lax.axis_index("dp"), lax.axis_size("dp")
    return [{"dp": lax.rem(dp + d, dp_n)} for d in range(1, dp_n)]


def every_peer():
    sizes = [lax.axis_size(a) for a in ALL]
    places = [lax.axis_index(a) for a in ALL]
    found = []
    for k in range(1, math.prod(sizes)):
        to, rest = {}, k
        for a, size, place in reversed(list(zip(ALL, sizes, places))):
            to[a] = lax.rem(place + rest % size, size)
            rest //= size
        found.append(to)
    return found


def gather_begin(rows_ref, out_ref, send, recv, local, held):
    blk, lo, mate, side = square_places()
    slot = lambda b, l: b * 2 + l
    mine = slot(blk, lo)
    to_mate, to_side, to_next = {"blk": mate}, {"blk": side}, {"lo": 1 - lo}
    step = rows_ref.shape[0] // PIECES

    def push(source, place, piece, kind, to):
        target = out_ref.at[place, pl.ds(piece * step, step)]
        return remote(source, target, send.at[kind, piece], recv.at[kind, piece], to)

    own = Carried(rows_ref, out_ref.at[mine], held, local)
    piece_of = lambda p: rows_ref.at[pl.ds(p * step, step)]
    came = lambda place, p: out_ref.at[place, pl.ds(p * step, step)]
    side_order, next_order = (2, 3, 0, 1), (0, 1, 2, 3)
    by_side, by_next, by_mate, across = {}, {}, [], {}
    for k in range(PIECES):
        p, q = side_order[k], next_order[k]
        by_side[p] = push(piece_of(p), mine, p, 0, to_side)
        by_next[q] = push(piece_of(q), mine, q, 1, to_next)
    for p in range(PIECES):
        by_mate.append(push(piece_of(p), mine, p, 3, to_mate))

    def end(between=lambda k: None):
        own.turn()
        from_side, from_next, from_across = slot(side, lo), slot(blk, 1 - lo), slot(side, 1 - lo)
        for k in range(PIECES):
            p, q = side_order[k], next_order[k]
            by_side[p].wait_recv()
            if p >= 2:
                across[p] = push(came(from_side, p), from_side, p, 2, to_next)
            by_mate.append(push(came(from_side, p), from_side, p, 4, to_mate))
            by_next[q].wait_recv()
            if q < 2:
                across[q] = push(came(from_next, q), from_next, q, 2, to_side)
            by_mate.append(push(came(from_next, q), from_next, q, 5, to_mate))
            between(k)
        for p in (0, 2, 1, 3):
            across[p].wait_recv()
            by_mate.append(push(came(from_across, p), from_across, p, 6, to_mate))
            between(PIECES + p)
        for copy in by_mate:
            copy.wait()
        for copies in (by_side, by_next, across):
            for copy in copies.values():
                copy.wait_send()
        own.wait()

    return end


def gather_scratch(tok, width):
    return [
        pltpu.SemaphoreType.DMA((7, PIECES)),
        pltpu.SemaphoreType.DMA((7, PIECES)),
        pltpu.SemaphoreType.DMA,
        pltpu.VMEM((tok, width), BF16),
    ]


def sems(count):
    return [pltpu.SemaphoreType.DMA((count,))] * 2


def swap_scratch(part):
    return sems(7) + [pltpu.SemaphoreType.DMA, pltpu.VMEM(part, BF16)]


def square_greeting():
    blk, lo, mate, side = square_places()
    return [{"blk": mate}, {"blk": side}, {"lo": 1 - lo}]


def gather_kernel(rows_ref, out_ref, send, recv, local, held):
    greet(square_greeting())
    gather_begin(rows_ref, out_ref, send, recv, local, held)()


def comm_call(kernel, number, arrays, shapes, scratch, name):
    anywhere = pl.BlockSpec(memory_space=pl.ANY)
    return pl.pallas_call(
        kernel,
        in_specs=[anywhere] * len(arrays),
        out_specs=[anywhere] * len(shapes),
        out_shape=[jax.ShapeDtypeStruct(shape, dtype) for shape, dtype in shapes],
        scratch_shapes=scratch,
        compiler_params=pltpu.CompilerParams(
            collective_id=number, has_side_effects=True, vmem_limit_bytes=VMEM_LIMIT
        ),
        cost_estimate=pl.CostEstimate(flops=0, bytes_accessed=120_000_000, transcendentals=0),
        name=name,
    )(*arrays)


def gather_square(rows, number):
    tok, width = rows.shape
    (out,) = comm_call(
        gather_kernel,
        number,
        [rows],
        [((8, tok, width), rows.dtype)],
        gather_scratch(tok, width),
        "gather_square",
    )
    return out.reshape(8 * tok, width)


def swap_begin(parts_ref, out_ref, send, recv, local, held):
    mine, others, ids = square_peers()
    own = Carried(parts_ref.at[mine], out_ref.at[mine], held, local)
    copies = [
        remote(parts_ref.at[o], out_ref.at[mine], send.at[d], recv.at[d], to)
        for d, (o, to) in enumerate(zip(others, ids))
    ]
    return copies + [own]


def dp_begin(pieces, out_ref, send, recv, local, held, first=0):
    dp = lax.axis_index("dp")
    copies = []
    for k, (place, ref) in enumerate(pieces, first):
        copies.append(Carried(ref, out_ref.at[dp, place], held.at[k], local.at[k]))
        for d, to in enumerate(dp_peers()):
            n = 2 * d + k
            copies.append(remote(ref, out_ref.at[dp, place], send.at[n], recv.at[n], to))
    return copies


def device_place():
    mine = 0
    for a in ALL:
        mine = mine * lax.axis_size(a) + lax.axis_index(a)
    return mine


def seq_peers():
    sizes = [lax.axis_size(a) for a in SEQ]
    places = [lax.axis_index(a) for a in SEQ]
    found = []
    for k in range(1, math.prod(sizes)):
        to, source, digits, rest = {}, 0, [], k
        for size in reversed(sizes):
            digits.append(rest % size)
            rest //= size
        for a, size, place, digit in zip(SEQ, sizes, places, reversed(digits)):
            to[a] = lax.rem(place + digit, size)
            source = source * size + lax.rem(place + size - digit, size)
        found.append((to, source))
    return found


def seq_place(to):
    place = 0
    for a in SEQ:
        place = place * lax.axis_size(a) + to[a]
    return place


def open_kernel(
    rows_ref, heads_ref, small_ref, wout_ref, out_ref, weight_ref, smalls_ref, wouts_ref, g_send, g_recv,
    g_local, g_held, w_send, w_recv, d_send, d_recv, s_send, s_recv, o_send, o_recv, local, w_held, o_held,
):
    blk, hi, lo = (lax.axis_index(a) for a in SEQ)
    mine = device_place()
    peers = every_peer()
    greet(peers)
    copies = [
        Carried(heads_ref.at[blk * 2 + lo], weight_ref.at[mine], w_held, local.at[0]),
        local_copy(small_ref, smalls_ref.at[mine], local.at[1]),
        Carried(wout_ref, wouts_ref.at[hi, lo], o_held, local.at[2]),
    ]
    for k, to in enumerate(peers):
        copies.append(remote(small_ref, smalls_ref.at[mine], s_send.at[k], s_recv.at[k], to))
    end = gather_begin(rows_ref, out_ref, g_send, g_recv, g_local, g_held)
    wout = remote(wout_ref, wouts_ref.at[hi, lo], o_send.at[0], o_recv.at[0], other_hi())
    next_lo = {"lo": 1 - lo}
    copies.append(remote(wout_ref, wouts_ref.at[hi, lo], o_send.at[1], o_recv.at[1], next_lo))
    dp, seq = lax.axis_index("dp"), seq_peers()
    seq_n = len(seq) + 1
    straight = []
    for k, (to, source) in enumerate(seq):
        part = heads_ref.at[to["blk"] * 2 + to["lo"]]
        straight.append(remote(part, weight_ref.at[mine], w_send.at[k], w_recv.at[k], to))

    def hand_on(part, place, k):
        for d, to in enumerate(dp_peers()):
            n = d * seq_n + k
            copies.append(remote(part, weight_ref.at[place], d_send.at[n], d_recv.at[n], to))

    hand_on(heads_ref.at[blk * 2 + lo], mine, seq_n - 1)

    def pass_on(turn):
        for k, (to, source) in enumerate(seq):
            if k * 2 * PIECES // len(seq) == turn:
                straight[k].wait()
                place = dp * seq_n + source
                hand_on(weight_ref.at[place], place, k)

    end(pass_on)
    wout.wait()
    there = wouts_ref.at[1 - hi, lo]
    copies.append(remote(there, there, o_send.at[2], o_recv.at[2], next_lo))
    finish(copies)


def keys_kernel(
    kv_ref, gate_ref, up_ref, down_ref, other_ref, gates_ref, ups_ref, downs_ref, k_send, k_recv, g_send,
    g_recv, g_local, g_held, u_send, u_recv, u_local, u_held, d_send, d_recv,
):
    greet(square_peers()[2] + [other_hi()] + dp_peers())
    copies = [remote(kv_ref, other_ref, k_send.at[0], k_recv.at[0], other_hi())]
    for d, to in enumerate(dp_peers()):
        copies.append(remote(down_ref, downs_ref.at[d], d_send.at[d], d_recv.at[d], to))
    copies += swap_begin(gate_ref, gates_ref, g_send, g_recv, g_local, g_held)
    copies += swap_begin(up_ref, ups_ref, u_send, u_recv, u_local, u_held)
    finish(copies)


def heads_kernel(
    heads_ref, gate_ref, gate_other_ref, up_ref, mixed_ref, gates_ref, up_other_ref, m_send, m_recv,
    m_local, m_held, g_send, g_recv, u_send, u_recv, g_local, g_held,
):
    hi = lax.axis_index("hi")
    greet(square_peers()[2] + [other_hi()] + dp_peers())
    copies = swap_begin(heads_ref, mixed_ref, m_send, m_recv, m_local, m_held)
    copies.append(remote(up_ref, up_other_ref, u_send.at[0], u_recv.at[0], other_hi()))
    copies += dp_begin(
        [(hi, gate_ref), (1 - hi, gate_other_ref)], gates_ref, g_send, g_recv, g_local, g_held
    )
    finish(copies)


def rows_kernel(
    rows_ref, up_ref, up_other_ref, down_ref, out_ref, ups_ref, down_other_ref, r_send, r_recv, r_local,
    r_held, u_send, u_recv, d_send, d_recv, u_local, u_held,
):
    hi = lax.axis_index("hi")
    greet(square_greeting() + [other_hi()] + dp_peers())
    end = gather_begin(rows_ref, out_ref, r_send, r_recv, r_local, r_held)
    copies = [remote(down_ref, down_other_ref, d_send.at[0], d_recv.at[0], other_hi())]
    copies += dp_begin(
        [(hi, up_ref), (1 - hi, up_other_ref)], ups_ref, u_send, u_recv, u_local, u_held
    )
    end()
    finish(copies)


def sum_begin(own_ref, got_ref, place, own, got, sem):
    return [
        local_copy(own_ref.at[place], own, sem.at[0]),
        local_copy(got_ref.at[place], got, sem.at[1]),
    ]


def wait_all(copies):
    for copy in copies:
        copy.wait()


def out_back_kernel(
    order, pairs, block, grad_ref, middle_ref, result_ref, gain_ref, weight_ref, gate_ref, gate_got_ref, up_ref,
    up_got_ref, sum_ref, rows_ref, out_ref, gate_away_ref, up_away_ref, weight, work, parts, send, recv, own, got, sem,
    w_sem,
):
    hi = lax.axis_index("hi")
    load = local_copy(weight_ref, weight, w_sem.at[0])
    loads = [
        [local_copy(ref.at[1 - hi], own.at[k], sem.at[k, 0]), local_copy(got_ref, got.at[k], sem.at[k, 1])]
        for k, (ref, got_ref) in enumerate(((gate_ref, gate_got_ref), (up_ref, up_got_ref)))
    ]
    mine, others, ids = square_peers()
    greet(ids)
    reorder(pairs, block, grad_ref, work, lambda v: v)
    normal, inverse = norm_parts(middle_ref[...])
    grad = work[...] * gain_ref[...]
    total = result_ref[...] + inverse * (
        grad - normal * jnp.mean(grad * normal, axis=-1, keepdims=True)
    )
    sum_ref[...] = total
    rows_ref[...] = (RESIDUAL_SCALE * total).astype(BF16)
    load.wait()
    cols = parts.shape[2]

    def make(n, f):
        part = weight[pl.ds(pl.multiple_of(order(f) * cols, cols), cols), :]
        parts[n] = dot32(rows_ref[...], part, ((1,), (1,))).astype(BF16)

    copies = []
    for d, (other, to) in enumerate(zip(others, ids)):
        make(d, other)
        copies.append(remote(parts.at[d], out_ref.at[mine], send.at[d], recv.at[d], to))
    make(7, mine)
    copies.append(local_copy(parts.at[7], out_ref.at[mine], w_sem.at[0]))
    for k, target in enumerate((gate_away_ref, up_away_ref)):
        wait_all(loads[k])
        target[...] = (own[k] + got[k].astype(F32)).astype(BF16)
    wait_all(copies)


def sum_three(place, own_ref, over_dp_ref, over_hi_ref, own, over_dp, over_hi, sem):
    return [
        local_copy(own_ref.at[place], own, sem.at[0]),
        local_copy(over_dp_ref, over_dp, sem.at[1]),
        local_copy(over_hi_ref, over_hi, sem.at[2]),
    ]


def dkeys_kernel(
    dkv_ref, gate_ref, gate_dp_ref, gate_hi_ref, first_ref, other_ref, gates_ref, k_send, k_recv, g_send, g_recv, g_local,
    g_held, own, over_dp, over_hi, made, sem,
):
    hi = lax.axis_index("hi")
    loads = sum_three(hi, gate_ref, gate_dp_ref, gate_hi_ref, own, over_dp, over_hi, sem)
    greet(square_peers()[2] + [other_hi()])
    copies = [remote(dkv_ref.at[1], other_ref, k_send.at[0], k_recv.at[0], other_hi())]
    wait_all(loads)
    made[...] = (own[...] + over_dp[...].astype(F32) + over_hi[...].astype(F32)).astype(BF16)
    copies += swap_begin(made, gates_ref, g_send, g_recv, g_local, g_held)
    finish(copies)


class OwnOut:
    def __init__(self, out_ref, outs_ref, send, recv, local, own, got, made):
        self.outs_ref, self.made, self.send, self.recv, self.local = outs_ref, made, send, recv, local
        self.own, self.got = own, got
        self.dp, self.hi, self.lo = (lax.axis_index(a) for a in ("dp", "hi", "lo"))
        self.load = local_copy(out_ref, own, local.at[0])
        self.over = remote(out_ref, got, send.at[0], recv.at[0], dp_peers()[0])

    def push(self, a, b):
        hi, lo = lax.rem(self.hi + a, 2), lax.rem(self.lo + b, 2)
        return pltpu.make_async_remote_copy(
            src_ref=self.made.at[hi, lo],
            dst_ref=self.outs_ref.at[self.hi],
            send_sem=self.send.at[1 + 2 * a + b],
            recv_sem=self.recv.at[1 + self.hi],
            device_id={"hi": hi, "lo": lo},
            device_id_type=MESH_ID,
        )

    def own_copy(self):
        return pltpu.make_async_copy(
            self.made.at[self.hi, self.lo], self.outs_ref.at[self.hi], self.local.at[1]
        )

    def turn(self):
        self.load.wait()
        self.over.wait()
        self.made[...] = (self.own[...].astype(F32) + self.got[...].astype(F32)).astype(BF16)

        @pl.when(self.dp == self.lo)
        def _():
            for a, b in ((0, 1), (1, 0), (1, 1)):
                self.push(a, b).start()
            self.own_copy().start()

    def wait(self):
        @pl.when(self.dp == self.lo)
        def _():
            for a, b in ((0, 1), (1, 0), (1, 1)):
                self.push(a, b).wait_send()
            self.own_copy().wait()

        for h in range(2):

            @pl.when(jnp.logical_not((h == self.hi) & (self.dp == self.lo)))
            def _(h=h):
                pltpu.make_async_remote_copy(
                    src_ref=self.made.at[0, 0],
                    dst_ref=self.outs_ref.at[h],
                    send_sem=self.send.at[1],
                    recv_sem=self.recv.at[1 + h],
                    device_id={"lo": 1 - self.lo},
                    device_id_type=MESH_ID,
                ).wait_recv()


def close_kernel(with_out, *refs):
    refs = iter(refs)
    take = lambda n: [next(refs) for _ in range(n)]
    parts_ref, heads_ref, up_ref, up_dp_ref, up_hi_ref, square_ref = take(6)
    out_rows_ref = next(refs) if with_out else None
    total_ref, head_ref, ups_ref, squares_ref = take(4)
    outs_ref = next(refs) if with_out else None
    scatter = take(9)
    h_send, h_recv, s_send, s_recv, local, h_own, h_got, h_made, h_sem = take(9)
    swap = take(4)
    own, over_dp, over_hi, made, sem = take(5)
    out_scratch = take(6) if with_out else None
    mine = device_place()
    peers, seq = every_peer(), seq_peers()
    place = seq_place({a: lax.axis_index(a) for a in SEQ})
    loads = scatter_load(parts_ref, scatter)
    hi = lax.axis_index("hi")
    up_loads = sum_three(hi, up_ref, up_dp_ref, up_hi_ref, own, over_dp, over_hi, sem)
    greet(peers)
    copies = [local_copy(square_ref, squares_ref.at[mine], local.at[1])]
    dp = lax.axis_index("dp")
    own_heads = local_copy(heads_ref.at[dp], h_own, local.at[0])
    over_heads = []
    for d, to in enumerate(dp_peers()):
        part = heads_ref.at[to["dp"]]
        over_heads.append(remote(part, h_got.at[d], h_sem.at[0, d], h_sem.at[1, d], to))
    mates = scatter_mates(parts_ref, scatter)
    for k, to in enumerate(peers):
        copies.append(remote(square_ref, squares_ref.at[mine], s_send.at[k], s_recv.at[k], to))

    def send_heads():
        own_heads.wait()
        wait_all(over_heads)
        total = h_own[...].astype(F32)
        for d in range(len(over_heads)):
            total = total + h_got[d].astype(F32)
        h_made[...] = total.astype(BF16)
        copies.append(local_copy(h_made.at[place], head_ref.at[place], local.at[0]))
        for k, (to, source) in enumerate(seq):
            part = h_made.at[seq_place(to)]
            copies.append(remote(part, head_ref.at[place], h_send.at[k], h_recv.at[k], to))

    own_out = OwnOut(out_rows_ref, outs_ref, *out_scratch) if with_out else None
    wait_all(up_loads)
    made[...] = (own[...] + over_dp[...].astype(F32) + over_hi[...].astype(F32)).astype(BF16)
    copies += swap_begin(made, ups_ref, *swap)
    nothing = lambda: None
    work = [nothing, send_heads, nothing, nothing, own_out.turn if with_out else nothing]
    scatter_end_square(loads, mates, total_ref, scatter, work)
    finish(copies)
    if with_out:
        own_out.wait()


def remote_to(source, target, sems_of, kind, piece, to):
    send, recv = sems_of
    return remote(source, target, send.at[kind, piece], recv.at[kind, piece], to)


def scatter_load(parts_ref, scratch):
    mine, local = scratch[0], scratch[8]
    blk, lo, mate, side = square_places()
    places = (side * 2 + 1 - lo, side * 2 + lo, blk * 2 + 1 - lo, blk * 2 + lo)
    return [local_copy(parts_ref.at[p], mine.at[k], local.at[k]) for k, p in enumerate(places)]


def scatter_mates(parts_ref, scratch):
    mates, sems_of = scratch[1], scratch[6:8]
    blk, lo, mate, side = square_places()
    mate_side = (mate + 2) % 4
    places = (mate_side * 2 + 1 - lo, mate_side * 2 + lo, mate * 2 + 1 - lo, mate * 2 + lo)
    step = parts_ref.shape[1] // PIECES
    rows = lambda p: pl.ds(p * step, step)
    orders = ((0, 2, 1, 3), (0, 1, 2, 3), (2, 3, 0, 1), (0, 1, 2, 3))
    return {
        (k, p): remote_to(
            parts_ref.at[places[k], rows(p)], mates.at[k, rows(p)], sems_of, k, p, {"blk": mate}
        )
        for k in range(4)
        for p in orders[k]
    }


def scatter_end_square(loads, from_mate, out_ref, scratch, work=()):
    work = list(work)
    mine, mates, made, got_across, got_side, got_next = scratch[:6]
    sems_of = scratch[6:8]
    blk, lo, mate, side = square_places()
    to_side, to_next = {"blk": side}, {"lo": 1 - lo}
    step = mine.shape[1] // PIECES
    rows = lambda p: pl.ds(p * step, step)

    def summed(k, p):
        from_mate[k, p].wait_recv()
        return mine[k, rows(p), :].astype(F32) + mates[k, rows(p), :].astype(F32)

    sent = {}
    loads[0].wait()
    for p in (0, 2, 1, 3):
        made[0, rows(p), :] = summed(0, p).astype(BF16)
        sent[0, p] = remote_to(
            made.at[0, rows(p)],
            got_across.at[rows(p)],
            sems_of,
            4,
            p,
            to_side if p < 2 else to_next,
        )
    loads[1].wait()
    loads[2].wait()
    for n, (k, p) in enumerate(((1, 0), (2, 2), (1, 1), (2, 3), (1, 2), (2, 0), (1, 3), (2, 1))):
        if work and n % 2 == 0:
            work.pop(0)()
        total = summed(k, p)
        if (k == 1) == (p >= 2):
            sent[0, p].wait_recv()
            total = total + got_across[rows(p), :].astype(F32)
        made[k, rows(p), :] = total.astype(BF16)
        sent[k, p] = remote_to(
            made.at[k, rows(p)],
            (got_side if k == 1 else got_next).at[rows(p)],
            sems_of,
            4 + k,
            p,
            to_side if k == 1 else to_next,
        )
    for one in work:
        one()
    loads[3].wait()
    for p in range(PIECES):
        total = summed(3, p)
        sent[1, p].wait_recv()
        sent[2, p].wait_recv()
        out_ref[rows(p), :] = (
            total + got_side[rows(p), :].astype(F32) + got_next[rows(p), :].astype(F32)
        )
    for copy in from_mate.values():
        copy.wait_send()
    for copy in sent.values():
        copy.wait_send()


def scatter_scratch(tok, width):
    return [
        pltpu.VMEM((4, tok, width), BF16),
        pltpu.VMEM((4, tok, width), BF16),
        pltpu.VMEM((3, tok, width), BF16),
        pltpu.VMEM((tok, width), BF16),
        pltpu.VMEM((tok, width), BF16),
        pltpu.VMEM((tok, width), BF16),
        pltpu.SemaphoreType.DMA((7, PIECES)),
        pltpu.SemaphoreType.DMA((7, PIECES)),
        pltpu.SemaphoreType.DMA((4,)),
    ]


def scatter_kernel(firsts, parts_ref, *refs):
    out_ref, scratch = refs[firsts], refs[firsts + 1 :]
    loads = scatter_load(parts_ref, scratch)
    greet(square_greeting())
    scatter_end_square(loads, scatter_mates(parts_ref, scratch), out_ref, scratch)


def scatter_square(parts, number, *first):
    count, width = parts.shape
    tok = count // 8
    return pl.pallas_call(
        functools.partial(scatter_kernel, len(first)),
        in_specs=[pl.BlockSpec(memory_space=pl.ANY)] * (1 + len(first)),
        out_specs=pl.BlockSpec(memory_space=pltpu.VMEM),
        out_shape=jax.ShapeDtypeStruct((tok, width), F32),
        scratch_shapes=scatter_scratch(tok, width),
        compiler_params=pltpu.CompilerParams(
            collective_id=number, has_side_effects=True, vmem_limit_bytes=VMEM_LIMIT
        ),
        cost_estimate=pl.CostEstimate(flops=0, bytes_accessed=120_000_000, transcendentals=0),
        name="scatter_square",
    )(parts.astype(BF16).reshape(8, tok, width), *first)


def scatter_down_kernel(
    parts_ref, down_ref, got_ref, rows_ref, dgate_ref, dup_ref, out_ref, sum_ref, gate_own_ref, up_own_ref,
    gate_stay_ref, up_stay_ref, gate_got_ref, up_got_ref, *scratch,
):
    scratch, rest = scratch[:9], scratch[9:]
    own, got, away, came, sem, send, recv, left, gate_right, up_right, gate_away, up_away, w_sem = rest
    dp, hi = lax.axis_index("dp"), lax.axis_index("hi")
    part = left.shape[2]
    blocks = ((1 - dp, 1 - hi), (dp, 1 - hi), (1 - dp, hi), (dp, hi))

    def load_left(n):
        d, h = blocks[n]
        cols = pl.ds(pl.multiple_of((d * 2 + h) * part, part), part)
        return local_copy(rows_ref.at[:, cols], left.at[n % 2], w_sem.at[n % 2])

    rights = [local_copy(dgate_ref, gate_right, w_sem.at[2]), local_copy(dup_ref, up_right, w_sem.at[3])]
    lefts = {0: load_left(0), 1: load_left(1)}
    down = sum_begin(down_ref, got_ref, 1 - hi, own, got, sem)
    loads = scatter_load(parts_ref, scratch)
    greet(square_greeting() + [other_hi()] + dp_peers())
    mates = scatter_mates(parts_ref, scratch)
    wait_all(down)
    away[...] = (own[...] + got[...].astype(F32)).astype(BF16)
    over = remote(away, came, send.at[0], recv.at[0], other_hi())
    down = sum_begin(down_ref, got_ref, hi, own, got, sem)
    pairs = []

    def gradient(n, up):
        if not up:
            lefts[n].wait()
        if n == 0:
            rights[up].wait()
        total = dot32(left[n % 2], (up_right if up else gate_right)[...], ((0,), (0,)))
        if n == 0:
            target, got_there = (up_away, up_got_ref) if up else (gate_away, gate_got_ref)
            target[...] = total.astype(BF16)
            pairs.append(remote(target, got_there, send.at[1 + up], recv.at[1 + up], dp_peers()[0]))
        elif n == 2:
            (up_stay_ref if up else gate_stay_ref)[...] = total.astype(BF16)
        else:
            (up_own_ref if up else gate_own_ref)[blocks[n][1]] = total
        if up and n < 2:
            lefts[n + 2] = load_left(n + 2)

    work = [functools.partial(gradient, n, up) for n in range(4) for up in range(2)]
    scatter_end_square(loads, mates, out_ref, scratch, work)
    wait_all(down)
    over.wait()
    sum_ref[...] = own[...] + got[...].astype(F32) + came[...].astype(F32)
    wait_all(pairs)


def scatter_down(parts, number, down, rows, dgate, dup):
    count, width = parts.shape
    tok = count // 8
    part = down[0].shape[1:]
    depth, cols = dgate.shape
    grad = (rows.shape[1] // 4, cols)
    anywhere, inside = pl.BlockSpec(memory_space=pl.ANY), pl.BlockSpec(memory_space=pltpu.VMEM)
    return pl.pallas_call(
        scatter_down_kernel,
        in_specs=[anywhere] * 6,
        out_specs=[inside] * 6 + [anywhere] * 2,
        out_shape=[
            jax.ShapeDtypeStruct((tok, width), F32),
            jax.ShapeDtypeStruct(part, F32),
            jax.ShapeDtypeStruct((2,) + grad, F32),
            jax.ShapeDtypeStruct((2,) + grad, F32),
        ]
        + [jax.ShapeDtypeStruct(grad, BF16)] * 4,
        scratch_shapes=scatter_scratch(tok, width)
        + [pltpu.VMEM(part, F32)]
        + [pltpu.VMEM(part, BF16)] * 3
        + [pltpu.SemaphoreType.DMA((2,))]
        + sems(3)
        + [
            pltpu.VMEM((2, depth, grad[0]), BF16),
            pltpu.VMEM((depth, cols), BF16),
            pltpu.VMEM((depth, cols), BF16),
            pltpu.VMEM(grad, BF16),
            pltpu.VMEM(grad, BF16),
            pltpu.SemaphoreType.DMA((4,)),
        ],
        compiler_params=pltpu.CompilerParams(
            collective_id=number, has_side_effects=True, vmem_limit_bytes=VMEM_LIMIT
        ),
        cost_estimate=pl.CostEstimate(
            flops=4 * depth * cols * rows.shape[1], bytes_accessed=160_000_000, transcendentals=0
        ),
        name="scatter_down",
    )(parts.reshape(8, tok, width), *down, rows, dgate, dup)


def swap_square(blocks):
    return lax.all_to_all(blocks, SQUARE, split_axis=0, concat_axis=0, tiled=True)


def swap_pair(block, axis):
    return lax.ppermute(block, axis, [(0, 1), (1, 0)])


def gather_start(rows, axis):
    if lax.axis_size(axis) != 2:
        return lax.all_gather(rows, axis, axis=0, tiled=False)
    return rows, swap_pair(rows, axis)


def gather_end(parts, axis):
    if lax.axis_size(axis) != 2:
        return parts
    rows, other = parts
    first = lax.axis_index(axis) == 0
    return jnp.stack([jnp.where(first, rows, other), jnp.where(first, other, rows)])


def scatter_start(parts, axis):
    if lax.axis_size(axis) != 2:
        return lax.psum_scatter(parts.astype(BF16), axis, scatter_dimension=0, tiled=False)
    place = lax.axis_index(axis)
    away = lax.dynamic_index_in_dim(parts, 1 - place, 0, False).astype(BF16)
    own = lax.dynamic_index_in_dim(parts, place, 0, False)
    return own, swap_pair(away, axis)


def scatter_end(parts, axis):
    if lax.axis_size(axis) != 2:
        return parts.astype(F32)
    return parts[0] + parts[1].astype(F32)


def by_copy(rows):
    dp_n, hi_n = lax.axis_size("dp"), lax.axis_size("hi")
    return rows.reshape((dp_n, hi_n, rows.shape[0] // (dp_n * hi_n)) + rows.shape[1:])


def total_of(value, axes, count):
    spread = jnp.broadcast_to(value.reshape(1, 1), (count, 1))
    return jnp.sum(lax.all_to_all(spread, axes, split_axis=0, concat_axis=0, tiled=True))


def norm_parts(rows):
    inverse = lax.rsqrt(jnp.mean(rows * rows, axis=-1, keepdims=True) + NORM_EPS)
    return rows * inverse, inverse


def reorder(pairs, block, source, target, cast):
    for at, to in pairs:
        target[:, to * block : to * block + block] = cast(source[:, at * block : at * block + block])


def out_kernel(order, pairs, block, mixed_ref, weight_ref, rows_ref, gain_ref, middle_ref, normed_ref, total):
    f = pl.program_id(0)

    @pl.when(f == 0)
    def _():
        total[...] = jnp.zeros_like(total)

    total[...] += dot32(mixed_ref[0], weight_ref[...])

    @pl.when(f == pl.num_programs(0) - 1)
    def _():
        middle = rows_ref[...].astype(F32) + RESIDUAL_SCALE * total[...]
        middle_ref[...] = middle
        total[...] = norm_parts(middle)[0] * gain_ref[...]
        reorder(pairs, block, total, normed_ref, lambda v: v.astype(BF16))


def out_project(mixed, weight, rows, gain, order, pairs, block):
    group, tok, cols = mixed.shape
    width = weight.shape[1]
    whole = pl.BlockSpec((tok, width), lambda f: (0, 0))
    return pl.pallas_call(
        functools.partial(out_kernel, order, pairs, block),
        grid=(group,),
        in_specs=[
            pl.BlockSpec((1, tok, cols), lambda f: (f, 0, 0)),
            pl.BlockSpec((cols, width), lambda f: (order(f), 0)),
            whole,
            pl.BlockSpec((1, width), lambda f: (0, 0)),
        ],
        out_specs=[whole, whole],
        out_shape=[
            jax.ShapeDtypeStruct((tok, width), F32),
            jax.ShapeDtypeStruct((tok, width), BF16),
        ],
        scratch_shapes=[pltpu.VMEM((tok, width), F32)],
        compiler_params=pltpu.CompilerParams(vmem_limit_bytes=VMEM_LIMIT),
        cost_estimate=pl.CostEstimate(
            flops=2 * tok * width * width, bytes_accessed=16_000_000, transcendentals=0
        ),
        name="out_project",
    )(mixed, weight, rows, gain)


def start_kernel(
    key_head, places, wide, query_ref, key_ref, value_ref, w_gate_ref, w_up_ref, rows_ref, small_ref, wout_ref,
    down_ref, cos_ref, sina_ref, sinb_ref, all_ref, weight_ref, smalls_ref, wouts_ref, gates_ref, ups_ref, downs_ref, other_ref, normed_ref, q_ref, kv_ref, g_send,
    g_recv, g_local, g_held, w_send, w_recv, d_send, d_recv, s_send, s_recv, o_send, o_recv, local, w_held, o_held,
    ga_send, ga_recv, ga_local, ga_held, up_send, up_recv, up_local, up_held, x_send, x_recv, k_send, k_recv, heads_ref,
    gate_ref, up_ref, weight, smalls, gain, chunks, cosines, sinas, sinbs, sem, t_sem,
):
    blk, hi, lo = (lax.axis_index(a) for a in SEQ)
    mine = device_place()
    peers = every_peer()
    unit = chunks.shape[1]
    tables = []
    for b in range(4):
        rows_of = pl.ds(pl.multiple_of((2 * b + hi) * unit, unit), unit)
        for t, (ref, table) in enumerate(((cos_ref, cosines), (sina_ref, sinas), (sinb_ref, sinbs))):
            tables.append(local_copy(ref.at[rows_of], table.at[b], t_sem.at[b, t]))
    deal_heads(key_head, query_ref, key_ref, value_ref, heads_ref)
    greet(peers)
    own_head = Carried(heads_ref.at[blk * 2 + lo], weight_ref.at[mine], w_held, local.at[0])
    small_copies = [local_copy(small_ref, smalls_ref.at[mine], local.at[1])]
    for k, to in enumerate(peers):
        small_copies.append(remote(small_ref, smalls_ref.at[mine], s_send.at[k], s_recv.at[k], to))
    end = gather_begin(rows_ref, all_ref, g_send, g_recv, g_local, g_held)
    dp, seq = lax.axis_index("dp"), seq_peers()
    seq_n = len(seq) + 1
    straight, handed = [], []
    for k, (to, source) in enumerate(seq):
        part = heads_ref.at[to["blk"] * 2 + to["lo"]]
        straight.append(remote(part, weight_ref.at[mine], w_send.at[k], w_recv.at[k], to))

    def hand_on(part, place, k):
        for d, to in enumerate(dp_peers()):
            n = d * seq_n + k
            handed.append(remote(part, weight_ref.at[place], d_send.at[n], d_recv.at[n], to))

    hand_on(heads_ref.at[blk * 2 + lo], mine, seq_n - 1)
    deal_units(places, wide, w_gate_ref, w_up_ref, gate_ref, up_ref)

    def pass_on(turn):
        for k, (to, source) in enumerate(seq):
            if k * 2 * PIECES // len(seq) == turn:
                straight[k].wait()
                place = dp * seq_n + source
                hand_on(weight_ref.at[place], place, k)

    end(pass_on)
    copies = [Carried(wout_ref, wouts_ref.at[hi, lo], o_held, local.at[2])]
    next_lo = {"lo": 1 - lo}
    wout = remote(wout_ref, wouts_ref.at[hi, lo], o_send.at[0], o_recv.at[0], other_hi())
    copies.append(remote(wout_ref, wouts_ref.at[hi, lo], o_send.at[1], o_recv.at[1], next_lo))
    copies += swap_begin(gate_ref, gates_ref, ga_send, ga_recv, ga_local, ga_held)
    copies += swap_begin(up_ref, ups_ref, up_send, up_recv, up_local, up_held)
    own_head.turn()
    wait_all(small_copies)
    load_smalls = local_copy(smalls_ref, smalls, sem.at[2])
    load_rows = lambda b: local_copy(all_ref.at[pl.ds(2 * b, 2)], chunks_of(chunks, b), sem.at[b % 2])
    loads = [load_rows(0), load_rows(1)]
    own_head.wait()
    wait_all(handed)
    load_weight = local_copy(weight_ref, weight, sem.at[3])
    for d, to in enumerate(dp_peers()):
        copies.append(remote(down_ref, downs_ref.at[d], x_send.at[d], x_recv.at[d], to))
    load_smalls.wait()
    low = lanes_low((1, 128))
    for j in range(smalls.shape[0] // 2):
        gain[:, 128 * j : 128 * j + 128] = jnp.where(
            low, smalls[2 * j, 0:1, :], pltpu.roll(smalls[2 * j + 1, 0:1, :], HEAD_SIZE, 1)
        )
    load_weight.wait()
    wait_all(tables)
    width = gain.shape[1]
    half = HEAD_SIZE // 2
    low = lanes_low((unit, 128))
    for b in range(4):
        here = slice(b * unit, b * unit + unit)
        loads[b].wait()
        rows = chunks[b % 2].astype(F32)
        normed_ref[here, :] = (norm_parts(rows)[0] * gain[...]).astype(BF16)
        if b + 2 < 4:
            loads.append(load_rows(b + 2))
        made = dot32(normed_ref[here, :], weight[...].reshape(width, -1))
        cosine, sina, sinb = cosines[b], sinas[b], sinbs[b]
        for part in range(3):
            u = made[:, 128 * part : 128 * part + 128]
            up, down = pltpu.roll(u, 128 - half, 1), pltpu.roll(u, half, 1)
            turned = u * cosine + up * sina + down * sinb
            if part < 2:
                q_ref[here, 128 * part : 128 * part + 128] = (
                    turned.astype(BF16).astype(F32) * ATTN_SCALE
                ).astype(BF16)
            else:
                kv_ref[here, :] = jnp.where(low, turned, u).astype(BF16)
        piece = pl.ds(b * unit, unit)
        copies.append(
            remote(kv_ref.at[piece], other_ref.at[piece], k_send.at[b], k_recv.at[b], other_hi())
        )
        if b == 2:
            wout.wait()
            there = wouts_ref.at[1 - hi, lo]
            copies.append(remote(there, there, o_send.at[2], o_recv.at[2], next_lo))
    finish(copies)


def chunks_of(chunks, b):
    return chunks.at[b % 2].reshape(2, chunks.shape[1] // 2, chunks.shape[2])


def through_start(key_head, places, wide_w, heads_shape, part_shape, weights, rows, small, wout, down, tables):
    tok, width = rows.shape
    rows_w = wout.shape[0]
    part = part_shape[1:]
    dp_n, hi_n, lo_n = (lax.axis_size(a) for a in ("dp", "hi", "lo"))
    every = dp_n * hi_n * lo_n * lax.axis_size("blk")
    wide = heads_shape[2]
    anywhere, inside = pl.BlockSpec(memory_space=pl.ANY), pl.BlockSpec(memory_space=pltpu.VMEM)
    shapes = [
        ((8, tok, width), BF16),
        ((every, rows_w, wide), BF16),
        ((every, 8, 128), F32),
        ((hi_n, lo_n, rows_w, width), BF16),
        (part_shape, BF16),
        (part_shape, BF16),
        ((dp_n - 1,) + down.shape, BF16),
        ((8 * tok, 128), BF16),
        ((8 * tok, width), BF16),
        ((8 * tok, 256), BF16),
        ((8 * tok, 128), BF16),
    ]
    return pl.pallas_call(
        functools.partial(start_kernel, key_head, places, wide_w),
        in_specs=[inside] * 5 + [anywhere] * 7,
        out_specs=[anywhere] * 8 + [inside] * 3,
        out_shape=[jax.ShapeDtypeStruct(shape, dtype) for shape, dtype in shapes],
        scratch_shapes=gather_scratch(tok, width)
        + sems(every // dp_n - 1)
        + sems((dp_n - 1) * every // dp_n)
        + sems(every - 1)
        + sems(3)
        + [
            pltpu.SemaphoreType.DMA((3,)),
            pltpu.VMEM((rows_w, wide), BF16),
            pltpu.VMEM((rows_w, width), BF16),
        ]
        + swap_scratch(part)
        + swap_scratch(part)
        + sems(dp_n - 1)
        + sems(4)
        + [
            pltpu.VMEM(heads_shape, BF16),
            pltpu.VMEM(part_shape, BF16),
            pltpu.VMEM(part_shape, BF16),
            pltpu.VMEM((every, rows_w, wide), BF16),
            pltpu.VMEM((every, 8, 128), F32),
            pltpu.VMEM((1, width), F32),
            pltpu.VMEM((2, 2 * tok, width), BF16),
        ]
        + [pltpu.VMEM((4, 2 * tok, 128), F32)] * 3
        + [pltpu.SemaphoreType.DMA((4,)), pltpu.SemaphoreType.DMA((4, 3))],
        compiler_params=pltpu.CompilerParams(
            collective_id=11, has_side_effects=True, vmem_limit_bytes=VMEM_LIMIT
        ),
        cost_estimate=pl.CostEstimate(
            flops=16 * tok * width * wide, bytes_accessed=250_000_000, transcendentals=0
        ),
        name="start",
    )(*weights, rows, small, wout, down, *tables)


def middle_kernel(
    order, pairs, block, heads_ref, gate_ref, gate_other_ref, up_ref, down_ref, weight_ref, rows_ref, gain_ref,
    out_ref, middle_ref, gates_ref, ups_ref, down_other_ref, up_other_ref, made_ref, m_send, m_recv, m_local,
    m_held, g_send, g_recv, g_local, g_held, u_send, u_recv, u_local, u_held, o_send, o_recv, r_send, r_recv,
    r_local, r_held, mixed, weight, rows, normed, total, gate_weight, chunks, sem,
):
    hi = lax.axis_index("hi")
    loads = [local_copy(weight_ref, weight, sem.at[0]), local_copy(rows_ref, rows, sem.at[1])]
    mine, others, ids = square_peers()
    greet(ids + [other_hi()] + dp_peers())
    heads = swap_begin(heads_ref, mixed, m_send, m_recv, m_local, m_held)
    up_over = remote(up_ref, up_other_ref, o_send.at[0], o_recv.at[0], other_hi())
    gates = dp_begin([(hi, gate_ref), (1 - hi, gate_other_ref)], gates_ref, g_send, g_recv, g_local, g_held)
    copies = dp_begin([(hi, up_ref)], ups_ref, u_send, u_recv, u_local, u_held)
    wait_all(loads)
    cols = mixed.shape[2]

    def add(f):
        g = order(f)
        part = weight[pl.ds(pl.multiple_of(g * cols, cols), cols), :]
        return dot32(mixed[f], part)

    heads[7].turn()
    heads[7].wait()
    total[...] = add(mine)
    for d in range(7):
        heads[d].wait_recv()
        total[...] += add(lax.rem(mine + 7 - d, 8))
    middle = rows[...].astype(F32) + RESIDUAL_SCALE * total[...]
    middle_ref[...] = middle
    total[...] = norm_parts(middle)[0] * gain_ref[...]
    reorder(pairs, block, total, normed, lambda v: v.astype(BF16))
    end = gather_begin(normed, out_ref, r_send, r_recv, r_local, r_held)

    def more(turn):
        if turn == PIECES - 1:
            up_over.wait()
            copies.append(remote(down_ref, down_other_ref, o_send.at[1], o_recv.at[1], other_hi()))
            copies.extend(
                dp_begin([(1 - hi, up_other_ref)], ups_ref, u_send, u_recv, u_local, u_held, 1)
            )

    end(more)
    finish(gates)
    step = 2
    load_gate = local_copy(gates_ref, gate_weight, sem.at[0])
    load_rows = lambda n: local_copy(out_ref.at[pl.ds(n * step, step)], chunks.at[n % 2], sem.at[1 + n % 2])
    loads = [load_rows(0), load_rows(1)]
    load_gate.wait()
    tok, width = rows.shape
    for n in range(8 // step):
        loads[n].wait()
        made_ref[n * step * tok : (n + 1) * step * tok, :] = dot32(
            chunks[n % 2].reshape(step * tok, width), gate_weight[...].reshape(width, -1)
        )
        if n + 2 < 8 // step:
            loads.append(load_rows(n + 2))
    for d in range(7):
        heads[d].wait_send()
    finish(copies)


def through_middle(heads, gate, gate_other, up, down, weight, rows, gain, order, pairs, block):
    group, tok, cols = heads.shape
    width = weight.shape[1]
    part_rows, ff_part = up.shape
    dp_n = lax.axis_size("dp")
    anywhere, inside = pl.BlockSpec(memory_space=pl.ANY), pl.BlockSpec(memory_space=pltpu.VMEM)
    dp_part = sems(2 * (dp_n - 1)) + [
        pltpu.SemaphoreType.DMA((2,)),
        pltpu.VMEM((2, part_rows, ff_part), BF16),
    ]
    spread = (dp_n, 2, part_rows, ff_part)
    return pl.pallas_call(
        functools.partial(middle_kernel, order, pairs, block),
        in_specs=[anywhere] * 7 + [inside],
        out_specs=[anywhere, inside, anywhere, anywhere, anywhere, anywhere, inside],
        out_shape=[
            jax.ShapeDtypeStruct((group, tok, width), BF16),
            jax.ShapeDtypeStruct((tok, width), F32),
            jax.ShapeDtypeStruct(spread, BF16),
            jax.ShapeDtypeStruct(spread, BF16),
            jax.ShapeDtypeStruct(down.shape, BF16),
            jax.ShapeDtypeStruct(up.shape, BF16),
            jax.ShapeDtypeStruct((group * tok, ff_part), F32),
        ],
        scratch_shapes=swap_scratch((tok, cols))
        + dp_part
        + dp_part
        + sems(2)
        + gather_scratch(tok, width)
        + [
            pltpu.VMEM((group, tok, cols), BF16),
            pltpu.VMEM(weight.shape, BF16),
            pltpu.VMEM((tok, width), BF16),
            pltpu.VMEM((tok, width), BF16),
            pltpu.VMEM((tok, width), F32),
            pltpu.VMEM(spread, BF16),
            pltpu.VMEM((2, 2, tok, width), BF16),
            pltpu.SemaphoreType.DMA((3,)),
        ],
        compiler_params=pltpu.CompilerParams(
            collective_id=10, has_side_effects=True, vmem_limit_bytes=VMEM_LIMIT
        ),
        cost_estimate=pl.CostEstimate(
            flops=2 * group * tok * width * ff_part, bytes_accessed=250_000_000, transcendentals=0
        ),
        name="middle",
    )(heads, gate, gate_other, up, down, weight, rows, gain)


def weight_grad_kernel(dp_ref, left_ref, right_ref, first_ref, away_ref, own_ref):
    i = pl.program_id(0)
    total = dot32(left_ref[...], right_ref[...], ((0,), (0,)))

    @pl.when(i < 2)
    def _():
        away_ref[0] = total.astype(BF16)

    @pl.when(i >= 2)
    def _():
        own_ref[0] = total


def weight_grad_start(left, right, first):
    dp_n, hi_n = lax.axis_size("dp"), lax.axis_size("hi")
    depth, rows = left.shape
    cols = right.shape[1]
    if dp_n != 2:
        sums = scatter_start(by_copy(dot32(left, right, ((0,), (0,)))), "dp")
        return sums.astype(F32), jnp.zeros(sums.shape, BF16)
    part = rows // (dp_n * hi_n)
    place = lax.axis_index("dp").astype(jnp.int32).reshape(1)
    away, own = pl.pallas_call(
        weight_grad_kernel,
        grid_spec=pltpu.PrefetchScalarGridSpec(
            num_scalar_prefetch=1,
            grid=(4,),
            in_specs=[
                pl.BlockSpec(
                    (depth, part),
                    lambda i, dp: (0, jnp.where(i < 2, 2 * (1 - dp[0]) + i, 2 * dp[0] + i - 2)),
                ),
                pl.BlockSpec((depth, cols), lambda i, dp: (0, 0)),
                pl.BlockSpec(memory_space=pl.ANY),
            ],
            out_specs=[
                pl.BlockSpec((1, part, cols), lambda i, dp: (jnp.minimum(i, 1), 0, 0)),
                pl.BlockSpec((1, part, cols), lambda i, dp: (jnp.maximum(i - 2, 0), 0, 0)),
            ],
        ),
        out_shape=[
            jax.ShapeDtypeStruct((2, part, cols), BF16),
            jax.ShapeDtypeStruct((2, part, cols), F32),
        ],
        compiler_params=pltpu.CompilerParams(vmem_limit_bytes=VMEM_LIMIT),
        cost_estimate=pl.CostEstimate(
            flops=2 * depth * rows * cols, bytes_accessed=24_000_000, transcendentals=0
        ),
        name="weight_grad",
    )(place, left, right, first)
    return own, away


def ff_back_kernel(
    tile, grad_ref, gate_slope_ref, up_slope_ref, gate_ref, up_ref, down_ref, first_ref, dgate_ref, dup_ref,
    out_ref, total,
):
    total[...] = jnp.zeros_like(total)

    def step(t, carry):
        cols = pl.ds(pl.multiple_of(t * tile, tile), tile)
        dunits = dot32(grad_ref[...], down_ref[cols, :], ((1,), (1,)))
        dgate = (dunits * gate_slope_ref[:, cols].astype(F32)).astype(BF16)
        dup = (dunits * up_slope_ref[:, cols].astype(F32)).astype(BF16)
        dgate_ref[:, cols] = dgate
        dup_ref[:, cols] = dup
        total[...] += dot32(dgate, gate_ref[:, cols], ((1,), (1,))) + dot32(
            dup, up_ref[:, cols], ((1,), (1,))
        )
        return carry

    lax.fori_loop(0, down_ref.shape[0] // tile, step, 0)
    out_ref[...] = total[...].astype(BF16)


def ff_back(grad, gate_slope, up_slope, gate_weight, up_weight, down_weight, first, tok):
    count, width = grad.shape
    ff = down_weight.shape[0]
    rows = lambda cols: pl.BlockSpec((tok, cols), lambda i: (i, 0))
    whole = lambda a: pl.BlockSpec(a.shape, lambda i: (0, 0), pipeline_mode=pl.Buffered(1))
    return pl.pallas_call(
        functools.partial(ff_back_kernel, ff),
        grid=(count // tok,),
        in_specs=[
            rows(width),
            rows(ff),
            rows(ff),
            whole(gate_weight),
            whole(up_weight),
            whole(down_weight),
            pl.BlockSpec(memory_space=pl.ANY),
        ],
        out_specs=[rows(ff), rows(ff), rows(width)],
        out_shape=[
            jax.ShapeDtypeStruct((count, ff), BF16),
            jax.ShapeDtypeStruct((count, ff), BF16),
            jax.ShapeDtypeStruct((count, width), BF16),
        ],
        scratch_shapes=[pltpu.VMEM((tok, width), F32)],
        compiler_params=pltpu.CompilerParams(vmem_limit_bytes=VMEM_LIMIT),
        cost_estimate=pl.CostEstimate(
            flops=6 * count * width * ff, bytes_accessed=40_000_000, transcendentals=0
        ),
        name="ff_back",
    )(grad, gate_slope, up_slope, gate_weight, up_weight, down_weight, first)


def deal_kernel(
    key_head, places, wide, query_ref, key_ref, value_ref, gate_ref, up_ref, heads_ref, gates_ref, ups_ref
):
    deal_heads(key_head, query_ref, key_ref, value_ref, heads_ref)
    deal_units(places, wide, gate_ref, up_ref, gates_ref, ups_ref)


def deal_heads(key_head, query_ref, key_ref, value_ref, heads_ref):
    columns, k_columns = query_ref.shape[1] // 8, key_ref.shape[1] // 8
    for f in range(8):
        g = key_head(f)
        cols, k_cols = slice(g * columns, g * columns + columns), slice(g * k_columns, g * k_columns + k_columns)
        heads_ref[f, :, :columns] = query_ref[:, cols]
        heads_ref[f, :, columns:] = jnp.concatenate([key_ref[:, k_cols], value_ref[:, k_cols]], axis=1)


def deal_units(places, wide, gate_ref, up_ref, gates_ref, ups_ref):
    for at, (f, to) in enumerate(places):
        here, there = slice(at * wide, at * wide + wide), slice(to * wide, to * wide + wide)
        gates_ref[f, :, there] = gate_ref[:, here]
        ups_ref[f, :, there] = up_ref[:, here]


def collect_kernel(
    places, wide, gates_ref, ups_ref, gate_ref, up_ref, gain_ref, dgate_ref, dup_ref, dgain_ref
):
    total = jnp.zeros((gate_ref.shape[0], wide), F32)
    for at, (f, to) in enumerate(places):
        here, there = slice(at * wide, at * wide + wide), slice(to * wide, to * wide + wide)
        dgate, dup = gates_ref[f, :, there].astype(F32), ups_ref[f, :, there].astype(F32)
        dgate_ref[:, here] = dgate
        dup_ref[:, here] = dup
        total += gate_ref[:, here].astype(F32) * dgate + up_ref[:, here].astype(F32) * dup
    dgain_ref[...] = jnp.sum(total, axis=1, keepdims=True) / gain_ref[...]


def final_kernel(
    key_head, places, wide, first_ref, middle_ref, rows_ref, gain_ref, heads_ref, query_ref, key_ref, value_ref,
    gates_ref, ups_ref, gate_ref, up_ref, small_ref, outs_ref, down_ref, dhidden_ref, dquery_ref, dkey_ref,
    dvalue_ref, dgain_one_ref, dgate_ref, dup_ref, dgain_two_ref, dout_ref, ddown_ref,
):
    rows_w = gate_ref.shape[0]
    normal, inverse = norm_parts(rows_ref[...].astype(F32))
    grad = first_ref[...] * gain_ref[...]
    dhidden_ref[...] = middle_ref[...] + inverse * (
        grad - normal * jnp.mean(grad * normal, axis=-1, keepdims=True)
    )
    gains = jnp.transpose(jnp.broadcast_to(small_ref[0:1, :], (128, 128)))[:, 0:1]
    columns = query_ref.shape[1] // 8
    k_columns = key_ref.shape[1] // 8
    total = jnp.zeros((rows_w, columns), F32)
    k_total = jnp.zeros((rows_w, k_columns), F32)
    for f in range(8):
        b, l, g = f // 2, f % 2, key_head(f)
        both = heads_ref[b * 4 + l].astype(F32) + heads_ref[b * 4 + 2 + l].astype(F32)
        cols, k_cols = slice(g * columns, g * columns + columns), slice(g * k_columns, g * k_columns + k_columns)
        dquery = both[:, :columns]
        dkey, dvalue = both[:, columns : columns + k_columns], both[:, columns + k_columns :]
        dquery_ref[:, cols], dkey_ref[:, k_cols], dvalue_ref[:, k_cols] = dquery, dkey, dvalue
        total += query_ref[:, cols].astype(F32) * dquery
        k_total += key_ref[:, k_cols].astype(F32) * dkey + value_ref[:, k_cols].astype(F32) * dvalue
    dgain_one_ref[...] = (
        jnp.sum(total, axis=1, keepdims=True) + jnp.sum(k_total, axis=1, keepdims=True)
    ) / gains[:rows_w]
    total = jnp.zeros((rows_w, wide), F32)
    for at, (f, to) in enumerate(places):
        here, there = slice(at * wide, at * wide + wide), slice(to * wide, to * wide + wide)
        dgate, dup = gates_ref[f, :, there].astype(F32), ups_ref[f, :, there].astype(F32)
        dgate_ref[:, here] = dgate
        dup_ref[:, here] = dup
        total += gate_ref[:, here].astype(F32) * dgate + up_ref[:, here].astype(F32) * dup
    dgain_two_ref[...] = jnp.sum(total, axis=1, keepdims=True) / gains[rows_w : 2 * rows_w]
    dout_ref[...] = outs_ref[0].astype(F32) + outs_ref[1].astype(F32)
    ddown_ref[...] = down_ref[...]


def shards(
    hidden,
    teacher,
    lengths,
    attn_gain,
    w_query,
    key_projection,
    value_projection,
    w_out,
    mlp_gain,
    w_gate,
    w_up,
    w_down,
):
    dp_n, blk_n, hi_n, lo_n = (lax.axis_size(a) for a in ALL)
    group = blk_n * lo_n
    every = dp_n * blk_n * hi_n * lo_n
    hi, lo = lax.axis_index("hi"), lax.axis_index("lo")
    blk = lax.axis_index("blk")
    tok = hidden.shape[1]
    seq_len = tok * blk_n * hi_n * lo_n
    width = hidden.shape[2]
    rows_w = w_query.shape[0]
    units_w = w_down.shape[0]
    ff_part = w_gate.shape[1] // group

    block = lo_n * rows_w
    if block % 128 == 0:
        to_inner = [
            ((d * blk_n + b) * hi_n + h, (d * hi_n + h) * blk_n + b)
            for d in range(dp_n)
            for b in range(blk_n)
            for h in range(hi_n)
        ]
        reblock = block
    else:
        to_inner, reblock = [(0, 0)], width
    to_outer = [(to, at) for at, to in to_inner]

    def inner(a):
        if reblock == block:
            return a
        return a.reshape(-1, dp_n, blk_n, hi_n, block).transpose(0, 1, 3, 2, 4).reshape(-1, width)

    def outer(a):
        if reblock == block:
            return a
        return a.reshape(-1, dp_n, hi_n, blk_n, block).transpose(0, 1, 3, 2, 4).reshape(-1, width)

    key_head = lambda f: (f % lo_n) * blk_n + f // lo_n

    def head_columns(w):
        cols = w.shape[1] // group
        return w.reshape(rows_w, lo_n, blk_n, cols).transpose(2, 1, 0, 3).reshape(group, rows_w, cols)

    def head_columns_back(g):
        cols = g.shape[2]
        return (
            g.reshape(blk_n, lo_n, rows_w, cols).transpose(2, 1, 0, 3).reshape(rows_w, group * cols)
        )

    def unit_columns(w):
        return (
            w.reshape(rows_w, dp_n, blk_n, hi_n, lo_n, units_w)
            .transpose(2, 4, 0, 1, 3, 5)
            .reshape(group, rows_w, ff_part)
        )

    def unit_columns_back(g):
        return (
            g.reshape(blk_n, lo_n, rows_w, dp_n, hi_n, units_w)
            .transpose(2, 3, 0, 4, 1, 5)
            .reshape(rows_w, group * ff_part)
        )

    q_cols = w_query.shape[1] // group
    k_cols = key_projection.shape[1] // group
    ff_places = [
        (b * lo_n + l, d * hi_n + h)
        for d in range(dp_n)
        for b in range(blk_n)
        for h in range(hi_n)
        for l in range(lo_n)
    ]
    part_shape = jax.ShapeDtypeStruct((group, rows_w, ff_part), BF16)
    params = pltpu.CompilerParams(vmem_limit_bytes=VMEM_LIMIT)
    one_start = reblock == block and rows_w == HEAD_SIZE and blk_n == 4 and units_w % 128 == 0
    head_wide = q_cols + 2 * k_cols
    if one_start:
        pass
    elif units_w % 128 == 0:
        head_shape = jax.ShapeDtypeStruct((group, rows_w, q_cols + 2 * k_cols), BF16)
        head_parts, gate_parts, up_parts = pl.pallas_call(
            functools.partial(deal_kernel, key_head, ff_places, units_w),
            out_shape=[head_shape, part_shape, part_shape],
            compiler_params=params,
            name="deal",
        )(w_query, key_projection, value_projection, w_gate, w_up)
    else:
        head_parts = jnp.concatenate(
            [head_columns(w) for w in (w_query, key_projection, value_projection)], axis=2
        )
        gate_parts, up_parts = unit_columns(w_gate), unit_columns(w_up)

    pad = jnp.zeros((7 * 128 + 128 - 2 * rows_w - 1,), F32)
    small = jnp.concatenate(
        [attn_gain.astype(F32), mlp_gain.astype(F32), lengths.astype(F32), pad]
    ).reshape(8, 128)
    hi_index = hi.astype(jnp.int32).reshape(1)
    tables = rope_tables(seq_len)
    unit = lo_n * tok
    part_rows = group * rows_w
    if one_start:
        _, qkv_weight, smalls, out_rows, gate_parts, up_parts, downs, other_kv, normed_one, q, kv = (
            through_start(
                key_head,
                ff_places,
                units_w,
                (group, rows_w, head_wide),
                (group, rows_w, ff_part),
                (w_query, key_projection, value_projection, w_gate, w_up),
                hidden[0],
                small,
                w_out,
                w_down,
                tables,
            )
        )
    else:
        rows_all, qkv_weight, smalls, out_rows = comm_call(
            open_kernel,
            0,
            [hidden[0], head_parts, small, w_out],
            [
                ((group, tok, width), BF16),
                ((every, rows_w, head_wide), BF16),
                ((every, 8, 128), F32),
                ((hi_n, lo_n, rows_w, width), BF16),
            ],
            gather_scratch(tok, width)
            + sems(every // dp_n - 1)
            + sems((dp_n - 1) * every // dp_n)
            + sems(every - 1)
            + sems(3)
            + [
                pltpu.SemaphoreType.DMA((3,)),
                pltpu.VMEM((rows_w, head_wide), BF16),
                pltpu.VMEM((rows_w, width), BF16),
            ],
            "open",
        )
        qkv_weight = qkv_weight.reshape(width, head_wide)
        gain_one = smalls[:, 0, :rows_w].reshape(1, width)
        normed_one, q, kv = project(
            hi_index, rows_all.reshape(group * tok, width), gain_one, qkv_weight, tables, tok
        )
        other_kv, gate_parts, up_parts, downs = comm_call(
            keys_kernel,
            2,
            [kv, gate_parts, up_parts, w_down],
            [
                (kv.shape, BF16),
                (gate_parts.shape, BF16),
                (up_parts.shape, BF16),
                ((dp_n - 1,) + w_down.shape, BF16),
            ],
            sems(1) + swap_scratch((rows_w, ff_part)) * 2 + sems(dp_n - 1),
            "keys",
        )
    qkv_weight = qkv_weight.reshape(width, head_wide)
    gain_one = smalls[:, 0, :rows_w].reshape(1, width)
    gain_two = smalls[:, 0, rows_w : 2 * rows_w].reshape(1, width)
    valid_count = jnp.sum(smalls.reshape(every, -1)[:: every // dp_n, 2 * rows_w])
    gate_parts = gate_parts.reshape(part_rows, -1)
    up_parts = up_parts.reshape(part_rows, -1)
    gate_other = swap_pair(gate_parts, "hi")
    out_weight = lax.all_gather(out_rows.reshape(-1, width), ("dp", "blk"), axis=0, tiled=True)
    q = q.reshape(blk_n, unit, q_cols)
    kv, other_kv = kv.reshape(blk_n, unit, -1), other_kv.reshape(blk_n, unit, -1)
    scalars = jnp.stack([lengths[0], hi.astype(jnp.int32)])
    out_heads, log_heads = attend(scalars, q, kv, other_kv)
    if reblock == block:
        normed_two, middle, gate_weight, up_weight, down_other, _, gate = through_middle(
            out_heads.reshape(group, tok, q_cols),
            gate_parts,
            gate_other,
            up_parts,
            w_down,
            out_weight,
            hidden[0],
            gain_two,
            key_head,
            to_inner,
            reblock,
        )
        gate_weight = gate_weight.reshape(width, ff_part)
    else:
        dp_sems = sems(2 * (dp_n - 1))
        dp_scratch = [pltpu.SemaphoreType.DMA((2,)), pltpu.VMEM((2, part_rows, ff_part), BF16)]
        weight_shape = ((dp_n, hi_n, part_rows, ff_part), BF16)
        mixed, gate_weight, up_other = comm_call(
            heads_kernel,
            3,
            [out_heads.reshape(group, tok, q_cols), gate_parts, gate_other, up_parts],
            [((group, tok, q_cols), BF16), weight_shape, (up_parts.shape, BF16)],
            swap_scratch((tok, q_cols)) + dp_sems + sems(1) + dp_scratch,
            "heads",
        )
        gate_weight = gate_weight.reshape(width, ff_part)
        middle, normed_two = out_project(
            mixed, out_weight, hidden[0], gain_two, key_head, to_inner, reblock
        )

        normed_two, up_weight, down_other = comm_call(
            rows_kernel,
            4,
            [inner(normed_two), up_parts, up_other, w_down],
            [((group, tok, width), BF16), weight_shape, (w_down.shape, BF16)],
            gather_scratch(tok, width) + dp_sems + sems(1) + dp_scratch,
            "rows",
        )
        gate = dot32(normed_two.reshape(group * tok, width), gate_weight)
    normed_two = normed_two.reshape(group * tok, width)
    up_weight = up_weight.reshape(width, ff_part)
    dp_index = lax.axis_index("dp")
    own_first = hi == 0

    def by_hi(own, other):
        return jnp.stack([jnp.where(own_first, own, other), jnp.where(own_first, other, own)])

    down_parts = by_hi(w_down, down_other)
    if dp_n == 2:
        far = by_hi(downs[0], swap_pair(down_other, "dp"))
        dp_first = dp_index == 0
        down_parts = jnp.stack(
            [jnp.where(dp_first, down_parts, far), jnp.where(dp_first, far, down_parts)]
        )
    else:
        down_parts = lax.all_gather(down_parts, "dp", axis=0, tiled=False)
    down_weight = down_parts.reshape(-1, width)
    upward = dot32(normed_two, up_weight)
    sigma = jax.nn.sigmoid(gate)
    silu = gate * sigma
    units = (silu * upward).astype(BF16)
    gate_slope = (upward * sigma * (1.0 + gate * (1.0 - sigma))).astype(BF16)
    up_slope = silu.astype(BF16)
    result = middle + RESIDUAL_SCALE * scatter_square(dot32(units, down_weight), 1)

    own_places = ((blk * hi_n + hi) * lo_n + lo) * tok + jnp.arange(tok)
    valid = own_places < lengths[0]
    misfit = jnp.where(valid[:, None], result - teacher[0].astype(F32), 0.0)
    squares = jnp.broadcast_to(jnp.sum(misfit * misfit), (8, 128))
    grad_result = misfit * (dp_n * seq_len / valid_count)

    branch = gather_square((RESIDUAL_SCALE * grad_result).astype(BF16), 5)
    down_sum = weight_grad_start(units, branch, branch)
    grad_gate_rows, grad_up_rows, grad_normal = ff_back(
        branch, gate_slope, up_slope, gate_weight, up_weight, down_weight, down_sum[0], 2 * tok
    )
    if dp_n == 2:
        down_got = swap_pair(down_sum[1], "dp")
        grad_normal, down_sum, gate_own, up_own, gate_stay, up_stay, gate_got, up_got = scatter_down(
            grad_normal, 9, (down_sum[0], down_got), normed_two, grad_gate_rows, grad_up_rows
        )
        gate_stay, up_stay = swap_pair(gate_stay, "dp"), swap_pair(up_stay, "dp")
    else:
        grad_normal = scatter_square(grad_normal, 9)
        down_sum = scatter_end(scatter_start(down_sum[0], "hi"), "hi")
        gate_own = weight_grad_start(normed_two, grad_gate_rows, grad_normal)[0]
        up_own = weight_grad_start(normed_two, grad_up_rows, grad_normal)[0]
        gate_stay = up_stay = gate_got = up_got = jnp.zeros(gate_own.shape[1:], BF16)
    grad_normal = outer(grad_normal)

    part_shape = (part_rows, ff_part)
    anywhere, inside = pl.BlockSpec(memory_space=pl.ANY), pl.BlockSpec(memory_space=pltpu.VMEM)
    grad_middle, attn_rows, dout, gate_away, up_away = pl.pallas_call(
        functools.partial(out_back_kernel, key_head, to_outer, reblock),
        in_specs=[inside] * 4 + [anywhere] * 5,
        out_specs=[inside] * 2 + [anywhere] + [inside] * 2,
        out_shape=[
            jax.ShapeDtypeStruct((tok, width), F32),
            jax.ShapeDtypeStruct((tok, width), BF16),
            jax.ShapeDtypeStruct((group, tok, q_cols), BF16),
            jax.ShapeDtypeStruct(part_shape, BF16),
            jax.ShapeDtypeStruct(part_shape, BF16),
        ],
        scratch_shapes=[
            pltpu.VMEM(out_weight.shape, BF16),
            pltpu.VMEM((tok, width), F32),
            pltpu.VMEM((group, tok, q_cols), BF16),
        ]
        + sems(7)
        + [
            pltpu.VMEM((2,) + part_shape, F32),
            pltpu.VMEM((2,) + part_shape, BF16),
            pltpu.SemaphoreType.DMA((2, 2)),
            pltpu.SemaphoreType.DMA((1,)),
        ],
        compiler_params=pltpu.CompilerParams(
            collective_id=6, has_side_effects=True, vmem_limit_bytes=VMEM_LIMIT
        ),
        cost_estimate=pl.CostEstimate(
            flops=2 * tok * width * width, bytes_accessed=60_000_000, transcendentals=0
        ),
        name="out_back",
    )(grad_normal, middle, grad_result, gain_two, out_weight, gate_own, gate_got, up_own, up_got)
    columns = (group, rows_w, ff_part)

    gate_dp, up_dp = gate_stay.reshape(columns), up_stay.reshape(columns)
    gate_hi, up_hi = (swap_pair(a, "hi").reshape(columns) for a in (gate_away, up_away))
    square_attn = lax.all_gather(attn_rows, SQUARE, axis=0, tiled=True)
    dout = dout.reshape(blk_n, unit, q_cols)
    dq, dkv = attend_back(scalars, q, kv, other_kv, dout, out_heads, log_heads, gate_away)
    dkv = dkv.reshape(2, group * tok, 2 * k_cols)
    sum_scratch = [pltpu.VMEM(columns, F32)] + [pltpu.VMEM(columns, BF16)] * 3
    sum_scratch.append(pltpu.SemaphoreType.DMA((3,)))
    own_out = dot32(out_heads.reshape(group * tok, q_cols), square_attn, ((0,), (0,))).astype(BF16)
    other_dkv, gate_parts = comm_call(
        dkeys_kernel,
        7,
        [dkv, gate_own.reshape((hi_n,) + columns), gate_dp, gate_hi, up_dp],
        [(dkv.shape[1:], BF16), (columns, BF16)],
        sems(1) + swap_scratch((rows_w, ff_part)) + sum_scratch,
        "dkeys",
    )
    grad_first, head_grads = project_back(
        hi_index,
        dq.reshape(group * tok, q_cols),
        dkv[0],
        other_dkv,
        normed_one,
        qkv_weight,
        tables,
        up_hi,
        unit,
    )
    head_grads = head_grads.reshape(dp_n, every // dp_n, rows_w, head_wide)
    with_out = dp_n == 2 and rows_w * hi_n * lo_n == q_cols
    arrays = [grad_first.reshape(group, tok, width), head_grads]
    arrays += [up_own.reshape((hi_n,) + columns), up_dp, up_hi, squares]
    shapes = [
        ((tok, width), F32),
        (head_grads.shape[1:], BF16),
        (columns, BF16),
        ((every, 8, 128), F32),
    ]
    scratch = scatter_scratch(tok, width) + sems(every // dp_n - 1) + sems(every - 1)
    scratch += [pltpu.SemaphoreType.DMA((2,)), pltpu.VMEM(head_grads.shape[1:], BF16)]
    scratch += [pltpu.VMEM((dp_n - 1,) + head_grads.shape[1:], BF16)]
    scratch += [pltpu.VMEM(head_grads.shape[1:], BF16), pltpu.SemaphoreType.DMA((2, dp_n - 1))]
    scratch += swap_scratch((rows_w, ff_part)) + sum_scratch
    if with_out:
        arrays.append(own_out.reshape(hi_n, lo_n, rows_w, width))
        shapes.append(((hi_n, rows_w, width), BF16))
        scratch += sems(5) + [pltpu.SemaphoreType.DMA((2,))]
        scratch += [pltpu.VMEM((hi_n, lo_n, rows_w, width), BF16)] * 3
    grad_first, head_grads, up_parts, squares, *outs = pl.pallas_call(
        functools.partial(close_kernel, with_out),
        in_specs=[anywhere] * len(arrays),
        out_specs=[pl.BlockSpec(memory_space=pltpu.VMEM)] + [anywhere] * (len(shapes) - 1),
        out_shape=[jax.ShapeDtypeStruct(shape, dtype) for shape, dtype in shapes],
        scratch_shapes=scratch,
        compiler_params=pltpu.CompilerParams(
            collective_id=8, has_side_effects=True, vmem_limit_bytes=VMEM_LIMIT
        ),
        cost_estimate=pl.CostEstimate(flops=0, bytes_accessed=120_000_000, transcendentals=0),
        name="close",
    )(*arrays)
    mse_loss = jnp.sum(squares[:, 0, 0]) / (width * valid_count)
    if with_out and units_w % 128 == 0 and 2 * rows_w == 128:
        shape = lambda *dims: jax.ShapeDtypeStruct(dims, F32)
        grads = pl.pallas_call(
            functools.partial(final_kernel, key_head, ff_places, units_w),
            out_shape=[
                shape(tok, width),
                shape(*w_query.shape),
                shape(*key_projection.shape),
                shape(*value_projection.shape),
                shape(rows_w, 1),
                shape(*w_gate.shape),
                shape(*w_up.shape),
                shape(rows_w, 1),
                shape(*w_out.shape),
                shape(*w_down.shape),
            ],
            compiler_params=params,
            name="final",
        )(
            grad_first,
            grad_middle,
            hidden[0],
            gain_one,
            head_grads,
            w_query,
            key_projection,
            value_projection,
            gate_parts,
            up_parts,
            w_gate,
            w_up,
            small,
            outs[0],
            down_sum,
        )
        return (
            result.astype(BF16)[None],
            mse_loss,
            grads[0][None],
            grads[4][:, 0],
            *grads[1:4],
            grads[8],
            grads[7][:, 0],
            grads[5],
            grads[6],
            grads[9],
        )
    if with_out:
        grad_out = jnp.sum(outs[0].astype(F32), axis=0)
    else:
        own_head = lo * blk_n + blk
        spread = jnp.where((jnp.arange(group) == own_head)[:, None, None], own_out[None], 0)
        grad_out = lax.psum_scatter(
            spread.reshape(width, width), ALL, scatter_dimension=0, tiled=True
        ).astype(F32)
    grad_first = grad_first * gain_one
    normal_one, inverse_one = norm_parts(hidden[0].astype(F32))
    grad_hidden = grad_middle + inverse_one * (
        grad_first - normal_one * jnp.mean(grad_first * normal_one, axis=-1, keepdims=True)
    )
    head_grads = jnp.sum(
        head_grads.reshape(blk_n, hi_n, lo_n, rows_w, head_wide).astype(F32), axis=1
    ).reshape(group, rows_w, head_wide)

    own_one, own_two = attn_gain.astype(F32)[:, None], mlp_gain.astype(F32)[:, None]
    grad_query = head_columns_back(head_grads[:, :, :q_cols])
    grad_key = head_columns_back(head_grads[:, :, q_cols : q_cols + k_cols])
    grad_value = head_columns_back(head_grads[:, :, q_cols + k_cols :])

    def row_sums(*pairs):
        return sum(jnp.sum(w.astype(F32) * g, axis=1, keepdims=True) for w, g in pairs)

    grad_gain_one = (
        row_sums((w_query, grad_query), (key_projection, grad_key), (value_projection, grad_value))
        / own_one
    )
    if units_w % 128 == 0:
        ff_shape = jax.ShapeDtypeStruct(w_gate.shape, F32)
        grad_gate, grad_up, grad_gain_two = pl.pallas_call(
            functools.partial(collect_kernel, ff_places, units_w),
            out_shape=[ff_shape, ff_shape, jax.ShapeDtypeStruct((rows_w, 1), F32)],
            compiler_params=params,
            name="collect",
        )(gate_parts, up_parts, w_gate, w_up, own_two)
    else:
        grad_gate = unit_columns_back(gate_parts.astype(F32))
        grad_up = unit_columns_back(up_parts.astype(F32))
        grad_gain_two = row_sums((w_gate, grad_gate), (w_up, grad_up)) / own_two
    return (
        result.astype(BF16)[None],
        mse_loss,
        grad_hidden[None],
        grad_gain_one[:, 0],
        grad_query,
        grad_key,
        grad_value,
        grad_out,
        grad_gain_two[:, 0],
        grad_gate,
        grad_up,
        down_sum,
    )


def solution(mesh):
    dp_n, blk_n, head_n = (mesh.shape[a] for a in ("dp", "blk", "head"))
    fine = Mesh(mesh.devices.reshape(dp_n, blk_n, 2, head_n // 2), ALL)
    tokens = P("dp", SEQ, None)
    rows, row = P(ALL, None), P(ALL)
    return jax.shard_map(
        shards,
        mesh=fine,
        in_specs=(tokens, tokens, P("dp"), row, rows, rows, rows, rows, row, rows, rows, rows),
        out_specs=(tokens, P(), tokens, row, rows, rows, rows, rows, row, rows, rows, rows),
        check_vma=False,
    )
```

```python
import functools
import math

import jax
import jax.numpy as jnp
import numpy as np
from jax import lax
from jax.experimental import pallas as pl
from jax.experimental.pallas import tpu as pltpu
from jax.sharding import Mesh, PartitionSpec as P

MODEL_WIDTH = 2048
HEAD_SIZE = 64
ROPE_BASE = 10000000.0
NORM_EPS = 1e-05
ATTN_SCALE = 0.015625
RESIDUAL_SCALE = 0.22
MASKED = -1e30

ALL = ("dp", "blk", "hi", "lo")
SQUARE = ("blk", "lo")
COPIES = ("dp", "hi")
SEQ = ("blk", "hi", "lo")
F32 = jnp.float32
BF16 = jnp.bfloat16
VMEM_LIMIT = 56 * 1024 * 1024


def dot32(a, b, dims=((1,), (0,))):
    return lax.dot_general(a, b, (dims, ((), ())), preferred_element_type=F32)


def rope_tables(seq_len):
    half = HEAD_SIZE // 2
    frequency = ROPE_BASE ** (-(np.arange(half) * 2.0) / HEAD_SIZE)
    angles = np.arange(seq_len).astype(np.float32)[:, None] * frequency.astype(np.float32)[None, :]
    cosine, sine = np.cos(angles.astype(np.float64)), np.sin(angles.astype(np.float64))
    none = np.zeros_like(cosine)
    rows = ([cosine] * 4, [-sine, none] * 2, [none, sine] * 2)
    return tuple(np.concatenate(row, axis=1).astype(np.float32) for row in rows)


def table_spec(tok):
    return pl.BlockSpec((tok, 128), lambda i, hi: ((i // 2 * 2 + hi[0]) * 2 + i % 2, 0))


def proj_kernel(hi_ref, rows_ref, gain_ref, weight_ref, cos_ref, sina_ref, sinb_ref, normed_ref, q_ref, kv_ref):
    normed_ref[...] = (norm_parts(rows_ref[...].astype(F32))[0] * gain_ref[...]).astype(BF16)
    made = dot32(normed_ref[...], weight_ref[...])
    cosine, sina, sinb = cos_ref[...], sina_ref[...], sinb_ref[...]
    low = lanes_low(cosine.shape)
    half = HEAD_SIZE // 2
    for part in range(3):
        u = made[:, 128 * part : 128 * part + 128]
        up, down = pltpu.roll(u, 128 - half, 1), pltpu.roll(u, half, 1)
        turned = u * cosine + up * sina + down * sinb
        if part < 2:
            q_ref[:, 128 * part : 128 * part + 128] = (
                turned.astype(BF16).astype(F32) * ATTN_SCALE
            ).astype(BF16)
        else:
            kv_ref[...] = jnp.where(low, turned, u).astype(BF16)


def project(hi, rows, gain, weight, tables, tile):
    count, depth = rows.shape
    wide = weight.shape[1]
    by_rows = lambda cols: pl.BlockSpec((tile, cols), lambda i, hi: (i, 0))
    whole = lambda *shape: pl.BlockSpec(shape, lambda i, hi: (0, 0))
    return pl.pallas_call(
        proj_kernel,
        grid_spec=pltpu.PrefetchScalarGridSpec(
            num_scalar_prefetch=1,
            grid=(count // tile,),
            in_specs=[by_rows(depth), whole(1, depth), whole(depth, wide)] + [table_spec(tile)] * 3,
            out_specs=[by_rows(depth), by_rows(256), by_rows(128)],
        ),
        out_shape=[
            jax.ShapeDtypeStruct((count, depth), BF16),
            jax.ShapeDtypeStruct((count, 256), BF16),
            jax.ShapeDtypeStruct((count, 128), BF16),
        ],
        compiler_params=pltpu.CompilerParams(vmem_limit_bytes=VMEM_LIMIT),
        cost_estimate=pl.CostEstimate(
            flops=2 * count * depth * wide, bytes_accessed=4 * count * depth, transcendentals=0
        ),
        name="project",
    )(hi, rows, gain, weight, *tables)


def proj_back_kernel(
    hi_ref, dq_ref, own_ref, other_ref, rows_ref, weight_ref, cos_ref, sina_ref, sinb_ref, first_ref, drows_ref,
    dweight_ref, made, total,
):
    i = pl.program_id(0)
    cosine, sina, sinb = cos_ref[...], sina_ref[...], sinb_ref[...]
    low = lanes_low(cosine.shape)
    half = HEAD_SIZE // 2
    shared = (own_ref[...].astype(F32) + other_ref[...].astype(F32)).astype(BF16)
    for part in range(3):
        w = (dq_ref[:, 128 * part : 128 * part + 128] if part < 2 else shared).astype(F32)
        turned = w * cosine + pltpu.roll(w * sinb, 128 - half, 1) + pltpu.roll(w * sina, half, 1)
        if part == 2:
            turned = jnp.where(low, turned, w)
        made[:, 128 * part : 128 * part + 128] = turned.astype(BF16)
    drows_ref[...] = dot32(made[...], weight_ref[...], ((1,), (1,))).astype(BF16)
    dweight = dot32(rows_ref[...], made[...], ((0,), (0,)))

    @pl.when(i == 0)
    def _():
        total[...] = dweight

    @pl.when(i > 0)
    def _():
        total[...] += dweight

    @pl.when(i == pl.num_programs(0) - 1)
    def _():
        dweight_ref[...] = total[...].astype(BF16)


def project_back(hi, dq, own, other, rows, weight, tables, first, unit):
    count, width = rows.shape
    wide = weight.shape[1]
    by_rows = lambda cols: pl.BlockSpec((unit, cols), lambda i, hi: (i, 0))
    whole = pl.BlockSpec((width, wide), lambda i, hi: (0, 0))
    table = pl.BlockSpec((unit, 128), lambda i, hi: (2 * i + hi[0], 0))
    return pl.pallas_call(
        proj_back_kernel,
        grid_spec=pltpu.PrefetchScalarGridSpec(
            num_scalar_prefetch=1,
            grid=(count // unit,),
            in_specs=[by_rows(256), by_rows(128), by_rows(128), by_rows(width), whole]
            + [table] * 3
            + [pl.BlockSpec(memory_space=pl.ANY)],
            out_specs=[by_rows(width), whole],
            scratch_shapes=[pltpu.VMEM((unit, wide), BF16), pltpu.VMEM((width, wide), F32)],
        ),
        out_shape=[
            jax.ShapeDtypeStruct((count, width), BF16),
            jax.ShapeDtypeStruct((width, wide), BF16),
        ],
        compiler_params=pltpu.CompilerParams(vmem_limit_bytes=VMEM_LIMIT),
        cost_estimate=pl.CostEstimate(
            flops=4 * count * width * wide, bytes_accessed=24_000_000, transcendentals=0
        ),
        name="project_back",
    )(hi, dq, own, other, rows, weight, *tables, first)


def lanes_low(shape):
    return lax.broadcasted_iota(jnp.int32, shape, 1) < HEAD_SIZE


def both_keys(kv):
    low = lanes_low(kv.shape)
    keys = kv.astype(F32)
    return (
        jnp.where(low, keys, 0.0).astype(BF16),
        jnp.where(low, 0.0, pltpu.roll(keys, HEAD_SIZE, 1)).astype(BF16),
    )


def both_values(kv):
    low = lanes_low(kv.shape)
    values = kv.astype(F32)
    return (
        jnp.where(low, pltpu.roll(values, HEAD_SIZE, 1), 0.0).astype(BF16),
        jnp.where(low, 0.0, values).astype(BF16),
    )


def attend_kernel(scalar_ref, q_ref, kv_ref, other_ref, out_ref, log_ref, keys, values, peak, sums):
    b = pl.program_id(0)
    blocks, unit, _ = q_ref.shape
    units = 2 * blocks
    length, hi = scalar_ref[0], scalar_ref[1]
    n = 2 * b + hi

    @pl.when(b == 0)
    def _():
        def spread(c, carry):
            for j, kv in (
                (2 * c + hi, kv_ref[c]),
                (2 * c + 1 - hi, other_ref[c]),
            ):
                keys[0, j], keys[1, j] = both_keys(kv)
                across = jnp.transpose(kv.astype(F32))[HEAD_SIZE:, :]
                values[j] = jnp.concatenate(
                    [across, jnp.ones((16, unit), F32)], axis=0
                ).astype(BF16)
            return carry

        lax.fori_loop(0, blocks, spread, 0)

    peak[...] = jnp.full_like(peak, MASKED)
    sums[...] = jnp.zeros_like(sums)

    def step(j, masked):
        for h in range(4):
            query = q_ref[b, :, 128 * (h // 2) : 128 * (h // 2) + 128]
            scores = dot32(keys[h % 2, j], query, ((1,), (1,)))
            if masked:
                row = j * unit + lax.broadcasted_iota(jnp.int32, scores.shape, 0)
                col = n * unit + lax.broadcasted_iota(jnp.int32, scores.shape, 1)
                scores = jnp.where((row <= col) & (row < length), scores, MASKED)
            old = peak[h, 0:1, :]
            new = jnp.maximum(old, jnp.max(scores, axis=0, keepdims=True))
            weights = jnp.exp(scores - new).astype(BF16)
            sums[h] = sums[h] * jnp.exp(old - new) + dot32(values[j], weights)
            peak[h, 0:1, :] = new

    first_ragged = units - units // 4

    def plain(j, carry):
        step(j, False)
        return carry

    def checked(j, carry):
        step(j, True)
        return carry

    lax.fori_loop(0, jnp.minimum(n, first_ragged), plain, 0)
    lax.fori_loop(jnp.minimum(n, first_ragged), n + 1, checked, 0)

    for pair in range(2):
        parts = []
        for h in (2 * pair, 2 * pair + 1):
            total = sums[h, HEAD_SIZE : HEAD_SIZE + 1, :]
            parts.append(sums[h, 0:HEAD_SIZE, :] / total)
            log_ref[0, h : h + 1, :] = peak[h, 0:1, :] + jnp.log(total)
        out_ref[0, :, 128 * pair : 128 * pair + 128] = jnp.transpose(
            jnp.concatenate(parts, axis=0)
        ).astype(BF16)


def attend(scalars, q, kv, other):
    blocks, unit, _ = q.shape
    units = 2 * blocks
    whole = lambda a: pl.BlockSpec(a.shape, lambda i: (0,) * a.ndim)
    return pl.pallas_call(
        attend_kernel,
        grid=(blocks,),
        in_specs=[pl.BlockSpec(memory_space=pltpu.SMEM), whole(q), whole(kv), whole(other)],
        out_specs=[
            pl.BlockSpec((1, unit, 256), lambda i: (i, 0, 0)),
            pl.BlockSpec((1, 8, unit), lambda i: (i, 0, 0)),
        ],
        out_shape=[
            jax.ShapeDtypeStruct((blocks, unit, 256), BF16),
            jax.ShapeDtypeStruct((blocks, 8, unit), F32),
        ],
        scratch_shapes=[
            pltpu.VMEM((2, units, unit, 128), BF16),
            pltpu.VMEM((units, HEAD_SIZE + 16, unit), BF16),
            pltpu.VMEM((4, 8, unit), F32),
            pltpu.VMEM((4, HEAD_SIZE + 16, unit), F32),
        ],
        compiler_params=pltpu.CompilerParams(vmem_limit_bytes=VMEM_LIMIT),
        cost_estimate=pl.CostEstimate(
            flops=40_000_000_000, bytes_accessed=8_000_000, transcendentals=20_000_000
        ),
        name="attend",
    )(scalars, q, kv, other)


def attend_back_kernel(
    scalar_ref,
    q_ref,
    kv_ref,
    other_ref,
    dout_ref,
    out_ref,
    log_ref,
    first_ref,
    dq_ref,
    dkv_ref,
    delta,
    dq,
    dk,
    dv,
):
    j = pl.program_id(0)
    blocks, unit, _ = q_ref.shape
    units = 2 * blocks
    length, hi = scalar_ref[0], scalar_ref[1]

    @pl.when(j == 0)
    def _():
        dq[...] = jnp.zeros_like(dq)
        pick = jnp.where(
            lax.broadcasted_iota(jnp.int32, (8, 256), 0)
            == lax.broadcasted_iota(jnp.int32, (8, 256), 1) // HEAD_SIZE,
            1.0,
            0.0,
        )

        def dots(b, carry):
            product = dout_ref[b].astype(F32) * out_ref[b].astype(F32)
            delta[b] = lax.dot_general(
                pick,
                product,
                (((1,), (1,)), ((), ())),
                precision=lax.Precision.HIGHEST,
                preferred_element_type=F32,
            )
            return carry

        lax.fori_loop(0, blocks, dots, 0)

    foreign = jnp.where(j % 2 == hi, 0, 1)
    kv = jnp.where(foreign == 0, kv_ref[j // 2], other_ref[j // 2])
    keys, values = both_keys(kv), both_values(kv)
    dk[...] = jnp.zeros_like(dk)
    dv[...] = jnp.zeros_like(dv)

    def step(b, masked):
        n = 2 * b + hi
        for pair in range(2):
            lanes = slice(128 * pair, 128 * pair + 128)
            query = q_ref[b, :, lanes]
            dout = dout_ref[b, :, lanes]
            dq_part = None
            for side in range(2):
                h = 2 * pair + side
                scores = dot32(keys[side], query, ((1,), (1,)))
                weights = jnp.exp(scores - log_ref[b, h : h + 1, :])
                if masked:
                    row = j * unit + lax.broadcasted_iota(jnp.int32, scores.shape, 0)
                    col = n * unit + lax.broadcasted_iota(jnp.int32, scores.shape, 1)
                    weights = jnp.where((row <= col) & (row < length), weights, 0.0)
                dweights = dot32(values[side], dout, ((1,), (1,)))
                dscores = (weights * (dweights - delta[b, h : h + 1, :])).astype(BF16)
                dv[side] += dot32(weights.astype(BF16), dout)
                dk[side] += dot32(dscores, query)
                part = dot32(dscores, keys[side], ((0,), (0,)))
                dq_part = part if dq_part is None else dq_part + part
            dq[b, :, lanes] += dq_part

    first_ragged = units - units // 4

    def plain(b, carry):
        step(b, False)
        return carry

    def checked(b, carry):
        step(b, True)
        return carry

    first = (j + 1 - hi) // 2
    masked_until = jnp.where(j >= first_ragged, blocks, jnp.where(foreign == 0, first + 1, first))
    lax.fori_loop(first, masked_until, checked, 0)
    lax.fori_loop(masked_until, blocks, plain, 0)

    low = lanes_low((unit, 128))
    dkey = dk[0] + pltpu.roll(dk[1], HEAD_SIZE, 1)
    dvalue = pltpu.roll(dv[0], HEAD_SIZE, 1) + dv[1]
    dkv_ref[foreign, j // 2] = jnp.where(low, dkey, dvalue).astype(BF16)

    @pl.when(j == units - 1)
    def _():
        def store(b, carry):
            dq_ref[b] = (dq[b] * ATTN_SCALE).astype(BF16)
            return carry

        lax.fori_loop(0, blocks, store, 0)


def attend_back(scalars, q, kv, other, dout, out, log, first):
    blocks, unit, _ = q.shape
    units = 2 * blocks
    whole = lambda a: pl.BlockSpec(a.shape, lambda i: (0,) * a.ndim)
    dq_shape = jax.ShapeDtypeStruct((blocks, unit, 256), BF16)
    dkv_shape = jax.ShapeDtypeStruct((2, blocks, unit, 128), BF16)
    return pl.pallas_call(
        attend_back_kernel,
        grid=(units,),
        in_specs=[
            pl.BlockSpec(memory_space=pltpu.SMEM),
            whole(q),
            whole(kv),
            whole(other),
            whole(dout),
            whole(out),
            whole(log),
            pl.BlockSpec(memory_space=pl.ANY),
        ],
        out_specs=[whole(dq_shape), whole(dkv_shape)],
        out_shape=[dq_shape, dkv_shape],
        scratch_shapes=[
            pltpu.VMEM((blocks, 8, unit), F32),
            pltpu.VMEM((blocks, unit, 256), F32),
            pltpu.VMEM((2, unit, 128), F32),
            pltpu.VMEM((2, unit, 128), F32),
        ],
        compiler_params=pltpu.CompilerParams(vmem_limit_bytes=VMEM_LIMIT),
        cost_estimate=pl.CostEstimate(
            flops=60_000_000_000, bytes_accessed=10_000_000, transcendentals=20_000_000
        ),
        name="attend_back",
    )(scalars, q, kv, other, dout, out, log, first)


PIECES = 4
MESH_ID = pl.DeviceIdType.MESH


def square_places():
    blk, lo = lax.axis_index("blk"), lax.axis_index("lo")
    mate, side = blk + 1 - 2 * (blk % 2), (blk + 2) % 4
    return blk, lo, mate, side


def greet(ids):
    barrier = pltpu.get_barrier_semaphore()
    for one in ids:
        pl.semaphore_signal(barrier, inc=1, device_id=one, device_id_type=MESH_ID)
    pl.semaphore_wait(barrier, len(ids))


def remote(source, target, send, recv, to):
    copy = pltpu.make_async_remote_copy(
        src_ref=source,
        dst_ref=target,
        send_sem=send,
        recv_sem=recv,
        device_id=to,
        device_id_type=MESH_ID,
    )
    copy.start()
    return copy


def local_copy(source, target, sem):
    copy = pltpu.make_async_copy(source, target, sem)
    copy.start()
    return copy


class Carried:
    def __init__(self, source, target, held, sem):
        self.held, self.target, self.sem = held, target, sem
        self.copy = local_copy(source, held, sem)

    def turn(self):
        self.copy.wait()
        self.copy = local_copy(self.held, self.target, self.sem)

    def wait(self):
        self.copy.wait()


def finish(copies):
    for copy in copies:
        if isinstance(copy, Carried):
            copy.turn()
    for copy in copies:
        copy.wait()


def square_peers():
    blk, lo = lax.axis_index("blk"), lax.axis_index("lo")
    mine = blk * 2 + lo
    others = [lax.rem(mine + d, 8) for d in range(1, 8)]
    return mine, others, [{"blk": o // 2, "lo": lax.rem(o, 2)} for o in others]


def other_hi():
    return {"hi": 1 - lax.axis_index("hi")}


def dp_peers():
    dp, dp_n = lax.axis_index("dp"), lax.axis_size("dp")
    return [{"dp": lax.rem(dp + d, dp_n)} for d in range(1, dp_n)]


def every_peer():
    sizes = [lax.axis_size(a) for a in ALL]
    places = [lax.axis_index(a) for a in ALL]
    found = []
    for k in range(1, math.prod(sizes)):
        to, rest = {}, k
        for a, size, place in reversed(list(zip(ALL, sizes, places))):
            to[a] = lax.rem(place + rest % size, size)
            rest //= size
        found.append(to)
    return found


def gather_begin(rows_ref, out_ref, send, recv, local, held):
    blk, lo, mate, side = square_places()
    slot = lambda b, l: b * 2 + l
    mine = slot(blk, lo)
    to_mate, to_side, to_next = {"blk": mate}, {"blk": side}, {"lo": 1 - lo}
    step = rows_ref.shape[0] // PIECES

    def push(source, place, piece, kind, to):
        target = out_ref.at[place, pl.ds(piece * step, step)]
        return remote(source, target, send.at[kind, piece], recv.at[kind, piece], to)

    own = Carried(rows_ref, out_ref.at[mine], held, local)
    piece_of = lambda p: rows_ref.at[pl.ds(p * step, step)]
    came = lambda place, p: out_ref.at[place, pl.ds(p * step, step)]
    side_order, next_order = (2, 3, 0, 1), (0, 1, 2, 3)
    by_side, by_next, by_mate, across = {}, {}, [], {}
    for k in range(PIECES):
        p, q = side_order[k], next_order[k]
        by_side[p] = push(piece_of(p), mine, p, 0, to_side)
        by_next[q] = push(piece_of(q), mine, q, 1, to_next)
    for p in range(PIECES):
        by_mate.append(push(piece_of(p), mine, p, 3, to_mate))

    def end(between=lambda k: None):
        own.turn()
        from_side, from_next, from_across = slot(side, lo), slot(blk, 1 - lo), slot(side, 1 - lo)
        for k in range(PIECES):
            p, q = side_order[k], next_order[k]
            by_side[p].wait_recv()
            if p >= 2:
                across[p] = push(came(from_side, p), from_side, p, 2, to_next)
            by_mate.append(push(came(from_side, p), from_side, p, 4, to_mate))
            by_next[q].wait_recv()
            if q < 2:
                across[q] = push(came(from_next, q), from_next, q, 2, to_side)
            by_mate.append(push(came(from_next, q), from_next, q, 5, to_mate))
            between(k)
        for p in (0, 2, 1, 3):
            across[p].wait_recv()
            by_mate.append(push(came(from_across, p), from_across, p, 6, to_mate))
            between(PIECES + p)
        for copy in by_mate:
            copy.wait()
        for copies in (by_side, by_next, across):
            for copy in copies.values():
                copy.wait_send()
        own.wait()

    return end


def gather_scratch(tok, width):
    return [
        pltpu.SemaphoreType.DMA((7, PIECES)),
        pltpu.SemaphoreType.DMA((7, PIECES)),
        pltpu.SemaphoreType.DMA,
        pltpu.VMEM((tok, width), BF16),
    ]


def sems(count):
    return [pltpu.SemaphoreType.DMA((count,))] * 2


def swap_scratch(part):
    return sems(7) + [pltpu.SemaphoreType.DMA, pltpu.VMEM(part, BF16)]


def square_greeting():
    blk, lo, mate, side = square_places()
    return [{"blk": mate}, {"blk": side}, {"lo": 1 - lo}]


def gather_kernel(rows_ref, out_ref, send, recv, local, held):
    greet(square_greeting())
    gather_begin(rows_ref, out_ref, send, recv, local, held)()


def comm_call(kernel, number, arrays, shapes, scratch, name):
    anywhere = pl.BlockSpec(memory_space=pl.ANY)
    return pl.pallas_call(
        kernel,
        in_specs=[anywhere] * len(arrays),
        out_specs=[anywhere] * len(shapes),
        out_shape=[jax.ShapeDtypeStruct(shape, dtype) for shape, dtype in shapes],
        scratch_shapes=scratch,
        compiler_params=pltpu.CompilerParams(
            collective_id=number, has_side_effects=True, vmem_limit_bytes=VMEM_LIMIT
        ),
        cost_estimate=pl.CostEstimate(flops=0, bytes_accessed=120_000_000, transcendentals=0),
        name=name,
    )(*arrays)


def gather_square(rows, number):
    tok, width = rows.shape
    (out,) = comm_call(
        gather_kernel,
        number,
        [rows],
        [((8, tok, width), rows.dtype)],
        gather_scratch(tok, width),
        "gather_square",
    )
    return out.reshape(8 * tok, width)


def swap_begin(parts_ref, out_ref, send, recv, local, held):
    mine, others, ids = square_peers()
    own = Carried(parts_ref.at[mine], out_ref.at[mine], held, local)
    copies = [
        remote(parts_ref.at[o], out_ref.at[mine], send.at[d], recv.at[d], to)
        for d, (o, to) in enumerate(zip(others, ids))
    ]
    return copies + [own]


def dp_begin(pieces, out_ref, send, recv, local, held, first=0):
    dp = lax.axis_index("dp")
    copies = []
    for k, (place, ref) in enumerate(pieces, first):
        copies.append(Carried(ref, out_ref.at[dp, place], held.at[k], local.at[k]))
        for d, to in enumerate(dp_peers()):
            n = 2 * d + k
            copies.append(remote(ref, out_ref.at[dp, place], send.at[n], recv.at[n], to))
    return copies


def device_place():
    mine = 0
    for a in ALL:
        mine = mine * lax.axis_size(a) + lax.axis_index(a)
    return mine


def seq_peers():
    sizes = [lax.axis_size(a) for a in SEQ]
    places = [lax.axis_index(a) for a in SEQ]
    found = []
    for k in range(1, math.prod(sizes)):
        to, source, digits, rest = {}, 0, [], k
        for size in reversed(sizes):
            digits.append(rest % size)
            rest //= size
        for a, size, place, digit in zip(SEQ, sizes, places, reversed(digits)):
            to[a] = lax.rem(place + digit, size)
            source = source * size + lax.rem(place + size - digit, size)
        found.append((to, source))
    return found


def seq_place(to):
    place = 0
    for a in SEQ:
        place = place * lax.axis_size(a) + to[a]
    return place


def open_kernel(
    rows_ref, heads_ref, small_ref, wout_ref, out_ref, weight_ref, smalls_ref, wouts_ref, g_send, g_recv,
    g_local, g_held, w_send, w_recv, d_send, d_recv, s_send, s_recv, o_send, o_recv, local, w_held, o_held,
):
    blk, hi, lo = (lax.axis_index(a) for a in SEQ)
    mine = device_place()
    peers = every_peer()
    greet(peers)
    copies = [
        Carried(heads_ref.at[blk * 2 + lo], weight_ref.at[mine], w_held, local.at[0]),
        local_copy(small_ref, smalls_ref.at[mine], local.at[1]),
        Carried(wout_ref, wouts_ref.at[hi, lo], o_held, local.at[2]),
    ]
    for k, to in enumerate(peers):
        copies.append(remote(small_ref, smalls_ref.at[mine], s_send.at[k], s_recv.at[k], to))
    end = gather_begin(rows_ref, out_ref, g_send, g_recv, g_local, g_held)
    wout = remote(wout_ref, wouts_ref.at[hi, lo], o_send.at[0], o_recv.at[0], other_hi())
    next_lo = {"lo": 1 - lo}
    copies.append(remote(wout_ref, wouts_ref.at[hi, lo], o_send.at[1], o_recv.at[1], next_lo))
    dp, seq = lax.axis_index("dp"), seq_peers()
    seq_n = len(seq) + 1
    straight = []
    for k, (to, source) in enumerate(seq):
        part = heads_ref.at[to["blk"] * 2 + to["lo"]]
        straight.append(remote(part, weight_ref.at[mine], w_send.at[k], w_recv.at[k], to))

    def hand_on(part, place, k):
        for d, to in enumerate(dp_peers()):
            n = d * seq_n + k
            copies.append(remote(part, weight_ref.at[place], d_send.at[n], d_recv.at[n], to))

    hand_on(heads_ref.at[blk * 2 + lo], mine, seq_n - 1)

    def pass_on(turn):
        for k, (to, source) in enumerate(seq):
            if k * 2 * PIECES // len(seq) == turn:
                straight[k].wait()
                place = dp * seq_n + source
                hand_on(weight_ref.at[place], place, k)

    end(pass_on)
    wout.wait()
    there = wouts_ref.at[1 - hi, lo]
    copies.append(remote(there, there, o_send.at[2], o_recv.at[2], next_lo))
    finish(copies)


def keys_kernel(
    kv_ref, gate_ref, up_ref, down_ref, other_ref, gates_ref, ups_ref, downs_ref, k_send, k_recv, g_send,
    g_recv, g_local, g_held, u_send, u_recv, u_local, u_held, d_send, d_recv,
):
    greet(square_peers()[2] + [other_hi()] + dp_peers())
    copies = [remote(kv_ref, other_ref, k_send.at[0], k_recv.at[0], other_hi())]
    for d, to in enumerate(dp_peers()):
        copies.append(remote(down_ref, downs_ref.at[d], d_send.at[d], d_recv.at[d], to))
    copies += swap_begin(gate_ref, gates_ref, g_send, g_recv, g_local, g_held)
    copies += swap_begin(up_ref, ups_ref, u_send, u_recv, u_local, u_held)
    finish(copies)


def heads_kernel(
    heads_ref, gate_ref, gate_other_ref, up_ref, mixed_ref, gates_ref, up_other_ref, m_send, m_recv,
    m_local, m_held, g_send, g_recv, u_send, u_recv, g_local, g_held,
):
    hi = lax.axis_index("hi")
    greet(square_peers()[2] + [other_hi()] + dp_peers())
    copies = swap_begin(heads_ref, mixed_ref, m_send, m_recv, m_local, m_held)
    copies.append(remote(up_ref, up_other_ref, u_send.at[0], u_recv.at[0], other_hi()))
    copies += dp_begin(
        [(hi, gate_ref), (1 - hi, gate_other_ref)], gates_ref, g_send, g_recv, g_local, g_held
    )
    finish(copies)


def rows_kernel(
    rows_ref, up_ref, up_other_ref, down_ref, out_ref, ups_ref, down_other_ref, r_send, r_recv, r_local,
    r_held, u_send, u_recv, d_send, d_recv, u_local, u_held,
):
    hi = lax.axis_index("hi")
    greet(square_greeting() + [other_hi()] + dp_peers())
    end = gather_begin(rows_ref, out_ref, r_send, r_recv, r_local, r_held)
    copies = [remote(down_ref, down_other_ref, d_send.at[0], d_recv.at[0], other_hi())]
    copies += dp_begin(
        [(hi, up_ref), (1 - hi, up_other_ref)], ups_ref, u_send, u_recv, u_local, u_held
    )
    end()
    finish(copies)


def sum_begin(own_ref, got_ref, place, own, got, sem):
    return [
        local_copy(own_ref.at[place], own, sem.at[0]),
        local_copy(got_ref.at[place], got, sem.at[1]),
    ]


def wait_all(copies):
    for copy in copies:
        copy.wait()


def out_back_kernel(
    order, pairs, block, grad_ref, middle_ref, result_ref, gain_ref, weight_ref, gate_ref, gate_got_ref, up_ref,
    up_got_ref, sum_ref, rows_ref, out_ref, gate_away_ref, up_away_ref, weight, work, parts, send, recv, own, got, sem,
    w_sem,
):
    hi = lax.axis_index("hi")
    load = local_copy(weight_ref, weight, w_sem.at[0])
    loads = [
        [local_copy(ref.at[1 - hi], own.at[k], sem.at[k, 0]), local_copy(got_ref, got.at[k], sem.at[k, 1])]
        for k, (ref, got_ref) in enumerate(((gate_ref, gate_got_ref), (up_ref, up_got_ref)))
    ]
    mine, others, ids = square_peers()
    greet(ids)
    reorder(pairs, block, grad_ref, work, lambda v: v)
    normal, inverse = norm_parts(middle_ref[...])
    grad = work[...] * gain_ref[...]
    total = result_ref[...] + inverse * (
        grad - normal * jnp.mean(grad * normal, axis=-1, keepdims=True)
    )
    sum_ref[...] = total
    rows_ref[...] = (RESIDUAL_SCALE * total).astype(BF16)
    load.wait()
    cols = parts.shape[2]

    def make(n, f):
        part = weight[pl.ds(pl.multiple_of(order(f) * cols, cols), cols), :]
        parts[n] = dot32(rows_ref[...], part, ((1,), (1,))).astype(BF16)

    copies = []
    for d, (other, to) in enumerate(zip(others, ids)):
        make(d, other)
        copies.append(remote(parts.at[d], out_ref.at[mine], send.at[d], recv.at[d], to))
    make(7, mine)
    copies.append(local_copy(parts.at[7], out_ref.at[mine], w_sem.at[0]))
    for k, target in enumerate((gate_away_ref, up_away_ref)):
        wait_all(loads[k])
        target[...] = (own[k] + got[k].astype(F32)).astype(BF16)
    wait_all(copies)


def sum_three(place, own_ref, over_dp_ref, over_hi_ref, own, over_dp, over_hi, sem):
    return [
        local_copy(own_ref.at[place], own, sem.at[0]),
        local_copy(over_dp_ref, over_dp, sem.at[1]),
        local_copy(over_hi_ref, over_hi, sem.at[2]),
    ]


def dkeys_kernel(
    dkv_ref, gate_ref, gate_dp_ref, gate_hi_ref, first_ref, other_ref, gates_ref, k_send, k_recv, g_send, g_recv, g_local,
    g_held, own, over_dp, over_hi, made, sem,
):
    hi = lax.axis_index("hi")
    loads = sum_three(hi, gate_ref, gate_dp_ref, gate_hi_ref, own, over_dp, over_hi, sem)
    greet(square_peers()[2] + [other_hi()])
    copies = [remote(dkv_ref.at[1], other_ref, k_send.at[0], k_recv.at[0], other_hi())]
    wait_all(loads)
    made[...] = (own[...] + over_dp[...].astype(F32) + over_hi[...].astype(F32)).astype(BF16)
    copies += swap_begin(made, gates_ref, g_send, g_recv, g_local, g_held)
    finish(copies)


class OwnOut:
    def __init__(self, out_ref, outs_ref, send, recv, local, own, got, made):
        self.outs_ref, self.made, self.send, self.recv, self.local = outs_ref, made, send, recv, local
        self.own, self.got = own, got
        self.dp, self.hi, self.lo = (lax.axis_index(a) for a in ("dp", "hi", "lo"))
        self.load = local_copy(out_ref, own, local.at[0])
        self.over = remote(out_ref, got, send.at[0], recv.at[0], dp_peers()[0])

    def push(self, a, b):
        hi, lo = lax.rem(self.hi + a, 2), lax.rem(self.lo + b, 2)
        return pltpu.make_async_remote_copy(
            src_ref=self.made.at[hi, lo],
            dst_ref=self.outs_ref.at[self.hi],
            send_sem=self.send.at[1 + 2 * a + b],
            recv_sem=self.recv.at[1 + self.hi],
            device_id={"hi": hi, "lo": lo},
            device_id_type=MESH_ID,
        )

    def own_copy(self):
        return pltpu.make_async_copy(
            self.made.at[self.hi, self.lo], self.outs_ref.at[self.hi], self.local.at[1]
        )

    def turn(self):
        self.load.wait()
        self.over.wait()
        self.made[...] = (self.own[...].astype(F32) + self.got[...].astype(F32)).astype(BF16)

        @pl.when(self.dp == self.lo)
        def _():
            for a, b in ((0, 1), (1, 0), (1, 1)):
                self.push(a, b).start()
            self.own_copy().start()

    def wait(self):
        @pl.when(self.dp == self.lo)
        def _():
            for a, b in ((0, 1), (1, 0), (1, 1)):
                self.push(a, b).wait_send()
            self.own_copy().wait()

        for h in range(2):

            @pl.when(jnp.logical_not((h == self.hi) & (self.dp == self.lo)))
            def _(h=h):
                pltpu.make_async_remote_copy(
                    src_ref=self.made.at[0, 0],
                    dst_ref=self.outs_ref.at[h],
                    send_sem=self.send.at[1],
                    recv_sem=self.recv.at[1 + h],
                    device_id={"lo": 1 - self.lo},
                    device_id_type=MESH_ID,
                ).wait_recv()


def close_kernel(with_out, *refs):
    refs = iter(refs)
    take = lambda n: [next(refs) for _ in range(n)]
    parts_ref, heads_ref, up_ref, up_dp_ref, up_hi_ref, square_ref = take(6)
    out_rows_ref = next(refs) if with_out else None
    total_ref, head_ref, ups_ref, squares_ref = take(4)
    outs_ref = next(refs) if with_out else None
    scatter = take(9)
    h_send, h_recv, s_send, s_recv, local, h_own, h_got, h_made, h_sem = take(9)
    swap = take(4)
    own, over_dp, over_hi, made, sem = take(5)
    out_scratch = take(6) if with_out else None
    mine = device_place()
    peers, seq = every_peer(), seq_peers()
    place = seq_place({a: lax.axis_index(a) for a in SEQ})
    loads = scatter_load(parts_ref, scatter)
    hi = lax.axis_index("hi")
    up_loads = sum_three(hi, up_ref, up_dp_ref, up_hi_ref, own, over_dp, over_hi, sem)
    greet(peers)
    copies = [local_copy(square_ref, squares_ref.at[mine], local.at[1])]
    dp = lax.axis_index("dp")
    own_heads = local_copy(heads_ref.at[dp], h_own, local.at[0])
    over_heads = []
    for d, to in enumerate(dp_peers()):
        part = heads_ref.at[to["dp"]]
        over_heads.append(remote(part, h_got.at[d], h_sem.at[0, d], h_sem.at[1, d], to))
    mates = scatter_mates(parts_ref, scatter)
    for k, to in enumerate(peers):
        copies.append(remote(square_ref, squares_ref.at[mine], s_send.at[k], s_recv.at[k], to))

    def send_heads():
        own_heads.wait()
        wait_all(over_heads)
        total = h_own[...].astype(F32)
        for d in range(len(over_heads)):
            total = total + h_got[d].astype(F32)
        h_made[...] = total.astype(BF16)
        copies.append(local_copy(h_made.at[place], head_ref.at[place], local.at[0]))
        for k, (to, source) in enumerate(seq):
            part = h_made.at[seq_place(to)]
            copies.append(remote(part, head_ref.at[place], h_send.at[k], h_recv.at[k], to))

    own_out = OwnOut(out_rows_ref, outs_ref, *out_scratch) if with_out else None
    wait_all(up_loads)
    made[...] = (own[...] + over_dp[...].astype(F32) + over_hi[...].astype(F32)).astype(BF16)
    copies += swap_begin(made, ups_ref, *swap)
    nothing = lambda: None
    work = [nothing, send_heads, nothing, nothing, own_out.turn if with_out else nothing]
    scatter_end_square(loads, mates, total_ref, scatter, work)
    finish(copies)
    if with_out:
        own_out.wait()


def remote_to(source, target, sems_of, kind, piece, to):
    send, recv = sems_of
    return remote(source, target, send.at[kind, piece], recv.at[kind, piece], to)


def scatter_load(parts_ref, scratch):
    mine, local = scratch[0], scratch[8]
    blk, lo, mate, side = square_places()
    places = (side * 2 + 1 - lo, side * 2 + lo, blk * 2 + 1 - lo, blk * 2 + lo)
    return [local_copy(parts_ref.at[p], mine.at[k], local.at[k]) for k, p in enumerate(places)]


def scatter_mates(parts_ref, scratch):
    mates, sems_of = scratch[1], scratch[6:8]
    blk, lo, mate, side = square_places()
    mate_side = (mate + 2) % 4
    places = (mate_side * 2 + 1 - lo, mate_side * 2 + lo, mate * 2 + 1 - lo, mate * 2 + lo)
    step = parts_ref.shape[1] // PIECES
    rows = lambda p: pl.ds(p * step, step)
    orders = ((0, 2, 1, 3), (0, 1, 2, 3), (2, 3, 0, 1), (0, 1, 2, 3))
    return {
        (k, p): remote_to(
            parts_ref.at[places[k], rows(p)], mates.at[k, rows(p)], sems_of, k, p, {"blk": mate}
        )
        for k in range(4)
        for p in orders[k]
    }


def scatter_end_square(loads, from_mate, out_ref, scratch, work=()):
    work = list(work)
    mine, mates, made, got_across, got_side, got_next = scratch[:6]
    sems_of = scratch[6:8]
    blk, lo, mate, side = square_places()
    to_side, to_next = {"blk": side}, {"lo": 1 - lo}
    step = mine.shape[1] // PIECES
    rows = lambda p: pl.ds(p * step, step)

    def summed(k, p):
        from_mate[k, p].wait_recv()
        return mine[k, rows(p), :].astype(F32) + mates[k, rows(p), :].astype(F32)

    sent = {}
    loads[0].wait()
    for p in (0, 2, 1, 3):
        made[0, rows(p), :] = summed(0, p).astype(BF16)
        sent[0, p] = remote_to(
            made.at[0, rows(p)],
            got_across.at[rows(p)],
            sems_of,
            4,
            p,
            to_side if p < 2 else to_next,
        )
    loads[1].wait()
    loads[2].wait()
    for n, (k, p) in enumerate(((1, 0), (2, 2), (1, 1), (2, 3), (1, 2), (2, 0), (1, 3), (2, 1))):
        if work and n % 2 == 0:
            work.pop(0)()
        total = summed(k, p)
        if (k == 1) == (p >= 2):
            sent[0, p].wait_recv()
            total = total + got_across[rows(p), :].astype(F32)
        made[k, rows(p), :] = total.astype(BF16)
        sent[k, p] = remote_to(
            made.at[k, rows(p)],
            (got_side if k == 1 else got_next).at[rows(p)],
            sems_of,
            4 + k,
            p,
            to_side if k == 1 else to_next,
        )
    for one in work:
        one()
    loads[3].wait()
    for p in range(PIECES):
        total = summed(3, p)
        sent[1, p].wait_recv()
        sent[2, p].wait_recv()
        out_ref[rows(p), :] = (
            total + got_side[rows(p), :].astype(F32) + got_next[rows(p), :].astype(F32)
        )
    for copy in from_mate.values():
        copy.wait_send()
    for copy in sent.values():
        copy.wait_send()


def scatter_scratch(tok, width):
    return [
        pltpu.VMEM((4, tok, width), BF16),
        pltpu.VMEM((4, tok, width), BF16),
        pltpu.VMEM((3, tok, width), BF16),
        pltpu.VMEM((tok, width), BF16),
        pltpu.VMEM((tok, width), BF16),
        pltpu.VMEM((tok, width), BF16),
        pltpu.SemaphoreType.DMA((7, PIECES)),
        pltpu.SemaphoreType.DMA((7, PIECES)),
        pltpu.SemaphoreType.DMA((4,)),
    ]


def scatter_kernel(firsts, parts_ref, *refs):
    out_ref, scratch = refs[firsts], refs[firsts + 1 :]
    loads = scatter_load(parts_ref, scratch)
    greet(square_greeting())
    scatter_end_square(loads, scatter_mates(parts_ref, scratch), out_ref, scratch)


def scatter_square(parts, number, *first):
    count, width = parts.shape
    tok = count // 8
    return pl.pallas_call(
        functools.partial(scatter_kernel, len(first)),
        in_specs=[pl.BlockSpec(memory_space=pl.ANY)] * (1 + len(first)),
        out_specs=pl.BlockSpec(memory_space=pltpu.VMEM),
        out_shape=jax.ShapeDtypeStruct((tok, width), F32),
        scratch_shapes=scatter_scratch(tok, width),
        compiler_params=pltpu.CompilerParams(
            collective_id=number, has_side_effects=True, vmem_limit_bytes=VMEM_LIMIT
        ),
        cost_estimate=pl.CostEstimate(flops=0, bytes_accessed=120_000_000, transcendentals=0),
        name="scatter_square",
    )(parts.astype(BF16).reshape(8, tok, width), *first)


class Then:
    def __init__(self, step):
        self.wait = step


def ff_end_kernel(units_ref, down_ref, out_ref, *scratch):
    scratch, (units, down, for_mate, sem) = scratch[:9], scratch[9:]
    mine, mates, sems_of = scratch[0], scratch[1], scratch[6:8]
    loads = [local_copy(down_ref, down, sem.at[0]), local_copy(units_ref, units, sem.at[1])]
    blk, lo, mate, side = square_places()
    mate_side = (mate + 2) % 4
    own_places = (side * 2 + 1 - lo, side * 2 + lo, blk * 2 + 1 - lo, blk * 2 + lo)
    mate_places = (mate_side * 2 + 1 - lo, mate_side * 2 + lo, mate * 2 + 1 - lo, mate * 2 + lo)
    step = units.shape[1] // PIECES
    rows = lambda p: pl.ds(p * step, step)
    orders = ((0, 2, 1, 3), (0, 1, 2, 3), (2, 3, 0, 1), (0, 1, 2, 3))
    from_mate = {}

    def made(place):
        return dot32(units[place], down[...]).astype(BF16)

    def own(k):
        mine[k] = made(own_places[k])

    def other(k):
        for_mate[k] = made(mate_places[k])
        for p in orders[k]:
            from_mate[k, p] = remote_to(
                for_mate.at[k, rows(p)], mates.at[k, rows(p)], sems_of, k, p, {"blk": mate}
            )

    greet(square_greeting())
    wait_all(loads)
    other(0)
    own(0)
    other(1)
    other(2)
    steps = [Then(lambda: None)] + [Then(functools.partial(own, k)) for k in (1, 2, 3)]
    scatter_end_square(steps, from_mate, out_ref, scratch, [functools.partial(other, 3)])


def ff_end(units, down, number):
    count, ff = units.shape
    width = down.shape[1]
    tok = count // 8
    return pl.pallas_call(
        ff_end_kernel,
        in_specs=[pl.BlockSpec(memory_space=pl.ANY)] * 2,
        out_specs=pl.BlockSpec(memory_space=pltpu.VMEM),
        out_shape=jax.ShapeDtypeStruct((tok, width), F32),
        scratch_shapes=scatter_scratch(tok, width)
        + [
            pltpu.VMEM((8, tok, ff), BF16),
            pltpu.VMEM(down.shape, BF16),
            pltpu.VMEM((4, tok, width), BF16),
            pltpu.SemaphoreType.DMA((2,)),
        ],
        compiler_params=pltpu.CompilerParams(
            collective_id=number, has_side_effects=True, vmem_limit_bytes=VMEM_LIMIT
        ),
        cost_estimate=pl.CostEstimate(
            flops=2 * count * ff * width, bytes_accessed=120_000_000, transcendentals=0
        ),
        name="ff_end",
    )(units.reshape(8, tok, ff), down)


def scatter_down_kernel(
    parts_ref, down_ref, got_ref, rows_ref, dgate_ref, dup_ref, out_ref, sum_ref, gate_own_ref, up_own_ref,
    gate_stay_ref, up_stay_ref, gate_got_ref, up_got_ref, *scratch,
):
    scratch, rest = scratch[:9], scratch[9:]
    own, got, away, came, sem, send, recv, left, gate_right, up_right, gate_away, up_away, w_sem = rest
    dp, hi = lax.axis_index("dp"), lax.axis_index("hi")
    part = left.shape[2]
    blocks = ((1 - dp, 1 - hi), (dp, 1 - hi), (1 - dp, hi), (dp, hi))

    def load_left(n):
        d, h = blocks[n]
        cols = pl.ds(pl.multiple_of((d * 2 + h) * part, part), part)
        return local_copy(rows_ref.at[:, cols], left.at[n % 2], w_sem.at[n % 2])

    rights = [local_copy(dgate_ref, gate_right, w_sem.at[2]), local_copy(dup_ref, up_right, w_sem.at[3])]
    lefts = {0: load_left(0), 1: load_left(1)}
    down = sum_begin(down_ref, got_ref, 1 - hi, own, got, sem)
    loads = scatter_load(parts_ref, scratch)
    greet(square_greeting() + [other_hi()] + dp_peers())
    mates = scatter_mates(parts_ref, scratch)
    wait_all(down)
    away[...] = (own[...] + got[...].astype(F32)).astype(BF16)
    over = remote(away, came, send.at[0], recv.at[0], other_hi())
    down = sum_begin(down_ref, got_ref, hi, own, got, sem)
    pairs = []

    def gradient(n, up):
        if not up:
            lefts[n].wait()
        if n == 0:
            rights[up].wait()
        total = dot32(left[n % 2], (up_right if up else gate_right)[...], ((0,), (0,)))
        if n == 0:
            target, got_there = (up_away, up_got_ref) if up else (gate_away, gate_got_ref)
            target[...] = total.astype(BF16)
            pairs.append(remote(target, got_there, send.at[1 + up], recv.at[1 + up], dp_peers()[0]))
        elif n == 2:
            (up_stay_ref if up else gate_stay_ref)[...] = total.astype(BF16)
        else:
            (up_own_ref if up else gate_own_ref)[blocks[n][1]] = total
        if up and n < 2:
            lefts[n + 2] = load_left(n + 2)

    work = [functools.partial(gradient, n, up) for n in range(4) for up in range(2)]
    scatter_end_square(loads, mates, out_ref, scratch, work)
    wait_all(down)
    over.wait()
    sum_ref[...] = own[...] + got[...].astype(F32) + came[...].astype(F32)
    wait_all(pairs)


def scatter_down(parts, number, down, rows, dgate, dup):
    count, width = parts.shape
    tok = count // 8
    part = down[0].shape[1:]
    depth, cols = dgate.shape
    grad = (rows.shape[1] // 4, cols)
    anywhere, inside = pl.BlockSpec(memory_space=pl.ANY), pl.BlockSpec(memory_space=pltpu.VMEM)
    return pl.pallas_call(
        scatter_down_kernel,
        in_specs=[anywhere] * 6,
        out_specs=[inside] * 6 + [anywhere] * 2,
        out_shape=[
            jax.ShapeDtypeStruct((tok, width), F32),
            jax.ShapeDtypeStruct(part, F32),
            jax.ShapeDtypeStruct((2,) + grad, F32),
            jax.ShapeDtypeStruct((2,) + grad, F32),
        ]
        + [jax.ShapeDtypeStruct(grad, BF16)] * 4,
        scratch_shapes=scatter_scratch(tok, width)
        + [pltpu.VMEM(part, F32)]
        + [pltpu.VMEM(part, BF16)] * 3
        + [pltpu.SemaphoreType.DMA((2,))]
        + sems(3)
        + [
            pltpu.VMEM((2, depth, grad[0]), BF16),
            pltpu.VMEM((depth, cols), BF16),
            pltpu.VMEM((depth, cols), BF16),
            pltpu.VMEM(grad, BF16),
            pltpu.VMEM(grad, BF16),
            pltpu.SemaphoreType.DMA((4,)),
        ],
        compiler_params=pltpu.CompilerParams(
            collective_id=number, has_side_effects=True, vmem_limit_bytes=VMEM_LIMIT
        ),
        cost_estimate=pl.CostEstimate(
            flops=4 * depth * cols * rows.shape[1], bytes_accessed=160_000_000, transcendentals=0
        ),
        name="scatter_down",
    )(parts.reshape(8, tok, width), *down, rows, dgate, dup)


def swap_square(blocks):
    return lax.all_to_all(blocks, SQUARE, split_axis=0, concat_axis=0, tiled=True)


def swap_pair(block, axis):
    return lax.ppermute(block, axis, [(0, 1), (1, 0)])


def gather_start(rows, axis):
    if lax.axis_size(axis) != 2:
        return lax.all_gather(rows, axis, axis=0, tiled=False)
    return rows, swap_pair(rows, axis)


def gather_end(parts, axis):
    if lax.axis_size(axis) != 2:
        return parts
    rows, other = parts
    first = lax.axis_index(axis) == 0
    return jnp.stack([jnp.where(first, rows, other), jnp.where(first, other, rows)])


def scatter_start(parts, axis):
    if lax.axis_size(axis) != 2:
        return lax.psum_scatter(parts.astype(BF16), axis, scatter_dimension=0, tiled=False)
    place = lax.axis_index(axis)
    away = lax.dynamic_index_in_dim(parts, 1 - place, 0, False).astype(BF16)
    own = lax.dynamic_index_in_dim(parts, place, 0, False)
    return own, swap_pair(away, axis)


def scatter_end(parts, axis):
    if lax.axis_size(axis) != 2:
        return parts.astype(F32)
    return parts[0] + parts[1].astype(F32)


def by_copy(rows):
    dp_n, hi_n = lax.axis_size("dp"), lax.axis_size("hi")
    return rows.reshape((dp_n, hi_n, rows.shape[0] // (dp_n * hi_n)) + rows.shape[1:])


def total_of(value, axes, count):
    spread = jnp.broadcast_to(value.reshape(1, 1), (count, 1))
    return jnp.sum(lax.all_to_all(spread, axes, split_axis=0, concat_axis=0, tiled=True))


def norm_parts(rows):
    inverse = lax.rsqrt(jnp.mean(rows * rows, axis=-1, keepdims=True) + NORM_EPS)
    return rows * inverse, inverse


def reorder(pairs, block, source, target, cast):
    for at, to in pairs:
        target[:, to * block : to * block + block] = cast(source[:, at * block : at * block + block])


def out_kernel(order, pairs, block, mixed_ref, weight_ref, rows_ref, gain_ref, middle_ref, normed_ref, total):
    f = pl.program_id(0)

    @pl.when(f == 0)
    def _():
        total[...] = jnp.zeros_like(total)

    total[...] += dot32(mixed_ref[0], weight_ref[...])

    @pl.when(f == pl.num_programs(0) - 1)
    def _():
        middle = rows_ref[...].astype(F32) + RESIDUAL_SCALE * total[...]
        middle_ref[...] = middle
        total[...] = norm_parts(middle)[0] * gain_ref[...]
        reorder(pairs, block, total, normed_ref, lambda v: v.astype(BF16))


def out_project(mixed, weight, rows, gain, order, pairs, block):
    group, tok, cols = mixed.shape
    width = weight.shape[1]
    whole = pl.BlockSpec((tok, width), lambda f: (0, 0))
    return pl.pallas_call(
        functools.partial(out_kernel, order, pairs, block),
        grid=(group,),
        in_specs=[
            pl.BlockSpec((1, tok, cols), lambda f: (f, 0, 0)),
            pl.BlockSpec((cols, width), lambda f: (order(f), 0)),
            whole,
            pl.BlockSpec((1, width), lambda f: (0, 0)),
        ],
        out_specs=[whole, whole],
        out_shape=[
            jax.ShapeDtypeStruct((tok, width), F32),
            jax.ShapeDtypeStruct((tok, width), BF16),
        ],
        scratch_shapes=[pltpu.VMEM((tok, width), F32)],
        compiler_params=pltpu.CompilerParams(vmem_limit_bytes=VMEM_LIMIT),
        cost_estimate=pl.CostEstimate(
            flops=2 * tok * width * width, bytes_accessed=16_000_000, transcendentals=0
        ),
        name="out_project",
    )(mixed, weight, rows, gain)


def start_kernel(
    key_head, places, wide, query_ref, key_ref, value_ref, w_gate_ref, w_up_ref, rows_ref, small_ref, wout_ref,
    down_ref, cos_ref, sina_ref, sinb_ref, all_ref, weight_ref, smalls_ref, wouts_ref, gates_ref, ups_ref, downs_ref, other_ref, normed_ref, q_ref, kv_ref, g_send,
    g_recv, g_local, g_held, w_send, w_recv, d_send, d_recv, s_send, s_recv, o_send, o_recv, local, w_held, o_held,
    ga_send, ga_recv, ga_local, ga_held, up_send, up_recv, up_local, up_held, x_send, x_recv, k_send, k_recv, heads_ref,
    gate_ref, up_ref, weight, smalls, gain, chunks, cosines, sinas, sinbs, sem, t_sem,
):
    blk, hi, lo = (lax.axis_index(a) for a in SEQ)
    mine = device_place()
    peers = every_peer()
    unit = chunks.shape[1]
    tables = []
    for b in range(4):
        rows_of = pl.ds(pl.multiple_of((2 * b + hi) * unit, unit), unit)
        for t, (ref, table) in enumerate(((cos_ref, cosines), (sina_ref, sinas), (sinb_ref, sinbs))):
            tables.append(local_copy(ref.at[rows_of], table.at[b], t_sem.at[b, t]))
    deal_heads(key_head, query_ref, key_ref, value_ref, heads_ref)
    greet(peers)
    own_head = Carried(heads_ref.at[blk * 2 + lo], weight_ref.at[mine], w_held, local.at[0])
    small_copies = [local_copy(small_ref, smalls_ref.at[mine], local.at[1])]
    for k, to in enumerate(peers):
        small_copies.append(remote(small_ref, smalls_ref.at[mine], s_send.at[k], s_recv.at[k], to))
    end = gather_begin(rows_ref, all_ref, g_send, g_recv, g_local, g_held)
    dp, seq = lax.axis_index("dp"), seq_peers()
    seq_n = len(seq) + 1
    straight, handed = [], []
    for k, (to, source) in enumerate(seq):
        part = heads_ref.at[to["blk"] * 2 + to["lo"]]
        straight.append(remote(part, weight_ref.at[mine], w_send.at[k], w_recv.at[k], to))

    def hand_on(part, place, k):
        for d, to in enumerate(dp_peers()):
            n = d * seq_n + k
            handed.append(remote(part, weight_ref.at[place], d_send.at[n], d_recv.at[n], to))

    hand_on(heads_ref.at[blk * 2 + lo], mine, seq_n - 1)
    deal_units(places, wide, w_gate_ref, w_up_ref, gate_ref, up_ref)

    def pass_on(turn):
        for k, (to, source) in enumerate(seq):
            if k * 2 * PIECES // len(seq) == turn:
                straight[k].wait()
                place = dp * seq_n + source
                hand_on(weight_ref.at[place], place, k)

    end(pass_on)
    copies = [Carried(wout_ref, wouts_ref.at[hi, lo], o_held, local.at[2])]
    next_lo = {"lo": 1 - lo}
    wout = remote(wout_ref, wouts_ref.at[hi, lo], o_send.at[0], o_recv.at[0], other_hi())
    copies.append(remote(wout_ref, wouts_ref.at[hi, lo], o_send.at[1], o_recv.at[1], next_lo))
    copies += swap_begin(gate_ref, gates_ref, ga_send, ga_recv, ga_local, ga_held)
    copies += swap_begin(up_ref, ups_ref, up_send, up_recv, up_local, up_held)
    own_head.turn()
    wait_all(small_copies)
    load_smalls = local_copy(smalls_ref, smalls, sem.at[2])
    load_rows = lambda b: local_copy(all_ref.at[pl.ds(2 * b, 2)], chunks_of(chunks, b), sem.at[b % 2])
    loads = [load_rows(0), load_rows(1)]
    own_head.wait()
    wait_all(handed)
    load_weight = local_copy(weight_ref, weight, sem.at[3])
    for d, to in enumerate(dp_peers()):
        copies.append(remote(down_ref, downs_ref.at[d], x_send.at[d], x_recv.at[d], to))
    load_smalls.wait()
    low = lanes_low((1, 128))
    for j in range(smalls.shape[0] // 2):
        gain[:, 128 * j : 128 * j + 128] = jnp.where(
            low, smalls[2 * j, 0:1, :], pltpu.roll(smalls[2 * j + 1, 0:1, :], HEAD_SIZE, 1)
        )
    load_weight.wait()
    wait_all(tables)
    width = gain.shape[1]
    half = HEAD_SIZE // 2
    low = lanes_low((unit, 128))
    for b in range(4):
        here = slice(b * unit, b * unit + unit)
        loads[b].wait()
        rows = chunks[b % 2].astype(F32)
        normed_ref[here, :] = (norm_parts(rows)[0] * gain[...]).astype(BF16)
        if b + 2 < 4:
            loads.append(load_rows(b + 2))
        made = dot32(normed_ref[here, :], weight[...].reshape(width, -1))
        cosine, sina, sinb = cosines[b], sinas[b], sinbs[b]
        for part in range(3):
            u = made[:, 128 * part : 128 * part + 128]
            up, down = pltpu.roll(u, 128 - half, 1), pltpu.roll(u, half, 1)
            turned = u * cosine + up * sina + down * sinb
            if part < 2:
                q_ref[here, 128 * part : 128 * part + 128] = (
                    turned.astype(BF16).astype(F32) * ATTN_SCALE
                ).astype(BF16)
            else:
                kv_ref[here, :] = jnp.where(low, turned, u).astype(BF16)
        piece = pl.ds(b * unit, unit)
        copies.append(
            remote(kv_ref.at[piece], other_ref.at[piece], k_send.at[b], k_recv.at[b], other_hi())
        )
        if b == 2:
            wout.wait()
            there = wouts_ref.at[1 - hi, lo]
            copies.append(remote(there, there, o_send.at[2], o_recv.at[2], next_lo))
    finish(copies)


def chunks_of(chunks, b):
    return chunks.at[b % 2].reshape(2, chunks.shape[1] // 2, chunks.shape[2])


def through_start(key_head, places, wide_w, heads_shape, part_shape, weights, rows, small, wout, down, tables):
    tok, width = rows.shape
    rows_w = wout.shape[0]
    part = part_shape[1:]
    dp_n, hi_n, lo_n = (lax.axis_size(a) for a in ("dp", "hi", "lo"))
    every = dp_n * hi_n * lo_n * lax.axis_size("blk")
    wide = heads_shape[2]
    anywhere, inside = pl.BlockSpec(memory_space=pl.ANY), pl.BlockSpec(memory_space=pltpu.VMEM)
    shapes = [
        ((8, tok, width), BF16),
        ((every, rows_w, wide), BF16),
        ((every, 8, 128), F32),
        ((hi_n, lo_n, rows_w, width), BF16),
        (part_shape, BF16),
        (part_shape, BF16),
        ((dp_n - 1,) + down.shape, BF16),
        ((8 * tok, 128), BF16),
        ((8 * tok, width), BF16),
        ((8 * tok, 256), BF16),
        ((8 * tok, 128), BF16),
    ]
    return pl.pallas_call(
        functools.partial(start_kernel, key_head, places, wide_w),
        in_specs=[inside] * 5 + [anywhere] * 7,
        out_specs=[anywhere] * 8 + [inside] * 3,
        out_shape=[jax.ShapeDtypeStruct(shape, dtype) for shape, dtype in shapes],
        scratch_shapes=gather_scratch(tok, width)
        + sems(every // dp_n - 1)
        + sems((dp_n - 1) * every // dp_n)
        + sems(every - 1)
        + sems(3)
        + [
            pltpu.SemaphoreType.DMA((3,)),
            pltpu.VMEM((rows_w, wide), BF16),
            pltpu.VMEM((rows_w, width), BF16),
        ]
        + swap_scratch(part)
        + swap_scratch(part)
        + sems(dp_n - 1)
        + sems(4)
        + [
            pltpu.VMEM(heads_shape, BF16),
            pltpu.VMEM(part_shape, BF16),
            pltpu.VMEM(part_shape, BF16),
            pltpu.VMEM((every, rows_w, wide), BF16),
            pltpu.VMEM((every, 8, 128), F32),
            pltpu.VMEM((1, width), F32),
            pltpu.VMEM((2, 2 * tok, width), BF16),
        ]
        + [pltpu.VMEM((4, 2 * tok, 128), F32)] * 3
        + [pltpu.SemaphoreType.DMA((4,)), pltpu.SemaphoreType.DMA((4, 3))],
        compiler_params=pltpu.CompilerParams(
            collective_id=11, has_side_effects=True, vmem_limit_bytes=VMEM_LIMIT
        ),
        cost_estimate=pl.CostEstimate(
            flops=16 * tok * width * wide, bytes_accessed=250_000_000, transcendentals=0
        ),
        name="start",
    )(*weights, rows, small, wout, down, *tables)


def middle_kernel(
    order, pairs, block, heads_ref, gate_ref, gate_other_ref, up_ref, down_ref, weight_ref, rows_ref, gain_ref,
    out_ref, middle_ref, gates_ref, ups_ref, down_other_ref, up_other_ref, made_ref, m_send, m_recv, m_local,
    m_held, g_send, g_recv, g_local, g_held, u_send, u_recv, u_local, u_held, o_send, o_recv, r_send, r_recv,
    r_local, r_held, mixed, weight, rows, normed, total, gate_weight, chunks, sem,
):
    hi = lax.axis_index("hi")
    loads = [local_copy(weight_ref, weight, sem.at[0]), local_copy(rows_ref, rows, sem.at[1])]
    mine, others, ids = square_peers()
    greet(ids + [other_hi()] + dp_peers())
    heads = swap_begin(heads_ref, mixed, m_send, m_recv, m_local, m_held)
    up_over = remote(up_ref, up_other_ref, o_send.at[0], o_recv.at[0], other_hi())
    gates = dp_begin([(hi, gate_ref), (1 - hi, gate_other_ref)], gates_ref, g_send, g_recv, g_local, g_held)
    copies = dp_begin([(hi, up_ref)], ups_ref, u_send, u_recv, u_local, u_held)
    wait_all(loads)
    cols = mixed.shape[2]

    def add(f):
        g = order(f)
        part = weight[pl.ds(pl.multiple_of(g * cols, cols), cols), :]
        return dot32(mixed[f], part)

    heads[7].turn()
    heads[7].wait()
    total[...] = add(mine)
    for d in range(7):
        heads[d].wait_recv()
        total[...] += add(lax.rem(mine + 7 - d, 8))
    middle = rows[...].astype(F32) + RESIDUAL_SCALE * total[...]
    middle_ref[...] = middle
    total[...] = norm_parts(middle)[0] * gain_ref[...]
    reorder(pairs, block, total, normed, lambda v: v.astype(BF16))
    end = gather_begin(normed, out_ref, r_send, r_recv, r_local, r_held)

    def more(turn):
        if turn == PIECES - 1:
            up_over.wait()
            copies.append(remote(down_ref, down_other_ref, o_send.at[1], o_recv.at[1], other_hi()))
            copies.extend(
                dp_begin([(1 - hi, up_other_ref)], ups_ref, u_send, u_recv, u_local, u_held, 1)
            )

    end(more)
    finish(gates)
    step = 2
    load_gate = local_copy(gates_ref, gate_weight, sem.at[0])
    load_rows = lambda n: local_copy(out_ref.at[pl.ds(n * step, step)], chunks.at[n % 2], sem.at[1 + n % 2])
    loads = [load_rows(0), load_rows(1)]
    load_gate.wait()
    tok, width = rows.shape
    for n in range(8 // step):
        loads[n].wait()
        made_ref[n * step * tok : (n + 1) * step * tok, :] = dot32(
            chunks[n % 2].reshape(step * tok, width), gate_weight[...].reshape(width, -1)
        )
        if n + 2 < 8 // step:
            loads.append(load_rows(n + 2))
    for d in range(7):
        heads[d].wait_send()
    finish(copies)


def through_middle(heads, gate, gate_other, up, down, weight, rows, gain, order, pairs, block):
    group, tok, cols = heads.shape
    width = weight.shape[1]
    part_rows, ff_part = up.shape
    dp_n = lax.axis_size("dp")
    anywhere, inside = pl.BlockSpec(memory_space=pl.ANY), pl.BlockSpec(memory_space=pltpu.VMEM)
    dp_part = sems(2 * (dp_n - 1)) + [
        pltpu.SemaphoreType.DMA((2,)),
        pltpu.VMEM((2, part_rows, ff_part), BF16),
    ]
    spread = (dp_n, 2, part_rows, ff_part)
    return pl.pallas_call(
        functools.partial(middle_kernel, order, pairs, block),
        in_specs=[anywhere] * 7 + [inside],
        out_specs=[anywhere, inside, anywhere, anywhere, anywhere, anywhere, inside],
        out_shape=[
            jax.ShapeDtypeStruct((group, tok, width), BF16),
            jax.ShapeDtypeStruct((tok, width), F32),
            jax.ShapeDtypeStruct(spread, BF16),
            jax.ShapeDtypeStruct(spread, BF16),
            jax.ShapeDtypeStruct(down.shape, BF16),
            jax.ShapeDtypeStruct(up.shape, BF16),
            jax.ShapeDtypeStruct((group * tok, ff_part), F32),
        ],
        scratch_shapes=swap_scratch((tok, cols))
        + dp_part
        + dp_part
        + sems(2)
        + gather_scratch(tok, width)
        + [
            pltpu.VMEM((group, tok, cols), BF16),
            pltpu.VMEM(weight.shape, BF16),
            pltpu.VMEM((tok, width), BF16),
            pltpu.VMEM((tok, width), BF16),
            pltpu.VMEM((tok, width), F32),
            pltpu.VMEM(spread, BF16),
            pltpu.VMEM((2, 2, tok, width), BF16),
            pltpu.SemaphoreType.DMA((3,)),
        ],
        compiler_params=pltpu.CompilerParams(
            collective_id=10, has_side_effects=True, vmem_limit_bytes=VMEM_LIMIT
        ),
        cost_estimate=pl.CostEstimate(
            flops=2 * group * tok * width * ff_part, bytes_accessed=250_000_000, transcendentals=0
        ),
        name="middle",
    )(heads, gate, gate_other, up, down, weight, rows, gain)


def weight_grad_kernel(dp_ref, left_ref, right_ref, first_ref, away_ref, own_ref):
    i = pl.program_id(0)
    total = dot32(left_ref[...], right_ref[...], ((0,), (0,)))

    @pl.when(i < 2)
    def _():
        away_ref[0] = total.astype(BF16)

    @pl.when(i >= 2)
    def _():
        own_ref[0] = total


def weight_grad_start(left, right, first):
    dp_n, hi_n = lax.axis_size("dp"), lax.axis_size("hi")
    depth, rows = left.shape
    cols = right.shape[1]
    if dp_n != 2:
        sums = scatter_start(by_copy(dot32(left, right, ((0,), (0,)))), "dp")
        return sums.astype(F32), jnp.zeros(sums.shape, BF16)
    part = rows // (dp_n * hi_n)
    place = lax.axis_index("dp").astype(jnp.int32).reshape(1)
    away, own = pl.pallas_call(
        weight_grad_kernel,
        grid_spec=pltpu.PrefetchScalarGridSpec(
            num_scalar_prefetch=1,
            grid=(4,),
            in_specs=[
                pl.BlockSpec(
                    (depth, part),
                    lambda i, dp: (0, jnp.where(i < 2, 2 * (1 - dp[0]) + i, 2 * dp[0] + i - 2)),
                ),
                pl.BlockSpec((depth, cols), lambda i, dp: (0, 0)),
                pl.BlockSpec(memory_space=pl.ANY),
            ],
            out_specs=[
                pl.BlockSpec((1, part, cols), lambda i, dp: (jnp.minimum(i, 1), 0, 0)),
                pl.BlockSpec((1, part, cols), lambda i, dp: (jnp.maximum(i - 2, 0), 0, 0)),
            ],
        ),
        out_shape=[
            jax.ShapeDtypeStruct((2, part, cols), BF16),
            jax.ShapeDtypeStruct((2, part, cols), F32),
        ],
        compiler_params=pltpu.CompilerParams(vmem_limit_bytes=VMEM_LIMIT),
        cost_estimate=pl.CostEstimate(
            flops=2 * depth * rows * cols, bytes_accessed=24_000_000, transcendentals=0
        ),
        name="weight_grad",
    )(place, left, right, first)
    return own, away


def ff_back_kernel(
    tile, grad_ref, gate_slope_ref, up_slope_ref, gate_ref, up_ref, down_ref, first_ref, dgate_ref, dup_ref,
    out_ref, total,
):
    total[...] = jnp.zeros_like(total)

    def step(t, carry):
        cols = pl.ds(pl.multiple_of(t * tile, tile), tile)
        dunits = dot32(grad_ref[...], down_ref[cols, :], ((1,), (1,)))
        dgate = (dunits * gate_slope_ref[:, cols].astype(F32)).astype(BF16)
        dup = (dunits * up_slope_ref[:, cols].astype(F32)).astype(BF16)
        dgate_ref[:, cols] = dgate
        dup_ref[:, cols] = dup
        total[...] += dot32(dgate, gate_ref[:, cols], ((1,), (1,))) + dot32(
            dup, up_ref[:, cols], ((1,), (1,))
        )
        return carry

    lax.fori_loop(0, down_ref.shape[0] // tile, step, 0)
    out_ref[...] = total[...].astype(BF16)


def ff_back(grad, gate_slope, up_slope, gate_weight, up_weight, down_weight, first, tok):
    count, width = grad.shape
    ff = down_weight.shape[0]
    rows = lambda cols: pl.BlockSpec((tok, cols), lambda i: (i, 0))
    whole = lambda a: pl.BlockSpec(a.shape, lambda i: (0, 0), pipeline_mode=pl.Buffered(1))
    return pl.pallas_call(
        functools.partial(ff_back_kernel, ff),
        grid=(count // tok,),
        in_specs=[
            rows(width),
            rows(ff),
            rows(ff),
            whole(gate_weight),
            whole(up_weight),
            whole(down_weight),
            pl.BlockSpec(memory_space=pl.ANY),
        ],
        out_specs=[rows(ff), rows(ff), rows(width)],
        out_shape=[
            jax.ShapeDtypeStruct((count, ff), BF16),
            jax.ShapeDtypeStruct((count, ff), BF16),
            jax.ShapeDtypeStruct((count, width), BF16),
        ],
        scratch_shapes=[pltpu.VMEM((tok, width), F32)],
        compiler_params=pltpu.CompilerParams(vmem_limit_bytes=VMEM_LIMIT),
        cost_estimate=pl.CostEstimate(
            flops=6 * count * width * ff, bytes_accessed=40_000_000, transcendentals=0
        ),
        name="ff_back",
    )(grad, gate_slope, up_slope, gate_weight, up_weight, down_weight, first)


def deal_kernel(
    key_head, places, wide, query_ref, key_ref, value_ref, gate_ref, up_ref, heads_ref, gates_ref, ups_ref
):
    deal_heads(key_head, query_ref, key_ref, value_ref, heads_ref)
    deal_units(places, wide, gate_ref, up_ref, gates_ref, ups_ref)


def deal_heads(key_head, query_ref, key_ref, value_ref, heads_ref):
    columns, k_columns = query_ref.shape[1] // 8, key_ref.shape[1] // 8
    for f in range(8):
        g = key_head(f)
        cols, k_cols = slice(g * columns, g * columns + columns), slice(g * k_columns, g * k_columns + k_columns)
        heads_ref[f, :, :columns] = query_ref[:, cols]
        heads_ref[f, :, columns:] = jnp.concatenate([key_ref[:, k_cols], value_ref[:, k_cols]], axis=1)


def deal_units(places, wide, gate_ref, up_ref, gates_ref, ups_ref):
    for at, (f, to) in enumerate(places):
        here, there = slice(at * wide, at * wide + wide), slice(to * wide, to * wide + wide)
        gates_ref[f, :, there] = gate_ref[:, here]
        ups_ref[f, :, there] = up_ref[:, here]


def collect_kernel(
    places, wide, gates_ref, ups_ref, gate_ref, up_ref, gain_ref, dgate_ref, dup_ref, dgain_ref
):
    total = jnp.zeros((gate_ref.shape[0], wide), F32)
    for at, (f, to) in enumerate(places):
        here, there = slice(at * wide, at * wide + wide), slice(to * wide, to * wide + wide)
        dgate, dup = gates_ref[f, :, there].astype(F32), ups_ref[f, :, there].astype(F32)
        dgate_ref[:, here] = dgate
        dup_ref[:, here] = dup
        total += gate_ref[:, here].astype(F32) * dgate + up_ref[:, here].astype(F32) * dup
    dgain_ref[...] = jnp.sum(total, axis=1, keepdims=True) / gain_ref[...]


def final_kernel(
    key_head, places, wide, first_ref, middle_ref, rows_ref, gain_ref, heads_ref, query_ref, key_ref, value_ref,
    gates_ref, ups_ref, gate_ref, up_ref, small_ref, outs_ref, down_ref, dhidden_ref, dquery_ref, dkey_ref,
    dvalue_ref, dgain_one_ref, dgate_ref, dup_ref, dgain_two_ref, dout_ref, ddown_ref,
):
    rows_w = gate_ref.shape[0]
    normal, inverse = norm_parts(rows_ref[...].astype(F32))
    grad = first_ref[...] * gain_ref[...]
    dhidden_ref[...] = middle_ref[...] + inverse * (
        grad - normal * jnp.mean(grad * normal, axis=-1, keepdims=True)
    )
    gains = jnp.transpose(jnp.broadcast_to(small_ref[0:1, :], (128, 128)))[:, 0:1]
    columns = query_ref.shape[1] // 8
    k_columns = key_ref.shape[1] // 8
    total = jnp.zeros((rows_w, columns), F32)
    k_total = jnp.zeros((rows_w, k_columns), F32)
    for f in range(8):
        b, l, g = f // 2, f % 2, key_head(f)
        both = heads_ref[b * 4 + l].astype(F32) + heads_ref[b * 4 + 2 + l].astype(F32)
        cols, k_cols = slice(g * columns, g * columns + columns), slice(g * k_columns, g * k_columns + k_columns)
        dquery = both[:, :columns]
        dkey, dvalue = both[:, columns : columns + k_columns], both[:, columns + k_columns :]
        dquery_ref[:, cols], dkey_ref[:, k_cols], dvalue_ref[:, k_cols] = dquery, dkey, dvalue
        total += query_ref[:, cols].astype(F32) * dquery
        k_total += key_ref[:, k_cols].astype(F32) * dkey + value_ref[:, k_cols].astype(F32) * dvalue
    dgain_one_ref[...] = (
        jnp.sum(total, axis=1, keepdims=True) + jnp.sum(k_total, axis=1, keepdims=True)
    ) / gains[:rows_w]
    total = jnp.zeros((rows_w, wide), F32)
    for at, (f, to) in enumerate(places):
        here, there = slice(at * wide, at * wide + wide), slice(to * wide, to * wide + wide)
        dgate, dup = gates_ref[f, :, there].astype(F32), ups_ref[f, :, there].astype(F32)
        dgate_ref[:, here] = dgate
        dup_ref[:, here] = dup
        total += gate_ref[:, here].astype(F32) * dgate + up_ref[:, here].astype(F32) * dup
    dgain_two_ref[...] = jnp.sum(total, axis=1, keepdims=True) / gains[rows_w : 2 * rows_w]
    dout_ref[...] = outs_ref[0].astype(F32) + outs_ref[1].astype(F32)
    ddown_ref[...] = down_ref[...]


def shards(
    hidden,
    teacher,
    lengths,
    attn_gain,
    w_query,
    key_projection,
    value_projection,
    w_out,
    mlp_gain,
    w_gate,
    w_up,
    w_down,
):
    dp_n, blk_n, hi_n, lo_n = (lax.axis_size(a) for a in ALL)
    group = blk_n * lo_n
    every = dp_n * blk_n * hi_n * lo_n
    hi, lo = lax.axis_index("hi"), lax.axis_index("lo")
    blk = lax.axis_index("blk")
    tok = hidden.shape[1]
    seq_len = tok * blk_n * hi_n * lo_n
    width = hidden.shape[2]
    rows_w = w_query.shape[0]
    units_w = w_down.shape[0]
    ff_part = w_gate.shape[1] // group

    block = lo_n * rows_w
    if block % 128 == 0:
        to_inner = [
            ((d * blk_n + b) * hi_n + h, (d * hi_n + h) * blk_n + b)
            for d in range(dp_n)
            for b in range(blk_n)
            for h in range(hi_n)
        ]
        reblock = block
    else:
        to_inner, reblock = [(0, 0)], width
    to_outer = [(to, at) for at, to in to_inner]

    def inner(a):
        if reblock == block:
            return a
        return a.reshape(-1, dp_n, blk_n, hi_n, block).transpose(0, 1, 3, 2, 4).reshape(-1, width)

    def outer(a):
        if reblock == block:
            return a
        return a.reshape(-1, dp_n, hi_n, blk_n, block).transpose(0, 1, 3, 2, 4).reshape(-1, width)

    key_head = lambda f: (f % lo_n) * blk_n + f // lo_n

    def head_columns(w):
        cols = w.shape[1] // group
        return w.reshape(rows_w, lo_n, blk_n, cols).transpose(2, 1, 0, 3).reshape(group, rows_w, cols)

    def head_columns_back(g):
        cols = g.shape[2]
        return (
            g.reshape(blk_n, lo_n, rows_w, cols).transpose(2, 1, 0, 3).reshape(rows_w, group * cols)
        )

    def unit_columns(w):
        return (
            w.reshape(rows_w, dp_n, blk_n, hi_n, lo_n, units_w)
            .transpose(2, 4, 0, 1, 3, 5)
            .reshape(group, rows_w, ff_part)
        )

    def unit_columns_back(g):
        return (
            g.reshape(blk_n, lo_n, rows_w, dp_n, hi_n, units_w)
            .transpose(2, 3, 0, 4, 1, 5)
            .reshape(rows_w, group * ff_part)
        )

    q_cols = w_query.shape[1] // group
    k_cols = key_projection.shape[1] // group
    ff_places = [
        (b * lo_n + l, d * hi_n + h)
        for d in range(dp_n)
        for b in range(blk_n)
        for h in range(hi_n)
        for l in range(lo_n)
    ]
    part_shape = jax.ShapeDtypeStruct((group, rows_w, ff_part), BF16)
    params = pltpu.CompilerParams(vmem_limit_bytes=VMEM_LIMIT)
    one_start = reblock == block and rows_w == HEAD_SIZE and blk_n == 4 and units_w % 128 == 0
    head_wide = q_cols + 2 * k_cols
    if one_start:
        pass
    elif units_w % 128 == 0:
        head_shape = jax.ShapeDtypeStruct((group, rows_w, q_cols + 2 * k_cols), BF16)
        head_parts, gate_parts, up_parts = pl.pallas_call(
            functools.partial(deal_kernel, key_head, ff_places, units_w),
            out_shape=[head_shape, part_shape, part_shape],
            compiler_params=params,
            name="deal",
        )(w_query, key_projection, value_projection, w_gate, w_up)
    else:
        head_parts = jnp.concatenate(
            [head_columns(w) for w in (w_query, key_projection, value_projection)], axis=2
        )
        gate_parts, up_parts = unit_columns(w_gate), unit_columns(w_up)

    pad = jnp.zeros((7 * 128 + 128 - 2 * rows_w - 1,), F32)
    small = jnp.concatenate(
        [attn_gain.astype(F32), mlp_gain.astype(F32), lengths.astype(F32), pad]
    ).reshape(8, 128)
    hi_index = hi.astype(jnp.int32).reshape(1)
    tables = rope_tables(seq_len)
    unit = lo_n * tok
    part_rows = group * rows_w
    if one_start:
        _, qkv_weight, smalls, out_rows, gate_parts, up_parts, downs, other_kv, normed_one, q, kv = (
            through_start(
                key_head,
                ff_places,
                units_w,
                (group, rows_w, head_wide),
                (group, rows_w, ff_part),
                (w_query, key_projection, value_projection, w_gate, w_up),
                hidden[0],
                small,
                w_out,
                w_down,
                tables,
            )
        )
    else:
        rows_all, qkv_weight, smalls, out_rows = comm_call(
            open_kernel,
            0,
            [hidden[0], head_parts, small, w_out],
            [
                ((group, tok, width), BF16),
                ((every, rows_w, head_wide), BF16),
                ((every, 8, 128), F32),
                ((hi_n, lo_n, rows_w, width), BF16),
            ],
            gather_scratch(tok, width)
            + sems(every // dp_n - 1)
            + sems((dp_n - 1) * every // dp_n)
            + sems(every - 1)
            + sems(3)
            + [
                pltpu.SemaphoreType.DMA((3,)),
                pltpu.VMEM((rows_w, head_wide), BF16),
                pltpu.VMEM((rows_w, width), BF16),
            ],
            "open",
        )
        qkv_weight = qkv_weight.reshape(width, head_wide)
        gain_one = smalls[:, 0, :rows_w].reshape(1, width)
        normed_one, q, kv = project(
            hi_index, rows_all.reshape(group * tok, width), gain_one, qkv_weight, tables, tok
        )
        other_kv, gate_parts, up_parts, downs = comm_call(
            keys_kernel,
            2,
            [kv, gate_parts, up_parts, w_down],
            [
                (kv.shape, BF16),
                (gate_parts.shape, BF16),
                (up_parts.shape, BF16),
                ((dp_n - 1,) + w_down.shape, BF16),
            ],
            sems(1) + swap_scratch((rows_w, ff_part)) * 2 + sems(dp_n - 1),
            "keys",
        )
    qkv_weight = qkv_weight.reshape(width, head_wide)
    gain_one = smalls[:, 0, :rows_w].reshape(1, width)
    gain_two = smalls[:, 0, rows_w : 2 * rows_w].reshape(1, width)
    valid_count = jnp.sum(smalls.reshape(every, -1)[:: every // dp_n, 2 * rows_w])
    gate_parts = gate_parts.reshape(part_rows, -1)
    up_parts = up_parts.reshape(part_rows, -1)
    gate_other = swap_pair(gate_parts, "hi")
    out_weight = lax.all_gather(out_rows.reshape(-1, width), ("dp", "blk"), axis=0, tiled=True)
    q = q.reshape(blk_n, unit, q_cols)
    kv, other_kv = kv.reshape(blk_n, unit, -1), other_kv.reshape(blk_n, unit, -1)
    scalars = jnp.stack([lengths[0], hi.astype(jnp.int32)])
    out_heads, log_heads = attend(scalars, q, kv, other_kv)
    if reblock == block:
        normed_two, middle, gate_weight, up_weight, down_other, _, gate = through_middle(
            out_heads.reshape(group, tok, q_cols),
            gate_parts,
            gate_other,
            up_parts,
            w_down,
            out_weight,
            hidden[0],
            gain_two,
            key_head,
            to_inner,
            reblock,
        )
        gate_weight = gate_weight.reshape(width, ff_part)
    else:
        dp_sems = sems(2 * (dp_n - 1))
        dp_scratch = [pltpu.SemaphoreType.DMA((2,)), pltpu.VMEM((2, part_rows, ff_part), BF16)]
        weight_shape = ((dp_n, hi_n, part_rows, ff_part), BF16)
        mixed, gate_weight, up_other = comm_call(
            heads_kernel,
            3,
            [out_heads.reshape(group, tok, q_cols), gate_parts, gate_other, up_parts],
            [((group, tok, q_cols), BF16), weight_shape, (up_parts.shape, BF16)],
            swap_scratch((tok, q_cols)) + dp_sems + sems(1) + dp_scratch,
            "heads",
        )
        gate_weight = gate_weight.reshape(width, ff_part)
        middle, normed_two = out_project(
            mixed, out_weight, hidden[0], gain_two, key_head, to_inner, reblock
        )

        normed_two, up_weight, down_other = comm_call(
            rows_kernel,
            4,
            [inner(normed_two), up_parts, up_other, w_down],
            [((group, tok, width), BF16), weight_shape, (w_down.shape, BF16)],
            gather_scratch(tok, width) + dp_sems + sems(1) + dp_scratch,
            "rows",
        )
        gate = dot32(normed_two.reshape(group * tok, width), gate_weight)
    normed_two = normed_two.reshape(group * tok, width)
    up_weight = up_weight.reshape(width, ff_part)
    dp_index = lax.axis_index("dp")
    own_first = hi == 0

    def by_hi(own, other):
        return jnp.stack([jnp.where(own_first, own, other), jnp.where(own_first, other, own)])

    down_parts = by_hi(w_down, down_other)
    if dp_n == 2:
        far = by_hi(downs[0], swap_pair(down_other, "dp"))
        dp_first = dp_index == 0
        down_parts = jnp.stack(
            [jnp.where(dp_first, down_parts, far), jnp.where(dp_first, far, down_parts)]
        )
    else:
        down_parts = lax.all_gather(down_parts, "dp", axis=0, tiled=False)
    down_weight = down_parts.reshape(-1, width)
    upward = dot32(normed_two, up_weight)
    sigma = jax.nn.sigmoid(gate)
    silu = gate * sigma
    units = (silu * upward).astype(BF16)
    gate_slope = (upward * sigma * (1.0 + gate * (1.0 - sigma))).astype(BF16)
    up_slope = silu.astype(BF16)
    result = middle + RESIDUAL_SCALE * ff_end(units, down_weight, 1)

    own_places = ((blk * hi_n + hi) * lo_n + lo) * tok + jnp.arange(tok)
    valid = own_places < lengths[0]
    misfit = jnp.where(valid[:, None], result - teacher[0].astype(F32), 0.0)
    squares = jnp.broadcast_to(jnp.sum(misfit * misfit), (8, 128))
    grad_result = misfit * (dp_n * seq_len / valid_count)

    branch = gather_square((RESIDUAL_SCALE * grad_result).astype(BF16), 5)
    down_sum = weight_grad_start(units, branch, branch)
    grad_gate_rows, grad_up_rows, grad_normal = ff_back(
        branch, gate_slope, up_slope, gate_weight, up_weight, down_weight, down_sum[0], 2 * tok
    )
    if dp_n == 2:
        down_got = swap_pair(down_sum[1], "dp")
        grad_normal, down_sum, gate_own, up_own, gate_stay, up_stay, gate_got, up_got = scatter_down(
            grad_normal, 9, (down_sum[0], down_got), normed_two, grad_gate_rows, grad_up_rows
        )
        gate_stay, up_stay = swap_pair(gate_stay, "dp"), swap_pair(up_stay, "dp")
    else:
        grad_normal = scatter_square(grad_normal, 9)
        down_sum = scatter_end(scatter_start(down_sum[0], "hi"), "hi")
        gate_own = weight_grad_start(normed_two, grad_gate_rows, grad_normal)[0]
        up_own = weight_grad_start(normed_two, grad_up_rows, grad_normal)[0]
        gate_stay = up_stay = gate_got = up_got = jnp.zeros(gate_own.shape[1:], BF16)
    grad_normal = outer(grad_normal)

    part_shape = (part_rows, ff_part)
    anywhere, inside = pl.BlockSpec(memory_space=pl.ANY), pl.BlockSpec(memory_space=pltpu.VMEM)
    grad_middle, attn_rows, dout, gate_away, up_away = pl.pallas_call(
        functools.partial(out_back_kernel, key_head, to_outer, reblock),
        in_specs=[inside] * 4 + [anywhere] * 5,
        out_specs=[inside] * 2 + [anywhere] + [inside] * 2,
        out_shape=[
            jax.ShapeDtypeStruct((tok, width), F32),
            jax.ShapeDtypeStruct((tok, width), BF16),
            jax.ShapeDtypeStruct((group, tok, q_cols), BF16),
            jax.ShapeDtypeStruct(part_shape, BF16),
            jax.ShapeDtypeStruct(part_shape, BF16),
        ],
        scratch_shapes=[
            pltpu.VMEM(out_weight.shape, BF16),
            pltpu.VMEM((tok, width), F32),
            pltpu.VMEM((group, tok, q_cols), BF16),
        ]
        + sems(7)
        + [
            pltpu.VMEM((2,) + part_shape, F32),
            pltpu.VMEM((2,) + part_shape, BF16),
            pltpu.SemaphoreType.DMA((2, 2)),
            pltpu.SemaphoreType.DMA((1,)),
        ],
        compiler_params=pltpu.CompilerParams(
            collective_id=6, has_side_effects=True, vmem_limit_bytes=VMEM_LIMIT
        ),
        cost_estimate=pl.CostEstimate(
            flops=2 * tok * width * width, bytes_accessed=60_000_000, transcendentals=0
        ),
        name="out_back",
    )(grad_normal, middle, grad_result, gain_two, out_weight, gate_own, gate_got, up_own, up_got)
    columns = (group, rows_w, ff_part)

    gate_dp, up_dp = gate_stay.reshape(columns), up_stay.reshape(columns)
    gate_hi, up_hi = (swap_pair(a, "hi").reshape(columns) for a in (gate_away, up_away))
    square_attn = lax.all_gather(attn_rows, SQUARE, axis=0, tiled=True)
    dout = dout.reshape(blk_n, unit, q_cols)
    dq, dkv = attend_back(scalars, q, kv, other_kv, dout, out_heads, log_heads, gate_away)
    dkv = dkv.reshape(2, group * tok, 2 * k_cols)
    sum_scratch = [pltpu.VMEM(columns, F32)] + [pltpu.VMEM(columns, BF16)] * 3
    sum_scratch.append(pltpu.SemaphoreType.DMA((3,)))
    own_out = dot32(out_heads.reshape(group * tok, q_cols), square_attn, ((0,), (0,))).astype(BF16)
    other_dkv, gate_parts = comm_call(
        dkeys_kernel,
        7,
        [dkv, gate_own.reshape((hi_n,) + columns), gate_dp, gate_hi, up_dp],
        [(dkv.shape[1:], BF16), (columns, BF16)],
        sems(1) + swap_scratch((rows_w, ff_part)) + sum_scratch,
        "dkeys",
    )
    grad_first, head_grads = project_back(
        hi_index,
        dq.reshape(group * tok, q_cols),
        dkv[0],
        other_dkv,
        normed_one,
        qkv_weight,
        tables,
        up_hi,
        unit,
    )
    head_grads = head_grads.reshape(dp_n, every // dp_n, rows_w, head_wide)
    with_out = dp_n == 2 and rows_w * hi_n * lo_n == q_cols
    arrays = [grad_first.reshape(group, tok, width), head_grads]
    arrays += [up_own.reshape((hi_n,) + columns), up_dp, up_hi, squares]
    shapes = [
        ((tok, width), F32),
        (head_grads.shape[1:], BF16),
        (columns, BF16),
        ((every, 8, 128), F32),
    ]
    scratch = scatter_scratch(tok, width) + sems(every // dp_n - 1) + sems(every - 1)
    scratch += [pltpu.SemaphoreType.DMA((2,)), pltpu.VMEM(head_grads.shape[1:], BF16)]
    scratch += [pltpu.VMEM((dp_n - 1,) + head_grads.shape[1:], BF16)]
    scratch += [pltpu.VMEM(head_grads.shape[1:], BF16), pltpu.SemaphoreType.DMA((2, dp_n - 1))]
    scratch += swap_scratch((rows_w, ff_part)) + sum_scratch
    if with_out:
        arrays.append(own_out.reshape(hi_n, lo_n, rows_w, width))
        shapes.append(((hi_n, rows_w, width), BF16))
        scratch += sems(5) + [pltpu.SemaphoreType.DMA((2,))]
        scratch += [pltpu.VMEM((hi_n, lo_n, rows_w, width), BF16)] * 3
    grad_first, head_grads, up_parts, squares, *outs = pl.pallas_call(
        functools.partial(close_kernel, with_out),
        in_specs=[anywhere] * len(arrays),
        out_specs=[pl.BlockSpec(memory_space=pltpu.VMEM)] + [anywhere] * (len(shapes) - 1),
        out_shape=[jax.ShapeDtypeStruct(shape, dtype) for shape, dtype in shapes],
        scratch_shapes=scratch,
        compiler_params=pltpu.CompilerParams(
            collective_id=8, has_side_effects=True, vmem_limit_bytes=VMEM_LIMIT
        ),
        cost_estimate=pl.CostEstimate(flops=0, bytes_accessed=120_000_000, transcendentals=0),
        name="close",
    )(*arrays)
    mse_loss = jnp.sum(squares[:, 0, 0]) / (width * valid_count)
    if with_out and units_w % 128 == 0 and 2 * rows_w == 128:
        shape = lambda *dims: jax.ShapeDtypeStruct(dims, F32)
        grads = pl.pallas_call(
            functools.partial(final_kernel, key_head, ff_places, units_w),
            out_shape=[
                shape(tok, width),
                shape(*w_query.shape),
                shape(*key_projection.shape),
                shape(*value_projection.shape),
                shape(rows_w, 1),
                shape(*w_gate.shape),
                shape(*w_up.shape),
                shape(rows_w, 1),
                shape(*w_out.shape),
                shape(*w_down.shape),
            ],
            compiler_params=params,
            name="final",
        )(
            grad_first,
            grad_middle,
            hidden[0],
            gain_one,
            head_grads,
            w_query,
            key_projection,
            value_projection,
            gate_parts,
            up_parts,
            w_gate,
            w_up,
            small,
            outs[0],
            down_sum,
        )
        return (
            result.astype(BF16)[None],
            mse_loss,
            grads[0][None],
            grads[4][:, 0],
            *grads[1:4],
            grads[8],
            grads[7][:, 0],
            grads[5],
            grads[6],
            grads[9],
        )
    if with_out:
        grad_out = jnp.sum(outs[0].astype(F32), axis=0)
    else:
        own_head = lo * blk_n + blk
        spread = jnp.where((jnp.arange(group) == own_head)[:, None, None], own_out[None], 0)
        grad_out = lax.psum_scatter(
            spread.reshape(width, width), ALL, scatter_dimension=0, tiled=True
        ).astype(F32)
    grad_first = grad_first * gain_one
    normal_one, inverse_one = norm_parts(hidden[0].astype(F32))
    grad_hidden = grad_middle + inverse_one * (
        grad_first - normal_one * jnp.mean(grad_first * normal_one, axis=-1, keepdims=True)
    )
    head_grads = jnp.sum(
        head_grads.reshape(blk_n, hi_n, lo_n, rows_w, head_wide).astype(F32), axis=1
    ).reshape(group, rows_w, head_wide)

    own_one, own_two = attn_gain.astype(F32)[:, None], mlp_gain.astype(F32)[:, None]
    grad_query = head_columns_back(head_grads[:, :, :q_cols])
    grad_key = head_columns_back(head_grads[:, :, q_cols : q_cols + k_cols])
    grad_value = head_columns_back(head_grads[:, :, q_cols + k_cols :])

    def row_sums(*pairs):
        return sum(jnp.sum(w.astype(F32) * g, axis=1, keepdims=True) for w, g in pairs)

    grad_gain_one = (
        row_sums((w_query, grad_query), (key_projection, grad_key), (value_projection, grad_value))
        / own_one
    )
    if units_w % 128 == 0:
        ff_shape = jax.ShapeDtypeStruct(w_gate.shape, F32)
        grad_gate, grad_up, grad_gain_two = pl.pallas_call(
            functools.partial(collect_kernel, ff_places, units_w),
            out_shape=[ff_shape, ff_shape, jax.ShapeDtypeStruct((rows_w, 1), F32)],
            compiler_params=params,
            name="collect",
        )(gate_parts, up_parts, w_gate, w_up, own_two)
    else:
        grad_gate = unit_columns_back(gate_parts.astype(F32))
        grad_up = unit_columns_back(up_parts.astype(F32))
        grad_gain_two = row_sums((w_gate, grad_gate), (w_up, grad_up)) / own_two
    return (
        result.astype(BF16)[None],
        mse_loss,
        grad_hidden[None],
        grad_gain_one[:, 0],
        grad_query,
        grad_key,
        grad_value,
        grad_out,
        grad_gain_two[:, 0],
        grad_gate,
        grad_up,
        down_sum,
    )


def solution(mesh):
    dp_n, blk_n, head_n = (mesh.shape[a] for a in ("dp", "blk", "head"))
    fine = Mesh(mesh.devices.reshape(dp_n, blk_n, 2, head_n // 2), ALL)
    tokens = P("dp", SEQ, None)
    rows, row = P(ALL, None), P(ALL)
    return jax.shard_map(
        shards,
        mesh=fine,
        in_specs=(tokens, tokens, P("dp"), row, rows, rows, rows, rows, row, rows, rows, rows),
        out_specs=(tokens, P(), tokens, row, rows, rows, rows, rows, row, rows, rows, rows),
        check_vma=False,
    )
```

```python
import functools
import math

import jax
import jax.numpy as jnp
import numpy as np
from jax import lax
from jax.experimental import pallas as pl
from jax.experimental.pallas import tpu as pltpu
from jax.sharding import Mesh, PartitionSpec as P

MODEL_WIDTH = 2048
HEAD_SIZE = 64
ROPE_BASE = 10000000.0
NORM_EPS = 1e-05
ATTN_SCALE = 0.015625
RESIDUAL_SCALE = 0.22
MASKED = -1e30

ALL = ("dp", "blk", "hi", "lo")
SQUARE = ("blk", "lo")
COPIES = ("dp", "hi")
SEQ = ("blk", "hi", "lo")
F32 = jnp.float32
BF16 = jnp.bfloat16
VMEM_LIMIT = 56 * 1024 * 1024


def dot32(a, b, dims=((1,), (0,))):
    return lax.dot_general(a, b, (dims, ((), ())), preferred_element_type=F32)


def rope_tables(seq_len):
    half = HEAD_SIZE // 2
    frequency = ROPE_BASE ** (-(np.arange(half) * 2.0) / HEAD_SIZE)
    angles = np.arange(seq_len).astype(np.float32)[:, None] * frequency.astype(np.float32)[None, :]
    cosine, sine = np.cos(angles.astype(np.float64)), np.sin(angles.astype(np.float64))
    none = np.zeros_like(cosine)
    rows = ([cosine] * 4, [-sine, none] * 2, [none, sine] * 2)
    return tuple(np.concatenate(row, axis=1).astype(np.float32) for row in rows)


def table_spec(tok):
    return pl.BlockSpec((tok, 128), lambda i, hi: ((i // 2 * 2 + hi[0]) * 2 + i % 2, 0))


def proj_kernel(hi_ref, rows_ref, gain_ref, weight_ref, cos_ref, sina_ref, sinb_ref, normed_ref, q_ref, kv_ref):
    normed_ref[...] = (norm_parts(rows_ref[...].astype(F32))[0] * gain_ref[...]).astype(BF16)
    made = dot32(normed_ref[...], weight_ref[...])
    cosine, sina, sinb = cos_ref[...], sina_ref[...], sinb_ref[...]
    low = lanes_low(cosine.shape)
    half = HEAD_SIZE // 2
    for part in range(3):
        u = made[:, 128 * part : 128 * part + 128]
        up, down = pltpu.roll(u, 128 - half, 1), pltpu.roll(u, half, 1)
        turned = u * cosine + up * sina + down * sinb
        if part < 2:
            q_ref[:, 128 * part : 128 * part + 128] = (
                turned.astype(BF16).astype(F32) * ATTN_SCALE
            ).astype(BF16)
        else:
            kv_ref[...] = jnp.where(low, turned, u).astype(BF16)


def project(hi, rows, gain, weight, tables, tile):
    count, depth = rows.shape
    wide = weight.shape[1]
    by_rows = lambda cols: pl.BlockSpec((tile, cols), lambda i, hi: (i, 0))
    whole = lambda *shape: pl.BlockSpec(shape, lambda i, hi: (0, 0))
    return pl.pallas_call(
        proj_kernel,
        grid_spec=pltpu.PrefetchScalarGridSpec(
            num_scalar_prefetch=1,
            grid=(count // tile,),
            in_specs=[by_rows(depth), whole(1, depth), whole(depth, wide)] + [table_spec(tile)] * 3,
            out_specs=[by_rows(depth), by_rows(256), by_rows(128)],
        ),
        out_shape=[
            jax.ShapeDtypeStruct((count, depth), BF16),
            jax.ShapeDtypeStruct((count, 256), BF16),
            jax.ShapeDtypeStruct((count, 128), BF16),
        ],
        compiler_params=pltpu.CompilerParams(vmem_limit_bytes=VMEM_LIMIT),
        cost_estimate=pl.CostEstimate(
            flops=2 * count * depth * wide, bytes_accessed=4 * count * depth, transcendentals=0
        ),
        name="project",
    )(hi, rows, gain, weight, *tables)


def proj_back_kernel(
    hi_ref, dq_ref, own_ref, other_ref, rows_ref, weight_ref, cos_ref, sina_ref, sinb_ref, first_ref, drows_ref,
    dweight_ref, made, total,
):
    i = pl.program_id(0)
    cosine, sina, sinb = cos_ref[...], sina_ref[...], sinb_ref[...]
    low = lanes_low(cosine.shape)
    half = HEAD_SIZE // 2
    shared = (own_ref[...].astype(F32) + other_ref[...].astype(F32)).astype(BF16)
    for part in range(3):
        w = (dq_ref[:, 128 * part : 128 * part + 128] if part < 2 else shared).astype(F32)
        turned = w * cosine + pltpu.roll(w * sinb, 128 - half, 1) + pltpu.roll(w * sina, half, 1)
        if part == 2:
            turned = jnp.where(low, turned, w)
        made[:, 128 * part : 128 * part + 128] = turned.astype(BF16)
    drows_ref[...] = dot32(made[...], weight_ref[...], ((1,), (1,))).astype(BF16)
    dweight = dot32(rows_ref[...], made[...], ((0,), (0,)))

    @pl.when(i == 0)
    def _():
        total[...] = dweight

    @pl.when(i > 0)
    def _():
        total[...] += dweight

    @pl.when(i == pl.num_programs(0) - 1)
    def _():
        dweight_ref[...] = total[...].astype(BF16)


def project_back(hi, dq, own, other, rows, weight, tables, first, unit):
    count, width = rows.shape
    wide = weight.shape[1]
    by_rows = lambda cols: pl.BlockSpec((unit, cols), lambda i, hi: (i, 0))
    whole = pl.BlockSpec((width, wide), lambda i, hi: (0, 0))
    table = pl.BlockSpec((unit, 128), lambda i, hi: (2 * i + hi[0], 0))
    return pl.pallas_call(
        proj_back_kernel,
        grid_spec=pltpu.PrefetchScalarGridSpec(
            num_scalar_prefetch=1,
            grid=(count // unit,),
            in_specs=[by_rows(256), by_rows(128), by_rows(128), by_rows(width), whole]
            + [table] * 3
            + [pl.BlockSpec(memory_space=pl.ANY)],
            out_specs=[by_rows(width), whole],
            scratch_shapes=[pltpu.VMEM((unit, wide), BF16), pltpu.VMEM((width, wide), F32)],
        ),
        out_shape=[
            jax.ShapeDtypeStruct((count, width), BF16),
            jax.ShapeDtypeStruct((width, wide), BF16),
        ],
        compiler_params=pltpu.CompilerParams(vmem_limit_bytes=VMEM_LIMIT),
        cost_estimate=pl.CostEstimate(
            flops=4 * count * width * wide, bytes_accessed=24_000_000, transcendentals=0
        ),
        name="project_back",
    )(hi, dq, own, other, rows, weight, *tables, first)


def lanes_low(shape):
    return lax.broadcasted_iota(jnp.int32, shape, 1) < HEAD_SIZE


def both_keys(kv):
    low = lanes_low(kv.shape)
    keys = kv.astype(F32)
    return (
        jnp.where(low, keys, 0.0).astype(BF16),
        jnp.where(low, 0.0, pltpu.roll(keys, HEAD_SIZE, 1)).astype(BF16),
    )


def both_values(kv):
    low = lanes_low(kv.shape)
    values = kv.astype(F32)
    return (
        jnp.where(low, pltpu.roll(values, HEAD_SIZE, 1), 0.0).astype(BF16),
        jnp.where(low, 0.0, values).astype(BF16),
    )


def attend_kernel(scalar_ref, q_ref, kv_ref, other_ref, out_ref, log_ref, keys, values, peak, sums):
    b = pl.program_id(0)
    blocks, unit, _ = q_ref.shape
    units = 2 * blocks
    length, hi = scalar_ref[0], scalar_ref[1]
    n = 2 * b + hi

    @pl.when(b == 0)
    def _():
        def spread(c, carry):
            for j, kv in (
                (2 * c + hi, kv_ref[c]),
                (2 * c + 1 - hi, other_ref[c]),
            ):
                keys[0, j], keys[1, j] = both_keys(kv)
                across = jnp.transpose(kv.astype(F32))[HEAD_SIZE:, :]
                values[j] = jnp.concatenate(
                    [across, jnp.ones((16, unit), F32)], axis=0
                ).astype(BF16)
            return carry

        lax.fori_loop(0, blocks, spread, 0)

    peak[...] = jnp.full_like(peak, MASKED)
    sums[...] = jnp.zeros_like(sums)

    def step(j, masked):
        for h in range(4):
            query = q_ref[b, :, 128 * (h // 2) : 128 * (h // 2) + 128]
            scores = dot32(keys[h % 2, j], query, ((1,), (1,)))
            if masked:
                row = j * unit + lax.broadcasted_iota(jnp.int32, scores.shape, 0)
                col = n * unit + lax.broadcasted_iota(jnp.int32, scores.shape, 1)
                scores = jnp.where((row <= col) & (row < length), scores, MASKED)
            old = peak[h, 0:1, :]
            new = jnp.maximum(old, jnp.max(scores, axis=0, keepdims=True))
            weights = jnp.exp(scores - new).astype(BF16)
            sums[h] = sums[h] * jnp.exp(old - new) + dot32(values[j], weights)
            peak[h, 0:1, :] = new

    first_ragged = units - units // 4

    def plain(j, carry):
        step(j, False)
        return carry

    def checked(j, carry):
        step(j, True)
        return carry

    lax.fori_loop(0, jnp.minimum(n, first_ragged), plain, 0)
    lax.fori_loop(jnp.minimum(n, first_ragged), n + 1, checked, 0)

    for pair in range(2):
        parts = []
        for h in (2 * pair, 2 * pair + 1):
            total = sums[h, HEAD_SIZE : HEAD_SIZE + 1, :]
            parts.append(sums[h, 0:HEAD_SIZE, :] / total)
            log_ref[0, h : h + 1, :] = peak[h, 0:1, :] + jnp.log(total)
        out_ref[0, :, 128 * pair : 128 * pair + 128] = jnp.transpose(
            jnp.concatenate(parts, axis=0)
        ).astype(BF16)


def attend(scalars, q, kv, other):
    blocks, unit, _ = q.shape
    units = 2 * blocks
    whole = lambda a: pl.BlockSpec(a.shape, lambda i: (0,) * a.ndim)
    return pl.pallas_call(
        attend_kernel,
        grid=(blocks,),
        in_specs=[pl.BlockSpec(memory_space=pltpu.SMEM), whole(q), whole(kv), whole(other)],
        out_specs=[
            pl.BlockSpec((1, unit, 256), lambda i: (i, 0, 0)),
            pl.BlockSpec((1, 8, unit), lambda i: (i, 0, 0)),
        ],
        out_shape=[
            jax.ShapeDtypeStruct((blocks, unit, 256), BF16),
            jax.ShapeDtypeStruct((blocks, 8, unit), F32),
        ],
        scratch_shapes=[
            pltpu.VMEM((2, units, unit, 128), BF16),
            pltpu.VMEM((units, HEAD_SIZE + 16, unit), BF16),
            pltpu.VMEM((4, 8, unit), F32),
            pltpu.VMEM((4, HEAD_SIZE + 16, unit), F32),
        ],
        compiler_params=pltpu.CompilerParams(vmem_limit_bytes=VMEM_LIMIT),
        cost_estimate=pl.CostEstimate(
            flops=40_000_000_000, bytes_accessed=8_000_000, transcendentals=20_000_000
        ),
        name="attend",
    )(scalars, q, kv, other)


def attend_back_kernel(
    scalar_ref,
    q_ref,
    kv_ref,
    other_ref,
    dout_ref,
    out_ref,
    log_ref,
    first_ref,
    dq_ref,
    dkv_ref,
    delta,
    dq,
    dk,
    dv,
):
    j = pl.program_id(0)
    blocks, unit, _ = q_ref.shape
    units = 2 * blocks
    length, hi = scalar_ref[0], scalar_ref[1]

    @pl.when(j == 0)
    def _():
        dq[...] = jnp.zeros_like(dq)
        pick = jnp.where(
            lax.broadcasted_iota(jnp.int32, (8, 256), 0)
            == lax.broadcasted_iota(jnp.int32, (8, 256), 1) // HEAD_SIZE,
            1.0,
            0.0,
        )

        def dots(b, carry):
            product = dout_ref[b].astype(F32) * out_ref[b].astype(F32)
            delta[b] = lax.dot_general(
                pick,
                product,
                (((1,), (1,)), ((), ())),
                precision=lax.Precision.HIGHEST,
                preferred_element_type=F32,
            )
            return carry

        lax.fori_loop(0, blocks, dots, 0)

    foreign = jnp.where(j % 2 == hi, 0, 1)
    kv = jnp.where(foreign == 0, kv_ref[j // 2], other_ref[j // 2])
    keys, values = both_keys(kv), both_values(kv)
    dk[...] = jnp.zeros_like(dk)
    dv[...] = jnp.zeros_like(dv)

    def step(b, masked):
        n = 2 * b + hi
        for pair in range(2):
            lanes = slice(128 * pair, 128 * pair + 128)
            query = q_ref[b, :, lanes]
            dout = dout_ref[b, :, lanes]
            dq_part = None
            for side in range(2):
                h = 2 * pair + side
                scores = dot32(keys[side], query, ((1,), (1,)))
                weights = jnp.exp(scores - log_ref[b, h : h + 1, :])
                if masked:
                    row = j * unit + lax.broadcasted_iota(jnp.int32, scores.shape, 0)
                    col = n * unit + lax.broadcasted_iota(jnp.int32, scores.shape, 1)
                    weights = jnp.where((row <= col) & (row < length), weights, 0.0)
                dweights = dot32(values[side], dout, ((1,), (1,)))
                dscores = (weights * (dweights - delta[b, h : h + 1, :])).astype(BF16)
                dv[side] += dot32(weights.astype(BF16), dout)
                dk[side] += dot32(dscores, query)
                part = dot32(dscores, keys[side], ((0,), (0,)))
                dq_part = part if dq_part is None else dq_part + part
            dq[b, :, lanes] += dq_part

    first_ragged = units - units // 4

    def plain(b, carry):
        step(b, False)
        return carry

    def checked(b, carry):
        step(b, True)
        return carry

    first = (j + 1 - hi) // 2
    masked_until = jnp.where(j >= first_ragged, blocks, jnp.where(foreign == 0, first + 1, first))
    lax.fori_loop(first, masked_until, checked, 0)
    lax.fori_loop(masked_until, blocks, plain, 0)

    low = lanes_low((unit, 128))
    dkey = dk[0] + pltpu.roll(dk[1], HEAD_SIZE, 1)
    dvalue = pltpu.roll(dv[0], HEAD_SIZE, 1) + dv[1]
    dkv_ref[foreign, j // 2] = jnp.where(low, dkey, dvalue).astype(BF16)

    @pl.when(j == units - 1)
    def _():
        def store(b, carry):
            dq_ref[b] = (dq[b] * ATTN_SCALE).astype(BF16)
            return carry

        lax.fori_loop(0, blocks, store, 0)


def attend_back(scalars, q, kv, other, dout, out, log, first):
    blocks, unit, _ = q.shape
    units = 2 * blocks
    whole = lambda a: pl.BlockSpec(a.shape, lambda i: (0,) * a.ndim)
    dq_shape = jax.ShapeDtypeStruct((blocks, unit, 256), BF16)
    dkv_shape = jax.ShapeDtypeStruct((2, blocks, unit, 128), BF16)
    return pl.pallas_call(
        attend_back_kernel,
        grid=(units,),
        in_specs=[
            pl.BlockSpec(memory_space=pltpu.SMEM),
            whole(q),
            whole(kv),
            whole(other),
            whole(dout),
            whole(out),
            whole(log),
            pl.BlockSpec(memory_space=pl.ANY),
        ],
        out_specs=[whole(dq_shape), whole(dkv_shape)],
        out_shape=[dq_shape, dkv_shape],
        scratch_shapes=[
            pltpu.VMEM((blocks, 8, unit), F32),
            pltpu.VMEM((blocks, unit, 256), F32),
            pltpu.VMEM((2, unit, 128), F32),
            pltpu.VMEM((2, unit, 128), F32),
        ],
        compiler_params=pltpu.CompilerParams(vmem_limit_bytes=VMEM_LIMIT),
        cost_estimate=pl.CostEstimate(
            flops=60_000_000_000, bytes_accessed=10_000_000, transcendentals=20_000_000
        ),
        name="attend_back",
    )(scalars, q, kv, other, dout, out, log, first)


PIECES = 4
MESH_ID = pl.DeviceIdType.MESH


def square_places():
    blk, lo = lax.axis_index("blk"), lax.axis_index("lo")
    mate, side = blk + 1 - 2 * (blk % 2), (blk + 2) % 4
    return blk, lo, mate, side


def greet(ids):
    barrier = pltpu.get_barrier_semaphore()
    for one in ids:
        pl.semaphore_signal(barrier, inc=1, device_id=one, device_id_type=MESH_ID)
    pl.semaphore_wait(barrier, len(ids))


def remote(source, target, send, recv, to):
    copy = pltpu.make_async_remote_copy(
        src_ref=source,
        dst_ref=target,
        send_sem=send,
        recv_sem=recv,
        device_id=to,
        device_id_type=MESH_ID,
    )
    copy.start()
    return copy


def local_copy(source, target, sem):
    copy = pltpu.make_async_copy(source, target, sem)
    copy.start()
    return copy


class Carried:
    def __init__(self, source, target, held, sem):
        self.held, self.target, self.sem = held, target, sem
        self.copy = local_copy(source, held, sem)

    def turn(self):
        self.copy.wait()
        self.copy = local_copy(self.held, self.target, self.sem)

    def wait(self):
        self.copy.wait()


def finish(copies):
    for copy in copies:
        if isinstance(copy, Carried):
            copy.turn()
    for copy in copies:
        copy.wait()


def square_peers():
    blk, lo = lax.axis_index("blk"), lax.axis_index("lo")
    mine = blk * 2 + lo
    others = [lax.rem(mine + d, 8) for d in range(1, 8)]
    return mine, others, [{"blk": o // 2, "lo": lax.rem(o, 2)} for o in others]


def other_hi():
    return {"hi": 1 - lax.axis_index("hi")}


def dp_peers():
    dp, dp_n = lax.axis_index("dp"), lax.axis_size("dp")
    return [{"dp": lax.rem(dp + d, dp_n)} for d in range(1, dp_n)]


def every_peer():
    sizes = [lax.axis_size(a) for a in ALL]
    places = [lax.axis_index(a) for a in ALL]
    found = []
    for k in range(1, math.prod(sizes)):
        to, rest = {}, k
        for a, size, place in reversed(list(zip(ALL, sizes, places))):
            to[a] = lax.rem(place + rest % size, size)
            rest //= size
        found.append(to)
    return found


def gather_begin(rows_ref, out_ref, send, recv, local, held):
    blk, lo, mate, side = square_places()
    slot = lambda b, l: b * 2 + l
    mine = slot(blk, lo)
    to_mate, to_side, to_next = {"blk": mate}, {"blk": side}, {"lo": 1 - lo}
    step = rows_ref.shape[0] // PIECES

    def push(source, place, piece, kind, to):
        target = out_ref.at[place, pl.ds(piece * step, step)]
        return remote(source, target, send.at[kind, piece], recv.at[kind, piece], to)

    own = Carried(rows_ref, out_ref.at[mine], held, local)
    piece_of = lambda p: rows_ref.at[pl.ds(p * step, step)]
    came = lambda place, p: out_ref.at[place, pl.ds(p * step, step)]
    side_order, next_order = (2, 3, 0, 1), (0, 1, 2, 3)
    by_side, by_next, by_mate, across = {}, {}, [], {}
    for k in range(PIECES):
        p, q = side_order[k], next_order[k]
        by_side[p] = push(piece_of(p), mine, p, 0, to_side)
        by_next[q] = push(piece_of(q), mine, q, 1, to_next)
    for p in range(PIECES):
        by_mate.append(push(piece_of(p), mine, p, 3, to_mate))

    def end(between=lambda k: None):
        own.turn()
        from_side, from_next, from_across = slot(side, lo), slot(blk, 1 - lo), slot(side, 1 - lo)
        for k in range(PIECES):
            p, q = side_order[k], next_order[k]
            by_side[p].wait_recv()
            if p >= 2:
                across[p] = push(came(from_side, p), from_side, p, 2, to_next)
            by_mate.append(push(came(from_side, p), from_side, p, 4, to_mate))
            by_next[q].wait_recv()
            if q < 2:
                across[q] = push(came(from_next, q), from_next, q, 2, to_side)
            by_mate.append(push(came(from_next, q), from_next, q, 5, to_mate))
            between(k)
        for p in (0, 2, 1, 3):
            across[p].wait_recv()
            by_mate.append(push(came(from_across, p), from_across, p, 6, to_mate))
            between(PIECES + p)
        for copy in by_mate:
            copy.wait()
        for copies in (by_side, by_next, across):
            for copy in copies.values():
                copy.wait_send()
        own.wait()

    return end


def gather_scratch(tok, width):
    return [
        pltpu.SemaphoreType.DMA((7, PIECES)),
        pltpu.SemaphoreType.DMA((7, PIECES)),
        pltpu.SemaphoreType.DMA,
        pltpu.VMEM((tok, width), BF16),
    ]


def sems(count):
    return [pltpu.SemaphoreType.DMA((count,))] * 2


def swap_scratch(part):
    return sems(7) + [pltpu.SemaphoreType.DMA, pltpu.VMEM(part, BF16)]


def square_greeting():
    blk, lo, mate, side = square_places()
    return [{"blk": mate}, {"blk": side}, {"lo": 1 - lo}]


def gather_kernel(rows_ref, out_ref, send, recv, local, held):
    greet(square_greeting())
    gather_begin(rows_ref, out_ref, send, recv, local, held)()


def comm_call(kernel, number, arrays, shapes, scratch, name):
    anywhere = pl.BlockSpec(memory_space=pl.ANY)
    return pl.pallas_call(
        kernel,
        in_specs=[anywhere] * len(arrays),
        out_specs=[anywhere] * len(shapes),
        out_shape=[jax.ShapeDtypeStruct(shape, dtype) for shape, dtype in shapes],
        scratch_shapes=scratch,
        compiler_params=pltpu.CompilerParams(
            collective_id=number, has_side_effects=True, vmem_limit_bytes=VMEM_LIMIT
        ),
        cost_estimate=pl.CostEstimate(flops=0, bytes_accessed=120_000_000, transcendentals=0),
        name=name,
    )(*arrays)


def gather_square(rows, number):
    tok, width = rows.shape
    (out,) = comm_call(
        gather_kernel,
        number,
        [rows],
        [((8, tok, width), rows.dtype)],
        gather_scratch(tok, width),
        "gather_square",
    )
    return out.reshape(8 * tok, width)


def swap_begin(parts_ref, out_ref, send, recv, local, held):
    mine, others, ids = square_peers()
    own = Carried(parts_ref.at[mine], out_ref.at[mine], held, local)
    copies = [
        remote(parts_ref.at[o], out_ref.at[mine], send.at[d], recv.at[d], to)
        for d, (o, to) in enumerate(zip(others, ids))
    ]
    return copies + [own]


def dp_begin(pieces, out_ref, send, recv, local, held, first=0):
    dp = lax.axis_index("dp")
    copies = []
    for k, (place, ref) in enumerate(pieces, first):
        copies.append(Carried(ref, out_ref.at[dp, place], held.at[k], local.at[k]))
        for d, to in enumerate(dp_peers()):
            n = 2 * d + k
            copies.append(remote(ref, out_ref.at[dp, place], send.at[n], recv.at[n], to))
    return copies


def device_place():
    mine = 0
    for a in ALL:
        mine = mine * lax.axis_size(a) + lax.axis_index(a)
    return mine


def seq_peers():
    sizes = [lax.axis_size(a) for a in SEQ]
    places = [lax.axis_index(a) for a in SEQ]
    found = []
    for k in range(1, math.prod(sizes)):
        to, source, digits, rest = {}, 0, [], k
        for size in reversed(sizes):
            digits.append(rest % size)
            rest //= size
        for a, size, place, digit in zip(SEQ, sizes, places, reversed(digits)):
            to[a] = lax.rem(place + digit, size)
            source = source * size + lax.rem(place + size - digit, size)
        found.append((to, source))
    return found


def seq_place(to):
    place = 0
    for a in SEQ:
        place = place * lax.axis_size(a) + to[a]
    return place


def open_kernel(
    rows_ref, heads_ref, small_ref, wout_ref, out_ref, weight_ref, smalls_ref, wouts_ref, g_send, g_recv,
    g_local, g_held, w_send, w_recv, d_send, d_recv, s_send, s_recv, o_send, o_recv, local, w_held, o_held,
):
    blk, hi, lo = (lax.axis_index(a) for a in SEQ)
    mine = device_place()
    peers = every_peer()
    greet(peers)
    copies = [
        Carried(heads_ref.at[blk * 2 + lo], weight_ref.at[mine], w_held, local.at[0]),
        local_copy(small_ref, smalls_ref.at[mine], local.at[1]),
        Carried(wout_ref, wouts_ref.at[hi, lo], o_held, local.at[2]),
    ]
    for k, to in enumerate(peers):
        copies.append(remote(small_ref, smalls_ref.at[mine], s_send.at[k], s_recv.at[k], to))
    end = gather_begin(rows_ref, out_ref, g_send, g_recv, g_local, g_held)
    wout = remote(wout_ref, wouts_ref.at[hi, lo], o_send.at[0], o_recv.at[0], other_hi())
    next_lo = {"lo": 1 - lo}
    copies.append(remote(wout_ref, wouts_ref.at[hi, lo], o_send.at[1], o_recv.at[1], next_lo))
    dp, seq = lax.axis_index("dp"), seq_peers()
    seq_n = len(seq) + 1
    straight = []
    for k, (to, source) in enumerate(seq):
        part = heads_ref.at[to["blk"] * 2 + to["lo"]]
        straight.append(remote(part, weight_ref.at[mine], w_send.at[k], w_recv.at[k], to))

    def hand_on(part, place, k):
        for d, to in enumerate(dp_peers()):
            n = d * seq_n + k
            copies.append(remote(part, weight_ref.at[place], d_send.at[n], d_recv.at[n], to))

    hand_on(heads_ref.at[blk * 2 + lo], mine, seq_n - 1)

    def pass_on(turn):
        for k, (to, source) in enumerate(seq):
            if k * 2 * PIECES // len(seq) == turn:
                straight[k].wait()
                place = dp * seq_n + source
                hand_on(weight_ref.at[place], place, k)

    end(pass_on)
    wout.wait()
    there = wouts_ref.at[1 - hi, lo]
    copies.append(remote(there, there, o_send.at[2], o_recv.at[2], next_lo))
    finish(copies)


def keys_kernel(
    kv_ref, gate_ref, up_ref, down_ref, other_ref, gates_ref, ups_ref, downs_ref, k_send, k_recv, g_send,
    g_recv, g_local, g_held, u_send, u_recv, u_local, u_held, d_send, d_recv,
):
    greet(square_peers()[2] + [other_hi()] + dp_peers())
    copies = [remote(kv_ref, other_ref, k_send.at[0], k_recv.at[0], other_hi())]
    for d, to in enumerate(dp_peers()):
        copies.append(remote(down_ref, downs_ref.at[d], d_send.at[d], d_recv.at[d], to))
    copies += swap_begin(gate_ref, gates_ref, g_send, g_recv, g_local, g_held)
    copies += swap_begin(up_ref, ups_ref, u_send, u_recv, u_local, u_held)
    finish(copies)


def heads_kernel(
    heads_ref, gate_ref, gate_other_ref, up_ref, mixed_ref, gates_ref, up_other_ref, m_send, m_recv,
    m_local, m_held, g_send, g_recv, u_send, u_recv, g_local, g_held,
):
    hi = lax.axis_index("hi")
    greet(square_peers()[2] + [other_hi()] + dp_peers())
    copies = swap_begin(heads_ref, mixed_ref, m_send, m_recv, m_local, m_held)
    copies.append(remote(up_ref, up_other_ref, u_send.at[0], u_recv.at[0], other_hi()))
    copies += dp_begin(
        [(hi, gate_ref), (1 - hi, gate_other_ref)], gates_ref, g_send, g_recv, g_local, g_held
    )
    finish(copies)


def rows_kernel(
    rows_ref, up_ref, up_other_ref, down_ref, out_ref, ups_ref, down_other_ref, r_send, r_recv, r_local,
    r_held, u_send, u_recv, d_send, d_recv, u_local, u_held,
):
    hi = lax.axis_index("hi")
    greet(square_greeting() + [other_hi()] + dp_peers())
    end = gather_begin(rows_ref, out_ref, r_send, r_recv, r_local, r_held)
    copies = [remote(down_ref, down_other_ref, d_send.at[0], d_recv.at[0], other_hi())]
    copies += dp_begin(
        [(hi, up_ref), (1 - hi, up_other_ref)], ups_ref, u_send, u_recv, u_local, u_held
    )
    end()
    finish(copies)


def sum_begin(own_ref, got_ref, place, own, got, sem):
    return [
        local_copy(own_ref.at[place], own, sem.at[0]),
        local_copy(got_ref.at[place], got, sem.at[1]),
    ]


def wait_all(copies):
    for copy in copies:
        copy.wait()


def out_back_kernel(
    order, pairs, block, grad_ref, middle_ref, result_ref, gain_ref, weight_ref, gate_ref, gate_got_ref, up_ref,
    up_got_ref, sum_ref, rows_ref, out_ref, gate_away_ref, up_away_ref, weight, work, parts, send, recv, own, got, sem,
    w_sem,
):
    hi = lax.axis_index("hi")
    load = local_copy(weight_ref, weight, w_sem.at[0])
    loads = [
        [local_copy(ref.at[1 - hi], own.at[k], sem.at[k, 0]), local_copy(got_ref, got.at[k], sem.at[k, 1])]
        for k, (ref, got_ref) in enumerate(((gate_ref, gate_got_ref), (up_ref, up_got_ref)))
    ]
    mine, others, ids = square_peers()
    greet(ids)
    reorder(pairs, block, grad_ref, work, lambda v: v)
    normal, inverse = norm_parts(middle_ref[...])
    grad = work[...] * gain_ref[...]
    total = result_ref[...] + inverse * (
        grad - normal * jnp.mean(grad * normal, axis=-1, keepdims=True)
    )
    sum_ref[...] = total
    rows_ref[...] = (RESIDUAL_SCALE * total).astype(BF16)
    load.wait()
    cols = parts.shape[2]

    def make(n, f):
        part = weight[pl.ds(pl.multiple_of(order(f) * cols, cols), cols), :]
        parts[n] = dot32(rows_ref[...], part, ((1,), (1,))).astype(BF16)

    copies = []
    for d, (other, to) in enumerate(zip(others, ids)):
        make(d, other)
        copies.append(remote(parts.at[d], out_ref.at[mine], send.at[d], recv.at[d], to))
    make(7, mine)
    copies.append(local_copy(parts.at[7], out_ref.at[mine], w_sem.at[0]))
    for k, target in enumerate((gate_away_ref, up_away_ref)):
        wait_all(loads[k])
        target[...] = (own[k] + got[k].astype(F32)).astype(BF16)
    wait_all(copies)


def sum_three(place, own_ref, over_dp_ref, over_hi_ref, own, over_dp, over_hi, sem):
    return [
        local_copy(own_ref.at[place], own, sem.at[0]),
        local_copy(over_dp_ref, over_dp, sem.at[1]),
        local_copy(over_hi_ref, over_hi, sem.at[2]),
    ]


def dkeys_kernel(
    dkv_ref, gate_ref, gate_dp_ref, gate_hi_ref, first_ref, other_ref, gates_ref, k_send, k_recv, g_send, g_recv, g_local,
    g_held, own, over_dp, over_hi, made, sem,
):
    hi = lax.axis_index("hi")
    loads = sum_three(hi, gate_ref, gate_dp_ref, gate_hi_ref, own, over_dp, over_hi, sem)
    greet(square_peers()[2] + [other_hi()])
    copies = [remote(dkv_ref.at[1], other_ref, k_send.at[0], k_recv.at[0], other_hi())]
    wait_all(loads)
    made[...] = (own[...] + over_dp[...].astype(F32) + over_hi[...].astype(F32)).astype(BF16)
    copies += swap_begin(made, gates_ref, g_send, g_recv, g_local, g_held)
    finish(copies)


class OwnOut:
    def __init__(self, out_ref, outs_ref, send, recv, local, own, got, made):
        self.outs_ref, self.made, self.send, self.recv, self.local = outs_ref, made, send, recv, local
        self.own, self.got = own, got
        self.dp, self.hi, self.lo = (lax.axis_index(a) for a in ("dp", "hi", "lo"))
        self.load = local_copy(out_ref, own, local.at[0])
        self.over = remote(out_ref, got, send.at[0], recv.at[0], dp_peers()[0])

    def push(self, a, b):
        hi, lo = lax.rem(self.hi + a, 2), lax.rem(self.lo + b, 2)
        return pltpu.make_async_remote_copy(
            src_ref=self.made.at[hi, lo],
            dst_ref=self.outs_ref.at[self.hi],
            send_sem=self.send.at[1 + 2 * a + b],
            recv_sem=self.recv.at[1 + self.hi],
            device_id={"hi": hi, "lo": lo},
            device_id_type=MESH_ID,
        )

    def own_copy(self):
        return pltpu.make_async_copy(
            self.made.at[self.hi, self.lo], self.outs_ref.at[self.hi], self.local.at[1]
        )

    def turn(self):
        self.load.wait()
        self.over.wait()
        self.made[...] = (self.own[...].astype(F32) + self.got[...].astype(F32)).astype(BF16)

        @pl.when(self.dp == self.lo)
        def _():
            for a, b in ((0, 1), (1, 0), (1, 1)):
                self.push(a, b).start()
            self.own_copy().start()

    def wait(self):
        @pl.when(self.dp == self.lo)
        def _():
            for a, b in ((0, 1), (1, 0), (1, 1)):
                self.push(a, b).wait_send()
            self.own_copy().wait()

        for h in range(2):

            @pl.when(jnp.logical_not((h == self.hi) & (self.dp == self.lo)))
            def _(h=h):
                pltpu.make_async_remote_copy(
                    src_ref=self.made.at[0, 0],
                    dst_ref=self.outs_ref.at[h],
                    send_sem=self.send.at[1],
                    recv_sem=self.recv.at[1 + h],
                    device_id={"lo": 1 - self.lo},
                    device_id_type=MESH_ID,
                ).wait_recv()


def close_kernel(with_out, *refs):
    refs = iter(refs)
    take = lambda n: [next(refs) for _ in range(n)]
    parts_ref, heads_ref, up_ref, up_dp_ref, up_hi_ref, square_ref = take(6)
    out_rows_ref = next(refs) if with_out else None
    total_ref, head_ref, ups_ref, squares_ref = take(4)
    outs_ref = next(refs) if with_out else None
    scatter = take(9)
    h_send, h_recv, s_send, s_recv, local, h_own, h_got, h_made, h_sem = take(9)
    swap = take(4)
    own, over_dp, over_hi, made, sem = take(5)
    out_scratch = take(6) if with_out else None
    mine = device_place()
    peers, seq = every_peer(), seq_peers()
    place = seq_place({a: lax.axis_index(a) for a in SEQ})
    loads = scatter_load(parts_ref, scatter)
    hi = lax.axis_index("hi")
    up_loads = sum_three(hi, up_ref, up_dp_ref, up_hi_ref, own, over_dp, over_hi, sem)
    greet(peers)
    copies = [local_copy(square_ref, squares_ref.at[mine], local.at[1])]
    dp = lax.axis_index("dp")
    own_heads = local_copy(heads_ref.at[dp], h_own, local.at[0])
    over_heads = []
    for d, to in enumerate(dp_peers()):
        part = heads_ref.at[to["dp"]]
        over_heads.append(remote(part, h_got.at[d], h_sem.at[0, d], h_sem.at[1, d], to))
    mates = scatter_mates(parts_ref, scatter)
    for k, to in enumerate(peers):
        copies.append(remote(square_ref, squares_ref.at[mine], s_send.at[k], s_recv.at[k], to))

    def send_heads():
        own_heads.wait()
        wait_all(over_heads)
        total = h_own[...].astype(F32)
        for d in range(len(over_heads)):
            total = total + h_got[d].astype(F32)
        h_made[...] = total.astype(BF16)
        copies.append(local_copy(h_made.at[place], head_ref.at[place], local.at[0]))
        for k, (to, source) in enumerate(seq):
            part = h_made.at[seq_place(to)]
            copies.append(remote(part, head_ref.at[place], h_send.at[k], h_recv.at[k], to))

    own_out = OwnOut(out_rows_ref, outs_ref, *out_scratch) if with_out else None
    wait_all(up_loads)
    made[...] = (own[...] + over_dp[...].astype(F32) + over_hi[...].astype(F32)).astype(BF16)
    copies += swap_begin(made, ups_ref, *swap)
    nothing = lambda: None
    work = [nothing, send_heads, nothing, nothing, own_out.turn if with_out else nothing]
    scatter_end_square(loads, mates, total_ref, scatter, work)
    finish(copies)
    if with_out:
        own_out.wait()


def remote_to(source, target, sems_of, kind, piece, to):
    send, recv = sems_of
    return remote(source, target, send.at[kind, piece], recv.at[kind, piece], to)


def scatter_load(parts_ref, scratch):
    mine, local = scratch[0], scratch[8]
    blk, lo, mate, side = square_places()
    places = (side * 2 + 1 - lo, side * 2 + lo, blk * 2 + 1 - lo, blk * 2 + lo)
    return [local_copy(parts_ref.at[p], mine.at[k], local.at[k]) for k, p in enumerate(places)]


def scatter_mates(parts_ref, scratch):
    mates, sems_of = scratch[1], scratch[6:8]
    blk, lo, mate, side = square_places()
    mate_side = (mate + 2) % 4
    places = (mate_side * 2 + 1 - lo, mate_side * 2 + lo, mate * 2 + 1 - lo, mate * 2 + lo)
    step = parts_ref.shape[1] // PIECES
    rows = lambda p: pl.ds(p * step, step)
    orders = ((0, 2, 1, 3), (0, 1, 2, 3), (2, 3, 0, 1), (0, 1, 2, 3))
    return {
        (k, p): remote_to(
            parts_ref.at[places[k], rows(p)], mates.at[k, rows(p)], sems_of, k, p, {"blk": mate}
        )
        for k in range(4)
        for p in orders[k]
    }


def scatter_end_square(loads, from_mate, out_ref, scratch, work=()):
    work = list(work)
    mine, mates, made, got_across, got_side, got_next = scratch[:6]
    sems_of = scratch[6:8]
    blk, lo, mate, side = square_places()
    to_side, to_next = {"blk": side}, {"lo": 1 - lo}
    step = mine.shape[1] // PIECES
    rows = lambda p: pl.ds(p * step, step)

    def summed(k, p):
        from_mate[k, p].wait_recv()
        return mine[k, rows(p), :].astype(F32) + mates[k, rows(p), :].astype(F32)

    sent = {}
    loads[0].wait()
    for p in (0, 2, 1, 3):
        made[0, rows(p), :] = summed(0, p).astype(BF16)
        sent[0, p] = remote_to(
            made.at[0, rows(p)],
            got_across.at[rows(p)],
            sems_of,
            4,
            p,
            to_side if p < 2 else to_next,
        )
    loads[1].wait()
    loads[2].wait()
    for n, (k, p) in enumerate(((1, 0), (2, 2), (1, 1), (2, 3), (1, 2), (2, 0), (1, 3), (2, 1))):
        if work and n % 2 == 0:
            work.pop(0)()
        total = summed(k, p)
        if (k == 1) == (p >= 2):
            sent[0, p].wait_recv()
            total = total + got_across[rows(p), :].astype(F32)
        made[k, rows(p), :] = total.astype(BF16)
        sent[k, p] = remote_to(
            made.at[k, rows(p)],
            (got_side if k == 1 else got_next).at[rows(p)],
            sems_of,
            4 + k,
            p,
            to_side if k == 1 else to_next,
        )
    for one in work:
        one()
    loads[3].wait()
    for p in range(PIECES):
        total = summed(3, p)
        sent[1, p].wait_recv()
        sent[2, p].wait_recv()
        out_ref[rows(p), :] = (
            total + got_side[rows(p), :].astype(F32) + got_next[rows(p), :].astype(F32)
        )
    for copy in from_mate.values():
        copy.wait_send()
    for copy in sent.values():
        copy.wait_send()


def scatter_scratch(tok, width):
    return [
        pltpu.VMEM((4, tok, width), BF16),
        pltpu.VMEM((4, tok, width), BF16),
        pltpu.VMEM((3, tok, width), BF16),
        pltpu.VMEM((tok, width), BF16),
        pltpu.VMEM((tok, width), BF16),
        pltpu.VMEM((tok, width), BF16),
        pltpu.SemaphoreType.DMA((7, PIECES)),
        pltpu.SemaphoreType.DMA((7, PIECES)),
        pltpu.SemaphoreType.DMA((4,)),
    ]


def scatter_kernel(firsts, parts_ref, *refs):
    out_ref, scratch = refs[firsts], refs[firsts + 1 :]
    loads = scatter_load(parts_ref, scratch)
    greet(square_greeting())
    scatter_end_square(loads, scatter_mates(parts_ref, scratch), out_ref, scratch)


def scatter_square(parts, number, *first):
    count, width = parts.shape
    tok = count // 8
    return pl.pallas_call(
        functools.partial(scatter_kernel, len(first)),
        in_specs=[pl.BlockSpec(memory_space=pl.ANY)] * (1 + len(first)),
        out_specs=pl.BlockSpec(memory_space=pltpu.VMEM),
        out_shape=jax.ShapeDtypeStruct((tok, width), F32),
        scratch_shapes=scatter_scratch(tok, width),
        compiler_params=pltpu.CompilerParams(
            collective_id=number, has_side_effects=True, vmem_limit_bytes=VMEM_LIMIT
        ),
        cost_estimate=pl.CostEstimate(flops=0, bytes_accessed=120_000_000, transcendentals=0),
        name="scatter_square",
    )(parts.astype(BF16).reshape(8, tok, width), *first)


class Then:
    def __init__(self, step):
        self.wait = step


def ff_end_kernel(units_ref, down_ref, out_ref, *scratch):
    scratch, (units, down, for_mate, sem) = scratch[:9], scratch[9:]
    mine, mates, sems_of = scratch[0], scratch[1], scratch[6:8]
    loads = [local_copy(down_ref, down, sem.at[0]), local_copy(units_ref, units, sem.at[1])]
    blk, lo, mate, side = square_places()
    mate_side = (mate + 2) % 4
    own_places = (side * 2 + 1 - lo, side * 2 + lo, blk * 2 + 1 - lo, blk * 2 + lo)
    mate_places = (mate_side * 2 + 1 - lo, mate_side * 2 + lo, mate * 2 + 1 - lo, mate * 2 + lo)
    step = units.shape[1] // PIECES
    rows = lambda p: pl.ds(p * step, step)
    orders = ((0, 2, 1, 3), (0, 1, 2, 3), (2, 3, 0, 1), (0, 1, 2, 3))
    from_mate = {}

    def made(place):
        return dot32(units[place], down[...]).astype(BF16)

    def own(k):
        mine[k] = made(own_places[k])

    def other(k):
        for_mate[k] = made(mate_places[k])
        for p in orders[k]:
            from_mate[k, p] = remote_to(
                for_mate.at[k, rows(p)], mates.at[k, rows(p)], sems_of, k, p, {"blk": mate}
            )

    greet(square_greeting())
    wait_all(loads)
    other(0)
    own(0)
    other(1)
    other(2)
    steps = [Then(lambda: None)] + [Then(functools.partial(own, k)) for k in (1, 2, 3)]
    scatter_end_square(steps, from_mate, out_ref, scratch, [functools.partial(other, 3)])


def ff_end(units, down, number):
    count, ff = units.shape
    width = down.shape[1]
    tok = count // 8
    return pl.pallas_call(
        ff_end_kernel,
        in_specs=[pl.BlockSpec(memory_space=pl.ANY)] * 2,
        out_specs=pl.BlockSpec(memory_space=pltpu.VMEM),
        out_shape=jax.ShapeDtypeStruct((tok, width), F32),
        scratch_shapes=scatter_scratch(tok, width)
        + [
            pltpu.VMEM((8, tok, ff), BF16),
            pltpu.VMEM(down.shape, BF16),
            pltpu.VMEM((4, tok, width), BF16),
            pltpu.SemaphoreType.DMA((2,)),
        ],
        compiler_params=pltpu.CompilerParams(
            collective_id=number, has_side_effects=True, vmem_limit_bytes=VMEM_LIMIT
        ),
        cost_estimate=pl.CostEstimate(
            flops=2 * count * ff * width, bytes_accessed=120_000_000, transcendentals=0
        ),
        name="ff_end",
    )(units.reshape(8, tok, ff), down)


def scatter_down_kernel(
    parts_ref, down_ref, got_ref, rows_ref, dgate_ref, dup_ref, out_ref, sum_ref, gate_own_ref, up_own_ref,
    gate_stay_ref, up_stay_ref, gate_got_ref, up_got_ref, *scratch,
):
    scratch, rest = scratch[:9], scratch[9:]
    own, got, away, came, sem, send, recv, left, gate_right, up_right, gate_away, up_away, w_sem = rest
    dp, hi = lax.axis_index("dp"), lax.axis_index("hi")
    part = left.shape[2]
    blocks = ((1 - dp, 1 - hi), (dp, 1 - hi), (1 - dp, hi), (dp, hi))

    def load_left(n):
        d, h = blocks[n]
        cols = pl.ds(pl.multiple_of((d * 2 + h) * part, part), part)
        return local_copy(rows_ref.at[:, cols], left.at[n % 2], w_sem.at[n % 2])

    rights = [local_copy(dgate_ref, gate_right, w_sem.at[2]), local_copy(dup_ref, up_right, w_sem.at[3])]
    lefts = {0: load_left(0), 1: load_left(1)}
    down = sum_begin(down_ref, got_ref, 1 - hi, own, got, sem)
    loads = scatter_load(parts_ref, scratch)
    greet(square_greeting() + [other_hi()] + dp_peers())
    mates = scatter_mates(parts_ref, scratch)
    wait_all(down)
    away[...] = (own[...] + got[...].astype(F32)).astype(BF16)
    over = remote(away, came, send.at[0], recv.at[0], other_hi())
    down = sum_begin(down_ref, got_ref, hi, own, got, sem)
    pairs = []

    def gradient(n, up):
        if not up:
            lefts[n].wait()
        if n == 0:
            rights[up].wait()
        total = dot32(left[n % 2], (up_right if up else gate_right)[...], ((0,), (0,)))
        if n == 0:
            target, got_there = (up_away, up_got_ref) if up else (gate_away, gate_got_ref)
            target[...] = total.astype(BF16)
            pairs.append(remote(target, got_there, send.at[1 + up], recv.at[1 + up], dp_peers()[0]))
        elif n == 2:
            (up_stay_ref if up else gate_stay_ref)[...] = total.astype(BF16)
        else:
            (up_own_ref if up else gate_own_ref)[blocks[n][1]] = total
        if up and n < 2:
            lefts[n + 2] = load_left(n + 2)

    work = [functools.partial(gradient, n, up) for n in range(4) for up in range(2)]
    scatter_end_square(loads, mates, out_ref, scratch, work)
    wait_all(down)
    over.wait()
    sum_ref[...] = own[...] + got[...].astype(F32) + came[...].astype(F32)
    wait_all(pairs)


def scatter_down(parts, number, down, rows, dgate, dup):
    count, width = parts.shape
    tok = count // 8
    part = down[0].shape[1:]
    depth, cols = dgate.shape
    grad = (rows.shape[1] // 4, cols)
    anywhere, inside = pl.BlockSpec(memory_space=pl.ANY), pl.BlockSpec(memory_space=pltpu.VMEM)
    return pl.pallas_call(
        scatter_down_kernel,
        in_specs=[anywhere] * 6,
        out_specs=[inside] * 6 + [anywhere] * 2,
        out_shape=[
            jax.ShapeDtypeStruct((tok, width), F32),
            jax.ShapeDtypeStruct(part, F32),
            jax.ShapeDtypeStruct((2,) + grad, F32),
            jax.ShapeDtypeStruct((2,) + grad, F32),
        ]
        + [jax.ShapeDtypeStruct(grad, BF16)] * 4,
        scratch_shapes=scatter_scratch(tok, width)
        + [pltpu.VMEM(part, F32)]
        + [pltpu.VMEM(part, BF16)] * 3
        + [pltpu.SemaphoreType.DMA((2,))]
        + sems(3)
        + [
            pltpu.VMEM((2, depth, grad[0]), BF16),
            pltpu.VMEM((depth, cols), BF16),
            pltpu.VMEM((depth, cols), BF16),
            pltpu.VMEM(grad, BF16),
            pltpu.VMEM(grad, BF16),
            pltpu.SemaphoreType.DMA((4,)),
        ],
        compiler_params=pltpu.CompilerParams(
            collective_id=number, has_side_effects=True, vmem_limit_bytes=VMEM_LIMIT
        ),
        cost_estimate=pl.CostEstimate(
            flops=4 * depth * cols * rows.shape[1], bytes_accessed=160_000_000, transcendentals=0
        ),
        name="scatter_down",
    )(parts.reshape(8, tok, width), *down, rows, dgate, dup)


def swap_square(blocks):
    return lax.all_to_all(blocks, SQUARE, split_axis=0, concat_axis=0, tiled=True)


def swap_pair(block, axis):
    return lax.ppermute(block, axis, [(0, 1), (1, 0)])


def gather_start(rows, axis):
    if lax.axis_size(axis) != 2:
        return lax.all_gather(rows, axis, axis=0, tiled=False)
    return rows, swap_pair(rows, axis)


def gather_end(parts, axis):
    if lax.axis_size(axis) != 2:
        return parts
    rows, other = parts
    first = lax.axis_index(axis) == 0
    return jnp.stack([jnp.where(first, rows, other), jnp.where(first, other, rows)])


def scatter_start(parts, axis):
    if lax.axis_size(axis) != 2:
        return lax.psum_scatter(parts.astype(BF16), axis, scatter_dimension=0, tiled=False)
    place = lax.axis_index(axis)
    away = lax.dynamic_index_in_dim(parts, 1 - place, 0, False).astype(BF16)
    own = lax.dynamic_index_in_dim(parts, place, 0, False)
    return own, swap_pair(away, axis)


def scatter_end(parts, axis):
    if lax.axis_size(axis) != 2:
        return parts.astype(F32)
    return parts[0] + parts[1].astype(F32)


def by_copy(rows):
    dp_n, hi_n = lax.axis_size("dp"), lax.axis_size("hi")
    return rows.reshape((dp_n, hi_n, rows.shape[0] // (dp_n * hi_n)) + rows.shape[1:])


def total_of(value, axes, count):
    spread = jnp.broadcast_to(value.reshape(1, 1), (count, 1))
    return jnp.sum(lax.all_to_all(spread, axes, split_axis=0, concat_axis=0, tiled=True))


def norm_parts(rows):
    inverse = lax.rsqrt(jnp.mean(rows * rows, axis=-1, keepdims=True) + NORM_EPS)
    return rows * inverse, inverse


def reorder(pairs, block, source, target, cast):
    for at, to in pairs:
        target[:, to * block : to * block + block] = cast(source[:, at * block : at * block + block])


def out_kernel(order, pairs, block, mixed_ref, weight_ref, rows_ref, gain_ref, middle_ref, normed_ref, total):
    f = pl.program_id(0)

    @pl.when(f == 0)
    def _():
        total[...] = jnp.zeros_like(total)

    total[...] += dot32(mixed_ref[0], weight_ref[...])

    @pl.when(f == pl.num_programs(0) - 1)
    def _():
        middle = rows_ref[...].astype(F32) + RESIDUAL_SCALE * total[...]
        middle_ref[...] = middle
        total[...] = norm_parts(middle)[0] * gain_ref[...]
        reorder(pairs, block, total, normed_ref, lambda v: v.astype(BF16))


def out_project(mixed, weight, rows, gain, order, pairs, block):
    group, tok, cols = mixed.shape
    width = weight.shape[1]
    whole = pl.BlockSpec((tok, width), lambda f: (0, 0))
    return pl.pallas_call(
        functools.partial(out_kernel, order, pairs, block),
        grid=(group,),
        in_specs=[
            pl.BlockSpec((1, tok, cols), lambda f: (f, 0, 0)),
            pl.BlockSpec((cols, width), lambda f: (order(f), 0)),
            whole,
            pl.BlockSpec((1, width), lambda f: (0, 0)),
        ],
        out_specs=[whole, whole],
        out_shape=[
            jax.ShapeDtypeStruct((tok, width), F32),
            jax.ShapeDtypeStruct((tok, width), BF16),
        ],
        scratch_shapes=[pltpu.VMEM((tok, width), F32)],
        compiler_params=pltpu.CompilerParams(vmem_limit_bytes=VMEM_LIMIT),
        cost_estimate=pl.CostEstimate(
            flops=2 * tok * width * width, bytes_accessed=16_000_000, transcendentals=0
        ),
        name="out_project",
    )(mixed, weight, rows, gain)


def start_kernel(
    key_head, places, wide, query_ref, key_ref, value_ref, w_gate_ref, w_up_ref, rows_ref, small_ref, wout_ref,
    down_ref, cos_ref, sina_ref, sinb_ref, all_ref, weight_ref, smalls_ref, wouts_ref, gates_ref, ups_ref, downs_ref, other_ref, normed_ref, q_ref, kv_ref, g_send,
    g_recv, g_local, g_held, w_send, w_recv, d_send, d_recv, s_send, s_recv, o_send, o_recv, local, w_held, o_held,
    ga_send, ga_recv, ga_local, ga_held, up_send, up_recv, up_local, up_held, x_send, x_recv, k_send, k_recv, heads_ref,
    gate_ref, up_ref, weight, smalls, gain, chunks, cosines, sinas, sinbs, sem, t_sem,
):
    blk, hi, lo = (lax.axis_index(a) for a in SEQ)
    mine = device_place()
    peers = every_peer()
    unit = chunks.shape[1]
    tables = []
    for b in range(4):
        rows_of = pl.ds(pl.multiple_of((2 * b + hi) * unit, unit), unit)
        for t, (ref, table) in enumerate(((cos_ref, cosines), (sina_ref, sinas), (sinb_ref, sinbs))):
            tables.append(local_copy(ref.at[rows_of], table.at[b], t_sem.at[b, t]))
    deal_heads(key_head, query_ref, key_ref, value_ref, heads_ref)
    greet(peers)
    own_head = Carried(heads_ref.at[blk * 2 + lo], weight_ref.at[mine], w_held, local.at[0])
    small_copies = [local_copy(small_ref, smalls_ref.at[mine], local.at[1])]
    for k, to in enumerate(peers):
        small_copies.append(remote(small_ref, smalls_ref.at[mine], s_send.at[k], s_recv.at[k], to))
    end = gather_begin(rows_ref, all_ref, g_send, g_recv, g_local, g_held)
    dp, seq = lax.axis_index("dp"), seq_peers()
    seq_n = len(seq) + 1
    straight, handed = [], []
    for k, (to, source) in enumerate(seq):
        part = heads_ref.at[to["blk"] * 2 + to["lo"]]
        straight.append(remote(part, weight_ref.at[mine], w_send.at[k], w_recv.at[k], to))

    def hand_on(part, place, k):
        for d, to in enumerate(dp_peers()):
            n = d * seq_n + k
            handed.append(remote(part, weight_ref.at[place], d_send.at[n], d_recv.at[n], to))

    hand_on(heads_ref.at[blk * 2 + lo], mine, seq_n - 1)
    deal_units(places, wide, w_gate_ref, w_up_ref, gate_ref, up_ref)
    copies, wouts = [], []
    next_lo = {"lo": 1 - lo}

    def pass_on(turn):
        for k, (to, source) in enumerate(seq):
            if k * 2 * PIECES // len(seq) == turn:
                straight[k].wait()
                place = dp * seq_n + source
                hand_on(weight_ref.at[place], place, k)
        if turn == PIECES - 1:
            copies.append(Carried(wout_ref, wouts_ref.at[hi, lo], o_held, local.at[2]))
            wouts.append(
                remote(wout_ref, wouts_ref.at[hi, lo], o_send.at[0], o_recv.at[0], other_hi())
            )
            copies.append(
                remote(wout_ref, wouts_ref.at[hi, lo], o_send.at[1], o_recv.at[1], next_lo)
            )
            copies.extend(swap_begin(gate_ref, gates_ref, ga_send, ga_recv, ga_local, ga_held))
            copies.extend(swap_begin(up_ref, ups_ref, up_send, up_recv, up_local, up_held))

    end(pass_on)
    own_head.turn()
    wait_all(small_copies)
    load_smalls = local_copy(smalls_ref, smalls, sem.at[2])
    load_rows = lambda b: local_copy(all_ref.at[pl.ds(2 * b, 2)], chunks_of(chunks, b), sem.at[b % 2])
    loads = [load_rows(0), load_rows(1)]
    own_head.wait()
    wait_all(handed)
    load_weight = local_copy(weight_ref, weight, sem.at[3])
    for d, to in enumerate(dp_peers()):
        copies.append(remote(down_ref, downs_ref.at[d], x_send.at[d], x_recv.at[d], to))
    load_smalls.wait()
    low = lanes_low((1, 128))
    for j in range(smalls.shape[0] // 2):
        gain[:, 128 * j : 128 * j + 128] = jnp.where(
            low, smalls[2 * j, 0:1, :], pltpu.roll(smalls[2 * j + 1, 0:1, :], HEAD_SIZE, 1)
        )
    load_weight.wait()
    wait_all(tables)
    width = gain.shape[1]
    half = HEAD_SIZE // 2
    low = lanes_low((unit, 128))
    for b in range(4):
        here = slice(b * unit, b * unit + unit)
        loads[b].wait()
        rows = chunks[b % 2].astype(F32)
        normed_ref[here, :] = (norm_parts(rows)[0] * gain[...]).astype(BF16)
        if b + 2 < 4:
            loads.append(load_rows(b + 2))
        made = dot32(normed_ref[here, :], weight[...].reshape(width, -1))
        cosine, sina, sinb = cosines[b], sinas[b], sinbs[b]
        for part in range(3):
            u = made[:, 128 * part : 128 * part + 128]
            up, down = pltpu.roll(u, 128 - half, 1), pltpu.roll(u, half, 1)
            turned = u * cosine + up * sina + down * sinb
            if part < 2:
                q_ref[here, 128 * part : 128 * part + 128] = (
                    turned.astype(BF16).astype(F32) * ATTN_SCALE
                ).astype(BF16)
            else:
                kv_ref[here, :] = jnp.where(low, turned, u).astype(BF16)
        piece = pl.ds(b * unit, unit)
        copies.append(
            remote(kv_ref.at[piece], other_ref.at[piece], k_send.at[b], k_recv.at[b], other_hi())
        )
        if b == 2:
            wouts[0].wait()
            there = wouts_ref.at[1 - hi, lo]
            copies.append(remote(there, there, o_send.at[2], o_recv.at[2], next_lo))
    finish(copies)


def chunks_of(chunks, b):
    return chunks.at[b % 2].reshape(2, chunks.shape[1] // 2, chunks.shape[2])


def through_start(key_head, places, wide_w, heads_shape, part_shape, weights, rows, small, wout, down, tables):
    tok, width = rows.shape
    rows_w = wout.shape[0]
    part = part_shape[1:]
    dp_n, hi_n, lo_n = (lax.axis_size(a) for a in ("dp", "hi", "lo"))
    every = dp_n * hi_n * lo_n * lax.axis_size("blk")
    wide = heads_shape[2]
    anywhere, inside = pl.BlockSpec(memory_space=pl.ANY), pl.BlockSpec(memory_space=pltpu.VMEM)
    shapes = [
        ((8, tok, width), BF16),
        ((every, rows_w, wide), BF16),
        ((every, 8, 128), F32),
        ((hi_n, lo_n, rows_w, width), BF16),
        (part_shape, BF16),
        (part_shape, BF16),
        ((dp_n - 1,) + down.shape, BF16),
        ((8 * tok, 128), BF16),
        ((8 * tok, width), BF16),
        ((8 * tok, 256), BF16),
        ((8 * tok, 128), BF16),
    ]
    return pl.pallas_call(
        functools.partial(start_kernel, key_head, places, wide_w),
        in_specs=[inside] * 5 + [anywhere] * 7,
        out_specs=[anywhere] * 8 + [inside] * 3,
        out_shape=[jax.ShapeDtypeStruct(shape, dtype) for shape, dtype in shapes],
        scratch_shapes=gather_scratch(tok, width)
        + sems(every // dp_n - 1)
        + sems((dp_n - 1) * every // dp_n)
        + sems(every - 1)
        + sems(3)
        + [
            pltpu.SemaphoreType.DMA((3,)),
            pltpu.VMEM((rows_w, wide), BF16),
            pltpu.VMEM((rows_w, width), BF16),
        ]
        + swap_scratch(part)
        + swap_scratch(part)
        + sems(dp_n - 1)
        + sems(4)
        + [
            pltpu.VMEM(heads_shape, BF16),
            pltpu.VMEM(part_shape, BF16),
            pltpu.VMEM(part_shape, BF16),
            pltpu.VMEM((every, rows_w, wide), BF16),
            pltpu.VMEM((every, 8, 128), F32),
            pltpu.VMEM((1, width), F32),
            pltpu.VMEM((2, 2 * tok, width), BF16),
        ]
        + [pltpu.VMEM((4, 2 * tok, 128), F32)] * 3
        + [pltpu.SemaphoreType.DMA((4,)), pltpu.SemaphoreType.DMA((4, 3))],
        compiler_params=pltpu.CompilerParams(
            collective_id=11, has_side_effects=True, vmem_limit_bytes=VMEM_LIMIT
        ),
        cost_estimate=pl.CostEstimate(
            flops=16 * tok * width * wide, bytes_accessed=250_000_000, transcendentals=0
        ),
        name="start",
    )(*weights, rows, small, wout, down, *tables)


def middle_kernel(
    order, pairs, block, heads_ref, gate_ref, gate_other_ref, up_ref, down_ref, weight_ref, rows_ref, gain_ref,
    out_ref, middle_ref, gates_ref, ups_ref, down_other_ref, up_other_ref, made_ref, m_send, m_recv, m_local,
    m_held, g_send, g_recv, g_local, g_held, u_send, u_recv, u_local, u_held, o_send, o_recv, r_send, r_recv,
    r_local, r_held, mixed, weight, rows, normed, total, gate_weight, chunks, sem,
):
    hi = lax.axis_index("hi")
    loads = [local_copy(weight_ref, weight, sem.at[0]), local_copy(rows_ref, rows, sem.at[1])]
    mine, others, ids = square_peers()
    greet(ids + [other_hi()] + dp_peers())
    heads = swap_begin(heads_ref, mixed, m_send, m_recv, m_local, m_held)
    up_over = remote(up_ref, up_other_ref, o_send.at[0], o_recv.at[0], other_hi())
    gates = dp_begin([(hi, gate_ref), (1 - hi, gate_other_ref)], gates_ref, g_send, g_recv, g_local, g_held)
    copies = dp_begin([(hi, up_ref)], ups_ref, u_send, u_recv, u_local, u_held)
    wait_all(loads)
    cols = mixed.shape[2]

    def add(f):
        g = order(f)
        part = weight[pl.ds(pl.multiple_of(g * cols, cols), cols), :]
        return dot32(mixed[f], part)

    heads[7].turn()
    heads[7].wait()
    total[...] = add(mine)
    for d in range(7):
        heads[d].wait_recv()
        total[...] += add(lax.rem(mine + 7 - d, 8))
    middle = rows[...].astype(F32) + RESIDUAL_SCALE * total[...]
    middle_ref[...] = middle
    total[...] = norm_parts(middle)[0] * gain_ref[...]
    reorder(pairs, block, total, normed, lambda v: v.astype(BF16))
    end = gather_begin(normed, out_ref, r_send, r_recv, r_local, r_held)

    def more(turn):
        if turn == PIECES - 1:
            up_over.wait()
            copies.append(remote(down_ref, down_other_ref, o_send.at[1], o_recv.at[1], other_hi()))
            copies.extend(
                dp_begin([(1 - hi, up_other_ref)], ups_ref, u_send, u_recv, u_local, u_held, 1)
            )

    end(more)
    finish(gates)
    step = 2
    load_gate = local_copy(gates_ref, gate_weight, sem.at[0])
    load_rows = lambda n: local_copy(out_ref.at[pl.ds(n * step, step)], chunks.at[n % 2], sem.at[1 + n % 2])
    loads = [load_rows(0), load_rows(1)]
    load_gate.wait()
    tok, width = rows.shape
    for n in range(8 // step):
        loads[n].wait()
        made_ref[n * step * tok : (n + 1) * step * tok, :] = dot32(
            chunks[n % 2].reshape(step * tok, width), gate_weight[...].reshape(width, -1)
        )
        if n + 2 < 8 // step:
            loads.append(load_rows(n + 2))
    for d in range(7):
        heads[d].wait_send()
    finish(copies)


def through_middle(heads, gate, gate_other, up, down, weight, rows, gain, order, pairs, block):
    group, tok, cols = heads.shape
    width = weight.shape[1]
    part_rows, ff_part = up.shape
    dp_n = lax.axis_size("dp")
    anywhere, inside = pl.BlockSpec(memory_space=pl.ANY), pl.BlockSpec(memory_space=pltpu.VMEM)
    dp_part = sems(2 * (dp_n - 1)) + [
        pltpu.SemaphoreType.DMA((2,)),
        pltpu.VMEM((2, part_rows, ff_part), BF16),
    ]
    spread = (dp_n, 2, part_rows, ff_part)
    return pl.pallas_call(
        functools.partial(middle_kernel, order, pairs, block),
        in_specs=[anywhere] * 7 + [inside],
        out_specs=[anywhere, inside, anywhere, anywhere, anywhere, anywhere, inside],
        out_shape=[
            jax.ShapeDtypeStruct((group, tok, width), BF16),
            jax.ShapeDtypeStruct((tok, width), F32),
            jax.ShapeDtypeStruct(spread, BF16),
            jax.ShapeDtypeStruct(spread, BF16),
            jax.ShapeDtypeStruct(down.shape, BF16),
            jax.ShapeDtypeStruct(up.shape, BF16),
            jax.ShapeDtypeStruct((group * tok, ff_part), F32),
        ],
        scratch_shapes=swap_scratch((tok, cols))
        + dp_part
        + dp_part
        + sems(2)
        + gather_scratch(tok, width)
        + [
            pltpu.VMEM((group, tok, cols), BF16),
            pltpu.VMEM(weight.shape, BF16),
            pltpu.VMEM((tok, width), BF16),
            pltpu.VMEM((tok, width), BF16),
            pltpu.VMEM((tok, width), F32),
            pltpu.VMEM(spread, BF16),
            pltpu.VMEM((2, 2, tok, width), BF16),
            pltpu.SemaphoreType.DMA((3,)),
        ],
        compiler_params=pltpu.CompilerParams(
            collective_id=10, has_side_effects=True, vmem_limit_bytes=VMEM_LIMIT
        ),
        cost_estimate=pl.CostEstimate(
            flops=2 * group * tok * width * ff_part, bytes_accessed=250_000_000, transcendentals=0
        ),
        name="middle",
    )(heads, gate, gate_other, up, down, weight, rows, gain)


def weight_grad_kernel(dp_ref, left_ref, right_ref, first_ref, away_ref, own_ref):
    i = pl.program_id(0)
    total = dot32(left_ref[...], right_ref[...], ((0,), (0,)))

    @pl.when(i < 2)
    def _():
        away_ref[0] = total.astype(BF16)

    @pl.when(i >= 2)
    def _():
        own_ref[0] = total


def weight_grad_start(left, right, first):
    dp_n, hi_n = lax.axis_size("dp"), lax.axis_size("hi")
    depth, rows = left.shape
    cols = right.shape[1]
    if dp_n != 2:
        sums = scatter_start(by_copy(dot32(left, right, ((0,), (0,)))), "dp")
        return sums.astype(F32), jnp.zeros(sums.shape, BF16)
    part = rows // (dp_n * hi_n)
    place = lax.axis_index("dp").astype(jnp.int32).reshape(1)
    away, own = pl.pallas_call(
        weight_grad_kernel,
        grid_spec=pltpu.PrefetchScalarGridSpec(
            num_scalar_prefetch=1,
            grid=(4,),
            in_specs=[
                pl.BlockSpec(
                    (depth, part),
                    lambda i, dp: (0, jnp.where(i < 2, 2 * (1 - dp[0]) + i, 2 * dp[0] + i - 2)),
                ),
                pl.BlockSpec((depth, cols), lambda i, dp: (0, 0)),
                pl.BlockSpec(memory_space=pl.ANY),
            ],
            out_specs=[
                pl.BlockSpec((1, part, cols), lambda i, dp: (jnp.minimum(i, 1), 0, 0)),
                pl.BlockSpec((1, part, cols), lambda i, dp: (jnp.maximum(i - 2, 0), 0, 0)),
            ],
        ),
        out_shape=[
            jax.ShapeDtypeStruct((2, part, cols), BF16),
            jax.ShapeDtypeStruct((2, part, cols), F32),
        ],
        compiler_params=pltpu.CompilerParams(vmem_limit_bytes=VMEM_LIMIT),
        cost_estimate=pl.CostEstimate(
            flops=2 * depth * rows * cols, bytes_accessed=24_000_000, transcendentals=0
        ),
        name="weight_grad",
    )(place, left, right, first)
    return own, away


def ff_back_kernel(
    tile, grad_ref, gate_slope_ref, up_slope_ref, gate_ref, up_ref, down_ref, first_ref, dgate_ref, dup_ref,
    out_ref, total,
):
    total[...] = jnp.zeros_like(total)

    def step(t, carry):
        cols = pl.ds(pl.multiple_of(t * tile, tile), tile)
        dunits = dot32(grad_ref[...], down_ref[cols, :], ((1,), (1,)))
        dgate = (dunits * gate_slope_ref[:, cols].astype(F32)).astype(BF16)
        dup = (dunits * up_slope_ref[:, cols].astype(F32)).astype(BF16)
        dgate_ref[:, cols] = dgate
        dup_ref[:, cols] = dup
        total[...] += dot32(dgate, gate_ref[:, cols], ((1,), (1,))) + dot32(
            dup, up_ref[:, cols], ((1,), (1,))
        )
        return carry

    lax.fori_loop(0, down_ref.shape[0] // tile, step, 0)
    out_ref[...] = total[...].astype(BF16)


def ff_back(grad, gate_slope, up_slope, gate_weight, up_weight, down_weight, first, tok):
    count, width = grad.shape
    ff = down_weight.shape[0]
    rows = lambda cols: pl.BlockSpec((tok, cols), lambda i: (i, 0))
    whole = lambda a: pl.BlockSpec(a.shape, lambda i: (0, 0), pipeline_mode=pl.Buffered(1))
    return pl.pallas_call(
        functools.partial(ff_back_kernel, ff),
        grid=(count // tok,),
        in_specs=[
            rows(width),
            rows(ff),
            rows(ff),
            whole(gate_weight),
            whole(up_weight),
            whole(down_weight),
            pl.BlockSpec(memory_space=pl.ANY),
        ],
        out_specs=[rows(ff), rows(ff), rows(width)],
        out_shape=[
            jax.ShapeDtypeStruct((count, ff), BF16),
            jax.ShapeDtypeStruct((count, ff), BF16),
            jax.ShapeDtypeStruct((count, width), BF16),
        ],
        scratch_shapes=[pltpu.VMEM((tok, width), F32)],
        compiler_params=pltpu.CompilerParams(vmem_limit_bytes=VMEM_LIMIT),
        cost_estimate=pl.CostEstimate(
            flops=6 * count * width * ff, bytes_accessed=40_000_000, transcendentals=0
        ),
        name="ff_back",
    )(grad, gate_slope, up_slope, gate_weight, up_weight, down_weight, first)


def deal_kernel(
    key_head, places, wide, query_ref, key_ref, value_ref, gate_ref, up_ref, heads_ref, gates_ref, ups_ref
):
    deal_heads(key_head, query_ref, key_ref, value_ref, heads_ref)
    deal_units(places, wide, gate_ref, up_ref, gates_ref, ups_ref)


def deal_heads(key_head, query_ref, key_ref, value_ref, heads_ref):
    columns, k_columns = query_ref.shape[1] // 8, key_ref.shape[1] // 8
    for f in range(8):
        g = key_head(f)
        cols, k_cols = slice(g * columns, g * columns + columns), slice(g * k_columns, g * k_columns + k_columns)
        heads_ref[f, :, :columns] = query_ref[:, cols]
        heads_ref[f, :, columns:] = jnp.concatenate([key_ref[:, k_cols], value_ref[:, k_cols]], axis=1)


def deal_units(places, wide, gate_ref, up_ref, gates_ref, ups_ref):
    for at, (f, to) in enumerate(places):
        here, there = slice(at * wide, at * wide + wide), slice(to * wide, to * wide + wide)
        gates_ref[f, :, there] = gate_ref[:, here]
        ups_ref[f, :, there] = up_ref[:, here]


def collect_kernel(
    places, wide, gates_ref, ups_ref, gate_ref, up_ref, gain_ref, dgate_ref, dup_ref, dgain_ref
):
    total = jnp.zeros((gate_ref.shape[0], wide), F32)
    for at, (f, to) in enumerate(places):
        here, there = slice(at * wide, at * wide + wide), slice(to * wide, to * wide + wide)
        dgate, dup = gates_ref[f, :, there].astype(F32), ups_ref[f, :, there].astype(F32)
        dgate_ref[:, here] = dgate
        dup_ref[:, here] = dup
        total += gate_ref[:, here].astype(F32) * dgate + up_ref[:, here].astype(F32) * dup
    dgain_ref[...] = jnp.sum(total, axis=1, keepdims=True) / gain_ref[...]


def final_kernel(
    key_head, places, wide, first_ref, middle_ref, rows_ref, gain_ref, heads_ref, query_ref, key_ref, value_ref,
    gates_ref, ups_ref, gate_ref, up_ref, small_ref, outs_ref, down_ref, dhidden_ref, dquery_ref, dkey_ref,
    dvalue_ref, dgain_one_ref, dgate_ref, dup_ref, dgain_two_ref, dout_ref, ddown_ref,
):
    rows_w = gate_ref.shape[0]
    normal, inverse = norm_parts(rows_ref[...].astype(F32))
    grad = first_ref[...] * gain_ref[...]
    dhidden_ref[...] = middle_ref[...] + inverse * (
        grad - normal * jnp.mean(grad * normal, axis=-1, keepdims=True)
    )
    gains = jnp.transpose(jnp.broadcast_to(small_ref[0:1, :], (128, 128)))[:, 0:1]
    columns = query_ref.shape[1] // 8
    k_columns = key_ref.shape[1] // 8
    total = jnp.zeros((rows_w, columns), F32)
    k_total = jnp.zeros((rows_w, k_columns), F32)
    for f in range(8):
        b, l, g = f // 2, f % 2, key_head(f)
        both = heads_ref[b * 4 + l].astype(F32) + heads_ref[b * 4 + 2 + l].astype(F32)
        cols, k_cols = slice(g * columns, g * columns + columns), slice(g * k_columns, g * k_columns + k_columns)
        dquery = both[:, :columns]
        dkey, dvalue = both[:, columns : columns + k_columns], both[:, columns + k_columns :]
        dquery_ref[:, cols], dkey_ref[:, k_cols], dvalue_ref[:, k_cols] = dquery, dkey, dvalue
        total += query_ref[:, cols].astype(F32) * dquery
        k_total += key_ref[:, k_cols].astype(F32) * dkey + value_ref[:, k_cols].astype(F32) * dvalue
    dgain_one_ref[...] = (
        jnp.sum(total, axis=1, keepdims=True) + jnp.sum(k_total, axis=1, keepdims=True)
    ) / gains[:rows_w]
    total = jnp.zeros((rows_w, wide), F32)
    for at, (f, to) in enumerate(places):
        here, there = slice(at * wide, at * wide + wide), slice(to * wide, to * wide + wide)
        dgate, dup = gates_ref[f, :, there].astype(F32), ups_ref[f, :, there].astype(F32)
        dgate_ref[:, here] = dgate
        dup_ref[:, here] = dup
        total += gate_ref[:, here].astype(F32) * dgate + up_ref[:, here].astype(F32) * dup
    dgain_two_ref[...] = jnp.sum(total, axis=1, keepdims=True) / gains[rows_w : 2 * rows_w]
    dout_ref[...] = outs_ref[0].astype(F32) + outs_ref[1].astype(F32)
    ddown_ref[...] = down_ref[...]


def shards(
    hidden,
    teacher,
    lengths,
    attn_gain,
    w_query,
    key_projection,
    value_projection,
    w_out,
    mlp_gain,
    w_gate,
    w_up,
    w_down,
):
    dp_n, blk_n, hi_n, lo_n = (lax.axis_size(a) for a in ALL)
    group = blk_n * lo_n
    every = dp_n * blk_n * hi_n * lo_n
    hi, lo = lax.axis_index("hi"), lax.axis_index("lo")
    blk = lax.axis_index("blk")
    tok = hidden.shape[1]
    seq_len = tok * blk_n * hi_n * lo_n
    width = hidden.shape[2]
    rows_w = w_query.shape[0]
    units_w = w_down.shape[0]
    ff_part = w_gate.shape[1] // group

    block = lo_n * rows_w
    if block % 128 == 0:
        to_inner = [
            ((d * blk_n + b) * hi_n + h, (d * hi_n + h) * blk_n + b)
            for d in range(dp_n)
            for b in range(blk_n)
            for h in range(hi_n)
        ]
        reblock = block
    else:
        to_inner, reblock = [(0, 0)], width
    to_outer = [(to, at) for at, to in to_inner]

    def inner(a):
        if reblock == block:
            return a
        return a.reshape(-1, dp_n, blk_n, hi_n, block).transpose(0, 1, 3, 2, 4).reshape(-1, width)

    def outer(a):
        if reblock == block:
            return a
        return a.reshape(-1, dp_n, hi_n, blk_n, block).transpose(0, 1, 3, 2, 4).reshape(-1, width)

    key_head = lambda f: (f % lo_n) * blk_n + f // lo_n

    def head_columns(w):
        cols = w.shape[1] // group
        return w.reshape(rows_w, lo_n, blk_n, cols).transpose(2, 1, 0, 3).reshape(group, rows_w, cols)

    def head_columns_back(g):
        cols = g.shape[2]
        return (
            g.reshape(blk_n, lo_n, rows_w, cols).transpose(2, 1, 0, 3).reshape(rows_w, group * cols)
        )

    def unit_columns(w):
        return (
            w.reshape(rows_w, dp_n, blk_n, hi_n, lo_n, units_w)
            .transpose(2, 4, 0, 1, 3, 5)
            .reshape(group, rows_w, ff_part)
        )

    def unit_columns_back(g):
        return (
            g.reshape(blk_n, lo_n, rows_w, dp_n, hi_n, units_w)
            .transpose(2, 3, 0, 4, 1, 5)
            .reshape(rows_w, group * ff_part)
        )

    q_cols = w_query.shape[1] // group
    k_cols = key_projection.shape[1] // group
    ff_places = [
        (b * lo_n + l, d * hi_n + h)
        for d in range(dp_n)
        for b in range(blk_n)
        for h in range(hi_n)
        for l in range(lo_n)
    ]
    part_shape = jax.ShapeDtypeStruct((group, rows_w, ff_part), BF16)
    params = pltpu.CompilerParams(vmem_limit_bytes=VMEM_LIMIT)
    one_start = reblock == block and rows_w == HEAD_SIZE and blk_n == 4 and units_w % 128 == 0
    head_wide = q_cols + 2 * k_cols
    if one_start:
        pass
    elif units_w % 128 == 0:
        head_shape = jax.ShapeDtypeStruct((group, rows_w, q_cols + 2 * k_cols), BF16)
        head_parts, gate_parts, up_parts = pl.pallas_call(
            functools.partial(deal_kernel, key_head, ff_places, units_w),
            out_shape=[head_shape, part_shape, part_shape],
            compiler_params=params,
            name="deal",
        )(w_query, key_projection, value_projection, w_gate, w_up)
    else:
        head_parts = jnp.concatenate(
            [head_columns(w) for w in (w_query, key_projection, value_projection)], axis=2
        )
        gate_parts, up_parts = unit_columns(w_gate), unit_columns(w_up)

    pad = jnp.zeros((7 * 128 + 128 - 2 * rows_w - 1,), F32)
    small = jnp.concatenate(
        [attn_gain.astype(F32), mlp_gain.astype(F32), lengths.astype(F32), pad]
    ).reshape(8, 128)
    hi_index = hi.astype(jnp.int32).reshape(1)
    tables = rope_tables(seq_len)
    unit = lo_n * tok
    part_rows = group * rows_w
    if one_start:
        _, qkv_weight, smalls, out_rows, gate_parts, up_parts, downs, other_kv, normed_one, q, kv = (
            through_start(
                key_head,
                ff_places,
                units_w,
                (group, rows_w, head_wide),
                (group, rows_w, ff_part),
                (w_query, key_projection, value_projection, w_gate, w_up),
                hidden[0],
                small,
                w_out,
                w_down,
                tables,
            )
        )
    else:
        rows_all, qkv_weight, smalls, out_rows = comm_call(
            open_kernel,
            0,
            [hidden[0], head_parts, small, w_out],
            [
                ((group, tok, width), BF16),
                ((every, rows_w, head_wide), BF16),
                ((every, 8, 128), F32),
                ((hi_n, lo_n, rows_w, width), BF16),
            ],
            gather_scratch(tok, width)
            + sems(every // dp_n - 1)
            + sems((dp_n - 1) * every // dp_n)
            + sems(every - 1)
            + sems(3)
            + [
                pltpu.SemaphoreType.DMA((3,)),
                pltpu.VMEM((rows_w, head_wide), BF16),
                pltpu.VMEM((rows_w, width), BF16),
            ],
            "open",
        )
        qkv_weight = qkv_weight.reshape(width, head_wide)
        gain_one = smalls[:, 0, :rows_w].reshape(1, width)
        normed_one, q, kv = project(
            hi_index, rows_all.reshape(group * tok, width), gain_one, qkv_weight, tables, tok
        )
        other_kv, gate_parts, up_parts, downs = comm_call(
            keys_kernel,
            2,
            [kv, gate_parts, up_parts, w_down],
            [
                (kv.shape, BF16),
                (gate_parts.shape, BF16),
                (up_parts.shape, BF16),
                ((dp_n - 1,) + w_down.shape, BF16),
            ],
            sems(1) + swap_scratch((rows_w, ff_part)) * 2 + sems(dp_n - 1),
            "keys",
        )
    qkv_weight = qkv_weight.reshape(width, head_wide)
    gain_one = smalls[:, 0, :rows_w].reshape(1, width)
    gain_two = smalls[:, 0, rows_w : 2 * rows_w].reshape(1, width)
    valid_count = jnp.sum(smalls.reshape(every, -1)[:: every // dp_n, 2 * rows_w])
    gate_parts = gate_parts.reshape(part_rows, -1)
    up_parts = up_parts.reshape(part_rows, -1)
    gate_other = swap_pair(gate_parts, "hi")
    out_weight = lax.all_gather(out_rows.reshape(-1, width), ("dp", "blk"), axis=0, tiled=True)
    q = q.reshape(blk_n, unit, q_cols)
    kv, other_kv = kv.reshape(blk_n, unit, -1), other_kv.reshape(blk_n, unit, -1)
    scalars = jnp.stack([lengths[0], hi.astype(jnp.int32)])
    out_heads, log_heads = attend(scalars, q, kv, other_kv)
    if reblock == block:
        normed_two, middle, gate_weight, up_weight, down_other, _, gate = through_middle(
            out_heads.reshape(group, tok, q_cols),
            gate_parts,
            gate_other,
            up_parts,
            w_down,
            out_weight,
            hidden[0],
            gain_two,
            key_head,
            to_inner,
            reblock,
        )
        gate_weight = gate_weight.reshape(width, ff_part)
    else:
        dp_sems = sems(2 * (dp_n - 1))
        dp_scratch = [pltpu.SemaphoreType.DMA((2,)), pltpu.VMEM((2, part_rows, ff_part), BF16)]
        weight_shape = ((dp_n, hi_n, part_rows, ff_part), BF16)
        mixed, gate_weight, up_other = comm_call(
            heads_kernel,
            3,
            [out_heads.reshape(group, tok, q_cols), gate_parts, gate_other, up_parts],
            [((group, tok, q_cols), BF16), weight_shape, (up_parts.shape, BF16)],
            swap_scratch((tok, q_cols)) + dp_sems + sems(1) + dp_scratch,
            "heads",
        )
        gate_weight = gate_weight.reshape(width, ff_part)
        middle, normed_two = out_project(
            mixed, out_weight, hidden[0], gain_two, key_head, to_inner, reblock
        )

        normed_two, up_weight, down_other = comm_call(
            rows_kernel,
            4,
            [inner(normed_two), up_parts, up_other, w_down],
            [((group, tok, width), BF16), weight_shape, (w_down.shape, BF16)],
            gather_scratch(tok, width) + dp_sems + sems(1) + dp_scratch,
            "rows",
        )
        gate = dot32(normed_two.reshape(group * tok, width), gate_weight)
    normed_two = normed_two.reshape(group * tok, width)
    up_weight = up_weight.reshape(width, ff_part)
    dp_index = lax.axis_index("dp")
    own_first = hi == 0

    def by_hi(own, other):
        return jnp.stack([jnp.where(own_first, own, other), jnp.where(own_first, other, own)])

    down_parts = by_hi(w_down, down_other)
    if dp_n == 2:
        far = by_hi(downs[0], swap_pair(down_other, "dp"))
        dp_first = dp_index == 0
        down_parts = jnp.stack(
            [jnp.where(dp_first, down_parts, far), jnp.where(dp_first, far, down_parts)]
        )
    else:
        down_parts = lax.all_gather(down_parts, "dp", axis=0, tiled=False)
    down_weight = down_parts.reshape(-1, width)
    upward = dot32(normed_two, up_weight)
    sigma = jax.nn.sigmoid(gate)
    silu = gate * sigma
    units = (silu * upward).astype(BF16)
    gate_slope = (upward * sigma * (1.0 + gate * (1.0 - sigma))).astype(BF16)
    up_slope = silu.astype(BF16)
    result = middle + RESIDUAL_SCALE * ff_end(units, down_weight, 1)

    own_places = ((blk * hi_n + hi) * lo_n + lo) * tok + jnp.arange(tok)
    valid = own_places < lengths[0]
    misfit = jnp.where(valid[:, None], result - teacher[0].astype(F32), 0.0)
    squares = jnp.broadcast_to(jnp.sum(misfit * misfit), (8, 128))
    grad_result = misfit * (dp_n * seq_len / valid_count)

    branch = gather_square((RESIDUAL_SCALE * grad_result).astype(BF16), 5)
    down_sum = weight_grad_start(units, branch, branch)
    grad_gate_rows, grad_up_rows, grad_normal = ff_back(
        branch, gate_slope, up_slope, gate_weight, up_weight, down_weight, down_sum[0], 2 * tok
    )
    if dp_n == 2:
        down_got = swap_pair(down_sum[1], "dp")
        grad_normal, down_sum, gate_own, up_own, gate_stay, up_stay, gate_got, up_got = scatter_down(
            grad_normal, 9, (down_sum[0], down_got), normed_two, grad_gate_rows, grad_up_rows
        )
        gate_stay, up_stay = swap_pair(gate_stay, "dp"), swap_pair(up_stay, "dp")
    else:
        grad_normal = scatter_square(grad_normal, 9)
        down_sum = scatter_end(scatter_start(down_sum[0], "hi"), "hi")
        gate_own = weight_grad_start(normed_two, grad_gate_rows, grad_normal)[0]
        up_own = weight_grad_start(normed_two, grad_up_rows, grad_normal)[0]
        gate_stay = up_stay = gate_got = up_got = jnp.zeros(gate_own.shape[1:], BF16)
    grad_normal = outer(grad_normal)

    part_shape = (part_rows, ff_part)
    anywhere, inside = pl.BlockSpec(memory_space=pl.ANY), pl.BlockSpec(memory_space=pltpu.VMEM)
    grad_middle, attn_rows, dout, gate_away, up_away = pl.pallas_call(
        functools.partial(out_back_kernel, key_head, to_outer, reblock),
        in_specs=[inside] * 4 + [anywhere] * 5,
        out_specs=[inside] * 2 + [anywhere] + [inside] * 2,
        out_shape=[
            jax.ShapeDtypeStruct((tok, width), F32),
            jax.ShapeDtypeStruct((tok, width), BF16),
            jax.ShapeDtypeStruct((group, tok, q_cols), BF16),
            jax.ShapeDtypeStruct(part_shape, BF16),
            jax.ShapeDtypeStruct(part_shape, BF16),
        ],
        scratch_shapes=[
            pltpu.VMEM(out_weight.shape, BF16),
            pltpu.VMEM((tok, width), F32),
            pltpu.VMEM((group, tok, q_cols), BF16),
        ]
        + sems(7)
        + [
            pltpu.VMEM((2,) + part_shape, F32),
            pltpu.VMEM((2,) + part_shape, BF16),
            pltpu.SemaphoreType.DMA((2, 2)),
            pltpu.SemaphoreType.DMA((1,)),
        ],
        compiler_params=pltpu.CompilerParams(
            collective_id=6, has_side_effects=True, vmem_limit_bytes=VMEM_LIMIT
        ),
        cost_estimate=pl.CostEstimate(
            flops=2 * tok * width * width, bytes_accessed=60_000_000, transcendentals=0
        ),
        name="out_back",
    )(grad_normal, middle, grad_result, gain_two, out_weight, gate_own, gate_got, up_own, up_got)
    columns = (group, rows_w, ff_part)

    gate_dp, up_dp = gate_stay.reshape(columns), up_stay.reshape(columns)
    gate_hi, up_hi = (swap_pair(a, "hi").reshape(columns) for a in (gate_away, up_away))
    square_attn = lax.all_gather(attn_rows, SQUARE, axis=0, tiled=True)
    dout = dout.reshape(blk_n, unit, q_cols)
    dq, dkv = attend_back(scalars, q, kv, other_kv, dout, out_heads, log_heads, gate_away)
    dkv = dkv.reshape(2, group * tok, 2 * k_cols)
    sum_scratch = [pltpu.VMEM(columns, F32)] + [pltpu.VMEM(columns, BF16)] * 3
    sum_scratch.append(pltpu.SemaphoreType.DMA((3,)))
    own_out = dot32(out_heads.reshape(group * tok, q_cols), square_attn, ((0,), (0,))).astype(BF16)
    other_dkv, gate_parts = comm_call(
        dkeys_kernel,
        7,
        [dkv, gate_own.reshape((hi_n,) + columns), gate_dp, gate_hi, up_dp],
        [(dkv.shape[1:], BF16), (columns, BF16)],
        sems(1) + swap_scratch((rows_w, ff_part)) + sum_scratch,
        "dkeys",
    )
    grad_first, head_grads = project_back(
        hi_index,
        dq.reshape(group * tok, q_cols),
        dkv[0],
        other_dkv,
        normed_one,
        qkv_weight,
        tables,
        up_hi,
        unit,
    )
    head_grads = head_grads.reshape(dp_n, every // dp_n, rows_w, head_wide)
    with_out = dp_n == 2 and rows_w * hi_n * lo_n == q_cols
    arrays = [grad_first.reshape(group, tok, width), head_grads]
    arrays += [up_own.reshape((hi_n,) + columns), up_dp, up_hi, squares]
    shapes = [
        ((tok, width), F32),
        (head_grads.shape[1:], BF16),
        (columns, BF16),
        ((every, 8, 128), F32),
    ]
    scratch = scatter_scratch(tok, width) + sems(every // dp_n - 1) + sems(every - 1)
    scratch += [pltpu.SemaphoreType.DMA((2,)), pltpu.VMEM(head_grads.shape[1:], BF16)]
    scratch += [pltpu.VMEM((dp_n - 1,) + head_grads.shape[1:], BF16)]
    scratch += [pltpu.VMEM(head_grads.shape[1:], BF16), pltpu.SemaphoreType.DMA((2, dp_n - 1))]
    scratch += swap_scratch((rows_w, ff_part)) + sum_scratch
    if with_out:
        arrays.append(own_out.reshape(hi_n, lo_n, rows_w, width))
        shapes.append(((hi_n, rows_w, width), BF16))
        scratch += sems(5) + [pltpu.SemaphoreType.DMA((2,))]
        scratch += [pltpu.VMEM((hi_n, lo_n, rows_w, width), BF16)] * 3
    grad_first, head_grads, up_parts, squares, *outs = pl.pallas_call(
        functools.partial(close_kernel, with_out),
        in_specs=[anywhere] * len(arrays),
        out_specs=[pl.BlockSpec(memory_space=pltpu.VMEM)] + [anywhere] * (len(shapes) - 1),
        out_shape=[jax.ShapeDtypeStruct(shape, dtype) for shape, dtype in shapes],
        scratch_shapes=scratch,
        compiler_params=pltpu.CompilerParams(
            collective_id=8, has_side_effects=True, vmem_limit_bytes=VMEM_LIMIT
        ),
        cost_estimate=pl.CostEstimate(flops=0, bytes_accessed=120_000_000, transcendentals=0),
        name="close",
    )(*arrays)
    mse_loss = jnp.sum(squares[:, 0, 0]) / (width * valid_count)
    if with_out and units_w % 128 == 0 and 2 * rows_w == 128:
        shape = lambda *dims: jax.ShapeDtypeStruct(dims, F32)
        grads = pl.pallas_call(
            functools.partial(final_kernel, key_head, ff_places, units_w),
            out_shape=[
                shape(tok, width),
                shape(*w_query.shape),
                shape(*key_projection.shape),
                shape(*value_projection.shape),
                shape(rows_w, 1),
                shape(*w_gate.shape),
                shape(*w_up.shape),
                shape(rows_w, 1),
                shape(*w_out.shape),
                shape(*w_down.shape),
            ],
            compiler_params=params,
            name="final",
        )(
            grad_first,
            grad_middle,
            hidden[0],
            gain_one,
            head_grads,
            w_query,
            key_projection,
            value_projection,
            gate_parts,
            up_parts,
            w_gate,
            w_up,
            small,
            outs[0],
            down_sum,
        )
        return (
            result.astype(BF16)[None],
            mse_loss,
            grads[0][None],
            grads[4][:, 0],
            *grads[1:4],
            grads[8],
            grads[7][:, 0],
            grads[5],
            grads[6],
            grads[9],
        )
    if with_out:
        grad_out = jnp.sum(outs[0].astype(F32), axis=0)
    else:
        own_head = lo * blk_n + blk
        spread = jnp.where((jnp.arange(group) == own_head)[:, None, None], own_out[None], 0)
        grad_out = lax.psum_scatter(
            spread.reshape(width, width), ALL, scatter_dimension=0, tiled=True
        ).astype(F32)
    grad_first = grad_first * gain_one
    normal_one, inverse_one = norm_parts(hidden[0].astype(F32))
    grad_hidden = grad_middle + inverse_one * (
        grad_first - normal_one * jnp.mean(grad_first * normal_one, axis=-1, keepdims=True)
    )
    head_grads = jnp.sum(
        head_grads.reshape(blk_n, hi_n, lo_n, rows_w, head_wide).astype(F32), axis=1
    ).reshape(group, rows_w, head_wide)

    own_one, own_two = attn_gain.astype(F32)[:, None], mlp_gain.astype(F32)[:, None]
    grad_query = head_columns_back(head_grads[:, :, :q_cols])
    grad_key = head_columns_back(head_grads[:, :, q_cols : q_cols + k_cols])
    grad_value = head_columns_back(head_grads[:, :, q_cols + k_cols :])

    def row_sums(*pairs):
        return sum(jnp.sum(w.astype(F32) * g, axis=1, keepdims=True) for w, g in pairs)

    grad_gain_one = (
        row_sums((w_query, grad_query), (key_projection, grad_key), (value_projection, grad_value))
        / own_one
    )
    if units_w % 128 == 0:
        ff_shape = jax.ShapeDtypeStruct(w_gate.shape, F32)
        grad_gate, grad_up, grad_gain_two = pl.pallas_call(
            functools.partial(collect_kernel, ff_places, units_w),
            out_shape=[ff_shape, ff_shape, jax.ShapeDtypeStruct((rows_w, 1), F32)],
            compiler_params=params,
            name="collect",
        )(gate_parts, up_parts, w_gate, w_up, own_two)
    else:
        grad_gate = unit_columns_back(gate_parts.astype(F32))
        grad_up = unit_columns_back(up_parts.astype(F32))
        grad_gain_two = row_sums((w_gate, grad_gate), (w_up, grad_up)) / own_two
    return (
        result.astype(BF16)[None],
        mse_loss,
        grad_hidden[None],
        grad_gain_one[:, 0],
        grad_query,
        grad_key,
        grad_value,
        grad_out,
        grad_gain_two[:, 0],
        grad_gate,
        grad_up,
        down_sum,
    )


def solution(mesh):
    dp_n, blk_n, head_n = (mesh.shape[a] for a in ("dp", "blk", "head"))
    fine = Mesh(mesh.devices.reshape(dp_n, blk_n, 2, head_n // 2), ALL)
    tokens = P("dp", SEQ, None)
    rows, row = P(ALL, None), P(ALL)
    return jax.shard_map(
        shards,
        mesh=fine,
        in_specs=(tokens, tokens, P("dp"), row, rows, rows, rows, rows, row, rows, rows, rows),
        out_specs=(tokens, P(), tokens, row, rows, rows, rows, rows, row, rows, rows, rows),
        check_vma=False,
    )
```
